32 devices in a mesh: pencil: 8 (over z, y), lev: 4 (over x, core).
Axes of the slice: x: 2, y: 2, z: 4, core: 2. Of those that a mesh axis runs over, the one named last changes fastest.
Arguments:
- background_std: float32 [4, 4096, 2048], P('lev', 'pencil'), may hold values from 0.4 to 6.1
- x_kernel: float32 [4, 31], P('lev'), may hold values from -0.06 to 0.12
- y_kernel: float32 [4, 31], P('lev'), may hold values from -0.06 to 0.12
- obs_owner: int32 [8192, 1], P(('pencil', 'lev')), may hold values from 0 to 7; in each aligned block of 256 rows (0 to 255, 256 to 511, ...) at most 64 rows name the same one
- obs_cells: int32 [8192, 16], P(('pencil', 'lev')), may hold values from 0 to 1048575, as said below
- obs_weights: float32 [8192, 16], P(('pencil', 'lev')), may hold values from -0.05 to 0.2
- innovation: float32 [8192], P(('pencil', 'lev')), may hold values from -6 to 6
- obs_precision: float32 [8192], P(('pencil', 'lev')), may hold values from 0.25 to 4
- obs_counts: int32 [32], P(('pencil', 'lev')), may hold values from 129 to 256, as said below
Outputs:
- control: float32 [4, 2048, 4096], P('lev', 'pencil')
- increment: float32 [4, 4096, 2048], P('lev', 'pencil')
The draws below stay inside these ranges and needn't reach their ends.
Inputs may be any that keep to these rules, and one draw needn't show every extreme that they name: `obs_owner`: no device holds more than 64 observations of one owner, and some device reaches 64. `obs_cells`: indices into the owner's tile of 1 slabs by 512 columns by 2048 rows, flattened in that order. `obs_counts`: some device has all 256 slots live.
All inputs are finite; a program needn't handle non-finite values.
Results may differ from the reference program's by a relative error of at most 0.0001.
Values sent between devices are 32-bit elements; how exact they have to be, the bound alone decides.
No kernel may reach another device: no remote copies, remote signals or barrier semaphores. Data moves between devices by JAX's collectives and lax.ppermute only.
A program may use at most 64 MiB of HBM per device.

```python
import math
import jax
import jax.numpy as jnp
import numpy as np

NX = 4096
NY = 2048
KW = 31
ITERS = 2
SLAB_DEV = 1
OBS_DEV = 256
SLABS = 4
TILE_X = 512
CAP = 64
OBS_TOT = 8192
DEVICES_ALL = 32
N_PENCIL = 8
N_LEV = 4


def draw_background_std(key, part):
    latitude = 1.0 + 2.0 * jnp.arange(NY, dtype=jnp.float32) / (NY - 1)
    rough = jnp.exp(jax.random.uniform(key, (SLABS, NX, NY), jnp.float32, -0.7, 0.7))
    return rough * latitude[None, None, :]


def draw_obs_cells(key, part):
    keys = jax.random.split(key, 5)
    slab_pick = jax.random.randint(keys[0], (OBS_TOT, 1), 0, SLAB_DEV)
    anchor_col = jax.random.randint(keys[1], (OBS_TOT, 1), 0, TILE_X)
    anchor_row = jax.random.randint(keys[2], (OBS_TOT, 1), 0, NY)
    offset_col = jax.random.randint(keys[3], (OBS_TOT, 16), 0, 4)
    offset_row = jax.random.randint(keys[4], (OBS_TOT, 16), 0, 4)
    column = (anchor_col + offset_col) % TILE_X
    row_pick = (anchor_row + offset_row) % NY
    return (slab_pick * TILE_X * NY + column * NY + row_pick).astype(jnp.int32)


def draw_obs_counts(key, part):
    first, second = jax.random.split(key)
    base_count = OBS_DEV - jax.random.randint(first, (DEVICES_ALL,), 0, OBS_DEV // 2)
    chosen = jax.random.randint(second, (), 0, DEVICES_ALL)
    return jnp.where(jnp.arange(DEVICES_ALL) == chosen, OBS_DEV, base_count).astype(jnp.int32)


def shard_levels(stream_key, dims, cuts, low, top_value):
    def one(dim, blocks):
        heights = jax.random.uniform(jax.random.fold_in(jax.random.fold_in(stream_key, 6), dim), (blocks,), jnp.float32, low / len(cuts), top_value / len(cuts))
        return jnp.repeat(jnp.exp(heights), dims[dim] // blocks).reshape((-1,) + (1,) * (len(dims) - dim - 1))

    gain = one(*cuts[0])
    for cut in cuts[1:]:
        gain = gain * one(*cut)
    return gain


def assign_block(key, own, number, rows, amount, top, most, slope):
    sequence = jax.random.permutation(key, amount)
    heavy_load, ordinary = shares(amount, rows * top, most, slope, True), shares(amount, rows * top, most, slope, False)
    places = jnp.arange(amount)

    def named(sizes, offset_by):
        used = int((sizes > 0).sum())
        fixed = max(1, used // 4)
        shifted = fixed + (places - fixed + offset_by * (used - fixed)) % max(1, amount - fixed)
        return jnp.zeros((amount,), jnp.int32).at[sequence[jnp.where(places < fixed, places, shifted)]].set(jnp.asarray(sizes, jnp.int32))

    sizes = jnp.where(number % 4 == 0, named(heavy_load, number // 4), named(ordinary, number - number // 4 - 1))
    mixed = jax.random.permutation(jax.random.fold_in(own, 3), amount)
    giver, sink = mixed[0:amount // 2 * 2:2], mixed[1:amount // 2 * 2:2]
    slack = jnp.minimum(sizes[giver] - 1, most - sizes[sink]) // 2
    slack = jnp.where((giver == sequence[0]) | (sink == sequence[0]) | (sizes[sink] == 0), 0, jnp.maximum(slack, 0))
    shifted = jax.random.randint(jax.random.fold_in(own, 4), (amount // 2,), 0, 1 << 20) % (slack + 1)
    sizes = sizes.at[giver].add(-shifted).at[sink].add(shifted)
    labels = jnp.searchsorted(jnp.cumsum(sizes), jnp.arange(rows * top), side="right").astype(jnp.int32)
    grid = labels.reshape(top, rows).T
    grid = grid[jax.random.permutation(jax.random.fold_in(own, 1), rows)]
    offset_by = jax.random.randint(jax.random.fold_in(own, 2), (rows, 1), 0, top)
    return jnp.take_along_axis(grid, (jnp.arange(top)[None, :] + offset_by) % top, axis=1)


def shares(number_of, total, most, lean, full):
    portions = [(1 << 20) // math.isqrt(rank ** lean) + 1 for rank in range(1, number_of + 1)]
    largest = most if full else min(most, max(-(-total // number_of), total * portions[0] // sum(portions)))
    least = 1 if total - largest >= number_of - 1 else 0
    counts, surplus = [largest] + [least] * (number_of - 1), total - largest - least * (number_of - 1)
    while surplus > 0:
        candidates = [i for i in range(1, number_of) if counts[i] < largest] or [i for i in range(1, number_of) if counts[i] < most]
        mass, remaining = sum([portions[i] for i in candidates]), surplus
        for i in candidates:
            more = min(most - counts[i], max(1, remaining * portions[i] // mass), surplus)
            counts[i] = counts[i] + more
            surplus = surplus - more
    return np.array(counts)


def bell_draw(stream_key, extent, width, limit, cuts=(), held_as=jnp.bfloat16):
    values = jax.random.normal(stream_key, extent, jnp.float32) * width
    if len(cuts) > 0:
        values = shard_levels(stream_key, extent, cuts, -0.22, 0.18) * values
    return jnp.clip(values, min=-limit, max=limit).astype(held_as)


def setup_inputs(seed: int = 0) -> dict:
    key_of = jax.random.split(jax.random.key(seed), 10)
    background_std = draw_background_std(jax.random.fold_in(key_of[9], 71), 0)
    x_kernel = jnp.clip(-0.06 + 0.179999996 * jax.random.uniform(key_of[1], (SLABS, KW), jnp.float32) ** shard_levels(key_of[1], (SLABS, KW), ((0, 4),), -0.2, 0.2), -0.06, 0.12)
    y_kernel = jnp.clip(-0.06 + 0.179999996 * jax.random.uniform(key_of[2], (SLABS, KW), jnp.float32) ** shard_levels(key_of[2], (SLABS, KW), ((0, 4),), -0.2, 0.2), -0.06, 0.12)
    obs_owner_keys = jax.random.split(jax.random.fold_in(key_of[3], 1), OBS_TOT // OBS_DEV)
    obs_owner_turns = jax.random.permutation(jax.random.fold_in(key_of[3], 3), OBS_TOT // OBS_DEV)
    obs_owner = jax.vmap(lambda own, number: assign_block(jax.random.fold_in(key_of[3], 2), own, number, OBS_DEV, N_PENCIL, 1, CAP, 2))(obs_owner_keys, obs_owner_turns).reshape((OBS_TOT, 1))
    obs_cells = draw_obs_cells(jax.random.fold_in(key_of[9], 71), 0)
    obs_weights = jnp.clip(-0.05 + 0.25 * jax.random.uniform(key_of[5], (OBS_TOT, 16), jnp.float32) ** shard_levels(key_of[5], (OBS_TOT, 16), ((0, 32),), -0.2, 0.2), -0.05, 0.2)
    innovation = bell_draw(key_of[6], (OBS_TOT,), 1.0, 6.0, ((0, 32),), jnp.float32)
    obs_precision = jnp.clip(jnp.exp(math.log(4.0) - 2.7725887 * jax.random.uniform(key_of[7], (OBS_TOT,), jnp.float32) ** shard_levels(key_of[7], (OBS_TOT,), ((0, 32),), -0.2, 0.2)), 0.25, 4.0)
    obs_counts = draw_obs_counts(jax.random.fold_in(key_of[9], 71), 0)
    return dict(background_std=background_std, x_kernel=x_kernel, y_kernel=y_kernel, obs_owner=obs_owner, obs_cells=obs_cells, obs_weights=obs_weights, innovation=innovation, obs_precision=obs_precision, obs_counts=obs_counts)


def smooth(grid_field, kernel_taps, periodic):
    taps = kernel_taps.shape[1]
    margin = taps // 2
    length = grid_field.shape[2]
    if periodic:
        padded = jnp.concatenate([grid_field[:, :, length - margin:], grid_field, grid_field[:, :, :margin]], axis=2)
    else:
        padded = jnp.pad(grid_field, ((0, 0), (0, 0), (margin, margin)))
    result = jnp.zeros(grid_field.shape, jnp.float32)
    for offset in range(taps):
        result = result + kernel_taps[:, offset][:, None, None] * padded[:, :, offset:offset + length]
    return result


def reference(background_std, x_kernel, y_kernel, obs_owner, obs_cells, obs_weights, innovation, obs_precision, obs_counts):
    tile_cols = NX // N_PENCIL
    ordinal = jnp.arange(OBS_TOT, dtype=jnp.int32)
    holder = ordinal // OBS_DEV
    group = (holder % N_LEV)[:, None]
    living = ((ordinal % OBS_DEV) < obs_counts[holder]).astype(jnp.float32)
    slab_index = group * SLAB_DEV + obs_cells // (tile_cols * NY)
    column = obs_owner[:, 0:1] * tile_cols + (obs_cells // NY) % tile_cols
    flat_index = ((slab_index * NX + column) * NY + obs_cells % NY).astype(jnp.int32)
    weight = obs_precision * living

    def forward(grid_field):
        along_x = smooth(grid_field, x_kernel, True)
        return background_std * smooth(jnp.swapaxes(along_x, 1, 2), y_kernel, False)

    def adjoint(grid_field):
        along_y = smooth(background_std * grid_field, y_kernel[:, ::-1], False)
        return smooth(jnp.swapaxes(along_y, 1, 2), x_kernel[:, ::-1], True)

    def observe(grid_field):
        return jnp.sum(obs_weights * grid_field.reshape(-1)[flat_index], axis=1)

    def spread(values):
        total = jnp.zeros((SLABS * NX * NY,), jnp.float32)
        total = total.at[flat_index.reshape(-1)].add((obs_weights * values[:, None]).reshape(-1))
        return total.reshape(SLABS, NX, NY)

    gradient_rhs = adjoint(spread(weight * innovation))
    control = jnp.zeros_like(gradient_rhs)
    resid = gradient_rhs
    direction = gradient_rhs
    norm_now = jnp.sum(resid * resid)
    for iteration in range(ITERS):
        image = direction + adjoint(spread(weight * observe(forward(direction))))
        step_length = norm_now / jnp.sum(direction * image)
        control = control + step_length * direction
        resid = resid - step_length * image
        norm_next = jnp.sum(resid * resid)
        direction = resid + (norm_next / norm_now) * direction
        norm_now = norm_next
    return control, forward(control)
```

```python
import functools

import jax
import jax.numpy as jnp
import numpy as np
from jax import lax
from jax.experimental import pallas as pl
from jax.experimental.pallas import tpu as pltpu
from jax.sharding import PartitionSpec as P


BF = jnp.bfloat16
F32 = jnp.float32
I32 = jnp.int32
LANES = 128
WIDE = 256
HALO = 32
PAD = 16
PACK = 40
INFO = 24
GROUP = 8
COPIES = 4
VMEM_LIMIT = 58 * 1024 * 1024


def vmem():
    return pl.BlockSpec(memory_space=pltpu.VMEM)


def smem():
    return pl.BlockSpec(memory_space=pltpu.SMEM)


def hbm():
    return pl.BlockSpec(memory_space=pl.ANY)


def params():
    return pltpu.CompilerParams(vmem_limit_bytes=VMEM_LIMIT)


def split2(x):
    high = x.astype(BF)
    return high, (x - high.astype(F32)).astype(BF)


def split3(x):
    high = x.astype(BF)
    rest = x - high.astype(F32)
    mid = rest.astype(BF)
    return high, mid, (rest - mid.astype(F32)).astype(BF)


def mm(a, b):
    return jnp.dot(a, b, preferred_element_type=F32)


def mm_parts(a_parts, b_parts):
    (ah, al), (bh, bl) = a_parts, b_parts
    return mm(ah, bh) + (mm(al, bh) + mm(ah, bl))


def iota(shape, dim):
    return lax.broadcasted_iota(I32, shape, dim)


def pack_kernel(counts, owner, cells, weights, extra, out, *, parts, columns, height, margin):
    hold = owner.shape[0]
    shift = height.bit_length() - 1
    block = height // parts
    reach = 2 * margin
    row_id = iota((hold, hold), 0)
    col_id = iota((hold, hold), 1)
    eye = row_id == col_id
    col_f = col_id.astype(F32)
    live = iota((hold, 1), 0) < counts[0]
    cell = cells[...]
    column = lax.shift_right_logical(cell, jnp.full(cell.shape, shift, I32))
    row = cell & (height - 1)

    def any_of(mask):
        return jnp.max(jnp.where(mask, 1.0, 0.0), axis=1, keepdims=True)

    left = any_of(column < reach)
    right = any_of(column >= columns - reach)
    side = left + 3.0 * right - 2.0 * left * right
    key = jnp.where(live, owner[...].astype(F32) * 4.0 + side, 4.0 * parts)
    key_row = jnp.sum(jnp.where(eye, key, 0.0), axis=0, keepdims=True)
    before = (key_row < key) | ((key_row == key) & (col_id < row_id))
    rank = jnp.sum(jnp.where(before, 1.0, 0.0), axis=1, keepdims=True)
    perm = jnp.where(rank == col_f, 1.0, 0.0).astype(BF)

    def sort_cols(values):
        total = None
        for part in split3(values):
            term = lax.dot_general(
                part, perm, (((0,), (0,)), ((), ())), preferred_element_type=F32
            )
            total = term if total is None else total + term
        return total

    def sort_rows(values):
        total = None
        for part in split3(values):
            term = mm(part, perm)
            total = term if total is None else total + term
        return total

    sorted_cells = sort_cols(cell.astype(F32))
    sorted_weights = sort_cols(weights[...])
    rest = jnp.concatenate([extra[0:2, :], key_row, jnp.zeros((5, hold), F32)], axis=0)
    rest = sort_rows(rest)
    line = iota((8, hold), 0)
    stencil = cells.shape[1]

    def per_part(part, carry):
        low = part * block - margin
        high = (part + 1) * block + margin
        flag = jnp.where(live, any_of((row >= low) & (row < high)), 0.0)
        flag_row = jnp.sum(jnp.where(eye, flag, 0.0), axis=0, keepdims=True)
        place = jnp.sum(jnp.where(col_id < row_id, flag_row, 0.0), axis=1, keepdims=True)
        chosen = (place == col_f) & (flag > 0.0)
        listed = jnp.sum(jnp.where(chosen, rank, 0.0), axis=0, keepdims=True)
        amount = jnp.sum(flag_row, axis=1, keepdims=True)
        tail = jnp.where(line == 3, listed, jnp.where(line == 4, amount, rest))
        out[part, 0:stencil, :] = sorted_cells
        out[part, stencil : 2 * stencil, :] = sorted_weights
        out[part, 2 * stencil : 2 * stencil + 8, :] = tail
        return carry

    lax.fori_loop(0, parts, per_part, 0)


def band(shape, taps, shift):
    distance = iota(shape, 1) - iota(shape, 0) + shift
    result = jnp.zeros(shape, F32)
    for tap in range(taps.shape[0]):
        result = jnp.where(distance == tap, taps[tap], result)
    return result


def band_rev(shape, taps, shift):
    distance = iota(shape, 0) - iota(shape, 1) + shift
    result = jnp.zeros(shape, F32)
    for tap in range(taps.shape[0]):
        result = jnp.where(distance == tap, taps[tap], result)
    return result


def exact_nt(a, b):
    return lax.dot_general(
        a,
        b,
        (((1,), (1,)), ((), ())),
        precision=lax.Precision.HIGHEST,
        preferred_element_type=F32,
    )


def store_split(ref, index, value):
    high, low = split2(value)
    ref[(0,) + index] = high
    ref[(1,) + index] = low


def bands_kernel(kx, ky, lat2, lon2, lat1, lon1, *, rows_block):
    margin = kx.shape[0] // 2
    window = lat2.shape[2]
    first = band((window, window), ky, margin)
    reach = first[LANES : LANES + WIDE, :]
    place = iota((window, window), 1)
    for variant in range(3):
        kept = first
        if variant == 0:
            kept = jnp.where(place >= LANES, first, 0.0)
        if variant == 2:
            kept = jnp.where(place < LANES + WIDE, first, 0.0)
        store_split(lat2, (variant,), exact_nt(kept, reach))
    size = lon2.shape[1]
    wide = size + 2 * HALO
    depth = (wide + 32 + LANES - 1) // LANES * LANES
    second = band((wide, depth), kx, -(16 - margin))
    store_split(lon2, (), exact_nt(second[HALO : HALO + size, :], second))
    store_split(lat1, (), band_rev((rows_block, rows_block + 2 * PAD), ky, PAD + margin))
    store_split(lon1, (), band((2 * WIDE, WIDE), kx, LANES + margin))


def for_each(sender_count, ranges, action):
    def per_sender(sender, carry):
        for low, high, tag in ranges(sender):

            def step(idx, inner, sender=sender, tag=tag):
                action(sender, idx, tag)
                return inner

            lax.fori_loop(low, high, step, 0)
        return carry

    lax.fori_loop(0, sender_count, per_sender, 0)


def zero_all(refs):
    rows = refs[0].shape[0]
    step = 256

    def clear(i, carry):
        for ref in refs:
            ref[pl.ds(pl.multiple_of(i * step, 8), step), :] = jnp.zeros((step, LANES), F32)
        return carry

    whole = rows // step
    lax.fori_loop(0, whole, clear, 0)
    if rows % step:
        for ref in refs:
            ref[whole * step : rows, :] = jnp.zeros((rows % step, LANES), F32)


def scatter_entries(copies, entry, lane, stencil):
    for start in range(0, stencil, len(copies)):
        group = []
        for j in range(min(len(copies), stencil - start)):
            address, value = entry(start + j)
            line = lax.shift_right_logical(address, 7)
            spread = jnp.where(lane == (address & (LANES - 1)), value, 0.0)
            group.append((copies[j], line, copies[j][pl.ds(line, 1), :] + spread))
        for ref, line, value in group:
            ref[pl.ds(line, 1), :] = value


def apply_kernel(
    *refs, first, columns, height, hold, stencil, capacity, senders, parts, table
):
    refs = list(refs)
    meta, addr_h, wgt_h, val_h, start_h = refs[:5]
    del refs[:5]
    if first:
        prec_h = refs.pop(0)
    std, std_l, std_r, lat2, lon2 = refs[:5]
    field, info = refs[5:7]
    del refs[:7]
    if first:
        column_info = refs.pop(0)
    addr, wgt, val, start = refs[:4]
    del refs[:4]
    if first:
        prec, std_flat, reply = refs[:3]
        del refs[:3]
    sums, high_s, low_s = refs[:3]
    del refs[:3]
    copies = refs[:COPIES]
    sems = refs[COPIES]

    me = meta[0]
    wide = columns + 2 * HALO
    blocks = height // LANES
    group = min(GROUP, senders)
    chunks = senders // group
    slots = senders * capacity
    lane = iota((1, LANES), 1)
    per = stencil * hold

    def chunk_copies(chunk):
        todo = [(addr_h, addr, group * per), (wgt_h, wgt, group * per)]
        todo.append((start_h, start, group * table))
        if first:
            todo.append((val_h, val, group * hold))
            todo.append((prec_h, prec, group * hold))
        result = []
        for i, (source, target, size) in enumerate(todo):
            part = source if chunks == 1 else source.at[pl.ds(chunk * size, size)]
            result.append(pltpu.make_async_copy(part, target, sems.at[i]))
        return result

    def load_chunk(chunk):
        for copy in chunk_copies(chunk):
            copy.start()
        for copy in chunk_copies(chunk):
            copy.wait()

    if not first:
        whole = pltpu.make_async_copy(val_h, val, sems.at[3])
        whole.start()
    if chunks == 1:
        pending = chunk_copies(0)
        for copy in pending:
            copy.start()
    zero_all(copies)
    zero_all([sums] + ([reply] if first else []))
    if chunks == 1:
        for copy in pending:
            copy.wait()
    if not first:
        whole.wait()

    after = lax.rem(me + 1, parts)
    ahead = lax.rem(me + parts - 1, parts)

    def start_of(sender, key):
        return start[sender * table + key]

    def scatter_chunk(chunk):
        def ranges(sender):
            for owner, low, high in ((me, 0, 4), (after, 1, 3), (ahead, 2, 4)):
                yield start_of(sender, owner * 4 + low), start_of(sender, owner * 4 + high), owner

        def action(sender, idx, owner):
            if first:
                value = val[sender * hold + idx]
            else:
                place = idx - start_of(sender, owner * 4)
                value = val[owner * slots + (chunk * group + sender) * capacity + place]
            base = sender * per + idx

            def entry(k):
                at = base + k * hold
                return addr[at], wgt[at] * value

            scatter_entries(copies, entry, lane, stencil)

        for_each(group, ranges, action)

    def over_chunks(work):
        if chunks == 1:
            work(0)
        else:

            def step(chunk, carry):
                load_chunk(chunk)
                work(chunk)
                return carry

            lax.fori_loop(0, chunks, step, 0)

    over_chunks(scatter_chunk)

    for jb in range(blocks):
        lanes = slice(jb * LANES, (jb + 1) * LANES)
        for low, size, source, at in (
            (0, HALO, std_l, 0),
            (HALO, columns, std, 0),
            (HALO + columns, HALO, std_r, 0),
        ):
            rows = slice(jb * wide + low, jb * wide + low + size)
            total = copies[0][rows, :]
            for ref in copies[1:]:
                total = total + ref[rows, :]
            high, lo = split2(total * source[:, lanes])
            high_s[low : low + size, lanes] = high
            low_s[low : low + size, lanes] = lo
        if first:
            std_flat[jb * wide + HALO : jb * wide + HALO + columns, :] = std[:, lanes]

    smoothed = copies[0]
    size = lon2.shape[1]
    count = height // WIDE
    for block in range(count):
        variant = 0 if block == 0 else (2 if block == count - 1 else 1)
        low = max(block * WIDE - LANES, 0)
        high = min(block * WIDE + WIDE + LANES, height)
        inner = slice(low - (block * WIDE - LANES), high - (block * WIDE - LANES))
        matrix = (lat2[0, variant, inner, :], lat2[1, variant, inner, :])
        along = mm_parts((high_s[:, low:high], low_s[:, low:high]), matrix)
        parts_y = split2(along)
        lanes = slice(block * WIDE, (block + 1) * WIDE)
        for part in range(columns // size):
            rows = slice(part * size, (part + 1) * size)
            window = slice(part * size, part * size + size + 2 * HALO)
            result = mm_parts(
                (lon2[0], lon2[1]), (parts_y[0][window, :], parts_y[1][window, :])
            )
            field[rows, lanes] = result
            scaled = result * std[rows, lanes]
            for half in range(WIDE // LANES):
                top = (block * (WIDE // LANES) + half) * wide + HALO + part * size
                smoothed[top : top + size, :] = scaled[:, half * LANES : (half + 1) * LANES]

    def gather_chunk(chunk):
        def ranges(sender):
            yield start_of(sender, me * 4), start_of(sender, me * 4 + 4), 0

        def action(sender, idx, tag):
            slot = (chunk * group + sender) * capacity + idx - start_of(sender, me * 4)
            base = sender * per + idx
            total = jnp.zeros((1, LANES), F32)
            factors = jnp.zeros((1, LANES), F32)
            for k in range(stencil):
                at = base + k * hold
                address = addr[at]
                weight = wgt[at]
                line = lax.shift_right_logical(address, 7)
                here = address & (LANES - 1)
                mask = lane == here
                total = total + jnp.where(mask, smoothed[pl.ds(line, 1), :] * weight, 0.0)
                if first:
                    picked = jnp.where(mask, std_flat[pl.ds(line, 1), :] * weight, 0.0)
                    move = lax.rem(k - here + LANES, LANES)
                    factors = factors + pltpu.roll(picked, move, 1)
            sums[pl.ds(slot, 1), :] = total
            if first:
                factors = jnp.where(lane == stencil, prec[sender * hold + idx], factors)
                factors = jnp.where(lane == stencil + 1, val[sender * hold + idx], factors)
                reply[pl.ds(slot, 1), :] = factors

        for_each(group, ranges, action)

    over_chunks(gather_chunk)

    total = jnp.sum(sums[...], axis=1, keepdims=True)
    lanes = iota((sums.shape[0], LANES), 1)
    if first:
        factors = reply[...]
        weight = jnp.sum(jnp.where(lanes == stencil, factors, 0.0), axis=1, keepdims=True)
        source = jnp.sum(jnp.where(lanes == stencil + 1, factors, 0.0), axis=1, keepdims=True)
        back = weight * total
        factors = jnp.where(lanes == stencil + 2, back, factors)
        factors = jnp.where(lanes == stencil + 3, total, factors)
        info[...] = factors.T[0:INFO, :]
        column_info[...] = jnp.where(
            iota(column_info.shape, 1) == 0,
            jnp.sum(source * total, axis=0, keepdims=True),
            jnp.sum(back * total, axis=0, keepdims=True),
        )
    else:
        info[...] = jnp.where(lanes == 0, total, 0.0).T[0:8, :]


def final_kernel(
    coef,
    addr_h,
    list_h,
    count_h,
    slot_h,
    reply_h,
    std,
    field0,
    field1,
    lat1,
    lon1,
    control,
    increment,
    addr,
    listed,
    amount,
    slot,
    reply,
    high_s,
    low_s,
    *rest,
    hold,
    stencil,
    capacity,
    senders,
    parts,
    length,
):
    copies = rest[:COPIES]
    sems = rest[COPIES]
    group = min(GROUP, senders)
    chunks = senders // group
    per = stencil * hold
    rows_block = control.shape[0]
    high_rows = rows_block + 2 * PAD
    lane = iota((1, LANES), 1)
    size_reply = parts * INFO * group * capacity
    stride = group * capacity

    def chunk_copies(chunk):
        todo = [
            (addr_h, addr, group * per),
            (list_h, listed, group * hold),
            (count_h, amount, group * LANES),
            (slot_h, slot, group * hold),
            (reply_h, reply, size_reply),
        ]
        result = []
        for i, (source, target, size) in enumerate(todo):
            part = source if chunks == 1 else source.at[pl.ds(chunk * size, size)]
            result.append(pltpu.make_async_copy(part, target, sems.at[i]))
        return result

    if chunks == 1:
        pending = chunk_copies(0)
        for copy in pending:
            copy.start()
    zero_all(copies)
    first, second = coef[0], coef[1]
    increment[...] = std[...] * (first * field0[...] + second * field1[...])

    def scatter_chunk():
        def ranges(sender):
            yield 0, amount[sender * LANES], 0

        def action(sender, at, tag):
            idx = listed[sender * hold + at]
            place = slot[sender * hold + idx]
            base = sender * per + idx
            value = (
                first * reply[place + (stencil + 1) * stride]
                + second * reply[place + (stencil + 2) * stride]
            )

            def entry(k):
                return addr[base + k * hold], reply[place + k * stride] * value

            scatter_entries(copies, entry, lane, stencil)

        for_each(group, ranges, action)

    if chunks == 1:
        for copy in pending:
            copy.wait()
        scatter_chunk()
    else:

        def step(chunk, carry):
            for copy in chunk_copies(chunk):
                copy.start()
            for copy in chunk_copies(chunk):
                copy.wait()
            scatter_chunk()
            return carry

        lax.fori_loop(0, chunks, step, 0)

    pair = WIDE // LANES
    count = length // WIDE
    for block in range(count):
        pieces = []
        for half in range(pair):
            rows = slice((block * pair + half) * high_rows, (block * pair + half + 1) * high_rows)
            total = copies[0][rows, :]
            for ref in copies[1:]:
                total = total + ref[rows, :]
            pieces.append(total)
        along = mm_parts((lat1[0], lat1[1]), split2(jnp.concatenate(pieces, axis=1)))
        high, low = split2(along)
        high_s[:, block * WIDE : (block + 1) * WIDE] = high
        low_s[:, block * WIDE : (block + 1) * WIDE] = low

    def window(ref, block):
        low, high = block * WIDE - LANES, (block + 1) * WIDE + LANES
        if low < 0:
            return jnp.concatenate([ref[:, length + low : length], ref[:, 0:high]], axis=1)
        if high > length:
            return jnp.concatenate([ref[:, low:length], ref[:, 0 : high - length]], axis=1)
        return ref[:, low:high]

    for block in range(count):
        control[:, block * WIDE : (block + 1) * WIDE] = mm_parts(
            (window(high_s, block), window(low_s, block)), (lon1[0], lon1[1])
        )


def body(
    background_std,
    x_kernel,
    y_kernel,
    obs_owner,
    obs_cells,
    obs_weights,
    innovation,
    obs_precision,
    obs_counts,
):
    parts = lax.axis_size("pencil")
    levels = lax.axis_size("lev")
    me = lax.axis_index("pencil")
    _, columns, height = background_std.shape
    hold, stencil = obs_cells.shape
    taps = x_kernel.shape[1]
    margin = taps // 2
    capacity = 2 * hold // parts
    senders = parts
    slots = senders * capacity
    rows_block = height // parts
    length = columns * parts
    blocks = height // LANES
    wide = columns + 2 * HALO
    table = (4 * parts + 1 + LANES - 1) // LANES * LANES
    group = min(GROUP, senders)
    chunks = senders // group
    std = background_std[0]

    right = [(p, (p + 1) % parts) for p in range(parts)]
    left = [(p, (p - 1) % parts) for p in range(parts)]
    std_l = lax.ppermute(std[columns - HALO :, :], "pencil", right)
    std_r = lax.ppermute(std[:HALO, :], "pencil", left)

    packed = pl.pallas_call(
        functools.partial(
            pack_kernel, parts=parts, columns=columns, height=height, margin=margin
        ),
        out_shape=jax.ShapeDtypeStruct((parts, PACK, hold), F32),
        in_specs=[smem(), vmem(), vmem(), vmem(), vmem()],
        out_specs=vmem(),
        compiler_params=params(),
        name="pack",
    )(
        obs_counts,
        obs_owner,
        obs_cells,
        obs_weights,
        jnp.concatenate([innovation[None, :], obs_precision[None, :]], axis=0),
    )
    recv = lax.all_to_all(packed, "pencil", split_axis=0, concat_axis=0, tiled=True)

    size = min(columns, WIDE)
    lat2, lon2, lat1, lon1 = pl.pallas_call(
        functools.partial(bands_kernel, rows_block=rows_block),
        out_shape=[
            jax.ShapeDtypeStruct((2, 3, 2 * WIDE, WIDE), BF),
            jax.ShapeDtypeStruct((2, size, size + 2 * HALO), BF),
            jax.ShapeDtypeStruct((2, rows_block, rows_block + 2 * PAD), BF),
            jax.ShapeDtypeStruct((2, 2 * WIDE, WIDE), BF),
        ],
        in_specs=[smem(), smem()],
        out_specs=[vmem()] * 4,
        compiler_params=params(),
        name="bands",
    )(x_kernel[0], y_kernel[0])

    cell = recv[:, :stencil, :].astype(I32)
    weights = recv[:, stencil : 2 * stencil, :]
    precision = recv[:, 2 * stencil + 1, :]
    source = precision * recv[:, 2 * stencil, :]
    key = recv[:, 2 * stencil + 2, :].astype(I32)
    listed = recv[:, 2 * stencil + 3, :].astype(I32)
    amount = recv[:, 2 * stencil + 4, :LANES].astype(I32)
    owner = key // 4
    offset = owner - me
    offset = jnp.where(offset > parts // 2, offset - parts, offset)
    offset = jnp.where(offset < -(parts // 2), offset + parts, offset)
    column = cell // height
    row = cell % height
    at = offset[:, None, :] * columns + column + HALO
    addr = jnp.where(
        (at >= 0) & (at < wide),
        ((row // LANES) * wide + at) * LANES + row % LANES,
        blocks * wide * LANES,
    )
    high_rows = rows_block + 2 * PAD
    at_row = row - (rows_block * me - PAD)
    whole_column = owner[:, None, :] * columns + column
    addr_rows = jnp.where(
        (at_row >= 0) & (at_row < high_rows) & (owner[:, None, :] < parts),
        ((whole_column // LANES) * high_rows + at_row) * LANES + whole_column % LANES,
        (length // LANES) * high_rows * LANES,
    )
    bound = jnp.arange(table, dtype=I32)
    start = jnp.sum((key[:, None, :] < bound[None, :, None]).astype(I32), axis=2)
    begin = start[:, 0 : 4 * parts : 4]
    mine = owner[:, None, :] == jnp.arange(parts, dtype=I32)[None, :, None]
    begin_own = jnp.sum(jnp.where(mine, begin[:, :, None], 0), axis=1)
    sender = jnp.arange(senders, dtype=I32)[:, None]
    slot = (
        jnp.minimum(owner, parts - 1) * (INFO * group * capacity)
        + (sender % group) * capacity
        + jnp.arange(hold, dtype=I32)[None, :]
        - begin_own
    )
    addr = addr.reshape(-1)
    weights = weights.reshape(-1)
    start = start.reshape(-1)

    acc = pltpu.VMEM((blocks * wide + 8, LANES), F32)
    static = dict(
        columns=columns,
        height=height,
        hold=hold,
        stencil=stencil,
        capacity=capacity,
        senders=senders,
        parts=parts,
        table=table,
    )
    per = group * stencil * hold
    meta = jnp.reshape(me, (1,)).astype(I32)
    smem_first = [
        pltpu.SMEM((per,), I32),
        pltpu.SMEM((per,), F32),
        pltpu.SMEM((group * hold,), F32),
        pltpu.SMEM((group * table,), I32),
        pltpu.SMEM((group * hold,), F32),
    ]
    work = [
        pltpu.VMEM((wide, height), BF),
        pltpu.VMEM((wide, height), BF),
    ] + [acc] * COPIES
    field0, reply, partial = pl.pallas_call(
        functools.partial(apply_kernel, first=True, **static),
        out_shape=[
            jax.ShapeDtypeStruct((columns, height), F32),
            jax.ShapeDtypeStruct((INFO, slots), F32),
            jax.ShapeDtypeStruct((8, LANES), F32),
        ],
        in_specs=[smem()] + [hbm()] * 5 + [vmem()] * 5,
        out_specs=[vmem()] * 3,
        scratch_shapes=smem_first
        + [acc, pltpu.VMEM((slots, LANES), F32), pltpu.VMEM((slots, LANES), F32)]
        + work
        + [pltpu.SemaphoreType.DMA((5,))],
        compiler_params=params(),
        name="apply_first",
    )(
        meta,
        addr,
        weights,
        source.reshape(-1),
        start,
        precision.reshape(-1),
        std,
        std_l,
        std_r,
        lat2,
        lon2,
    )

    def total_of(values):
        spread = jnp.broadcast_to(values[None], (parts * levels,) + values.shape)
        everyone = lax.all_to_all(
            spread, ("pencil", "lev"), split_axis=0, concat_axis=0, tiled=True
        )
        return jnp.sum(everyone, axis=0)

    replies = lax.all_to_all(
        jnp.broadcast_to(reply[None], (parts, INFO, slots)),
        "pencil",
        split_axis=0,
        concat_axis=0,
        tiled=True,
    )
    moments = total_of(partial)
    norm0, quad0 = moments[0, 0], moments[0, 1]
    back_all = replies[:, stencil + 2, :].reshape(-1)

    field1, second = pl.pallas_call(
        functools.partial(apply_kernel, first=False, **static),
        out_shape=[
            jax.ShapeDtypeStruct((columns, height), F32),
            jax.ShapeDtypeStruct((8, slots), F32),
        ],
        in_specs=[smem()] + [hbm()] * 4 + [vmem()] * 5,
        out_specs=[vmem()] * 2,
        scratch_shapes=[
            pltpu.SMEM((per,), I32),
            pltpu.SMEM((per,), F32),
            pltpu.SMEM((parts * slots,), F32),
            pltpu.SMEM((group * table,), I32),
            pltpu.VMEM((slots, LANES), F32),
        ]
        + work
        + [pltpu.SemaphoreType.DMA((5,))],
        compiler_params=params(),
        name="apply_second",
    )(meta, addr, weights, back_all, start, std, std_l, std_r, lat2, lon2)

    weight = reply[stencil]
    z0 = reply[stencil + 1]
    u = reply[stencil + 2]
    y0 = reply[stencil + 3]
    step0 = norm0 / (norm0 + quad0)
    resid = z0 - step0 * (z0 + u)
    image = y0 - step0 * (y0 + second[0])
    lanes = jnp.arange(LANES)[None, :]
    sums = [
        jnp.sum(resid * image),
        jnp.sum(resid * y0),
        jnp.sum(weight * image * image),
        jnp.sum(weight * image * y0),
    ]
    values = jnp.zeros((8, LANES), F32)
    for i, value in enumerate(sums):
        values = jnp.where(lanes == i, value, values)
    totals = total_of(values)
    norm1, cross, quad1, quad01 = (totals[0, i] for i in range(4))
    ratio = norm1 / norm0
    curvature = (
        norm1
        + 2.0 * ratio * cross
        + ratio * ratio * norm0
        + quad1
        + 2.0 * ratio * quad01
        + ratio * ratio * quad0
    )
    step1 = norm1 / curvature
    coef = jnp.stack([step0 + step1 * (1.0 - step0 + ratio), -step0 * step1])

    by_chunk = replies.reshape(parts, INFO, chunks, group * capacity)
    by_chunk = jnp.transpose(by_chunk, (2, 0, 1, 3)).reshape(-1)
    acc_rows = pltpu.VMEM(((length // LANES) * high_rows + 8, LANES), F32)
    control, increment = pl.pallas_call(
        functools.partial(
            final_kernel,
            hold=hold,
            stencil=stencil,
            capacity=capacity,
            senders=senders,
            parts=parts,
            length=length,
        ),
        out_shape=[
            jax.ShapeDtypeStruct((rows_block, length), F32),
            jax.ShapeDtypeStruct((columns, height), F32),
        ],
        in_specs=[smem()] + [hbm()] * 5 + [vmem()] * 5,
        out_specs=[vmem()] * 2,
        scratch_shapes=[
            pltpu.SMEM((per,), I32),
            pltpu.SMEM((group * hold,), I32),
            pltpu.SMEM((group * LANES,), I32),
            pltpu.SMEM((group * hold,), I32),
            pltpu.SMEM((parts * INFO * group * capacity,), F32),
            pltpu.VMEM((rows_block, length), BF),
            pltpu.VMEM((rows_block, length), BF),
        ]
        + [acc_rows] * COPIES
        + [pltpu.SemaphoreType.DMA((5,))],
        compiler_params=params(),
        name="outputs",
    )(
        coef,
        addr_rows.reshape(-1),
        listed.reshape(-1),
        amount.reshape(-1),
        slot.reshape(-1),
        by_chunk,
        std,
        field0,
        field1,
        lat1,
        lon1,
    )
    return control[None], increment[None]


def solution(mesh):
    return jax.shard_map(
        body,
        mesh=mesh,
        in_specs=(
            P("lev", "pencil", None),
            P("lev", None),
            P("lev", None),
            P(("pencil", "lev"), None),
            P(("pencil", "lev"), None),
            P(("pencil", "lev"), None),
            P(("pencil", "lev")),
            P(("pencil", "lev")),
            P(("pencil", "lev")),
        ),
        out_specs=(P("lev", "pencil", None), P("lev", "pencil", None)),
        check_vma=False,
    )
```

```python
import functools

import jax
import jax.numpy as jnp
import numpy as np
from jax import lax
from jax.experimental import pallas as pl
from jax.experimental.pallas import tpu as pltpu
from jax.sharding import PartitionSpec as P


BF = jnp.bfloat16
F32 = jnp.float32
I32 = jnp.int32
LANES = 128
WIDE = 256
HALO = 32
PAD = 16
PACK = 40
GROUP = 8
COPIES = 4
VMEM_LIMIT = 58 * 1024 * 1024


def vmem():
    return pl.BlockSpec(memory_space=pltpu.VMEM)


def smem():
    return pl.BlockSpec(memory_space=pltpu.SMEM)


def hbm():
    return pl.BlockSpec(memory_space=pl.ANY)


def params():
    return pltpu.CompilerParams(vmem_limit_bytes=VMEM_LIMIT)


def split2(x):
    high = x.astype(BF)
    return high, (x - high.astype(F32)).astype(BF)


def split3(x):
    high = x.astype(BF)
    rest = x - high.astype(F32)
    mid = rest.astype(BF)
    return high, mid, (rest - mid.astype(F32)).astype(BF)


def mm(a, b):
    return jnp.dot(a, b, preferred_element_type=F32)


def mm_parts(a_parts, b_parts):
    (ah, al), (bh, bl) = a_parts, b_parts
    return mm(ah, bh) + (mm(al, bh) + mm(ah, bl))


def iota(shape, dim):
    return lax.broadcasted_iota(I32, shape, dim)


def pack_kernel(
    counts, owner, cells, weights, depart, prec, out, *, parts, columns, height, margin
):
    stencil, hold = cells.shape
    shift = height.bit_length() - 1
    block = height // parts
    reach = 2 * margin
    row_id = iota((hold, hold), 0)
    col_id = iota((hold, hold), 1)
    eye = row_id == col_id
    col_f = col_id.astype(F32)
    live = iota((1, hold), 1) < counts[0]
    cell = cells[...]
    column = lax.shift_right_logical(cell, jnp.full(cell.shape, shift, I32))
    row = cell & (height - 1)

    def any_of(mask):
        return jnp.max(jnp.where(mask, 1.0, 0.0), axis=0, keepdims=True)

    def turn(line):
        return jnp.sum(jnp.where(eye, line, 0.0), axis=1, keepdims=True)

    left = any_of(column < reach)
    right = any_of(column >= columns - reach)
    side = left + 3.0 * right - 2.0 * left * right
    base = jnp.where(live, owner[...].astype(F32) * 4.0, 4.0 * parts)
    key = jnp.where(live, base + side, base)
    key_col = turn(key)
    before = (key_col < key) | ((key_col == key) & (row_id < col_id))
    rank = jnp.sum(jnp.where(before, 1.0, 0.0), axis=0, keepdims=True)
    begin = jnp.sum(jnp.where(key_col < base, 1.0, 0.0), axis=0, keepdims=True)
    rank_col = turn(rank)
    perm = jnp.where(rank_col == col_f, 1.0, 0.0).astype(BF)

    def sort(values):
        total = None
        for part in split3(values):
            term = mm(part, perm)
            total = term if total is None else total + term
        return total

    weight = jnp.where(live, prec[...], 0.0)
    rest = [weight * depart[...], weight, key, rank - begin, jnp.zeros((4, hold), F32)]
    values = [cell.astype(F32), weights[...]] + rest
    ordered = sort(jnp.concatenate(values, axis=0))
    line = iota((8, hold), 0)
    tail = ordered[2 * stencil : 2 * stencil + 8, :]
    for i in range(3):
        if i * hold <= 4 * parts:
            begins = jnp.sum(
                jnp.where(key_col < (col_f + float(i * hold)), 1.0, 0.0), axis=0, keepdims=True
            )
            tail = jnp.where(line == 5 + i, begins, tail)
    last = (line == 7) & (iota((8, hold), 1) == hold - 1)

    def per_part(part, carry):
        low = part * block - margin
        high = (part + 1) * block + margin
        flag = jnp.where(live, any_of((row >= low) & (row < high)), 0.0)
        place = jnp.sum(jnp.where(col_id < row_id, flag, 0.0), axis=1, keepdims=True)
        chosen = (place == col_f) & (turn(flag) > 0.0)
        listed = jnp.sum(jnp.where(chosen, rank_col, 0.0), axis=0, keepdims=True)
        amount = jnp.sum(flag, axis=1, keepdims=True)
        out[part, 0 : 2 * stencil, :] = ordered[0 : 2 * stencil, :]
        out[part, 2 * stencil : 2 * stencil + 8, :] = jnp.where(
            line == 4, listed, jnp.where(last, amount, tail)
        )
        return carry

    lax.fori_loop(0, parts, per_part, 0)


class Layout:
    def __init__(self, senders, hold, stencil, parts):
        lines = hold // LANES
        self.table = 3 * hold
        sizes = dict(
            addr=stencil * lines, rows=stencil * lines, listed=lines, slot=lines, back=lines
        )
        sizes.update(start=3 * lines)
        self.ints = {}
        at = 0
        for name, size in sizes.items():
            self.ints[name] = (at, size)
            at += senders * size
        self.int_rows = at
        self.floats = {}
        at = 0
        for name, size in dict(wgt=stencil * lines, val=lines, prec=lines).items():
            self.floats[name] = (at, size)
            at += senders * size
        self.float_rows = at


def unpack_kernel(
    meta, recv, ints, floats, *, layout, parts, columns, height, capacity, stencil, group
):
    senders, _, hold = recv.shape
    lines = hold // LANES
    me = meta[0]
    shift = height.bit_length() - 1
    wide = columns + 2 * HALO
    block = height // parts
    high_rows = block + 2 * PAD
    length = columns * parts
    slots = senders * capacity

    def put(ref, place, sender, value):
        begin, size = place
        count = value.shape[0]
        for i in range(lines):
            part = value[:, i * LANES : (i + 1) * LANES]
            if count % 8 == 0:
                at = pl.multiple_of(begin + sender * size + i * count, 8)
                ref[pl.ds(at, count), :] = part
            else:
                for j in range(count):
                    ref[pl.ds(begin + sender * size + i + j * lines, 1), :] = part[j : j + 1]

    def right(x, by):
        return lax.shift_right_logical(x, jnp.full(x.shape, by, I32))

    def per_sender(sender, carry):
        cell = recv[sender, 0:stencil, :].astype(I32)
        tail = recv[sender, 2 * stencil : 2 * stencil + 8, :]
        whole = tail.astype(I32)
        key = whole[2:3, :]
        pos = whole[3:4, :]
        owner = right(key, 2)
        offset = owner - me
        offset = jnp.where(offset > parts // 2, offset - parts, offset)
        offset = jnp.where(offset < -(parts // 2), offset + parts, offset)
        column = right(cell, shift)
        row = cell & (height - 1)
        at = offset * columns + column + HALO
        addr = jnp.where(
            (at >= 0) & (at < wide),
            (right(row, 7) * wide + at) * LANES + (row & (LANES - 1)),
            (height // LANES) * wide * LANES,
        )
        at_row = row - (block * me - PAD)
        across = owner * columns + column
        rows = jnp.where(
            (at_row >= 0) & (at_row < high_rows) & (owner < parts),
            (right(across, 7) * high_rows + at_row) * LANES + (across & (LANES - 1)),
            (length // LANES) * high_rows * LANES,
        )
        within = lax.rem(sender, group) * capacity + pos
        owner = jnp.minimum(owner, parts - 1)
        put(ints, layout.ints["addr"], sender, addr)
        put(ints, layout.ints["rows"], sender, rows)
        put(ints, layout.ints["listed"], sender, whole[4:5, :])
        put(ints, layout.ints["slot"], sender, owner * (stencil * group * capacity) + within)
        put(ints, layout.ints["back"], sender, owner * slots + sender * capacity + pos)
        put(ints, layout.ints["start"], sender, whole[5:8, :])
        put(floats, layout.floats["wgt"], sender, recv[sender, stencil : 2 * stencil, :])
        put(floats, layout.floats["val"], sender, tail[0:1, :])
        put(floats, layout.floats["prec"], sender, tail[1:2, :])
        return carry

    lax.fori_loop(0, senders, per_sender, 0)


def band(shape, taps, shift):
    distance = iota(shape, 1) - iota(shape, 0) + shift
    result = jnp.zeros(shape, F32)
    for tap in range(taps.shape[0]):
        result = jnp.where(distance == tap, taps[tap], result)
    return result


def band_rev(shape, taps, shift):
    distance = iota(shape, 0) - iota(shape, 1) + shift
    result = jnp.zeros(shape, F32)
    for tap in range(taps.shape[0]):
        result = jnp.where(distance == tap, taps[tap], result)
    return result


def exact_nt(a, b):
    return lax.dot_general(
        a,
        b,
        (((1,), (1,)), ((), ())),
        precision=lax.Precision.HIGHEST,
        preferred_element_type=F32,
    )


def store_split(ref, index, value):
    high, low = split2(value)
    ref[(0,) + index] = high
    ref[(1,) + index] = low


def bands_kernel(kx, ky, lat2, lon2, lat1, lon1, *, rows_block):
    margin = kx.shape[0] // 2
    window = lat2.shape[2]
    first = band((window, window), ky, margin)
    reach = first[LANES : LANES + WIDE, :]
    place = iota((window, window), 1)
    for variant in range(3):
        kept = first
        if variant == 0:
            kept = jnp.where(place >= LANES, first, 0.0)
        if variant == 2:
            kept = jnp.where(place < LANES + WIDE, first, 0.0)
        store_split(lat2, (variant,), exact_nt(kept, reach))
    size = lon2.shape[1]
    wide = size + 2 * HALO
    depth = (wide + 32 + LANES - 1) // LANES * LANES
    second = band((wide, depth), kx, -(16 - margin))
    store_split(lon2, (), exact_nt(second[HALO : HALO + size, :], second))
    store_split(lat1, (), band_rev((rows_block, rows_block + 2 * PAD), ky, PAD + margin))
    store_split(lon1, (), band((2 * WIDE, WIDE), kx, LANES + margin))


def pairs(low, high, action):
    def step(i, carry):
        one = low + 2 * i
        action(one, jnp.minimum(one + 1, high - 1), one + 1 < high)
        return carry

    lax.fori_loop(0, lax.shift_right_logical(high - low + 1, 1), step, 0)


def zero_all(refs):
    rows = refs[0].shape[0]
    step = 256

    def clear(i, carry):
        for ref in refs:
            ref[pl.ds(pl.multiple_of(i * step, 8), step), :] = jnp.zeros((step, LANES), F32)
        return carry

    whole = rows // step
    lax.fori_loop(0, whole, clear, 0)
    if rows % step:
        for ref in refs:
            ref[whole * step : rows, :] = jnp.zeros((rows % step, LANES), F32)


def scatter_entries(copies, entries, lane):
    for start in range(0, len(entries), len(copies)):
        group = []
        for ref, (address, value) in zip(copies, entries[start : start + len(copies)]):
            line = lax.shift_right_logical(address, 7)
            spread = jnp.where(lane == (address & (LANES - 1)), value, 0.0)
            group.append((ref, line, ref[pl.ds(line, 1), :] + spread))
        for ref, line, value in group:
            ref[pl.ds(line, 1), :] = value


def spot(sender, idx, per, stencil):
    return sender * per + idx + lax.shift_right_logical(idx, 7) * ((stencil - 1) * LANES)


def copy_parts(layout, source, target, place, chunk, chunks, group, sem):
    begin, size = place
    words = group * size * LANES
    at = begin * LANES + chunk * words
    return pltpu.make_async_copy(source.at[pl.ds(at, words)], target, sem)


def apply_kernel(
    *refs, first, layout, columns, height, hold, stencil, capacity, senders, parts, levels
):
    refs = list(refs)

    def take(count):
        taken = refs[:count]
        del refs[:count]
        return taken

    meta, ints, floats = take(3)
    if not first:
        back, moments, column_info = take(3)
    std_h, std_l_h, std_r_h, lat2_h, lon2_h = take(5)
    field_h, send = take(2)
    if first:
        factors_out, info_out = take(2)
    addr, wgt, start = take(3)
    if first:
        val, prec, std_flat, info, picked = take(5)
    sums, high_s, low_s, std, std_l, std_r, lat2, lon2, field = take(9)
    copies = take(COPIES)
    sems, in_sems, out_sems = take(3)

    me = meta[0]
    wide = columns + 2 * HALO
    blocks = height // LANES
    group = min(GROUP, senders)
    chunks = senders // group
    slots = senders * capacity
    lane = iota((1, LANES), 1)
    per = stencil * hold
    table = layout.table

    def chunk_copies(chunk):
        todo = [
            (ints, addr, layout.ints["addr"]),
            (floats, wgt, layout.floats["wgt"]),
            (ints, start, layout.ints["start"]),
        ]
        if first:
            todo.append((floats, val, layout.floats["val"]))
            todo.append((floats, prec, layout.floats["prec"]))
        return [
            copy_parts(layout, source, target, place, chunk, chunks, group, sems.at[i])
            for i, (source, target, place) in enumerate(todo)
        ]

    def load_chunk(chunk):
        for copy in chunk_copies(chunk):
            copy.start()
        for copy in chunk_copies(chunk):
            copy.wait()

    pending = []
    if chunks == 1:
        pending = chunk_copies(0)
        for copy in pending:
            copy.start()
    operands = [
        pltpu.make_async_copy(source, target, in_sems.at[i])
        for i, (source, target) in enumerate(
            (
                (std_h, std),
                (std_l_h, std_l),
                (std_r_h, std_r),
                (lat2_h, lat2),
                (lon2_h, lon2),
            )
        )
    ]
    for copy in operands:
        copy.start()
    zero_all(copies)
    zero_all([sums] + ([info] if first else []))
    for copy in pending:
        copy.wait()

    after = lax.rem(me + 1, parts)
    ahead = lax.rem(me + parts - 1, parts)

    def start_of(sender, key):
        return start[sender * table + key]

    def entries_of(sender, idx, value):
        base = spot(sender, idx, per, stencil)
        return [
            (addr[base + k * LANES], wgt[base + k * LANES] * value) for k in range(stencil)
        ]

    def scatter_chunk(chunk):
        def per_sender(sender, carry):
            for owner, low, high in ((me, 0, 4), (after, 1, 3), (ahead, 2, 4)):
                begin = start_of(sender, owner * 4)

                def value_of(idx, owner=owner, begin=begin):
                    if first:
                        return val[sender * hold + idx]
                    place = (chunk * group + sender) * capacity + idx - begin
                    return back[owner * (8 * LANES) + place]

                def action(one, two, has_two, value_of=value_of):
                    second = jnp.where(has_two, value_of(two), 0.0)
                    scatter_entries(
                        copies,
                        entries_of(sender, one, value_of(one)) + entries_of(sender, two, second),
                        lane,
                    )

                pairs(
                    start_of(sender, owner * 4 + low), start_of(sender, owner * 4 + high), action
                )
            return carry

        lax.fori_loop(0, group, per_sender, 0)

    def over_chunks(work):
        if chunks == 1:
            work(0)
        else:

            def step(chunk, carry):
                load_chunk(chunk)
                work(chunk)
                return carry

            lax.fori_loop(0, chunks, step, 0)

    over_chunks(scatter_chunk)
    for copy in operands:
        copy.wait()

    for jb in range(blocks):
        lanes = slice(jb * LANES, (jb + 1) * LANES)
        for low, size, source in (
            (0, HALO, std_l),
            (HALO, columns, std),
            (HALO + columns, HALO, std_r),
        ):
            rows = slice(jb * wide + low, jb * wide + low + size)
            total = copies[0][rows, :]
            for ref in copies[1:]:
                total = total + ref[rows, :]
            high, lo = split2(total * source[:, lanes])
            high_s[low : low + size, lanes] = high
            low_s[low : low + size, lanes] = lo
        if first:
            std_flat[jb * wide + HALO : jb * wide + HALO + columns, :] = std[:, lanes]

    smoothed = copies[0]
    size = lon2.shape[1]
    count = height // WIDE
    outgoing = []
    for block in range(count):
        variant = 0 if block == 0 else (2 if block == count - 1 else 1)
        low = max(block * WIDE - LANES, 0)
        high = min(block * WIDE + WIDE + LANES, height)
        inner = slice(low - (block * WIDE - LANES), high - (block * WIDE - LANES))
        matrix = (lat2[0, variant, inner, :], lat2[1, variant, inner, :])
        along = mm_parts((high_s[:, low:high], low_s[:, low:high]), matrix)
        parts_y = split2(along)
        lanes = slice(block * WIDE, (block + 1) * WIDE)
        for part in range(columns // size):
            rows = slice(part * size, (part + 1) * size)
            window = slice(part * size, part * size + size + 2 * HALO)
            result = mm_parts(
                (lon2[0], lon2[1]), (parts_y[0][window, :], parts_y[1][window, :])
            )
            field[rows, lanes] = result
            scaled = result * std[rows, lanes]
            for half in range(WIDE // LANES):
                top = (block * (WIDE // LANES) + half) * wide + HALO + part * size
                smoothed[top : top + size, :] = scaled[:, half * LANES : (half + 1) * LANES]
        outgoing.append(
            pltpu.make_async_copy(field.at[:, lanes], field_h.at[:, lanes], out_sems.at[block])
        )
        outgoing[-1].start()

    def gather_chunk(chunk):
        def per_sender(sender, carry):
            begin = start_of(sender, me * 4)

            def gather(idx):
                slot = (chunk * group + sender) * capacity + idx - begin
                base = spot(sender, idx, per, stencil)
                total = [jnp.zeros((1, LANES), F32)] * 4
                for k in range(stencil):
                    address = addr[base + k * LANES]
                    line = lax.shift_right_logical(address, 7)
                    spread = jnp.where(
                        lane == (address & (LANES - 1)), wgt[base + k * LANES], 0.0
                    )
                    total[k % 4] = total[k % 4] + spread * smoothed[pl.ds(line, 1), :]
                    if first:
                        picked[pl.ds(k * slots + slot, 1), :] = (
                            spread * std_flat[pl.ds(line, 1), :]
                        )
                sums[pl.ds(slot, 1), :] = (total[0] + total[1]) + (total[2] + total[3])
                if first:
                    info[pl.ds(slot, 1), :] = jnp.where(
                        lane == 0,
                        prec[sender * hold + idx],
                        jnp.where(lane == 1, val[sender * hold + idx], 0.0),
                    )

            def action(one, two, has_two):
                gather(one)
                gather(two)

            pairs(begin, start_of(sender, me * 4 + 4), action)
            return carry

        lax.fori_loop(0, group, per_sender, 0)

    over_chunks(gather_chunk)

    def whole(x):
        return jnp.sum(x, axis=0, keepdims=True)

    total = jnp.sum(sums[...], axis=1, keepdims=True)
    lanes = iota((slots, LANES), 1)
    lines = slots // LANES
    if first:
        known = info[...]
        weight = known[:, 0:1]
        source = known[:, 1:2]
        reply = weight * total
        known = jnp.where(lanes == 2, reply, jnp.where(lanes == 3, total, known))
        info_out[...] = known
        turned = known.T
        message = [turned[2:3, i * LANES : (i + 1) * LANES] for i in range(lines)]
        message.append(
            jnp.where(lane == 0, whole(source * total), jnp.where(lane == 1, whole(reply * total), 0.0))
        )
        message.append(jnp.zeros((8 - len(message), LANES), F32))
        message = jnp.concatenate(message, axis=0)
        ones = jnp.ones((8, LANES), BF)
        for k in range(stencil):
            row = None
            for part in split3(picked[k * slots : (k + 1) * slots, :]):
                term = lax.dot_general(
                    ones, part, (((1,), (1,)), ((), ())), preferred_element_type=F32
                )
                row = term if row is None else row + term
            factors_out[k : k + 1, :] = row[0:1, :]
    else:
        known = column_info[...]
        weight, source, reply, image0 = (known[:, i : i + 1] for i in range(4))
        slab = jnp.sum(moments[...], axis=0)[lines : lines + 1, :]
        length = slab[:, 0:1] / (slab[:, 0:1] + slab[:, 1:2])
        both = source + reply
        s_both = image0 + total
        resid = source - length * both
        s_resid = image0 - length * s_both
        values = [
            resid * s_resid,
            resid * s_both,
            both * s_both,
            resid * image0,
            both * image0,
            weight * s_resid * s_resid,
            weight * s_resid * s_both,
            weight * s_both * s_both,
            weight * s_resid * image0,
            weight * s_both * image0,
            source * image0,
            reply * image0,
        ]
        message = jnp.where(lane == len(values), length, 0.0)
        for i, value in enumerate(values):
            message = jnp.where(lane == i, whole(value), message)
        message = jnp.concatenate([message, jnp.zeros((7, LANES), F32)], axis=0)

    def send_to(i, carry):
        send[i] = message
        return carry

    lax.fori_loop(0, send.shape[0], send_to, 0)
    for copy in outgoing:
        copy.wait()


def final_kernel(
    ints,
    floats,
    factors_h,
    back,
    totals,
    std_h,
    field0_h,
    field1_h,
    lat1,
    lon1,
    control_h,
    increment_h,
    addr,
    listed,
    start,
    slot,
    back_at,
    val,
    factors,
    std,
    field0,
    field1,
    control,
    high_s,
    low_s,
    *rest,
    layout,
    hold,
    stencil,
    capacity,
    senders,
    parts,
    length,
):
    copies = rest[:COPIES]
    sems, in_sems, out_sems = rest[COPIES:]
    group = min(GROUP, senders)
    chunks = senders // group
    per = stencil * hold
    rows_block = control.shape[0]
    high_rows = rows_block + 2 * PAD
    lane = iota((1, LANES), 1)
    stride = group * capacity
    slots = senders * capacity

    def chunk_copies(chunk):
        todo = [
            (ints, addr, layout.ints["rows"]),
            (ints, listed, layout.ints["listed"]),
            (ints, start, layout.ints["start"]),
            (ints, slot, layout.ints["slot"]),
            (ints, back_at, layout.ints["back"]),
            (floats, val, layout.floats["val"]),
        ]
        result = [
            copy_parts(layout, source, target, place, chunk, chunks, group, sems.at[i])
            for i, (source, target, place) in enumerate(todo)
        ]
        words = parts * stencil * stride
        result.append(
            pltpu.make_async_copy(
                factors_h.at[pl.ds(chunk * words, words)], factors, sems.at[len(todo)]
            )
        )
        return result

    pending = []
    if chunks == 1:
        pending = chunk_copies(0)
        for copy in pending:
            copy.start()
    operands = [
        pltpu.make_async_copy(source, target, in_sems.at[i])
        for i, (source, target) in enumerate(
            ((std_h, std), (field0_h, field0), (field1_h, field1))
        )
    ]
    for copy in operands:
        copy.start()

    slabs = totals.shape[1]
    every = jnp.sum(totals[...], axis=0)
    norm0 = quad0 = None
    for i in range(slabs):
        line = every[i, 0:1, :]
        a, b = line[:, 10:11], line[:, 11:12]
        norm0 = a if norm0 is None else norm0 + a
        quad0 = b if quad0 is None else quad0 + b
    step0 = norm0 / (norm0 + quad0)
    norm1 = cross = quad1 = quad01 = jnp.zeros((1, 1), F32)
    for i in range(slabs):
        line = every[i, 0:1, :]
        v = [line[:, j : j + 1] for j in range(10)]
        shift = totals[0, i, 0:1, 12:13] - step0
        norm1 = norm1 + (v[0] + shift * (2.0 * v[1] + shift * v[2]))
        cross = cross + (v[3] + shift * v[4])
        quad1 = quad1 + (v[5] + shift * (2.0 * v[6] + shift * v[7]))
        quad01 = quad01 + (v[8] + shift * v[9])
    ratio = norm1 / norm0
    curvature = norm1 + quad1 + ratio * (
        2.0 * (cross + quad01) + ratio * (norm0 + quad0)
    )
    step1 = norm1 / curvature
    first = step0 + step1 * (1.0 - step0 + ratio)
    second = -step0 * step1
    first_line = jnp.broadcast_to(first, (1, LANES))
    second_line = jnp.broadcast_to(second, (1, LANES))

    zero_all(copies)
    for copy in operands:
        copy.wait()
    increment = field0
    increment[...] = std[...] * (first * field0[...] + second * field1[...])
    outgoing = [pltpu.make_async_copy(increment, increment_h, out_sems.at[0])]
    outgoing[0].start()

    def scatter_chunk():
        def per_sender(sender, carry):
            def entries_of(at, scale):
                idx = listed[sender * hold + at]
                place = slot[sender * hold + idx]
                base = spot(sender, idx, per, stencil)
                z0 = val[sender * hold + idx] * scale
                u = back[_back_index(back_at[sender * hold + idx], slots)] * scale
                value = first_line * z0 + second_line * u
                return [
                    (addr[base + k * LANES], factors[place + k * stride] * value)
                    for k in range(stencil)
                ]

            def action(one, two, has_two):
                scale = jnp.where(has_two, 1.0, 0.0)
                scatter_entries(copies, entries_of(one, 1.0) + entries_of(two, scale), lane)

            pairs(0, start[sender * layout.table + layout.table - 1], action)
            return carry

        lax.fori_loop(0, group, per_sender, 0)

    if chunks == 1:
        for copy in pending:
            copy.wait()
        scatter_chunk()
    else:

        def step(chunk, carry):
            for copy in chunk_copies(chunk):
                copy.start()
            for copy in chunk_copies(chunk):
                copy.wait()
            scatter_chunk()
            return carry

        lax.fori_loop(0, chunks, step, 0)

    pair = WIDE // LANES
    count = length // WIDE
    for block in range(count):
        pieces = []
        for half in range(pair):
            rows = slice((block * pair + half) * high_rows, (block * pair + half + 1) * high_rows)
            total = copies[0][rows, :]
            for ref in copies[1:]:
                total = total + ref[rows, :]
            pieces.append(total)
        along = mm_parts((lat1[0], lat1[1]), split2(jnp.concatenate(pieces, axis=1)))
        high, low = split2(along)
        high_s[:, block * WIDE : (block + 1) * WIDE] = high
        low_s[:, block * WIDE : (block + 1) * WIDE] = low

    def window(ref, block):
        low, high = block * WIDE - LANES, (block + 1) * WIDE + LANES
        if low < 0:
            return jnp.concatenate([ref[:, length + low : length], ref[:, 0:high]], axis=1)
        if high > length:
            return jnp.concatenate([ref[:, low:length], ref[:, 0 : high - length]], axis=1)
        return ref[:, low:high]

    every_lanes = 4
    for block in range(count):
        control[:, block * WIDE : (block + 1) * WIDE] = mm_parts(
            (window(high_s, block), window(low_s, block)), (lon1[0], lon1[1])
        )
        if block % every_lanes == every_lanes - 1:
            lanes = slice((block + 1 - every_lanes) * WIDE, (block + 1) * WIDE)
            outgoing.append(
                pltpu.make_async_copy(
                    control.at[:, lanes], control_h.at[:, lanes], out_sems.at[len(outgoing)]
                )
            )
            outgoing[-1].start()
    for copy in outgoing:
        copy.wait()


def _back_index(at, slots):
    return at + lax.div(at, slots) * (8 * LANES - slots)


def body(
    background_std,
    x_kernel,
    y_kernel,
    obs_owner,
    obs_cells,
    obs_weights,
    innovation,
    obs_precision,
    obs_counts,
):
    parts = lax.axis_size("pencil")
    levels = lax.axis_size("lev")
    me = lax.axis_index("pencil")
    _, columns, height = background_std.shape
    hold, stencil = obs_cells.shape
    margin = x_kernel.shape[1] // 2
    capacity = 2 * hold // parts
    senders = parts
    slots = senders * capacity
    rows_block = height // parts
    length = columns * parts
    blocks = height // LANES
    wide = columns + 2 * HALO
    group = min(GROUP, senders)
    chunks = senders // group
    layout = Layout(senders, hold, stencil, parts)
    std = background_std[0]

    packed = pl.pallas_call(
        functools.partial(
            pack_kernel, parts=parts, columns=columns, height=height, margin=margin
        ),
        out_shape=jax.ShapeDtypeStruct((parts, PACK, hold), F32),
        in_specs=[smem()] + [vmem()] * 5,
        out_specs=vmem(),
        compiler_params=params(),
        name="pack",
    )(
        obs_counts,
        obs_owner.T,
        obs_cells.T,
        obs_weights.T,
        innovation[None, :],
        obs_precision[None, :],
    )
    recv = lax.all_to_all(packed, "pencil", split_axis=0, concat_axis=0, tiled=True)

    right = [(p, (p + 1) % parts) for p in range(parts)]
    left = [(p, (p - 1) % parts) for p in range(parts)]
    std_l = lax.ppermute(std[columns - HALO :, :], "pencil", right)
    std_r = lax.ppermute(std[:HALO, :], "pencil", left)

    size = min(columns, WIDE)
    lat2, lon2, lat1, lon1 = pl.pallas_call(
        functools.partial(bands_kernel, rows_block=rows_block),
        out_shape=[
            jax.ShapeDtypeStruct((2, 3, 2 * WIDE, WIDE), BF),
            jax.ShapeDtypeStruct((2, size, size + 2 * HALO), BF),
            jax.ShapeDtypeStruct((2, rows_block, rows_block + 2 * PAD), BF),
            jax.ShapeDtypeStruct((2, 2 * WIDE, WIDE), BF),
        ],
        in_specs=[smem(), smem()],
        out_specs=[vmem()] * 4,
        compiler_params=params(),
        name="bands",
    )(x_kernel[0], y_kernel[0])

    meta = jnp.reshape(me, (1,)).astype(I32)
    ints, floats = pl.pallas_call(
        functools.partial(
            unpack_kernel,
            layout=layout,
            parts=parts,
            columns=columns,
            height=height,
            capacity=capacity,
            stencil=stencil,
            group=group,
        ),
        out_shape=[
            jax.ShapeDtypeStruct((layout.int_rows, LANES), I32),
            jax.ShapeDtypeStruct((layout.float_rows, LANES), F32),
        ],
        in_specs=[smem(), vmem()],
        out_specs=[vmem()] * 2,
        compiler_params=params(),
        name="unpack",
    )(meta, recv)
    ints = ints.reshape(-1)
    floats = floats.reshape(-1)

    acc = pltpu.VMEM((blocks * wide + 8, LANES), F32)
    column_slots = pltpu.VMEM((slots, LANES), F32)
    static = dict(
        layout=layout,
        columns=columns,
        height=height,
        hold=hold,
        stencil=stencil,
        capacity=capacity,
        senders=senders,
        parts=parts,
        levels=levels,
    )
    per = group * stencil * hold
    line = group * hold
    index_scratch = [
        pltpu.SMEM((per,), I32),
        pltpu.SMEM((per,), F32),
        pltpu.SMEM((group * layout.table,), I32),
    ]
    work = (
        [column_slots]
        + [pltpu.VMEM((wide, height), BF)] * 2
        + [
            pltpu.VMEM((columns, height), F32),
            pltpu.VMEM((HALO, height), F32),
            pltpu.VMEM((HALO, height), F32),
            pltpu.VMEM(lat2.shape, BF),
            pltpu.VMEM(lon2.shape, BF),
            pltpu.VMEM((columns, height), F32),
        ]
        + [acc] * COPIES
        + [
            pltpu.SemaphoreType.DMA((5,)),
            pltpu.SemaphoreType.DMA((5,)),
            pltpu.SemaphoreType.DMA((height // WIDE,)),
        ]
    )
    field_shape = jax.ShapeDtypeStruct((columns, height), F32)
    field0, message, factors, info = pl.pallas_call(
        functools.partial(apply_kernel, first=True, **static),
        out_shape=[
            field_shape,
            jax.ShapeDtypeStruct((parts, 8, LANES), F32),
            jax.ShapeDtypeStruct((stencil, slots), F32),
            jax.ShapeDtypeStruct((slots, LANES), F32),
        ],
        in_specs=[smem()] + [hbm()] * 7,
        out_specs=[hbm()] + [vmem()] * 3,
        scratch_shapes=index_scratch
        + [
            pltpu.SMEM((line,), F32),
            pltpu.SMEM((line,), F32),
            acc,
            column_slots,
            pltpu.VMEM((stencil * slots, LANES), F32),
        ]
        + work,
        compiler_params=params(),
        name="apply_first",
    )(meta, ints, floats, std, std_l, std_r, lat2, lon2)

    replies = lax.all_to_all(message, "pencil", split_axis=0, concat_axis=0, tiled=True)
    factors_all = lax.all_gather(factors, "pencil", axis=0)
    back = replies.reshape(-1)

    field1, sums = pl.pallas_call(
        functools.partial(apply_kernel, first=False, **static),
        out_shape=[
            field_shape,
            jax.ShapeDtypeStruct((parts * levels, 8, LANES), F32),
        ],
        in_specs=[smem()] + [hbm()] * 2 + [smem(), vmem(), vmem()] + [hbm()] * 5,
        out_specs=[hbm(), vmem()],
        scratch_shapes=index_scratch + work,
        compiler_params=params(),
        name="apply_second",
    )(meta, ints, floats, back, replies, info, std, std_l, std_r, lat2, lon2)

    totals = lax.all_to_all(sums, ("pencil", "lev"), split_axis=0, concat_axis=0, tiled=True)
    totals = totals.reshape(parts, levels, 8, LANES)

    by_chunk = factors_all.reshape(parts, stencil, chunks, group * capacity)
    by_chunk = jnp.transpose(by_chunk, (2, 0, 1, 3)).reshape(-1)
    high_rows = rows_block + 2 * PAD
    acc_rows = pltpu.VMEM(((length // LANES) * high_rows + 8, LANES), F32)
    control, increment = pl.pallas_call(
        functools.partial(
            final_kernel,
            layout=layout,
            hold=hold,
            stencil=stencil,
            capacity=capacity,
            senders=senders,
            parts=parts,
            length=length,
        ),
        out_shape=[
            jax.ShapeDtypeStruct((rows_block, length), F32),
            field_shape,
        ],
        in_specs=[hbm()] * 3 + [smem(), vmem()] + [hbm()] * 3 + [vmem()] * 2,
        out_specs=[hbm()] * 2,
        scratch_shapes=[
            pltpu.SMEM((per,), I32),
            pltpu.SMEM((line,), I32),
            pltpu.SMEM((group * layout.table,), I32),
            pltpu.SMEM((line,), I32),
            pltpu.SMEM((line,), I32),
            pltpu.SMEM((line,), F32),
            pltpu.SMEM((parts * stencil * group * capacity,), F32),
            pltpu.VMEM((columns, height), F32),
            pltpu.VMEM((columns, height), F32),
            pltpu.VMEM((columns, height), F32),
            pltpu.VMEM((rows_block, length), F32),
            pltpu.VMEM((rows_block, length), BF),
            pltpu.VMEM((rows_block, length), BF),
        ]
        + [acc_rows] * COPIES
        + [
            pltpu.SemaphoreType.DMA((7,)),
            pltpu.SemaphoreType.DMA((3,)),
            pltpu.SemaphoreType.DMA((1 + length // WIDE,)),
        ],
        compiler_params=params(),
        name="outputs",
    )(ints, floats, by_chunk, back, totals, std, field0, field1, lat1, lon1)
    return control[None], increment[None]


def solution(mesh):
    return jax.shard_map(
        body,
        mesh=mesh,
        in_specs=(
            P("lev", "pencil", None),
            P("lev", None),
            P("lev", None),
            P(("pencil", "lev"), None),
            P(("pencil", "lev"), None),
            P(("pencil", "lev"), None),
            P(("pencil", "lev")),
            P(("pencil", "lev")),
            P(("pencil", "lev")),
        ),
        out_specs=(P("lev", "pencil", None), P("lev", "pencil", None)),
        check_vma=False,
    )
```

```python
import functools

import jax
import jax.numpy as jnp
import numpy as np
from jax import lax
from jax.experimental import pallas as pl
from jax.experimental.pallas import tpu as pltpu
from jax.sharding import PartitionSpec as P


BF = jnp.bfloat16
F32 = jnp.float32
I32 = jnp.int32
LANES = 128
WIDE = 256
HALO = 32
PAD = 16
PACK = 40
GROUP = 8
COPIES = 4
VMEM_LIMIT = 58 * 1024 * 1024


def vmem():
    return pl.BlockSpec(memory_space=pltpu.VMEM)


def smem():
    return pl.BlockSpec(memory_space=pltpu.SMEM)


def hbm():
    return pl.BlockSpec(memory_space=pl.ANY)


def params():
    return pltpu.CompilerParams(vmem_limit_bytes=VMEM_LIMIT)


def split2(x):
    high = x.astype(BF)
    return high, (x - high.astype(F32)).astype(BF)


def split3(x):
    high = x.astype(BF)
    rest = x - high.astype(F32)
    mid = rest.astype(BF)
    return high, mid, (rest - mid.astype(F32)).astype(BF)


def mm(a, b):
    return jnp.dot(a, b, preferred_element_type=F32)


def mm_parts(a_parts, b_parts):
    (ah, al), (bh, bl) = a_parts, b_parts
    return mm(ah, bh) + (mm(al, bh) + mm(ah, bl))


def iota(shape, dim):
    return lax.broadcasted_iota(I32, shape, dim)


def pack_kernel(
    counts, owner, cells, weights, depart, prec, out, *, parts, columns, height, margin
):
    stencil, hold = cells.shape
    shift = height.bit_length() - 1
    block = height // parts
    reach = 2 * margin
    row_id = iota((hold, hold), 0)
    col_id = iota((hold, hold), 1)
    eye = row_id == col_id
    col_f = col_id.astype(F32)
    live = iota((1, hold), 1) < counts[0]
    cell = cells[...]
    column = lax.shift_right_logical(cell, jnp.full(cell.shape, shift, I32))
    row = cell & (height - 1)

    def any_of(mask):
        return jnp.max(jnp.where(mask, 1.0, 0.0), axis=0, keepdims=True)

    def turn(line):
        return jnp.sum(jnp.where(eye, line, 0.0), axis=1, keepdims=True)

    left = any_of(column < reach)
    right = any_of(column >= columns - reach)
    side = left + 3.0 * right - 2.0 * left * right
    base = jnp.where(live, owner[...].astype(F32) * 4.0, 4.0 * parts)
    key = jnp.where(live, base + side, base)
    key_col = turn(key)
    before = (key_col < key) | ((key_col == key) & (row_id < col_id))
    rank = jnp.sum(jnp.where(before, 1.0, 0.0), axis=0, keepdims=True)
    begin = jnp.sum(jnp.where(key_col < base, 1.0, 0.0), axis=0, keepdims=True)
    rank_col = turn(rank)
    perm = jnp.where(rank_col == col_f, 1.0, 0.0).astype(BF)

    def sort(values):
        total = None
        for part in split3(values):
            term = mm(part, perm)
            total = term if total is None else total + term
        return total

    weight = jnp.where(live, prec[...], 0.0)
    rest = [weight * depart[...], weight, key, rank - begin, jnp.zeros((4, hold), F32)]
    values = [cell.astype(F32), weights[...]] + rest
    ordered = sort(jnp.concatenate(values, axis=0))
    line = iota((8, hold), 0)
    tail = ordered[2 * stencil : 2 * stencil + 8, :]
    first_half = col_f < float(LANES)
    fourfold = 4.0 * jnp.where(first_half, col_f, col_f - float(LANES))
    for i, (low, high) in enumerate(((0.0, 4.0), (1.0, 3.0), (2.0, 2.0))):
        bound = fourfold + jnp.where(first_half, low, high)
        begins = jnp.sum(jnp.where(key_col < bound, 1.0, 0.0), axis=0, keepdims=True)
        tail = jnp.where(line == 5 + i, begins, tail)
    last = (line == 7) & (iota((8, hold), 1) == hold - 1)

    def per_part(part, carry):
        low = part * block - margin
        high = (part + 1) * block + margin
        flag = jnp.where(live, any_of((row >= low) & (row < high)), 0.0)
        place = jnp.sum(jnp.where(col_id < row_id, flag, 0.0), axis=1, keepdims=True)
        chosen = (place == col_f) & (turn(flag) > 0.0)
        listed = jnp.sum(jnp.where(chosen, rank_col, 0.0), axis=0, keepdims=True)
        amount = jnp.sum(flag, axis=1, keepdims=True)
        out[part, 0 : 2 * stencil, :] = ordered[0 : 2 * stencil, :]
        out[part, 2 * stencil : 2 * stencil + 8, :] = jnp.where(
            line == 4, listed, jnp.where(last, amount, tail)
        )
        return carry

    lax.fori_loop(0, parts, per_part, 0)


class Layout:
    def __init__(self, senders, hold, stencil, parts):
        lines = hold // LANES
        self.table = 3 * hold
        sizes = dict(
            addr=stencil * lines, rows=stencil * lines, listed=lines, slot=lines, start=3 * lines
        )
        self.ints = {}
        at = 0
        for name, size in sizes.items():
            self.ints[name] = (at, size)
            at += senders * size
        self.int_rows = at
        self.floats = {}
        at = 0
        for name, size in dict(wgt=stencil * lines, val=lines).items():
            self.floats[name] = (at, size)
            at += senders * size
        self.float_rows = at


def unpack_kernel(
    meta,
    recv,
    ints,
    floats,
    own_lines,
    own,
    own_sum,
    line_sum,
    *,
    layout,
    parts,
    columns,
    height,
    capacity,
    stencil,
    group,
):
    senders, _, hold = recv.shape
    lines = hold // LANES
    me = meta[0]
    shift = height.bit_length() - 1
    wide = columns + 2 * HALO
    block = height // parts
    high_rows = block + 2 * PAD
    length = columns * parts
    slots = senders * capacity

    def put(ref, place, sender, value):
        begin, size = place
        count = value.shape[0]
        for i in range(lines):
            part = value[:, i * LANES : (i + 1) * LANES]
            if count % 8 == 0:
                at = pl.multiple_of(begin + sender * size + i * count, 8)
                ref[pl.ds(at, count), :] = part
            else:
                for j in range(count):
                    ref[pl.ds(begin + sender * size + i + j * lines, 1), :] = part[j : j + 1]

    def right(x, by):
        return lax.shift_right_logical(x, jnp.full(x.shape, by, I32))

    def nt(a, b):
        return lax.dot_general(a, b, (((1,), (1,)), ((), ())), preferred_element_type=F32)

    own_sum[...] = jnp.zeros(own_sum.shape, F32)
    line_sum[...] = jnp.zeros(line_sum.shape, F32)
    place = iota((LANES, hold), 0)
    index = iota((LANES, hold), 1)

    def per_sender(sender, carry):
        cell = recv[sender, 0:stencil, :].astype(I32)
        tail = recv[sender, 2 * stencil : 2 * stencil + 8, :]
        whole = tail.astype(I32)
        key = whole[2:3, :]
        pos = whole[3:4, :]
        owner = right(key, 2)
        offset = owner - me
        offset = jnp.where(offset > parts // 2, offset - parts, offset)
        offset = jnp.where(offset < -(parts // 2), offset + parts, offset)
        column = right(cell, shift)
        row = cell & (height - 1)
        at = offset * columns + column + HALO
        addr = jnp.where(
            (at >= 0) & (at < wide),
            (right(row, 7) * wide + at) * LANES + (row & (LANES - 1)),
            (height // LANES) * wide * LANES,
        )
        at_row = row - (block * me - PAD)
        across = owner * columns + column
        rows = jnp.where(
            (at_row >= 0) & (at_row < high_rows) & (owner < parts),
            (right(across, 7) * high_rows + at_row) * LANES + (across & (LANES - 1)),
            (length // LANES) * high_rows * LANES,
        )
        within = lax.rem(sender, group) * capacity + pos
        owner = jnp.minimum(owner, parts - 1)
        put(ints, layout.ints["addr"], sender, addr)
        put(ints, layout.ints["rows"], sender, rows)
        put(ints, layout.ints["listed"], sender, whole[4:5, :])
        put(ints, layout.ints["slot"], sender, owner * (group * capacity) + within)
        put(ints, layout.ints["start"], sender, whole[5:8, :])
        put(floats, layout.floats["wgt"], sender, recv[sender, stencil : 2 * stencil, :])
        put(floats, layout.floats["val"], sender, tail[0:1, :])

        here = iota((1, LANES), 1) == me
        begin = jnp.sum(jnp.where(here, whole[5:6, :LANES], 0), axis=1, keepdims=True)
        end = jnp.sum(jnp.where(here, whole[5:6, LANES : 2 * LANES], 0), axis=1, keepdims=True)
        first_slot = sender * capacity
        block_of = first_slot // LANES
        within = place - (first_slot - block_of * LANES)
        chosen = (within >= 0) & (index == begin + within) & (index < end)
        select = jnp.where(chosen, 1.0, 0.0).astype(BF)
        fields = jnp.concatenate(
            [
                (addr & (LANES - 1)).astype(F32),
                recv[sender, stencil : 2 * stencil + 8, :],
                jnp.zeros((LANES - 2 * stencil - 8, hold), F32),
            ],
            axis=0,
        )
        total = None
        for part in split3(fields):
            term = nt(select, part)
            total = term if total is None else total + term
        own_sum[block_of] += total
        total = None
        for part in split2(right(addr, 7).astype(F32)):
            term = nt(part, select)
            total = term if total is None else total + term
        line_sum[block_of] += total
        return carry

    lax.fori_loop(0, senders, per_sender, 0)
    for i in range(slots // LANES):
        own[i * LANES : (i + 1) * LANES, :] = own_sum[i]
        own_lines[i * stencil : (i + 1) * stencil, :] = line_sum[i].astype(I32)


def band(shape, taps, shift):
    distance = iota(shape, 1) - iota(shape, 0) + shift
    result = jnp.zeros(shape, F32)
    for tap in range(taps.shape[0]):
        result = jnp.where(distance == tap, taps[tap], result)
    return result


def band_rev(shape, taps, shift):
    distance = iota(shape, 0) - iota(shape, 1) + shift
    result = jnp.zeros(shape, F32)
    for tap in range(taps.shape[0]):
        result = jnp.where(distance == tap, taps[tap], result)
    return result


def exact_nt(a, b):
    return lax.dot_general(
        a,
        b,
        (((1,), (1,)), ((), ())),
        precision=lax.Precision.HIGHEST,
        preferred_element_type=F32,
    )


def store_split(ref, index, value):
    high, low = split2(value)
    ref[(0,) + index] = high
    ref[(1,) + index] = low


def bands_kernel(kx, ky, lat2, lon2, lat1, lon1, *, rows_block):
    margin = kx.shape[0] // 2
    window = lat2.shape[2]
    first = band((window, window), ky, margin)
    reach = first[LANES : LANES + WIDE, :]
    place = iota((window, window), 1)
    for variant in range(3):
        kept = first
        if variant == 0:
            kept = jnp.where(place >= LANES, first, 0.0)
        if variant == 2:
            kept = jnp.where(place < LANES + WIDE, first, 0.0)
        store_split(lat2, (variant,), exact_nt(kept, reach))
    size = lon2.shape[1]
    wide = size + 2 * HALO
    depth = (wide + 32 + LANES - 1) // LANES * LANES
    second = band((wide, depth), kx, -(16 - margin))
    store_split(lon2, (), exact_nt(second[HALO : HALO + size, :], second))
    store_split(lat1, (), band_rev((rows_block, rows_block + 2 * PAD), ky, PAD + margin))
    store_split(lon1, (), band((2 * WIDE, WIDE), kx, LANES + margin))


def pairs(low, high, action):
    def step(i, carry):
        one = low + 2 * i
        action(one, jnp.minimum(one + 1, high - 1), one + 1 < high)
        return carry

    lax.fori_loop(0, lax.shift_right_logical(high - low + 1, 1), step, 0)


def zero_all(refs):
    rows = refs[0].shape[0]
    step = 256

    def clear(i, carry):
        for ref in refs:
            ref[pl.ds(pl.multiple_of(i * step, 8), step), :] = jnp.zeros((step, LANES), F32)
        return carry

    whole = rows // step
    lax.fori_loop(0, whole, clear, 0)
    if rows % step:
        for ref in refs:
            ref[whole * step : rows, :] = jnp.zeros((rows % step, LANES), F32)


def scatter_entries(copies, entries, lane):
    for start in range(0, len(entries), len(copies)):
        group = []
        for ref, (address, value) in zip(copies, entries[start : start + len(copies)]):
            line = lax.shift_right_logical(address, 7)
            spread = jnp.where(lane == (address & (LANES - 1)), value, 0.0)
            group.append((ref, line, ref[pl.ds(line, 1), :] + spread))
        for ref, line, value in group:
            ref[pl.ds(line, 1), :] = value


def spot(sender, idx, per, stencil):
    return sender * per + idx + lax.shift_right_logical(idx, 7) * ((stencil - 1) * LANES)


def copy_parts(layout, source, target, place, chunk, chunks, group, sem):
    begin, size = place
    words = group * size * LANES
    at = begin * LANES + chunk * words
    return pltpu.make_async_copy(source.at[pl.ds(at, words)], target, sem)


def apply_kernel(
    *refs, first, layout, columns, height, hold, stencil, capacity, senders, parts, levels
):
    refs = list(refs)

    def take(count):
        taken = refs[:count]
        del refs[:count]
        return taken

    meta, ints, floats, own_lines, own = take(5)
    if not first:
        replies_h, replies = take(2)
    std_h, std_l_h, std_r_h, lat2_h, lon2_h = take(5)
    field_h, send = take(2)
    if first:
        info_out = take(1)[0]
    addr, wgt, start, lines_s, val = take(5)
    if first:
        std_flat, picked = take(2)
    scale, spread, sums, high_s, low_s, std, std_l, std_r, lat2, lon2, field = take(11)
    copies = take(COPIES)
    sems, in_sems, out_sems, val_sem = take(4)

    me = meta[0]
    wide = columns + 2 * HALO
    blocks = height // LANES
    group = min(GROUP, senders)
    chunks = senders // group
    slots = senders * capacity
    lane = iota((1, LANES), 1)
    per = stencil * hold
    table = layout.table

    def chunk_copies(chunk):
        todo = [
            (ints, addr, layout.ints["addr"]),
            (floats, wgt, layout.floats["wgt"]),
            (ints, start, layout.ints["start"]),
        ]
        if first:
            todo.append((floats, val, layout.floats["val"]))
        return [
            copy_parts(layout, source, target, place, chunk, chunks, group, sems.at[i])
            for i, (source, target, place) in enumerate(todo)
        ]

    def load_chunk(chunk):
        for copy in chunk_copies(chunk):
            copy.start()
        for copy in chunk_copies(chunk):
            copy.wait()

    pending = []
    if chunks == 1:
        pending = chunk_copies(0)
        for copy in pending:
            copy.start()
    operands = [
        pltpu.make_async_copy(source, target, in_sems.at[i])
        for i, (source, target) in enumerate(
            (
                (std_h, std),
                (std_l_h, std_l),
                (std_r_h, std_r),
                (lat2_h, lat2),
                (lon2_h, lon2),
            )
        )
    ]
    own_copy = pltpu.make_async_copy(own_lines, lines_s, in_sems.at[5])
    own_copy.start()
    for copy in operands:
        copy.start()

    def value_copy(owner):
        at = pl.multiple_of(owner * (replies.shape[1] * LANES), 1024)
        return pltpu.make_async_copy(
            replies_h.at[pl.ds(at, slots)], val.at[pl.ds(owner * slots, slots)], val_sem.at[owner]
        )

    def each_owner(action):
        def step(owner, carry):
            action(value_copy(owner))
            return carry

        lax.fori_loop(0, parts, step, 0)

    if not first:
        each_owner(lambda copy: copy.start())
    zero_all(copies)
    zero_all([sums])

    lane_of = iota((slots, LANES), 1)
    known = own[...]
    value = known[:, 2 * stencil : 2 * stencil + 1]
    if not first:
        value = known[:, 2 * stencil + 2 : 2 * stencil + 3]
    scale[...] = jnp.broadcast_to(value, (slots, LANES))
    lane_f = lane_of.astype(F32)
    for k in range(stencil):
        spread[k * slots : (k + 1) * slots, :] = jnp.where(
            lane_f == known[:, k : k + 1], known[:, stencil + k : stencil + k + 1], 0.0
        )
    own_copy.wait()

    after = lax.rem(me + 1, parts)
    ahead = lax.rem(me + parts - 1, parts)

    def start_of(sender, owner, row, half):
        return start[sender * table + row * hold + half * LANES + owner]

    def entries_of(sender, idx, value):
        base = spot(sender, idx, per, stencil)
        return [
            (addr[base + k * LANES], wgt[base + k * LANES] * value) for k in range(stencil)
        ]

    def own_line(slot, k):
        at = lax.shift_right_logical(slot, 7) * ((stencil - 1) * LANES) + slot
        return lines_s[at + k * LANES]

    def own_pairs(chunk, action):
        def per_sender(sender, carry):
            amount = start_of(sender, me, 0, 1) - start_of(sender, me, 0, 0)
            base = (chunk * group + sender) * capacity
            pairs(base, base + amount, action)
            return carry

        lax.fori_loop(0, group, per_sender, 0)

    def scatter_own(chunk):
        def action(one, two, has_two):
            second = jnp.where(has_two, 1.0, 0.0)
            for slot, value in (
                (one, scale[pl.ds(one, 1), :]),
                (two, scale[pl.ds(two, 1), :] * second),
            ):
                for begin in range(0, stencil, COPIES):
                    todo = []
                    for j in range(min(COPIES, stencil - begin)):
                        line = own_line(slot, begin + j)
                        row = spread[pl.ds((begin + j) * slots + slot, 1), :] * value
                        todo.append((copies[j], line, copies[j][pl.ds(line, 1), :] + row))
                    for ref, line, row in todo:
                        ref[pl.ds(line, 1), :] = row

        own_pairs(chunk, action)

    def scatter_halo(chunk):
        def per_sender(sender, carry):
            for owner, low, high in ((after, (1, 0), (1, 1)), (ahead, (2, 0), (0, 1))):
                begin = start_of(sender, owner, 0, 0)

                def value_of(idx, owner=owner, begin=begin):
                    if first:
                        return val[sender * hold + idx]
                    place = (chunk * group + sender) * capacity + idx - begin
                    return val[owner * slots + place]

                def action(one, two, has_two, value_of=value_of):
                    second = jnp.where(has_two, value_of(two), 0.0)
                    scatter_entries(
                        copies,
                        entries_of(sender, one, value_of(one)) + entries_of(sender, two, second),
                        lane,
                    )

                pairs(start_of(sender, owner, *low), start_of(sender, owner, *high), action)
            return carry

        lax.fori_loop(0, group, per_sender, 0)

    def scatter_chunk(chunk):
        scatter_own(chunk)
        scatter_halo(chunk)

    def over_chunks(work):
        if chunks == 1:
            work(0)
        else:

            def step(chunk, carry):
                load_chunk(chunk)
                work(chunk)
                return carry

            lax.fori_loop(0, chunks, step, 0)

    for copy in pending:
        copy.wait()
    if not first:
        each_owner(lambda copy: copy.wait())
    over_chunks(scatter_chunk)
    for copy in operands:
        copy.wait()

    for jb in range(blocks):
        lanes = slice(jb * LANES, (jb + 1) * LANES)
        for low, size, source in (
            (0, HALO, std_l),
            (HALO, columns, std),
            (HALO + columns, HALO, std_r),
        ):
            rows = slice(jb * wide + low, jb * wide + low + size)
            total = copies[0][rows, :]
            for ref in copies[1:]:
                total = total + ref[rows, :]
            high, lo = split2(total * source[:, lanes])
            high_s[low : low + size, lanes] = high
            low_s[low : low + size, lanes] = lo
        if first:
            std_flat[jb * wide + HALO : jb * wide + HALO + columns, :] = std[:, lanes]

    smoothed = copies[0]
    size = lon2.shape[1]
    count = height // WIDE
    outgoing = []
    for block in range(count):
        variant = 0 if block == 0 else (2 if block == count - 1 else 1)
        low = max(block * WIDE - LANES, 0)
        high = min(block * WIDE + WIDE + LANES, height)
        inner = slice(low - (block * WIDE - LANES), high - (block * WIDE - LANES))
        matrix = (lat2[0, variant, inner, :], lat2[1, variant, inner, :])
        along = mm_parts((high_s[:, low:high], low_s[:, low:high]), matrix)
        parts_y = split2(along)
        lanes = slice(block * WIDE, (block + 1) * WIDE)
        for part in range(columns // size):
            rows = slice(part * size, (part + 1) * size)
            window = slice(part * size, part * size + size + 2 * HALO)
            result = mm_parts(
                (lon2[0], lon2[1]), (parts_y[0][window, :], parts_y[1][window, :])
            )
            field[rows, lanes] = result
            scaled = result * std[rows, lanes]
            for half in range(WIDE // LANES):
                top = (block * (WIDE // LANES) + half) * wide + HALO + part * size
                smoothed[top : top + size, :] = scaled[:, half * LANES : (half + 1) * LANES]
        outgoing.append(
            pltpu.make_async_copy(field.at[:, lanes], field_h.at[:, lanes], out_sems.at[block])
        )
        outgoing[-1].start()

    def gather_chunk(chunk):
        def gather(slot):
            total = [jnp.zeros((1, LANES), F32)] * 4
            for k in range(stencil):
                line = own_line(slot, k)
                row = spread[pl.ds(k * slots + slot, 1), :]
                total[k % 4] = total[k % 4] + row * smoothed[pl.ds(line, 1), :]
                if first:
                    picked[pl.ds(k * slots + slot, 1), :] = row * std_flat[pl.ds(line, 1), :]
            sums[pl.ds(slot, 1), :] = (total[0] + total[1]) + (total[2] + total[3])

        def action(one, two, has_two):
            gather(one)
            gather(two)

        own_pairs(chunk, action)

    over_chunks(gather_chunk)

    def whole(x):
        return jnp.sum(x, axis=0, keepdims=True)

    total = jnp.sum(sums[...], axis=1, keepdims=True)
    lines = slots // LANES
    known = own[...]
    source, weight, reply, image0 = (
        known[:, 2 * stencil + i : 2 * stencil + i + 1] for i in range(4)
    )
    if first:
        reply = weight * total
        known = jnp.where(lane_of == 2 * stencil + 2, reply, known)
        known = jnp.where(lane_of == 2 * stencil + 3, total, known)
        info_out[...] = known
        turned = known.T[2 * stencil + 2 : 2 * stencil + 3, :]
        message = [turned[:, i * LANES : (i + 1) * LANES] for i in range(lines)]
        message.append(
            jnp.where(
                lane == 0, whole(source * total), jnp.where(lane == 1, whole(reply * total), 0.0)
            )
        )
        message.append(jnp.zeros((8 - len(message), LANES), F32))
        ones = jnp.ones((8, LANES), BF)
        for k in range(stencil):
            row = None
            for part in split3(picked[k * slots : (k + 1) * slots, :]):
                term = lax.dot_general(
                    ones, part, (((1,), (1,)), ((), ())), preferred_element_type=F32
                )
                row = term if row is None else row + term
            for i in range(lines):
                message.append(row[0:1, i * LANES : (i + 1) * LANES])
        message = jnp.concatenate(message, axis=0)
    else:
        slab = jnp.sum(replies[:, 0:8, :], axis=0)[lines : lines + 1, :]
        length = slab[:, 0:1] / (slab[:, 0:1] + slab[:, 1:2])
        both = source + reply
        s_both = image0 + total
        resid = source - length * both
        s_resid = image0 - length * s_both
        values = [
            resid * s_resid,
            resid * s_both,
            both * s_both,
            resid * image0,
            both * image0,
            weight * s_resid * s_resid,
            weight * s_resid * s_both,
            weight * s_both * s_both,
            weight * s_resid * image0,
            weight * s_both * image0,
            source * image0,
            reply * image0,
        ]
        message = jnp.where(lane == len(values), length, 0.0)
        for i, value in enumerate(values):
            message = jnp.where(lane == i, whole(value), message)
        message = jnp.concatenate([message, jnp.zeros((7, LANES), F32)], axis=0)

    def send_to(i, carry):
        send[i] = message
        return carry

    lax.fori_loop(0, send.shape[0], send_to, 0)
    for copy in outgoing:
        copy.wait()


def final_kernel(
    ints,
    floats,
    replies_h,
    totals,
    std_h,
    field0_h,
    field1_h,
    lat1,
    lon1,
    control_h,
    increment_h,
    addr,
    listed,
    start,
    slot,
    val,
    factors,
    std,
    field0,
    field1,
    control,
    high_s,
    low_s,
    *rest,
    layout,
    hold,
    stencil,
    capacity,
    senders,
    parts,
    length,
):
    copies = rest[:COPIES]
    sems, in_sems, out_sems = rest[COPIES:]
    group = min(GROUP, senders)
    chunks = senders // group
    per = stencil * hold
    rows_block = control.shape[0]
    high_rows = rows_block + 2 * PAD
    lane = iota((1, LANES), 1)
    stride = group * capacity
    owner_words = factors.shape[0] // parts
    to_factors = owner_words - stencil * stride

    def chunk_copies(chunk):
        todo = [
            (ints, addr, layout.ints["rows"]),
            (ints, listed, layout.ints["listed"]),
            (ints, start, layout.ints["start"]),
            (ints, slot, layout.ints["slot"]),
            (floats, val, layout.floats["val"]),
        ]
        result = [
            copy_parts(layout, source, target, place, chunk, chunks, group, sems.at[i])
            for i, (source, target, place) in enumerate(todo)
        ]
        words = parts * owner_words
        result.append(
            pltpu.make_async_copy(
                replies_h.at[pl.ds(chunk * words, words)], factors, sems.at[len(todo)]
            )
        )
        return result

    pending = []
    if chunks == 1:
        pending = chunk_copies(0)
        for copy in pending:
            copy.start()
    operands = [
        pltpu.make_async_copy(source, target, in_sems.at[i])
        for i, (source, target) in enumerate(
            ((std_h, std), (field0_h, field0), (field1_h, field1))
        )
    ]
    for copy in operands:
        copy.start()

    slabs = totals.shape[1]
    every = jnp.sum(totals[...], axis=0)
    norm0 = quad0 = None
    for i in range(slabs):
        line = every[i, 0:1, :]
        a, b = line[:, 10:11], line[:, 11:12]
        norm0 = a if norm0 is None else norm0 + a
        quad0 = b if quad0 is None else quad0 + b
    step0 = norm0 / (norm0 + quad0)
    norm1 = cross = quad1 = quad01 = jnp.zeros((1, 1), F32)
    for i in range(slabs):
        line = every[i, 0:1, :]
        v = [line[:, j : j + 1] for j in range(10)]
        shift = totals[0, i, 0:1, 12:13] - step0
        norm1 = norm1 + (v[0] + shift * (2.0 * v[1] + shift * v[2]))
        cross = cross + (v[3] + shift * v[4])
        quad1 = quad1 + (v[5] + shift * (2.0 * v[6] + shift * v[7]))
        quad01 = quad01 + (v[8] + shift * v[9])
    ratio = norm1 / norm0
    curvature = norm1 + quad1 + ratio * (
        2.0 * (cross + quad01) + ratio * (norm0 + quad0)
    )
    step1 = norm1 / curvature
    first = step0 + step1 * (1.0 - step0 + ratio)
    second = -step0 * step1
    first_line = jnp.broadcast_to(first, (1, LANES))
    second_line = jnp.broadcast_to(second, (1, LANES))

    zero_all(copies)

    def scatter_chunk():
        def per_sender(sender, carry):
            def entries_of(at, scale):
                idx = listed[sender * hold + at]
                place = slot[sender * hold + idx]
                place = place + lax.div(place, stride) * (owner_words - stride)
                base = spot(sender, idx, per, stencil)
                z0 = val[sender * hold + idx] * scale
                u = factors[place] * scale
                value = first_line * z0 + second_line * u
                return [
                    (addr[base + k * LANES], factors[place + to_factors + k * stride] * value)
                    for k in range(stencil)
                ]

            def action(one, two, has_two):
                scale = jnp.where(has_two, 1.0, 0.0)
                scatter_entries(copies, entries_of(one, 1.0) + entries_of(two, scale), lane)

            pairs(0, start[sender * layout.table + layout.table - 1], action)
            return carry

        lax.fori_loop(0, group, per_sender, 0)

    if chunks == 1:
        for copy in pending:
            copy.wait()
        scatter_chunk()
    else:

        def step(chunk, carry):
            for copy in chunk_copies(chunk):
                copy.start()
            for copy in chunk_copies(chunk):
                copy.wait()
            scatter_chunk()
            return carry

        lax.fori_loop(0, chunks, step, 0)

    for copy in operands:
        copy.wait()
    increment = field0
    increment[...] = std[...] * (first * field0[...] + second * field1[...])
    outgoing = [pltpu.make_async_copy(increment, increment_h, out_sems.at[0])]
    outgoing[0].start()

    pair = WIDE // LANES
    count = length // WIDE
    for block in range(count):
        pieces = []
        for half in range(pair):
            rows = slice((block * pair + half) * high_rows, (block * pair + half + 1) * high_rows)
            total = copies[0][rows, :]
            for ref in copies[1:]:
                total = total + ref[rows, :]
            pieces.append(total)
        along = mm_parts((lat1[0], lat1[1]), split2(jnp.concatenate(pieces, axis=1)))
        high, low = split2(along)
        high_s[:, block * WIDE : (block + 1) * WIDE] = high
        low_s[:, block * WIDE : (block + 1) * WIDE] = low

    def window(ref, block):
        low, high = block * WIDE - LANES, (block + 1) * WIDE + LANES
        if low < 0:
            return jnp.concatenate([ref[:, length + low : length], ref[:, 0:high]], axis=1)
        if high > length:
            return jnp.concatenate([ref[:, low:length], ref[:, 0 : high - length]], axis=1)
        return ref[:, low:high]

    every_lanes = 4
    for block in range(count):
        control[:, block * WIDE : (block + 1) * WIDE] = mm_parts(
            (window(high_s, block), window(low_s, block)), (lon1[0], lon1[1])
        )
        if block % every_lanes == every_lanes - 1:
            lanes = slice((block + 1 - every_lanes) * WIDE, (block + 1) * WIDE)
            outgoing.append(
                pltpu.make_async_copy(
                    control.at[:, lanes], control_h.at[:, lanes], out_sems.at[len(outgoing)]
                )
            )
            outgoing[-1].start()
    for copy in outgoing:
        copy.wait()


def body(
    background_std,
    x_kernel,
    y_kernel,
    obs_owner,
    obs_cells,
    obs_weights,
    innovation,
    obs_precision,
    obs_counts,
):
    parts = lax.axis_size("pencil")
    levels = lax.axis_size("lev")
    me = lax.axis_index("pencil")
    _, columns, height = background_std.shape
    hold, stencil = obs_cells.shape
    margin = x_kernel.shape[1] // 2
    capacity = 2 * hold // parts
    senders = parts
    slots = senders * capacity
    rows_block = height // parts
    length = columns * parts
    blocks = height // LANES
    wide = columns + 2 * HALO
    group = min(GROUP, senders)
    chunks = senders // group
    layout = Layout(senders, hold, stencil, parts)
    std = background_std[0]

    packed = pl.pallas_call(
        functools.partial(
            pack_kernel, parts=parts, columns=columns, height=height, margin=margin
        ),
        out_shape=jax.ShapeDtypeStruct((parts, PACK, hold), F32),
        in_specs=[smem()] + [vmem()] * 5,
        out_specs=vmem(),
        compiler_params=params(),
        name="pack",
    )(
        obs_counts,
        obs_owner.T,
        obs_cells.T,
        obs_weights.T,
        innovation[None, :],
        obs_precision[None, :],
    )
    recv = lax.all_to_all(packed, "pencil", split_axis=0, concat_axis=0, tiled=True)

    right = [(p, (p + 1) % parts) for p in range(parts)]
    left = [(p, (p - 1) % parts) for p in range(parts)]
    std_l = lax.ppermute(std[columns - HALO :, :], "pencil", right)
    std_r = lax.ppermute(std[:HALO, :], "pencil", left)

    size = min(columns, WIDE)
    lat2, lon2, lat1, lon1 = pl.pallas_call(
        functools.partial(bands_kernel, rows_block=rows_block),
        out_shape=[
            jax.ShapeDtypeStruct((2, 3, 2 * WIDE, WIDE), BF),
            jax.ShapeDtypeStruct((2, size, size + 2 * HALO), BF),
            jax.ShapeDtypeStruct((2, rows_block, rows_block + 2 * PAD), BF),
            jax.ShapeDtypeStruct((2, 2 * WIDE, WIDE), BF),
        ],
        in_specs=[smem(), smem()],
        out_specs=[vmem()] * 4,
        compiler_params=params(),
        name="bands",
    )(x_kernel[0], y_kernel[0])

    meta = jnp.reshape(me, (1,)).astype(I32)
    ints, floats, own_lines, own = pl.pallas_call(
        functools.partial(
            unpack_kernel,
            layout=layout,
            parts=parts,
            columns=columns,
            height=height,
            capacity=capacity,
            stencil=stencil,
            group=group,
        ),
        out_shape=[
            jax.ShapeDtypeStruct((layout.int_rows, LANES), I32),
            jax.ShapeDtypeStruct((layout.float_rows, LANES), F32),
            jax.ShapeDtypeStruct((slots // LANES * stencil, LANES), I32),
            jax.ShapeDtypeStruct((slots, LANES), F32),
        ],
        in_specs=[smem(), vmem()],
        out_specs=[vmem()] * 4,
        scratch_shapes=[
            pltpu.VMEM((slots // LANES, LANES, LANES), F32),
            pltpu.VMEM((slots // LANES, stencil, LANES), F32),
        ],
        compiler_params=params(),
        name="unpack",
    )(meta, recv)
    ints = ints.reshape(-1)
    floats = floats.reshape(-1)
    own_lines = own_lines.reshape(-1)

    acc = pltpu.VMEM((blocks * wide + 8, LANES), F32)
    column_slots = pltpu.VMEM((slots, LANES), F32)
    static = dict(
        layout=layout,
        columns=columns,
        height=height,
        hold=hold,
        stencil=stencil,
        capacity=capacity,
        senders=senders,
        parts=parts,
        levels=levels,
    )
    per = group * stencil * hold
    line = group * hold
    index_scratch = [
        pltpu.SMEM((per,), I32),
        pltpu.SMEM((per,), F32),
        pltpu.SMEM((group * layout.table,), I32),
        pltpu.SMEM((slots * stencil,), I32),
    ]
    work = (
        [column_slots, pltpu.VMEM((stencil * slots, LANES), F32), column_slots]
        + [pltpu.VMEM((wide, height), BF)] * 2
        + [
            pltpu.VMEM((columns, height), F32),
            pltpu.VMEM((HALO, height), F32),
            pltpu.VMEM((HALO, height), F32),
            pltpu.VMEM(lat2.shape, BF),
            pltpu.VMEM(lon2.shape, BF),
            pltpu.VMEM((columns, height), F32),
        ]
        + [acc] * COPIES
        + [
            pltpu.SemaphoreType.DMA((4,)),
            pltpu.SemaphoreType.DMA((6,)),
            pltpu.SemaphoreType.DMA((height // WIDE,)),
            pltpu.SemaphoreType.DMA((parts,)),
        ]
    )
    field_shape = jax.ShapeDtypeStruct((columns, height), F32)
    reply_rows = 8 + stencil * slots // LANES
    field0, message, info = pl.pallas_call(
        functools.partial(apply_kernel, first=True, **static),
        out_shape=[
            field_shape,
            jax.ShapeDtypeStruct((parts, reply_rows, LANES), F32),
            jax.ShapeDtypeStruct((slots, LANES), F32),
        ],
        in_specs=[smem()] + [hbm()] * 3 + [vmem()] + [hbm()] * 5,
        out_specs=[hbm()] + [vmem()] * 2,
        scratch_shapes=index_scratch
        + [
            pltpu.SMEM((line,), F32),
            acc,
            pltpu.VMEM((stencil * slots, LANES), F32),
        ]
        + work,
        compiler_params=params(),
        name="apply_first",
    )(meta, ints, floats, own_lines, own, std, std_l, std_r, lat2, lon2)

    replies = lax.all_to_all(message, "pencil", split_axis=0, concat_axis=0, tiled=True)
    back = replies.reshape(-1)

    field1, sums = pl.pallas_call(
        functools.partial(apply_kernel, first=False, **static),
        out_shape=[
            field_shape,
            jax.ShapeDtypeStruct((parts * levels, 8, LANES), F32),
        ],
        in_specs=[smem()] + [hbm()] * 3 + [vmem(), hbm(), vmem()] + [hbm()] * 5,
        out_specs=[hbm(), vmem()],
        scratch_shapes=index_scratch + [pltpu.SMEM((parts * slots,), F32)] + work,
        compiler_params=params(),
        name="apply_second",
    )(meta, ints, floats, own_lines, info, back, replies, std, std_l, std_r, lat2, lon2)

    totals = lax.all_to_all(sums, ("pencil", "lev"), split_axis=0, concat_axis=0, tiled=True)
    totals = totals.reshape(parts, levels, 8, LANES)

    by_chunk = back
    if chunks > 1:
        by_chunk = jnp.concatenate(
            [replies[:, : slots // LANES, :], replies[:, 8:, :]], axis=1
        ).reshape(parts, stencil + 1, chunks, group * capacity)
        by_chunk = jnp.transpose(by_chunk, (2, 0, 1, 3)).reshape(-1)
    owner_words = by_chunk.shape[0] // (chunks * parts)
    high_rows = rows_block + 2 * PAD
    acc_rows = pltpu.VMEM(((length // LANES) * high_rows + 8, LANES), F32)
    control, increment = pl.pallas_call(
        functools.partial(
            final_kernel,
            layout=layout,
            hold=hold,
            stencil=stencil,
            capacity=capacity,
            senders=senders,
            parts=parts,
            length=length,
        ),
        out_shape=[
            jax.ShapeDtypeStruct((rows_block, length), F32),
            field_shape,
        ],
        in_specs=[hbm()] * 3 + [vmem()] + [hbm()] * 3 + [vmem()] * 2,
        out_specs=[hbm()] * 2,
        scratch_shapes=[
            pltpu.SMEM((per,), I32),
            pltpu.SMEM((line,), I32),
            pltpu.SMEM((group * layout.table,), I32),
            pltpu.SMEM((line,), I32),
            pltpu.SMEM((line,), F32),
            pltpu.SMEM((parts * owner_words,), F32),
            pltpu.VMEM((columns, height), F32),
            pltpu.VMEM((columns, height), F32),
            pltpu.VMEM((columns, height), F32),
            pltpu.VMEM((rows_block, length), F32),
            pltpu.VMEM((rows_block, length), BF),
            pltpu.VMEM((rows_block, length), BF),
        ]
        + [acc_rows] * COPIES
        + [
            pltpu.SemaphoreType.DMA((7,)),
            pltpu.SemaphoreType.DMA((3,)),
            pltpu.SemaphoreType.DMA((1 + length // WIDE,)),
        ],
        compiler_params=params(),
        name="outputs",
    )(ints, floats, by_chunk, totals, std, field0, field1, lat1, lon1)
    return control[None], increment[None]


def solution(mesh):
    return jax.shard_map(
        body,
        mesh=mesh,
        in_specs=(
            P("lev", "pencil", None),
            P("lev", None),
            P("lev", None),
            P(("pencil", "lev"), None),
            P(("pencil", "lev"), None),
            P(("pencil", "lev"), None),
            P(("pencil", "lev")),
            P(("pencil", "lev")),
            P(("pencil", "lev")),
        ),
        out_specs=(P("lev", "pencil", None), P("lev", "pencil", None)),
        check_vma=False,
    )
```

```python
import functools

import jax
import jax.numpy as jnp
import numpy as np
from jax import lax
from jax.experimental import pallas as pl
from jax.experimental.pallas import tpu as pltpu
from jax.sharding import PartitionSpec as P


BF = jnp.bfloat16
F32 = jnp.float32
I32 = jnp.int32
LANES = 128
WIDE = 256
HALO = 32
PAD = 16
PACK = 40
GROUP = 8
COPIES = 4
PAIR = 2
BATCH = 4
CODES = 40
VMEM_LIMIT = 58 * 1024 * 1024


def vmem():
    return pl.BlockSpec(memory_space=pltpu.VMEM)


def smem():
    return pl.BlockSpec(memory_space=pltpu.SMEM)


def hbm():
    return pl.BlockSpec(memory_space=pl.ANY)


def params():
    return pltpu.CompilerParams(vmem_limit_bytes=VMEM_LIMIT)


def split2(x):
    high = x.astype(BF)
    return high, (x - high.astype(F32)).astype(BF)


def split3(x):
    high = x.astype(BF)
    rest = x - high.astype(F32)
    mid = rest.astype(BF)
    return high, mid, (rest - mid.astype(F32)).astype(BF)


def mm(a, b):
    return jnp.dot(a, b, preferred_element_type=F32)


def mm_parts(a_parts, b_parts):
    (ah, al), (bh, bl) = a_parts, b_parts
    return mm(ah, bh) + (mm(al, bh) + mm(ah, bl))


def iota(shape, dim):
    return lax.broadcasted_iota(I32, shape, dim)


def pack_kernel(
    counts, owner, cells, weights, depart, prec, out, *, parts, columns, height, margin
):
    stencil, hold = cells.shape
    shift = height.bit_length() - 1
    block = height // parts
    reach = 2 * margin
    row_id = iota((hold, hold), 0)
    col_id = iota((hold, hold), 1)
    eye = row_id == col_id
    col_f = col_id.astype(F32)
    live = iota((1, hold), 1) < counts[0]
    cell = cells[...]
    column = lax.shift_right_logical(cell, jnp.full(cell.shape, shift, I32))
    row = cell & (height - 1)

    def any_of(mask):
        return jnp.max(jnp.where(mask, 1.0, 0.0), axis=0, keepdims=True)

    def turn(line):
        return jnp.sum(jnp.where(eye, line, 0.0), axis=1, keepdims=True)

    left = any_of(column < reach)
    right = any_of(column >= columns - reach)
    side = left + 3.0 * right - 2.0 * left * right
    base = jnp.where(live, owner[...].astype(F32) * 4.0, 4.0 * parts)
    key = jnp.where(live, base + side, base)
    key_col = turn(key)
    before = (key_col < key) | ((key_col == key) & (row_id < col_id))
    rank = jnp.sum(jnp.where(before, 1.0, 0.0), axis=0, keepdims=True)
    begin = jnp.sum(jnp.where(key_col < base, 1.0, 0.0), axis=0, keepdims=True)
    rank_col = turn(rank)
    perm = jnp.where(rank_col == col_f, 1.0, 0.0).astype(BF)

    def sort(values):
        total = None
        for part in split3(values):
            term = mm(part, perm)
            total = term if total is None else total + term
        return total

    weight = jnp.where(live, prec[...], 0.0)
    rest = [weight * depart[...], weight, key, rank - begin, jnp.zeros((4, hold), F32)]
    values = [cell.astype(F32), weights[...]] + rest
    ordered = sort(jnp.concatenate(values, axis=0))
    line = iota((8, hold), 0)
    tail = ordered[2 * stencil : 2 * stencil + 8, :]
    first_half = col_f < float(LANES)
    fourfold = 4.0 * jnp.where(first_half, col_f, col_f - float(LANES))
    for i, (low, high) in enumerate(((0.0, 4.0), (1.0, 3.0), (2.0, 2.0))):
        bound = fourfold + jnp.where(first_half, low, high)
        begins = jnp.sum(jnp.where(key_col < bound, 1.0, 0.0), axis=0, keepdims=True)
        tail = jnp.where(line == 5 + i, begins, tail)
    last = (line == 7) & (iota((8, hold), 1) == hold - 1)

    def per_part(part, carry):
        low = part * block - margin
        high = (part + 1) * block + margin
        flag = jnp.where(live, any_of((row >= low) & (row < high)), 0.0)
        place = jnp.sum(jnp.where(col_id < row_id, flag, 0.0), axis=1, keepdims=True)
        chosen = (place == col_f) & (turn(flag) > 0.0)
        listed = jnp.sum(jnp.where(chosen, rank_col, 0.0), axis=0, keepdims=True)
        amount = jnp.sum(flag, axis=1, keepdims=True)
        out[part, 0 : 2 * stencil, :] = ordered[0 : 2 * stencil, :]
        out[part, 2 * stencil : 2 * stencil + 8, :] = jnp.where(
            line == 4, listed, jnp.where(last, amount, tail)
        )
        return carry

    lax.fori_loop(0, parts, per_part, 0)


class Layout:
    def __init__(self, senders, hold, stencil, parts):
        lines = hold // LANES
        self.table = 3 * hold
        sizes = dict(
            addr=stencil * lines, rows=stencil * lines, listed=lines, slot=lines, start=3 * lines
        )
        self.ints = {}
        at = 0
        for name, size in sizes.items():
            self.ints[name] = (at, size)
            at += senders * size
        self.int_rows = at
        self.floats = {}
        at = 0
        for name, size in dict(wgt=stencil * lines, val=lines).items():
            self.floats[name] = (at, size)
            at += senders * size
        self.float_rows = at


def unpack_kernel(
    meta,
    recv,
    ints,
    floats,
    own_lines,
    own,
    own_sum,
    line_sum,
    lane_sum,
    *,
    layout,
    parts,
    columns,
    height,
    capacity,
    stencil,
    group,
):
    senders, _, hold = recv.shape
    lines = hold // LANES
    me = meta[0]
    shift = height.bit_length() - 1
    wide = columns + 2 * HALO
    block = height // parts
    high_rows = block + 2 * PAD
    length = columns * parts
    slots = senders * capacity

    def put(ref, place, sender, value):
        begin, size = place
        count = value.shape[0]
        for i in range(lines):
            part = value[:, i * LANES : (i + 1) * LANES]
            if count % 8 == 0:
                at = pl.multiple_of(begin + sender * size + i * count, 8)
                ref[pl.ds(at, count), :] = part
            else:
                for j in range(count):
                    ref[pl.ds(begin + sender * size + i + j * lines, 1), :] = part[j : j + 1]

    def right(x, by):
        return lax.shift_right_logical(x, jnp.full(x.shape, by, I32))

    def nt(a, b):
        return lax.dot_general(a, b, (((1,), (1,)), ((), ())), preferred_element_type=F32)

    own_sum[...] = jnp.zeros(own_sum.shape, F32)
    line_sum[...] = jnp.zeros(line_sum.shape, F32)
    lane_sum[...] = jnp.zeros(lane_sum.shape, F32)
    place = iota((LANES, hold), 0)
    index = iota((LANES, hold), 1)

    def per_sender(sender, carry):
        cell = recv[sender, 0:stencil, :].astype(I32)
        tail = recv[sender, 2 * stencil : 2 * stencil + 8, :]
        whole = tail.astype(I32)
        key = whole[2:3, :]
        pos = whole[3:4, :]
        owner = right(key, 2)
        offset = owner - me
        offset = jnp.where(offset > parts // 2, offset - parts, offset)
        offset = jnp.where(offset < -(parts // 2), offset + parts, offset)
        column = right(cell, shift)
        row = cell & (height - 1)
        at = offset * columns + column + HALO
        addr = jnp.where(
            (at >= 0) & (at < wide),
            (right(row, 7) * wide + at) * LANES + (row & (LANES - 1)),
            (height // LANES) * wide * LANES,
        )
        at_row = row - (block * me - PAD)
        across = owner * columns + column
        rows = jnp.where(
            (at_row >= 0) & (at_row < high_rows) & (owner < parts),
            (right(across, 7) * high_rows + at_row) * LANES + (across & (LANES - 1)),
            (length // LANES) * high_rows * LANES,
        )
        within = lax.rem(sender, group) * capacity + pos
        owner = jnp.minimum(owner, parts - 1)
        put(ints, layout.ints["addr"], sender, addr)
        put(ints, layout.ints["rows"], sender, rows)
        put(ints, layout.ints["listed"], sender, whole[4:5, :])
        put(ints, layout.ints["slot"], sender, owner * (group * capacity) + within)
        put(ints, layout.ints["start"], sender, whole[5:8, :])
        put(floats, layout.floats["wgt"], sender, recv[sender, stencil : 2 * stencil, :])
        put(floats, layout.floats["val"], sender, tail[0:1, :])

        here = iota((1, LANES), 1) == me
        begin = jnp.sum(jnp.where(here, whole[5:6, :LANES], 0), axis=1, keepdims=True)
        end = jnp.sum(jnp.where(here, whole[5:6, LANES : 2 * LANES], 0), axis=1, keepdims=True)
        first_slot = sender * capacity
        block_of = first_slot // LANES
        within = place - (first_slot - block_of * LANES)
        chosen = (within >= 0) & (index == begin + within) & (index < end)
        select = jnp.where(chosen, 1.0, 0.0).astype(BF)
        at_lane = (addr & (LANES - 1)).astype(F32)
        fields = jnp.concatenate([at_lane, recv[sender, stencil : 2 * stencil + 8, :]], axis=0)
        total = None
        for part in split3(fields):
            term = nt(select, part)
            total = term if total is None else total + term
        own_sum[block_of, :, 0:CODES] += total
        lane_sum[block_of] += nt(at_lane.astype(BF), select)
        total = None
        for part in split2(right(addr, 7).astype(F32)):
            term = nt(part, select)
            total = term if total is None else total + term
        line_sum[block_of] += total
        return carry

    lax.fori_loop(0, senders, per_sender, 0)

    number = iota((stencil, LANES), 0).astype(F32)
    nowhere = float((height // LANES) * wide)
    for i in range(slots // LANES):
        line = line_sum[i]
        leader = jnp.zeros(line.shape, F32)
        for k in reversed(range(stencil)):
            leader = jnp.where(line == line[k : k + 1, :], float(k), leader)
        leads = jnp.where(leader == number, 1.0, 0.0)
        count = jnp.zeros((1, LANES), F32)
        ranks = []
        for k in range(stencil):
            ranks.append(count)
            count = count + leads[k : k + 1, :]
        place = jnp.zeros(line.shape, F32)
        for k in range(stencil):
            place = jnp.where(leader == float(k), ranks[k], place)
        lists = []
        for k in range(stencil):
            found = jnp.where((leads > 0.0) & (place == float(k)), line, 0.0)
            found = jnp.sum(found, axis=0, keepdims=True)
            lists.append(jnp.where(count > float(k), found, nowhere))
        batches = lax.shift_right_logical(
            count.astype(I32) + (BATCH - 1), jnp.full(count.shape, BATCH.bit_length() - 1, I32)
        )
        lists = jnp.concatenate(lists, axis=0).astype(I32)
        top = i * (stencil + 8)
        own_lines[top : top + stencil, :] = lists
        own_lines[top + stencil : top + stencil + 8, :] = jnp.broadcast_to(batches, (8, LANES))
        codes = jnp.concatenate(
            [
                jnp.zeros((CODES, LANES), F32),
                place * float(LANES) + lane_sum[i],
                jnp.zeros((LANES - CODES - stencil, LANES), F32),
            ],
            axis=0,
        )
        own[i * LANES : (i + 1) * LANES, :] = own_sum[i] + codes.T


def band(shape, taps, shift):
    distance = iota(shape, 1) - iota(shape, 0) + shift
    result = jnp.zeros(shape, F32)
    for tap in range(taps.shape[0]):
        result = jnp.where(distance == tap, taps[tap], result)
    return result


def band_rev(shape, taps, shift):
    distance = iota(shape, 0) - iota(shape, 1) + shift
    result = jnp.zeros(shape, F32)
    for tap in range(taps.shape[0]):
        result = jnp.where(distance == tap, taps[tap], result)
    return result


def exact_nt(a, b):
    return lax.dot_general(
        a,
        b,
        (((1,), (1,)), ((), ())),
        precision=lax.Precision.HIGHEST,
        preferred_element_type=F32,
    )


def store_split(ref, index, value):
    high, low = split2(value)
    ref[(0,) + index] = high
    ref[(1,) + index] = low


def bands_kernel(kx, ky, lat2, lon2, lat1, lon1, *, rows_block):
    margin = kx.shape[0] // 2
    window = lat2.shape[2]
    first = band((window, window), ky, margin)
    reach = first[LANES : LANES + WIDE, :]
    place = iota((window, window), 1)
    for variant in range(3):
        kept = first
        if variant == 0:
            kept = jnp.where(place >= LANES, first, 0.0)
        if variant == 2:
            kept = jnp.where(place < LANES + WIDE, first, 0.0)
        store_split(lat2, (variant,), exact_nt(kept, reach))
    size = lon2.shape[1]
    wide = size + 2 * HALO
    depth = (wide + 32 + LANES - 1) // LANES * LANES
    second = band((wide, depth), kx, -(16 - margin))
    store_split(lon2, (), exact_nt(second[HALO : HALO + size, :], second))
    store_split(lat1, (), band_rev((rows_block, rows_block + 2 * PAD), ky, PAD + margin))
    store_split(lon1, (), band((2 * WIDE, WIDE), kx, LANES + margin))


def pairs(low, high, action):
    def step(i, carry):
        one = low + 2 * i
        action(one, jnp.minimum(one + 1, high - 1), one + 1 < high)
        return carry

    lax.fori_loop(0, lax.shift_right_logical(high - low + 1, 1), step, 0)


def zero_all(refs):
    rows = refs[0].shape[0]
    step = 256

    def clear(i, carry):
        for ref in refs:
            ref[pl.ds(pl.multiple_of(i * step, 8), step), :] = jnp.zeros((step, LANES), F32)
        return carry

    whole = rows // step
    lax.fori_loop(0, whole, clear, 0)
    if rows % step:
        for ref in refs:
            ref[whole * step : rows, :] = jnp.zeros((rows % step, LANES), F32)


def scatter_entries(copies, entries, lane):
    for start in range(0, len(entries), len(copies)):
        group = []
        for ref, (address, value) in zip(copies, entries[start : start + len(copies)]):
            line = lax.shift_right_logical(address, 7)
            spread = jnp.where(lane == (address & (LANES - 1)), value, 0.0)
            group.append((ref, line, ref[pl.ds(line, 1), :] + spread))
        for ref, line, value in group:
            ref[pl.ds(line, 1), :] = value


def spot(sender, idx, per, stencil):
    return sender * per + idx + lax.shift_right_logical(idx, 7) * ((stencil - 1) * LANES)


def copy_parts(layout, source, target, place, chunk, chunks, group, sem):
    begin, size = place
    words = group * size * LANES
    at = begin * LANES + chunk * words
    return pltpu.make_async_copy(source.at[pl.ds(at, words)], target, sem)


def apply_kernel(
    *refs, first, layout, columns, height, hold, stencil, capacity, senders, parts, levels
):
    refs = list(refs)

    def take(count):
        taken = refs[:count]
        del refs[:count]
        return taken

    meta, ints, floats, own_lines, own = take(5)
    if not first:
        replies_h, replies = take(2)
    std_h, std_l_h, std_r_h, lat2_h, lon2_h = take(5)
    if not first:
        merged_h = take(1)[0]
    field_h, send = take(2)
    if first:
        info_out, merged_h = take(2)
    addr, wgt, start, lines_s, val = take(5)
    if first:
        std_flat, picked, spread = take(3)
    scale, merged, sums, high_s, low_s, std, std_l, std_r, lat2, lon2, field = take(11)
    copies = take(PAIR)
    sems, in_sems, out_sems, val_sem = take(4)

    me = meta[0]
    wide = columns + 2 * HALO
    blocks = height // LANES
    group = min(GROUP, senders)
    chunks = senders // group
    slots = senders * capacity
    lane = iota((1, LANES), 1)
    per = stencil * hold
    table = layout.table

    def chunk_copies(chunk):
        todo = [
            (ints, addr, layout.ints["addr"]),
            (floats, wgt, layout.floats["wgt"]),
            (ints, start, layout.ints["start"]),
        ]
        if first:
            todo.append((floats, val, layout.floats["val"]))
        return [
            copy_parts(layout, source, target, place, chunk, chunks, group, sems.at[i])
            for i, (source, target, place) in enumerate(todo)
        ]

    def load_chunk(chunk):
        for copy in chunk_copies(chunk):
            copy.start()
        for copy in chunk_copies(chunk):
            copy.wait()

    pending = []
    if chunks == 1:
        pending = chunk_copies(0)
        for copy in pending:
            copy.start()
    operands = [
        pltpu.make_async_copy(source, target, in_sems.at[i])
        for i, (source, target) in enumerate(
            (
                (std_h, std),
                (std_l_h, std_l),
                (std_r_h, std_r),
                (lat2_h, lat2),
                (lon2_h, lon2),
            )
        )
    ]
    own_copy = pltpu.make_async_copy(own_lines, lines_s, in_sems.at[5])
    own_copy.start()
    for copy in operands:
        copy.start()

    def value_copy(owner):
        at = pl.multiple_of(owner * (replies.shape[1] * LANES), 1024)
        return pltpu.make_async_copy(
            replies_h.at[pl.ds(at, slots)], val.at[pl.ds(owner * slots, slots)], val_sem.at[owner]
        )

    def each_owner(action):
        def step(owner, carry):
            action(value_copy(owner))
            return carry

        lax.fori_loop(0, parts, step, 0)

    if not first:
        each_owner(lambda copy: copy.start())
    zero_all(copies)
    zero_all([sums])

    merged_copy = pltpu.make_async_copy(
        *((merged, merged_h) if first else (merged_h, merged)), in_sems.at[6]
    )
    if not first:
        merged_copy.start()

    lane_of = iota((slots, LANES), 1)
    known = own[...]
    column = 2 * stencil if first else 2 * stencil + 2
    scale[...] = jnp.broadcast_to(known[:, column : column + 1], (slots, LANES))
    if first:
        lane_f = iota((8, LANES), 1).astype(F32)

        def build(i, carry):
            top = pl.multiple_of(i * 8, 8)
            info = own[pl.ds(top, 8), :]

            def wide_of(at):
                return jnp.broadcast_to(info[:, at : at + 1], (8, LANES))

            rows = [None] * stencil
            for k in range(stencil):
                weight = wide_of(stencil + k)
                code = wide_of(CODES + k)
                spread[pl.ds(k * slots + top, 8), :] = jnp.where(
                    lane_f == wide_of(k), weight, 0.0
                )
                for place in range(k + 1):
                    term = jnp.where(lane_f + float(LANES * place) == code, weight, 0.0)
                    rows[place] = term if rows[place] is None else rows[place] + term
            for place in range(stencil):
                merged[pl.ds(place * slots + top, 8), :] = rows[place]
            return carry

        lax.fori_loop(0, slots // 8, build, 0)
        merged_copy.start()
    own_copy.wait()
    if not first:
        merged_copy.wait()

    after = lax.rem(me + 1, parts)
    ahead = lax.rem(me + parts - 1, parts)

    def start_of(sender, owner, row, half):
        return start[sender * table + row * hold + half * LANES + owner]

    def entries_of(sender, idx, value):
        base = spot(sender, idx, per, stencil)
        return [
            (addr[base + k * LANES], wgt[base + k * LANES] * value) for k in range(stencil)
        ]

    def own_line(slot, k):
        at = lax.shift_right_logical(slot, 7) * ((stencil + 7) * LANES) + slot
        return lines_s[at + k * LANES]

    def batches_of(one, two):
        return jnp.maximum(own_line(one, stencil), own_line(two, stencil))

    def own_pairs(chunk, action):
        def per_sender(sender, carry):
            amount = start_of(sender, me, 0, 1) - start_of(sender, me, 0, 0)
            base = (chunk * group + sender) * capacity
            pairs(base, base + amount, action)
            return carry

        lax.fori_loop(0, group, per_sender, 0)

    def scatter_own(chunk):
        def action(one, two, has_two):
            second = jnp.where(has_two, 1.0, 0.0)
            values = (scale[pl.ds(one, 1), :], scale[pl.ds(two, 1), :] * second)

            def batch(begin):
                todo = []
                for slot, value, ref in zip((one, two), values, copies):
                    for j in range(BATCH):
                        line = own_line(slot, begin + j)
                        row = merged[pl.ds((begin + j) * slots + slot, 1), :] * value
                        todo.append((ref, line, ref[pl.ds(line, 1), :] + row))
                for ref, line, row in todo:
                    ref[pl.ds(line, 1), :] = row

            def more(i, carry):
                batch(i * BATCH)
                return carry

            batch(0)
            lax.fori_loop(1, batches_of(one, two), more, 0)

        own_pairs(chunk, action)

    def scatter_halo(chunk):
        def per_sender(sender, carry):
            for owner, low, high in ((after, (1, 0), (1, 1)), (ahead, (2, 0), (0, 1))):
                begin = start_of(sender, owner, 0, 0)

                def value_of(idx, owner=owner, begin=begin):
                    if first:
                        return val[sender * hold + idx]
                    place = (chunk * group + sender) * capacity + idx - begin
                    return val[owner * slots + place]

                def action(one, two, has_two, value_of=value_of):
                    second = jnp.where(has_two, value_of(two), 0.0)
                    scatter_entries(
                        copies,
                        entries_of(sender, one, value_of(one)) + entries_of(sender, two, second),
                        lane,
                    )

                pairs(start_of(sender, owner, *low), start_of(sender, owner, *high), action)
            return carry

        lax.fori_loop(0, group, per_sender, 0)

    def scatter_chunk(chunk):
        scatter_own(chunk)
        scatter_halo(chunk)

    def over_chunks(work):
        if chunks == 1:
            work(0)
        else:

            def step(chunk, carry):
                load_chunk(chunk)
                work(chunk)
                return carry

            lax.fori_loop(0, chunks, step, 0)

    for copy in pending:
        copy.wait()
    if not first:
        each_owner(lambda copy: copy.wait())
    over_chunks(scatter_chunk)
    for copy in operands:
        copy.wait()

    for jb in range(blocks):
        lanes = slice(jb * LANES, (jb + 1) * LANES)
        for low, size, source in (
            (0, HALO, std_l),
            (HALO, columns, std),
            (HALO + columns, HALO, std_r),
        ):
            rows = slice(jb * wide + low, jb * wide + low + size)
            total = copies[0][rows, :]
            for ref in copies[1:]:
                total = total + ref[rows, :]
            high, lo = split2(total * source[:, lanes])
            high_s[low : low + size, lanes] = high
            low_s[low : low + size, lanes] = lo
        if first:
            std_flat[jb * wide + HALO : jb * wide + HALO + columns, :] = std[:, lanes]

    smoothed = copies[0]
    size = lon2.shape[1]
    count = height // WIDE
    outgoing = [merged_copy] if first else []
    for block in range(count):
        variant = 0 if block == 0 else (2 if block == count - 1 else 1)
        low = max(block * WIDE - LANES, 0)
        high = min(block * WIDE + WIDE + LANES, height)
        inner = slice(low - (block * WIDE - LANES), high - (block * WIDE - LANES))
        matrix = (lat2[0, variant, inner, :], lat2[1, variant, inner, :])
        along = mm_parts((high_s[:, low:high], low_s[:, low:high]), matrix)
        parts_y = split2(along)
        lanes = slice(block * WIDE, (block + 1) * WIDE)
        for begin in range(0, columns, size):
            some = min(size, columns - begin)
            rows = slice(begin, begin + some)
            window = slice(begin, begin + some + 2 * HALO)
            matrix = tuple(lon2[i, 0:some, 0 : some + 2 * HALO] for i in range(2))
            result = mm_parts(matrix, (parts_y[0][window, :], parts_y[1][window, :]))
            field[rows, lanes] = result
            scaled = result * std[rows, lanes]
            for half in range(WIDE // LANES):
                top = (block * (WIDE // LANES) + half) * wide + HALO + begin
                smoothed[top : top + some, :] = scaled[:, half * LANES : (half + 1) * LANES]
        outgoing.append(
            pltpu.make_async_copy(field.at[:, lanes], field_h.at[:, lanes], out_sems.at[block])
        )
        outgoing[-1].start()

    def gather_chunk(chunk):
        def action(one, two, has_two):
            def batch(begin, totals):
                result = []
                for slot, total in zip((one, two), totals):
                    terms = []
                    for j in range(BATCH):
                        line = own_line(slot, begin + j)
                        row = merged[pl.ds((begin + j) * slots + slot, 1), :]
                        terms.append(row * smoothed[pl.ds(line, 1), :])
                    result.append(total + ((terms[0] + terms[1]) + (terms[2] + terms[3])))
                return tuple(result)

            zero = jnp.zeros((1, LANES), F32)
            totals = lax.fori_loop(
                1,
                batches_of(one, two),
                lambda i, totals: batch(i * BATCH, totals),
                batch(0, (zero, zero)),
            )
            for slot, total in zip((one, two), totals):
                sums[pl.ds(slot, 1), :] = total

        own_pairs(chunk, action)

        if first:

            def per_sender(sender, carry):
                begin = start_of(sender, me, 0, 0)
                amount = start_of(sender, me, 0, 1) - begin
                base = (chunk * group + sender) * capacity

                def pick(idx):
                    slot = base + idx - begin
                    at = spot(sender, idx, per, stencil)
                    for k in range(stencil):
                        line = lax.shift_right_logical(addr[at + k * LANES], 7)
                        row = spread[pl.ds(k * slots + slot, 1), :]
                        picked[pl.ds(k * slots + slot, 1), :] = row * std_flat[pl.ds(line, 1), :]

                def both(one, two, has_two):
                    pick(one)
                    pick(two)

                pairs(begin, begin + amount, both)
                return carry

            lax.fori_loop(0, group, per_sender, 0)

    over_chunks(gather_chunk)

    def whole(x):
        return jnp.sum(x, axis=0, keepdims=True)

    total = jnp.sum(sums[...], axis=1, keepdims=True)
    lines = slots // LANES
    known = own[...]
    source, weight, reply, image0 = (
        known[:, 2 * stencil + i : 2 * stencil + i + 1] for i in range(4)
    )
    if first:
        reply = weight * total
        known = jnp.where(lane_of == 2 * stencil + 2, reply, known)
        known = jnp.where(lane_of == 2 * stencil + 3, total, known)
        info_out[...] = known
        turned = known.T[2 * stencil + 2 : 2 * stencil + 3, :]
        message = [turned[:, i * LANES : (i + 1) * LANES] for i in range(lines)]
        message.append(
            jnp.where(
                lane == 0, whole(source * total), jnp.where(lane == 1, whole(reply * total), 0.0)
            )
        )
        message.append(jnp.zeros((8 - len(message), LANES), F32))
        ones = jnp.ones((8, LANES), BF)
        for k in range(stencil):
            row = None
            for part in split3(picked[k * slots : (k + 1) * slots, :]):
                term = lax.dot_general(
                    ones, part, (((1,), (1,)), ((), ())), preferred_element_type=F32
                )
                row = term if row is None else row + term
            for i in range(lines):
                message.append(row[0:1, i * LANES : (i + 1) * LANES])
        message = jnp.concatenate(message, axis=0)
    else:
        slab = jnp.sum(replies[:, 0:8, :], axis=0)[lines : lines + 1, :]
        length = slab[:, 0:1] / (slab[:, 0:1] + slab[:, 1:2])
        both = source + reply
        s_both = image0 + total
        resid = source - length * both
        s_resid = image0 - length * s_both
        values = [
            resid * s_resid,
            resid * s_both,
            both * s_both,
            resid * image0,
            both * image0,
            weight * s_resid * s_resid,
            weight * s_resid * s_both,
            weight * s_both * s_both,
            weight * s_resid * image0,
            weight * s_both * image0,
            source * image0,
            reply * image0,
        ]
        message = jnp.where(lane == len(values), length, 0.0)
        for i, value in enumerate(values):
            message = jnp.where(lane == i, whole(value), message)
        message = jnp.concatenate([message, jnp.zeros((7, LANES), F32)], axis=0)

    def send_to(i, carry):
        send[i] = message
        return carry

    lax.fori_loop(0, send.shape[0], send_to, 0)
    for copy in outgoing:
        copy.wait()


def final_kernel(
    ints,
    floats,
    replies_h,
    totals,
    std_h,
    field0_h,
    field1_h,
    lat1,
    lon1,
    control_h,
    increment_h,
    addr,
    listed,
    start,
    slot,
    val,
    factors,
    std,
    field0,
    field1,
    control,
    high_s,
    low_s,
    *rest,
    layout,
    hold,
    stencil,
    capacity,
    senders,
    parts,
    length,
):
    copies = rest[:COPIES]
    sems, in_sems, out_sems = rest[COPIES:]
    group = min(GROUP, senders)
    chunks = senders // group
    per = stencil * hold
    rows_block = control.shape[0]
    high_rows = rows_block + 2 * PAD
    lane = iota((1, LANES), 1)
    stride = group * capacity
    owner_words = factors.shape[0] // parts
    to_factors = owner_words - stencil * stride

    def chunk_copies(chunk):
        todo = [
            (ints, addr, layout.ints["rows"]),
            (ints, listed, layout.ints["listed"]),
            (ints, start, layout.ints["start"]),
            (ints, slot, layout.ints["slot"]),
            (floats, val, layout.floats["val"]),
        ]
        result = [
            copy_parts(layout, source, target, place, chunk, chunks, group, sems.at[i])
            for i, (source, target, place) in enumerate(todo)
        ]
        words = parts * owner_words
        result.append(
            pltpu.make_async_copy(
                replies_h.at[pl.ds(chunk * words, words)], factors, sems.at[len(todo)]
            )
        )
        return result

    pending = []
    if chunks == 1:
        pending = chunk_copies(0)
        for copy in pending:
            copy.start()
    operands = [
        pltpu.make_async_copy(source, target, in_sems.at[i])
        for i, (source, target) in enumerate(
            ((std_h, std), (field0_h, field0), (field1_h, field1))
        )
    ]
    for copy in operands:
        copy.start()

    slabs = totals.shape[1]
    every = jnp.sum(totals[...], axis=0)
    norm0 = quad0 = None
    for i in range(slabs):
        line = every[i, 0:1, :]
        a, b = line[:, 10:11], line[:, 11:12]
        norm0 = a if norm0 is None else norm0 + a
        quad0 = b if quad0 is None else quad0 + b
    step0 = norm0 / (norm0 + quad0)
    norm1 = cross = quad1 = quad01 = jnp.zeros((1, 1), F32)
    for i in range(slabs):
        line = every[i, 0:1, :]
        v = [line[:, j : j + 1] for j in range(10)]
        shift = totals[0, i, 0:1, 12:13] - step0
        norm1 = norm1 + (v[0] + shift * (2.0 * v[1] + shift * v[2]))
        cross = cross + (v[3] + shift * v[4])
        quad1 = quad1 + (v[5] + shift * (2.0 * v[6] + shift * v[7]))
        quad01 = quad01 + (v[8] + shift * v[9])
    ratio = norm1 / norm0
    curvature = norm1 + quad1 + ratio * (
        2.0 * (cross + quad01) + ratio * (norm0 + quad0)
    )
    step1 = norm1 / curvature
    first = step0 + step1 * (1.0 - step0 + ratio)
    second = -step0 * step1
    first_line = jnp.broadcast_to(first, (1, LANES))
    second_line = jnp.broadcast_to(second, (1, LANES))

    zero_all(copies)

    def scatter_chunk():
        def per_sender(sender, carry):
            def entries_of(at, scale):
                idx = listed[sender * hold + at]
                place = slot[sender * hold + idx]
                place = place + lax.div(place, stride) * (owner_words - stride)
                base = spot(sender, idx, per, stencil)
                z0 = val[sender * hold + idx] * scale
                u = factors[place] * scale
                value = first_line * z0 + second_line * u
                return [
                    (addr[base + k * LANES], factors[place + to_factors + k * stride] * value)
                    for k in range(stencil)
                ]

            def action(one, two, has_two):
                scale = jnp.where(has_two, 1.0, 0.0)
                scatter_entries(copies, entries_of(one, 1.0) + entries_of(two, scale), lane)

            pairs(0, start[sender * layout.table + layout.table - 1], action)
            return carry

        lax.fori_loop(0, group, per_sender, 0)

    if chunks == 1:
        for copy in pending:
            copy.wait()
        scatter_chunk()
    else:

        def step(chunk, carry):
            for copy in chunk_copies(chunk):
                copy.start()
            for copy in chunk_copies(chunk):
                copy.wait()
            scatter_chunk()
            return carry

        lax.fori_loop(0, chunks, step, 0)

    for copy in operands:
        copy.wait()
    increment = field0
    increment[...] = std[...] * (first * field0[...] + second * field1[...])
    outgoing = [pltpu.make_async_copy(increment, increment_h, out_sems.at[0])]
    outgoing[0].start()

    pair = WIDE // LANES
    count = length // WIDE
    for block in range(count):
        pieces = []
        for half in range(pair):
            rows = slice((block * pair + half) * high_rows, (block * pair + half + 1) * high_rows)
            total = copies[0][rows, :]
            for ref in copies[1:]:
                total = total + ref[rows, :]
            pieces.append(total)
        whole = split2(jnp.concatenate(pieces, axis=1))
        size = lat1.shape[1]
        for top in range(0, rows_block, size):
            window = slice(top, top + size + 2 * PAD)
            along = mm_parts((lat1[0], lat1[1]), (whole[0][window, :], whole[1][window, :]))
            high, low = split2(along)
            high_s[top : top + size, block * WIDE : (block + 1) * WIDE] = high
            low_s[top : top + size, block * WIDE : (block + 1) * WIDE] = low

    def window(ref, block):
        low, high = block * WIDE - LANES, (block + 1) * WIDE + LANES
        if low < 0:
            return jnp.concatenate([ref[:, length + low : length], ref[:, 0:high]], axis=1)
        if high > length:
            return jnp.concatenate([ref[:, low:length], ref[:, 0 : high - length]], axis=1)
        return ref[:, low:high]

    every_lanes = 4
    for block in range(count):
        control[:, block * WIDE : (block + 1) * WIDE] = mm_parts(
            (window(high_s, block), window(low_s, block)), (lon1[0], lon1[1])
        )
        if block % every_lanes == every_lanes - 1:
            lanes = slice((block + 1 - every_lanes) * WIDE, (block + 1) * WIDE)
            outgoing.append(
                pltpu.make_async_copy(
                    control.at[:, lanes], control_h.at[:, lanes], out_sems.at[len(outgoing)]
                )
            )
            outgoing[-1].start()
    for copy in outgoing:
        copy.wait()


def body(
    background_std,
    x_kernel,
    y_kernel,
    obs_owner,
    obs_cells,
    obs_weights,
    innovation,
    obs_precision,
    obs_counts,
):
    parts = lax.axis_size("pencil")
    levels = lax.axis_size("lev")
    me = lax.axis_index("pencil")
    _, columns, height = background_std.shape
    hold, stencil = obs_cells.shape
    margin = x_kernel.shape[1] // 2
    capacity = 2 * hold // parts
    senders = parts
    slots = senders * capacity
    rows_block = height // parts
    length = columns * parts
    blocks = height // LANES
    wide = columns + 2 * HALO
    group = min(GROUP, senders)
    chunks = senders // group
    layout = Layout(senders, hold, stencil, parts)
    std = background_std[0]

    packed = pl.pallas_call(
        functools.partial(
            pack_kernel, parts=parts, columns=columns, height=height, margin=margin
        ),
        out_shape=jax.ShapeDtypeStruct((parts, PACK, hold), F32),
        in_specs=[smem()] + [vmem()] * 5,
        out_specs=vmem(),
        compiler_params=params(),
        name="pack",
    )(
        obs_counts,
        obs_owner.T,
        obs_cells.T,
        obs_weights.T,
        innovation[None, :],
        obs_precision[None, :],
    )
    recv = lax.all_to_all(packed, "pencil", split_axis=0, concat_axis=0, tiled=True)

    right = [(p, (p + 1) % parts) for p in range(parts)]
    left = [(p, (p - 1) % parts) for p in range(parts)]
    std_l = lax.ppermute(std[columns - HALO :, :], "pencil", right)
    std_r = lax.ppermute(std[:HALO, :], "pencil", left)

    size = min(columns, WIDE - 2 * HALO)
    row_size = min(rows_block, LANES)
    lat2, lon2, lat1, lon1 = pl.pallas_call(
        functools.partial(bands_kernel, rows_block=row_size),
        out_shape=[
            jax.ShapeDtypeStruct((2, 3, 2 * WIDE, WIDE), BF),
            jax.ShapeDtypeStruct((2, size, size + 2 * HALO), BF),
            jax.ShapeDtypeStruct((2, row_size, row_size + 2 * PAD), BF),
            jax.ShapeDtypeStruct((2, 2 * WIDE, WIDE), BF),
        ],
        in_specs=[smem(), smem()],
        out_specs=[vmem()] * 4,
        compiler_params=params(),
        name="bands",
    )(x_kernel[0], y_kernel[0])

    meta = jnp.reshape(me, (1,)).astype(I32)
    ints, floats, own_lines, own = pl.pallas_call(
        functools.partial(
            unpack_kernel,
            layout=layout,
            parts=parts,
            columns=columns,
            height=height,
            capacity=capacity,
            stencil=stencil,
            group=group,
        ),
        out_shape=[
            jax.ShapeDtypeStruct((layout.int_rows, LANES), I32),
            jax.ShapeDtypeStruct((layout.float_rows, LANES), F32),
            jax.ShapeDtypeStruct((slots // LANES * (stencil + 8), LANES), I32),
            jax.ShapeDtypeStruct((slots, LANES), F32),
        ],
        in_specs=[smem(), vmem()],
        out_specs=[vmem()] * 4,
        scratch_shapes=[
            pltpu.VMEM((slots // LANES, LANES, LANES), F32),
            pltpu.VMEM((slots // LANES, stencil, LANES), F32),
            pltpu.VMEM((slots // LANES, stencil, LANES), F32),
        ],
        compiler_params=params(),
        name="unpack",
    )(meta, recv)
    ints = ints.reshape(-1)
    floats = floats.reshape(-1)
    own_lines = own_lines.reshape(-1)

    acc = pltpu.VMEM((blocks * wide + 8, LANES), F32)
    column_slots = pltpu.VMEM((slots, LANES), F32)
    static = dict(
        layout=layout,
        columns=columns,
        height=height,
        hold=hold,
        stencil=stencil,
        capacity=capacity,
        senders=senders,
        parts=parts,
        levels=levels,
    )
    per = group * stencil * hold
    line = group * hold
    index_scratch = [
        pltpu.SMEM((per,), I32),
        pltpu.SMEM((per,), F32),
        pltpu.SMEM((group * layout.table,), I32),
        pltpu.SMEM((slots * (stencil + 8),), I32),
    ]
    work = (
        [column_slots, pltpu.VMEM((stencil * slots, LANES), F32), column_slots]
        + [pltpu.VMEM((wide, height), BF)] * 2
        + [
            pltpu.VMEM((columns, height), F32),
            pltpu.VMEM((HALO, height), F32),
            pltpu.VMEM((HALO, height), F32),
            pltpu.VMEM(lat2.shape, BF),
            pltpu.VMEM(lon2.shape, BF),
            pltpu.VMEM((columns, height), F32),
        ]
        + [acc] * PAIR
        + [
            pltpu.SemaphoreType.DMA((4,)),
            pltpu.SemaphoreType.DMA((7,)),
            pltpu.SemaphoreType.DMA((height // WIDE,)),
            pltpu.SemaphoreType.DMA((parts,)),
        ]
    )
    field_shape = jax.ShapeDtypeStruct((columns, height), F32)
    reply_rows = 8 + stencil * slots // LANES
    field0, message, info, merged = pl.pallas_call(
        functools.partial(apply_kernel, first=True, **static),
        out_shape=[
            field_shape,
            jax.ShapeDtypeStruct((parts, reply_rows, LANES), F32),
            jax.ShapeDtypeStruct((slots, LANES), F32),
            jax.ShapeDtypeStruct((stencil * slots, LANES), F32),
        ],
        in_specs=[smem()] + [hbm()] * 3 + [vmem()] + [hbm()] * 5,
        out_specs=[hbm()] + [vmem()] * 2 + [hbm()],
        scratch_shapes=index_scratch
        + [
            pltpu.SMEM((line,), F32),
            acc,
            pltpu.VMEM((stencil * slots, LANES), F32),
            pltpu.VMEM((stencil * slots, LANES), F32),
        ]
        + work,
        compiler_params=params(),
        name="apply_first",
    )(meta, ints, floats, own_lines, own, std, std_l, std_r, lat2, lon2)

    replies = lax.all_to_all(message, "pencil", split_axis=0, concat_axis=0, tiled=True)
    back = replies.reshape(-1)

    field1, sums = pl.pallas_call(
        functools.partial(apply_kernel, first=False, **static),
        out_shape=[
            field_shape,
            jax.ShapeDtypeStruct((parts * levels, 8, LANES), F32),
        ],
        in_specs=[smem()] + [hbm()] * 3 + [vmem(), hbm(), vmem()] + [hbm()] * 6,
        out_specs=[hbm(), vmem()],
        scratch_shapes=index_scratch + [pltpu.SMEM((parts * slots,), F32)] + work,
        compiler_params=params(),
        name="apply_second",
    )(
        meta,
        ints,
        floats,
        own_lines,
        info,
        back,
        replies,
        std,
        std_l,
        std_r,
        lat2,
        lon2,
        merged,
    )

    totals = lax.all_to_all(sums, ("pencil", "lev"), split_axis=0, concat_axis=0, tiled=True)
    totals = totals.reshape(parts, levels, 8, LANES)

    by_chunk = back
    if chunks > 1:
        by_chunk = jnp.concatenate(
            [replies[:, : slots // LANES, :], replies[:, 8:, :]], axis=1
        ).reshape(parts, stencil + 1, chunks, group * capacity)
        by_chunk = jnp.transpose(by_chunk, (2, 0, 1, 3)).reshape(-1)
    owner_words = by_chunk.shape[0] // (chunks * parts)
    high_rows = rows_block + 2 * PAD
    acc_rows = pltpu.VMEM(((length // LANES) * high_rows + 8, LANES), F32)
    control, increment = pl.pallas_call(
        functools.partial(
            final_kernel,
            layout=layout,
            hold=hold,
            stencil=stencil,
            capacity=capacity,
            senders=senders,
            parts=parts,
            length=length,
        ),
        out_shape=[
            jax.ShapeDtypeStruct((rows_block, length), F32),
            field_shape,
        ],
        in_specs=[hbm()] * 3 + [vmem()] + [hbm()] * 3 + [vmem()] * 2,
        out_specs=[hbm()] * 2,
        scratch_shapes=[
            pltpu.SMEM((per,), I32),
            pltpu.SMEM((line,), I32),
            pltpu.SMEM((group * layout.table,), I32),
            pltpu.SMEM((line,), I32),
            pltpu.SMEM((line,), F32),
            pltpu.SMEM((parts * owner_words,), F32),
            pltpu.VMEM((columns, height), F32),
            pltpu.VMEM((columns, height), F32),
            pltpu.VMEM((columns, height), F32),
            pltpu.VMEM((rows_block, length), F32),
            pltpu.VMEM((rows_block, length), BF),
            pltpu.VMEM((rows_block, length), BF),
        ]
        + [acc_rows] * COPIES
        + [
            pltpu.SemaphoreType.DMA((7,)),
            pltpu.SemaphoreType.DMA((3,)),
            pltpu.SemaphoreType.DMA((1 + length // WIDE,)),
        ],
        compiler_params=params(),
        name="outputs",
    )(ints, floats, by_chunk, totals, std, field0, field1, lat1, lon1)
    return control[None], increment[None]


def solution(mesh):
    return jax.shard_map(
        body,
        mesh=mesh,
        in_specs=(
            P("lev", "pencil", None),
            P("lev", None),
            P("lev", None),
            P(("pencil", "lev"), None),
            P(("pencil", "lev"), None),
            P(("pencil", "lev"), None),
            P(("pencil", "lev")),
            P(("pencil", "lev")),
            P(("pencil", "lev")),
        ),
        out_specs=(P("lev", "pencil", None), P("lev", "pencil", None)),
        check_vma=False,
    )
```

```python
import functools

import jax
import jax.numpy as jnp
import numpy as np
from jax import lax
from jax.experimental import pallas as pl
from jax.experimental.pallas import tpu as pltpu
from jax.sharding import PartitionSpec as P


BF = jnp.bfloat16
F32 = jnp.float32
I32 = jnp.int32
LANES = 128
WIDE = 256
HALO = 32
PAD = 16
PACK = 40
GROUP = 8
COPIES = 4
PAIR = 2
BATCH = 4
CODES = 40
VMEM_LIMIT = 58 * 1024 * 1024


def vmem():
    return pl.BlockSpec(memory_space=pltpu.VMEM)


def smem():
    return pl.BlockSpec(memory_space=pltpu.SMEM)


def hbm():
    return pl.BlockSpec(memory_space=pl.ANY)


def params():
    return pltpu.CompilerParams(vmem_limit_bytes=VMEM_LIMIT)


def split2(x):
    high = x.astype(BF)
    return high, (x - high.astype(F32)).astype(BF)


def split3(x):
    high = x.astype(BF)
    rest = x - high.astype(F32)
    mid = rest.astype(BF)
    return high, mid, (rest - mid.astype(F32)).astype(BF)


def mm(a, b):
    return jnp.dot(a, b, preferred_element_type=F32)


def mm_parts(a_parts, b_parts):
    (ah, al), (bh, bl) = a_parts, b_parts
    return mm(ah, bh) + (mm(al, bh) + mm(ah, bl))


def iota(shape, dim):
    return lax.broadcasted_iota(I32, shape, dim)


def pack_kernel(
    counts, owner, cells, weights, depart, prec, out, *, parts, columns, height, margin
):
    stencil, hold = cells.shape
    shift = height.bit_length() - 1
    block = height // parts
    reach = 2 * margin
    row_id = iota((hold, hold), 0)
    col_id = iota((hold, hold), 1)
    eye = row_id == col_id
    col_f = col_id.astype(F32)
    live = iota((1, hold), 1) < counts[0]
    cell = cells[...]
    column = lax.shift_right_logical(cell, jnp.full(cell.shape, shift, I32))
    row = cell & (height - 1)

    def any_of(mask):
        return jnp.max(jnp.where(mask, 1.0, 0.0), axis=0, keepdims=True)

    def turn(line):
        return jnp.sum(jnp.where(eye, line, 0.0), axis=1, keepdims=True)

    left = any_of(column < reach)
    right = any_of(column >= columns - reach)
    side = left + 3.0 * right - 2.0 * left * right
    base = jnp.where(live, owner[...].astype(F32) * 4.0, 4.0 * parts)
    key = jnp.where(live, base + side, base)
    key_col = turn(key)
    before = (key_col < key) | ((key_col == key) & (row_id < col_id))
    rank = jnp.sum(jnp.where(before, 1.0, 0.0), axis=0, keepdims=True)
    begin = jnp.sum(jnp.where(key_col < base, 1.0, 0.0), axis=0, keepdims=True)
    rank_col = turn(rank)
    perm = jnp.where(rank_col == col_f, 1.0, 0.0).astype(BF)

    def sort(values):
        total = None
        for part in split3(values):
            term = mm(part, perm)
            total = term if total is None else total + term
        return total

    weight = jnp.where(live, prec[...], 0.0)
    rest = [weight * depart[...], weight, key, rank - begin, jnp.zeros((4, hold), F32)]
    values = [cell.astype(F32), weights[...]] + rest
    ordered = sort(jnp.concatenate(values, axis=0))
    line = iota((8, hold), 0)
    tail = ordered[2 * stencil : 2 * stencil + 8, :]
    first_half = col_f < float(LANES)
    fourfold = 4.0 * jnp.where(first_half, col_f, col_f - float(LANES))
    for i, (low, high) in enumerate(((0.0, 4.0), (1.0, 3.0), (2.0, 2.0))):
        bound = fourfold + jnp.where(first_half, low, high)
        begins = jnp.sum(jnp.where(key_col < bound, 1.0, 0.0), axis=0, keepdims=True)
        tail = jnp.where(line == 5 + i, begins, tail)
    last = (line == 7) & (iota((8, hold), 1) == hold - 1)

    def per_part(part, carry):
        low = part * block - margin
        high = (part + 1) * block + margin
        flag = jnp.where(live, any_of((row >= low) & (row < high)), 0.0)
        place = jnp.sum(jnp.where(col_id < row_id, flag, 0.0), axis=1, keepdims=True)
        chosen = (place == col_f) & (turn(flag) > 0.0)
        listed = jnp.sum(jnp.where(chosen, rank_col, 0.0), axis=0, keepdims=True)
        amount = jnp.sum(flag, axis=1, keepdims=True)
        out[part, 0 : 2 * stencil, :] = ordered[0 : 2 * stencil, :]
        out[part, 2 * stencil : 2 * stencil + 8, :] = jnp.where(
            line == 4, listed, jnp.where(last, amount, tail)
        )
        return carry

    lax.fori_loop(0, parts, per_part, 0, unroll=parts <= GROUP)


class Layout:
    def __init__(self, senders, hold, stencil, parts):
        lines = hold // LANES
        self.table = 3 * hold
        sizes = dict(
            addr=stencil * lines, rows=stencil * lines, listed=lines, slot=lines, start=3 * lines
        )
        self.ints = {}
        at = 0
        for name, size in sizes.items():
            self.ints[name] = (at, size)
            at += senders * size
        self.int_rows = at
        self.floats = {}
        at = 0
        for name, size in dict(wgt=stencil * lines, val=lines).items():
            self.floats[name] = (at, size)
            at += senders * size
        self.float_rows = at


def unpack_kernel(
    meta,
    recv,
    ints,
    floats,
    own_lines,
    own,
    own_sum,
    line_sum,
    lane_sum,
    *,
    layout,
    parts,
    columns,
    height,
    capacity,
    stencil,
    group,
):
    senders, _, hold = recv.shape
    lines = hold // LANES
    me = meta[0]
    shift = height.bit_length() - 1
    wide = columns + 2 * HALO
    block = height // parts
    high_rows = block + 2 * PAD
    length = columns * parts
    slots = senders * capacity

    def put(ref, place, sender, value):
        begin, size = place
        count = value.shape[0]
        for i in range(lines):
            part = value[:, i * LANES : (i + 1) * LANES]
            if count % 8 == 0:
                at = pl.multiple_of(begin + sender * size + i * count, 8)
                ref[pl.ds(at, count), :] = part
            else:
                for j in range(count):
                    ref[pl.ds(begin + sender * size + i + j * lines, 1), :] = part[j : j + 1]

    def right(x, by):
        return lax.shift_right_logical(x, jnp.full(x.shape, by, I32))

    def nt(a, b):
        return lax.dot_general(a, b, (((1,), (1,)), ((), ())), preferred_element_type=F32)

    own_sum[...] = jnp.zeros(own_sum.shape, F32)
    line_sum[...] = jnp.zeros(line_sum.shape, F32)
    lane_sum[...] = jnp.zeros(lane_sum.shape, F32)
    place = iota((LANES, hold), 0)
    index = iota((LANES, hold), 1)

    def per_sender(sender, carry):
        cell = recv[sender, 0:stencil, :].astype(I32)
        tail = recv[sender, 2 * stencil : 2 * stencil + 8, :]
        whole = tail.astype(I32)
        key = whole[2:3, :]
        pos = whole[3:4, :]
        owner = right(key, 2)
        offset = owner - me
        offset = jnp.where(offset > parts // 2, offset - parts, offset)
        offset = jnp.where(offset < -(parts // 2), offset + parts, offset)
        column = right(cell, shift)
        row = cell & (height - 1)
        at = offset * columns + column + HALO
        addr = jnp.where(
            (at >= 0) & (at < wide),
            (right(row, 7) * wide + at) * LANES + (row & (LANES - 1)),
            (height // LANES) * wide * LANES,
        )
        at_row = row - (block * me - PAD)
        across = owner * columns + column
        rows = jnp.where(
            (at_row >= 0) & (at_row < high_rows) & (owner < parts),
            (right(across, 7) * high_rows + at_row) * LANES + (across & (LANES - 1)),
            (length // LANES) * high_rows * LANES,
        )
        within = lax.rem(sender, group) * capacity + pos
        owner = jnp.minimum(owner, parts - 1)
        put(ints, layout.ints["addr"], sender, addr)
        put(ints, layout.ints["rows"], sender, rows)
        put(ints, layout.ints["listed"], sender, whole[4:5, :])
        put(ints, layout.ints["slot"], sender, owner * (group * capacity) + within)
        put(ints, layout.ints["start"], sender, whole[5:8, :])
        put(floats, layout.floats["wgt"], sender, recv[sender, stencil : 2 * stencil, :])
        put(floats, layout.floats["val"], sender, tail[0:1, :])

        here = iota((1, LANES), 1) == me
        begin = jnp.sum(jnp.where(here, whole[5:6, :LANES], 0), axis=1, keepdims=True)
        end = jnp.sum(jnp.where(here, whole[5:6, LANES : 2 * LANES], 0), axis=1, keepdims=True)
        first_slot = sender * capacity
        block_of = first_slot // LANES
        within = place - (first_slot - block_of * LANES)
        chosen = (within >= 0) & (index == begin + within) & (index < end)
        select = jnp.where(chosen, 1.0, 0.0).astype(BF)
        at_lane = (addr & (LANES - 1)).astype(F32)
        fields = jnp.concatenate([at_lane, recv[sender, stencil : 2 * stencil + 8, :]], axis=0)
        total = None
        for part in split3(fields):
            term = nt(select, part)
            total = term if total is None else total + term
        own_sum[block_of, :, 0:CODES] += total
        lane_sum[block_of] += nt(at_lane.astype(BF), select)
        total = None
        for part in split2(right(addr, 7).astype(F32)):
            term = nt(part, select)
            total = term if total is None else total + term
        line_sum[block_of] += total
        return carry

    lax.fori_loop(0, senders, per_sender, 0, unroll=senders <= GROUP)

    number = iota((stencil, LANES), 0).astype(F32)
    nowhere = float((height // LANES) * wide)
    for i in range(slots // LANES):
        line = line_sum[i]
        leader = jnp.zeros(line.shape, F32)
        for k in reversed(range(stencil)):
            leader = jnp.where(line == line[k : k + 1, :], float(k), leader)
        leads = jnp.where(leader == number, 1.0, 0.0)
        count = jnp.zeros((1, LANES), F32)
        ranks = []
        for k in range(stencil):
            ranks.append(count)
            count = count + leads[k : k + 1, :]
        place = jnp.zeros(line.shape, F32)
        for k in range(stencil):
            place = jnp.where(leader == float(k), ranks[k], place)
        lists = []
        for k in range(stencil):
            found = jnp.where((leads > 0.0) & (place == float(k)), line, 0.0)
            found = jnp.sum(found, axis=0, keepdims=True)
            lists.append(jnp.where(count > float(k), found, nowhere))
        batches = lax.shift_right_logical(
            count.astype(I32) + (BATCH - 1), jnp.full(count.shape, BATCH.bit_length() - 1, I32)
        )
        lists = jnp.concatenate(lists, axis=0).astype(I32)
        top = i * (stencil + 8)
        own_lines[top : top + stencil, :] = lists
        own_lines[top + stencil : top + stencil + 8, :] = jnp.broadcast_to(batches, (8, LANES))
        codes = jnp.concatenate(
            [
                jnp.zeros((CODES, LANES), F32),
                place * float(LANES) + lane_sum[i],
                jnp.zeros((LANES - CODES - stencil, LANES), F32),
            ],
            axis=0,
        )
        own[i * LANES : (i + 1) * LANES, :] = own_sum[i] + codes.T


def band(shape, taps, shift):
    distance = iota(shape, 1) - iota(shape, 0) + shift
    result = jnp.zeros(shape, F32)
    for tap in range(taps.shape[0]):
        result = jnp.where(distance == tap, taps[tap], result)
    return result


def band_rev(shape, taps, shift):
    distance = iota(shape, 0) - iota(shape, 1) + shift
    result = jnp.zeros(shape, F32)
    for tap in range(taps.shape[0]):
        result = jnp.where(distance == tap, taps[tap], result)
    return result


def exact_nt(a, b):
    return lax.dot_general(
        a,
        b,
        (((1,), (1,)), ((), ())),
        precision=lax.Precision.HIGHEST,
        preferred_element_type=F32,
    )


def store_split(ref, index, value):
    high, low = split2(value)
    ref[(0,) + index] = high
    ref[(1,) + index] = low


def bands_kernel(kx, ky, lat2, lon2, lat1, lon1, *, rows_block):
    margin = kx.shape[0] // 2
    window = lat2.shape[2]
    first = band((window, window), ky, margin)
    reach = first[LANES : LANES + WIDE, :]
    place = iota((window, window), 1)
    for variant in range(3):
        kept = first
        if variant == 0:
            kept = jnp.where(place >= LANES, first, 0.0)
        if variant == 2:
            kept = jnp.where(place < LANES + WIDE, first, 0.0)
        store_split(lat2, (variant,), exact_nt(kept, reach))
    size = lon2.shape[1]
    wide = size + 2 * HALO
    depth = (wide + 32 + LANES - 1) // LANES * LANES
    second = band((wide, depth), kx, -(16 - margin))
    store_split(lon2, (), exact_nt(second[HALO : HALO + size, :], second))
    store_split(lat1, (), band_rev((rows_block, rows_block + 2 * PAD), ky, PAD + margin))
    store_split(lon1, (), band((2 * WIDE, WIDE), kx, LANES + margin))


def pairs(low, high, action):
    def step(i, carry):
        one = low + 2 * i
        action(one, jnp.minimum(one + 1, high - 1), one + 1 < high)
        return carry

    lax.fori_loop(0, lax.shift_right_logical(high - low + 1, 1), step, 0)


def zero_all(refs):
    rows = refs[0].shape[0]
    step = 256

    def clear(i, carry):
        for ref in refs:
            ref[pl.ds(pl.multiple_of(i * step, 8), step), :] = jnp.zeros((step, LANES), F32)
        return carry

    whole = rows // step
    lax.fori_loop(0, whole, clear, 0)
    if rows % step:
        for ref in refs:
            ref[whole * step : rows, :] = jnp.zeros((rows % step, LANES), F32)


def scatter_entries(copies, entries, lane):
    for start in range(0, len(entries), len(copies)):
        group = []
        for ref, (address, value) in zip(copies, entries[start : start + len(copies)]):
            line = lax.shift_right_logical(address, 7)
            spread = jnp.where(lane == (address & (LANES - 1)), value, 0.0)
            group.append((ref, line, ref[pl.ds(line, 1), :] + spread))
        for ref, line, value in group:
            ref[pl.ds(line, 1), :] = value


def spot(sender, idx, per, stencil):
    return sender * per + idx + lax.shift_right_logical(idx, 7) * ((stencil - 1) * LANES)


def copy_parts(layout, source, target, place, chunk, chunks, group, sem):
    begin, size = place
    words = group * size * LANES
    at = begin * LANES + chunk * words
    return pltpu.make_async_copy(source.at[pl.ds(at, words)], target, sem)


def apply_kernel(
    *refs, first, layout, columns, height, hold, stencil, capacity, senders, parts, levels
):
    refs = list(refs)

    def take(count):
        taken = refs[:count]
        del refs[:count]
        return taken

    meta, ints, floats, own_lines, own = take(5)
    if not first:
        replies_h, replies = take(2)
    std_h, std_l_h, std_r_h, lat2_h, lon2_h = take(5)
    if not first:
        merged_h = take(1)[0]
    field_h, send = take(2)
    if first:
        info_out, merged_h = take(2)
    addr, wgt, start, lines_s, val = take(5)
    if first:
        std_flat, picked, chosen = take(3)
    scale, merged, sums, high_s, low_s, std, std_l, std_r, lat2, lon2, field = take(11)
    copies = take(PAIR)
    sems, in_sems, out_sems, val_sem = take(4)

    me = meta[0]
    wide = columns + 2 * HALO
    blocks = height // LANES
    group = min(GROUP, senders)
    chunks = senders // group
    slots = senders * capacity
    lane = iota((1, LANES), 1)
    per = stencil * hold
    table = layout.table

    def chunk_copies(chunk):
        todo = [
            (ints, addr, layout.ints["addr"]),
            (floats, wgt, layout.floats["wgt"]),
            (ints, start, layout.ints["start"]),
        ]
        if first:
            todo.append((floats, val, layout.floats["val"]))
        return [
            copy_parts(layout, source, target, place, chunk, chunks, group, sems.at[i])
            for i, (source, target, place) in enumerate(todo)
        ]

    def load_chunk(chunk):
        for copy in chunk_copies(chunk):
            copy.start()
        for copy in chunk_copies(chunk):
            copy.wait()

    pending = []
    if chunks == 1:
        pending = chunk_copies(0)
        for copy in pending:
            copy.start()
    operands = [
        pltpu.make_async_copy(source, target, in_sems.at[i])
        for i, (source, target) in enumerate(
            (
                (std_h, std),
                (std_l_h, std_l),
                (std_r_h, std_r),
                (lat2_h, lat2),
                (lon2_h, lon2),
            )
        )
    ]
    own_copy = pltpu.make_async_copy(own_lines, lines_s, in_sems.at[5])
    own_copy.start()
    for copy in operands:
        copy.start()

    def value_copy(owner):
        at = pl.multiple_of(owner * (replies.shape[1] * LANES), 1024)
        return pltpu.make_async_copy(
            replies_h.at[pl.ds(at, slots)], val.at[pl.ds(owner * slots, slots)], val_sem.at[owner]
        )

    def each_owner(action):
        def step(owner, carry):
            action(value_copy(owner))
            return carry

        lax.fori_loop(0, parts, step, 0)

    if not first:
        each_owner(lambda copy: copy.start())
    zero_all(copies)
    zero_all([sums])

    merged_copy = pltpu.make_async_copy(
        *((merged, merged_h) if first else (merged_h, merged)), in_sems.at[6]
    )
    if not first:
        merged_copy.start()

    lane_of = iota((slots, LANES), 1)
    known = own[...]
    column = 2 * stencil if first else 2 * stencil + 2
    scale[...] = jnp.broadcast_to(known[:, column : column + 1], (slots, LANES))
    own_copy.wait()
    if pending:
        pending.pop(2).wait()
    if not first:
        merged_copy.wait()

    after = lax.rem(me + 1, parts)
    ahead = lax.rem(me + parts - 1, parts)

    def start_of(sender, owner, row, half):
        return start[sender * table + row * hold + half * LANES + owner]

    def entries_of(sender, idx, value):
        base = spot(sender, idx, per, stencil)
        return [
            (addr[base + k * LANES], wgt[base + k * LANES] * value) for k in range(stencil)
        ]

    def own_line(slot, k):
        at = lax.shift_right_logical(slot, 7) * ((stencil + 7) * LANES) + slot
        return lines_s[at + k * LANES]

    def batches_of(one, two):
        return jnp.maximum(own_line(one, stencil), own_line(two, stencil))

    def own_groups(action):
        def group_at(top):
            top = pl.multiple_of(top, 8)
            most = own_line(top, stencil)
            for i in range(1, 8):
                most = jnp.maximum(most, own_line(top + i, stencil))

            @pl.when(most <= 1)
            def _():
                action(top, True)

            @pl.when(most > 1)
            def _():
                action(top, False)

        if capacity % 8 or chunks > 1:

            def step(i, carry):
                group_at(i * 8)
                return carry

            lax.fori_loop(0, slots // 8, step, 0)
        else:

            def per_sender(sender, carry):
                amount = start_of(sender, me, 0, 1) - start_of(sender, me, 0, 0)

                def step(i, inner):
                    group_at(sender * capacity + i * 8)
                    return inner

                lax.fori_loop(0, lax.shift_right_logical(amount + 7, 3), step, 0)
                return carry

            lax.fori_loop(0, senders, per_sender, 0)

    lane_f = iota((8, LANES), 1).astype(F32)

    def columns_of(info, begin):
        return [
            jnp.broadcast_to(info[:, begin + k : begin + k + 1], (8, LANES))
            for k in range(stencil)
        ]

    def build(top, short):
        info = own[pl.ds(top, 8), :]
        codes = columns_of(info, CODES)
        weights = columns_of(info, stencil)
        for place in range(stencil):
            row = jnp.zeros((8, LANES), F32)
            if place < BATCH or not short:
                at = lane_f + float(LANES * place)
                for k in range(place, stencil):
                    row = row + jnp.where(at == codes[k], weights[k], 0.0)
            merged[pl.ds(place * slots + top, 8), :] = row

    if first:
        own_groups(build)
        merged_copy.start()

    def own_pairs(chunk, action):
        def per_sender(sender, carry):
            amount = start_of(sender, me, 0, 1) - start_of(sender, me, 0, 0)
            base = (chunk * group + sender) * capacity
            pairs(base, base + amount, action)
            return carry

        lax.fori_loop(0, group, per_sender, 0)

    def scatter_own(chunk):
        def action(one, two, has_two):
            second = jnp.where(has_two, 1.0, 0.0)
            values = (scale[pl.ds(one, 1), :], scale[pl.ds(two, 1), :] * second)

            def batch(begin):
                todo = []
                for slot, value, ref in zip((one, two), values, copies):
                    for j in range(BATCH):
                        line = own_line(slot, begin + j)
                        row = merged[pl.ds((begin + j) * slots + slot, 1), :] * value
                        todo.append((ref, line, ref[pl.ds(line, 1), :] + row))
                for ref, line, row in todo:
                    ref[pl.ds(line, 1), :] = row

            def more(i, carry):
                batch(i * BATCH)
                return carry

            batch(0)
            lax.fori_loop(1, batches_of(one, two), more, 0)

        own_pairs(chunk, action)

    def scatter_halo(chunk):
        def per_sender(sender, carry):
            for owner, low, high in ((after, (1, 0), (1, 1)), (ahead, (2, 0), (0, 1))):
                begin = start_of(sender, owner, 0, 0)

                def value_of(idx, owner=owner, begin=begin):
                    if first:
                        return val[sender * hold + idx]
                    place = (chunk * group + sender) * capacity + idx - begin
                    return val[owner * slots + place]

                def action(one, two, has_two, value_of=value_of):
                    second = jnp.where(has_two, value_of(two), 0.0)
                    scatter_entries(
                        copies,
                        entries_of(sender, one, value_of(one)) + entries_of(sender, two, second),
                        lane,
                    )

                pairs(start_of(sender, owner, *low), start_of(sender, owner, *high), action)
            return carry

        lax.fori_loop(0, group, per_sender, 0)

    def scatter_chunk(chunk):
        scatter_own(chunk)
        for copy in pending:
            copy.wait()
        scatter_halo(chunk)

    def over_chunks(work):
        if chunks == 1:
            work(0)
        else:

            def step(chunk, carry):
                load_chunk(chunk)
                work(chunk)
                return carry

            lax.fori_loop(0, chunks, step, 0)

    if not first:
        each_owner(lambda copy: copy.wait())
    over_chunks(scatter_chunk)
    for copy in operands:
        copy.wait()

    for jb in range(blocks):
        lanes = slice(jb * LANES, (jb + 1) * LANES)
        for low, size, source in (
            (0, HALO, std_l),
            (HALO, columns, std),
            (HALO + columns, HALO, std_r),
        ):
            rows = slice(jb * wide + low, jb * wide + low + size)
            total = copies[0][rows, :]
            for ref in copies[1:]:
                total = total + ref[rows, :]
            high, lo = split2(total * source[:, lanes])
            high_s[low : low + size, lanes] = high
            low_s[low : low + size, lanes] = lo
        if first:
            std_flat[jb * wide + HALO : jb * wide + HALO + columns, :] = std[:, lanes]

    smoothed = copies[0]
    size = lon2.shape[1]
    count = height // WIDE
    outgoing = [merged_copy] if first else []
    for block in range(count):
        variant = 0 if block == 0 else (2 if block == count - 1 else 1)
        low = max(block * WIDE - LANES, 0)
        high = min(block * WIDE + WIDE + LANES, height)
        inner = slice(low - (block * WIDE - LANES), high - (block * WIDE - LANES))
        matrix = (lat2[0, variant, inner, :], lat2[1, variant, inner, :])
        along = mm_parts((high_s[:, low:high], low_s[:, low:high]), matrix)
        parts_y = split2(along)
        lanes = slice(block * WIDE, (block + 1) * WIDE)
        for begin in range(0, columns, size):
            some = min(size, columns - begin)
            rows = slice(begin, begin + some)
            window = slice(begin, begin + some + 2 * HALO)
            matrix = tuple(lon2[i, 0:some, 0 : some + 2 * HALO] for i in range(2))
            result = mm_parts(matrix, (parts_y[0][window, :], parts_y[1][window, :]))
            field[rows, lanes] = result
            scaled = result * std[rows, lanes]
            for half in range(WIDE // LANES):
                top = (block * (WIDE // LANES) + half) * wide + HALO + begin
                smoothed[top : top + some, :] = scaled[:, half * LANES : (half + 1) * LANES]
        outgoing.append(
            pltpu.make_async_copy(field.at[:, lanes], field_h.at[:, lanes], out_sems.at[block])
        )
        outgoing[-1].start()

    def gather_chunk(chunk):
        def action(one, two, has_two):
            def batch(begin, totals):
                result = []
                for slot, total in zip((one, two), totals):
                    terms = []
                    for j in range(BATCH):
                        line = own_line(slot, begin + j)
                        row = merged[pl.ds((begin + j) * slots + slot, 1), :]
                        terms.append(row * smoothed[pl.ds(line, 1), :])
                        if first:
                            picked[pl.ds((begin + j) * slots + slot, 1), :] = std_flat[
                                pl.ds(line, 1), :
                            ]
                    result.append(total + ((terms[0] + terms[1]) + (terms[2] + terms[3])))
                return tuple(result)

            zero = jnp.zeros((1, LANES), F32)
            totals = lax.fori_loop(
                1,
                batches_of(one, two),
                lambda i, totals: batch(i * BATCH, totals),
                batch(0, (zero, zero)),
            )
            for slot, total in zip((one, two), totals):
                sums[pl.ds(slot, 1), :] = total

        own_pairs(chunk, action)

    over_chunks(gather_chunk)

    def pick(top, short):
        info = own[pl.ds(top, 8), :]
        codes = columns_of(info, CODES)
        places = BATCH if short else stencil
        rows = [picked[pl.ds(place * slots + top, 8), :] for place in range(places)]
        result = jnp.zeros((8, LANES), F32)
        for k in range(stencil):
            cell = jnp.zeros((8, LANES), F32)
            for place in range(min(k + 1, places)):
                at = lane_f + float(LANES * place)
                cell = jnp.where(at == codes[k], rows[place], cell)
            cell = jnp.sum(cell, axis=1, keepdims=True)
            result = jnp.where(lane_f == float(stencil + k), cell, result)
        chosen[pl.ds(top, 8), :] = result * info

    if first:
        own_groups(pick)

    def whole(x):
        return jnp.sum(x, axis=0, keepdims=True)

    total = jnp.sum(sums[...], axis=1, keepdims=True)
    lines = slots // LANES
    known = own[...]
    source, weight, reply, image0 = (
        known[:, 2 * stencil + i : 2 * stencil + i + 1] for i in range(4)
    )
    if first:
        reply = weight * total
        known = jnp.where(lane_of == 2 * stencil + 2, reply, known)
        known = jnp.where(lane_of == 2 * stencil + 3, total, known)
        info_out[...] = known
        turned = known.T[2 * stencil + 2 : 2 * stencil + 3, :]
        message = [turned[:, i * LANES : (i + 1) * LANES] for i in range(lines)]
        message.append(
            jnp.where(
                lane == 0, whole(source * total), jnp.where(lane == 1, whole(reply * total), 0.0)
            )
        )
        message.append(jnp.zeros((8 - len(message), LANES), F32))
        factors = chosen[...].T
        for k in range(stencil):
            row = factors[stencil + k : stencil + k + 1, :]
            message += [row[:, i * LANES : (i + 1) * LANES] for i in range(lines)]
        message = jnp.concatenate(message, axis=0)
    else:
        slab = jnp.sum(replies[:, 0:8, :], axis=0)[lines : lines + 1, :]
        length = slab[:, 0:1] / (slab[:, 0:1] + slab[:, 1:2])
        both = source + reply
        s_both = image0 + total
        resid = source - length * both
        s_resid = image0 - length * s_both
        values = [
            resid * s_resid,
            resid * s_both,
            both * s_both,
            resid * image0,
            both * image0,
            weight * s_resid * s_resid,
            weight * s_resid * s_both,
            weight * s_both * s_both,
            weight * s_resid * image0,
            weight * s_both * image0,
            source * image0,
            reply * image0,
        ]
        message = jnp.where(lane == len(values), length, 0.0)
        for i, value in enumerate(values):
            message = jnp.where(lane == i, whole(value), message)
        message = jnp.concatenate([message, jnp.zeros((7, LANES), F32)], axis=0)

    def send_to(i, carry):
        send[i] = message
        return carry

    lax.fori_loop(0, send.shape[0], send_to, 0)
    for copy in outgoing:
        copy.wait()


def final_kernel(
    ints,
    floats,
    replies_h,
    totals,
    std_h,
    field0_h,
    field1_h,
    lat1,
    lon1,
    control_h,
    increment_h,
    addr,
    listed,
    start,
    slot,
    val,
    factors,
    std,
    field0,
    field1,
    control,
    high_s,
    low_s,
    *rest,
    layout,
    hold,
    stencil,
    capacity,
    senders,
    parts,
    length,
):
    copies = rest[:COPIES]
    sems, in_sems, out_sems = rest[COPIES:]
    group = min(GROUP, senders)
    chunks = senders // group
    per = stencil * hold
    rows_block = control.shape[0]
    high_rows = rows_block + 2 * PAD
    lane = iota((1, LANES), 1)
    stride = group * capacity
    owner_words = factors.shape[0] // parts
    to_factors = owner_words - stencil * stride

    def chunk_copies(chunk):
        todo = [
            (ints, addr, layout.ints["rows"]),
            (ints, listed, layout.ints["listed"]),
            (ints, start, layout.ints["start"]),
            (ints, slot, layout.ints["slot"]),
            (floats, val, layout.floats["val"]),
        ]
        result = [
            copy_parts(layout, source, target, place, chunk, chunks, group, sems.at[i])
            for i, (source, target, place) in enumerate(todo)
        ]
        words = parts * owner_words
        result.append(
            pltpu.make_async_copy(
                replies_h.at[pl.ds(chunk * words, words)], factors, sems.at[len(todo)]
            )
        )
        return result

    pending = []
    if chunks == 1:
        pending = chunk_copies(0)
        for copy in pending:
            copy.start()
    operands = [
        pltpu.make_async_copy(source, target, in_sems.at[i])
        for i, (source, target) in enumerate(
            ((std_h, std), (field0_h, field0), (field1_h, field1))
        )
    ]
    for copy in operands:
        copy.start()

    slabs = totals.shape[1]
    every = jnp.sum(totals[...], axis=0)
    norm0 = quad0 = None
    for i in range(slabs):
        line = every[i, 0:1, :]
        a, b = line[:, 10:11], line[:, 11:12]
        norm0 = a if norm0 is None else norm0 + a
        quad0 = b if quad0 is None else quad0 + b
    step0 = norm0 / (norm0 + quad0)
    norm1 = cross = quad1 = quad01 = jnp.zeros((1, 1), F32)
    for i in range(slabs):
        line = every[i, 0:1, :]
        v = [line[:, j : j + 1] for j in range(10)]
        shift = totals[0, i, 0:1, 12:13] - step0
        norm1 = norm1 + (v[0] + shift * (2.0 * v[1] + shift * v[2]))
        cross = cross + (v[3] + shift * v[4])
        quad1 = quad1 + (v[5] + shift * (2.0 * v[6] + shift * v[7]))
        quad01 = quad01 + (v[8] + shift * v[9])
    ratio = norm1 / norm0
    curvature = norm1 + quad1 + ratio * (
        2.0 * (cross + quad01) + ratio * (norm0 + quad0)
    )
    step1 = norm1 / curvature
    first = step0 + step1 * (1.0 - step0 + ratio)
    second = -step0 * step1
    first_line = jnp.broadcast_to(first, (1, LANES))
    second_line = jnp.broadcast_to(second, (1, LANES))

    zero_all(copies)

    def scatter_chunk():
        def per_sender(sender, carry):
            def entries_of(at, scale):
                idx = listed[sender * hold + at]
                place = slot[sender * hold + idx]
                place = place + lax.div(place, stride) * (owner_words - stride)
                base = spot(sender, idx, per, stencil)
                z0 = val[sender * hold + idx] * scale
                u = factors[place] * scale
                value = first_line * z0 + second_line * u
                return [
                    (addr[base + k * LANES], factors[place + to_factors + k * stride] * value)
                    for k in range(stencil)
                ]

            def action(one, two, has_two):
                scale = jnp.where(has_two, 1.0, 0.0)
                scatter_entries(copies, entries_of(one, 1.0) + entries_of(two, scale), lane)

            pairs(0, start[sender * layout.table + layout.table - 1], action)
            return carry

        lax.fori_loop(0, group, per_sender, 0)

    if chunks == 1:
        for copy in pending:
            copy.wait()
        scatter_chunk()
    else:

        def step(chunk, carry):
            for copy in chunk_copies(chunk):
                copy.start()
            for copy in chunk_copies(chunk):
                copy.wait()
            scatter_chunk()
            return carry

        lax.fori_loop(0, chunks, step, 0)

    for copy in operands:
        copy.wait()
    increment = field0
    increment[...] = std[...] * (first * field0[...] + second * field1[...])
    outgoing = [pltpu.make_async_copy(increment, increment_h, out_sems.at[0])]
    outgoing[0].start()

    pair = WIDE // LANES
    count = length // WIDE
    for block in range(count):
        pieces = []
        for half in range(pair):
            rows = slice((block * pair + half) * high_rows, (block * pair + half + 1) * high_rows)
            total = copies[0][rows, :]
            for ref in copies[1:]:
                total = total + ref[rows, :]
            pieces.append(total)
        whole = split2(jnp.concatenate(pieces, axis=1))
        size = lat1.shape[1]
        for top in range(0, rows_block, size):
            window = slice(top, top + size + 2 * PAD)
            along = mm_parts((lat1[0], lat1[1]), (whole[0][window, :], whole[1][window, :]))
            high, low = split2(along)
            high_s[top : top + size, block * WIDE : (block + 1) * WIDE] = high
            low_s[top : top + size, block * WIDE : (block + 1) * WIDE] = low

    def window(ref, block):
        low, high = block * WIDE - LANES, (block + 1) * WIDE + LANES
        if low < 0:
            return jnp.concatenate([ref[:, length + low : length], ref[:, 0:high]], axis=1)
        if high > length:
            return jnp.concatenate([ref[:, low:length], ref[:, 0 : high - length]], axis=1)
        return ref[:, low:high]

    every_lanes = 4
    for block in range(count):
        control[:, block * WIDE : (block + 1) * WIDE] = mm_parts(
            (window(high_s, block), window(low_s, block)), (lon1[0], lon1[1])
        )
        if block % every_lanes == every_lanes - 1:
            lanes = slice((block + 1 - every_lanes) * WIDE, (block + 1) * WIDE)
            outgoing.append(
                pltpu.make_async_copy(
                    control.at[:, lanes], control_h.at[:, lanes], out_sems.at[len(outgoing)]
                )
            )
            outgoing[-1].start()
    for copy in outgoing:
        copy.wait()


def body(
    background_std,
    x_kernel,
    y_kernel,
    obs_owner,
    obs_cells,
    obs_weights,
    innovation,
    obs_precision,
    obs_counts,
):
    parts = lax.axis_size("pencil")
    levels = lax.axis_size("lev")
    me = lax.axis_index("pencil")
    _, columns, height = background_std.shape
    hold, stencil = obs_cells.shape
    margin = x_kernel.shape[1] // 2
    capacity = 2 * hold // parts
    senders = parts
    slots = senders * capacity
    rows_block = height // parts
    length = columns * parts
    blocks = height // LANES
    wide = columns + 2 * HALO
    group = min(GROUP, senders)
    chunks = senders // group
    layout = Layout(senders, hold, stencil, parts)
    std = background_std[0]

    packed = pl.pallas_call(
        functools.partial(
            pack_kernel, parts=parts, columns=columns, height=height, margin=margin
        ),
        out_shape=jax.ShapeDtypeStruct((parts, PACK, hold), F32),
        in_specs=[smem()] + [vmem()] * 5,
        out_specs=vmem(),
        compiler_params=params(),
        name="pack",
    )(
        obs_counts,
        obs_owner.T,
        obs_cells.T,
        obs_weights.T,
        innovation[None, :],
        obs_precision[None, :],
    )
    recv = lax.all_to_all(packed, "pencil", split_axis=0, concat_axis=0, tiled=True)

    right = [(p, (p + 1) % parts) for p in range(parts)]
    left = [(p, (p - 1) % parts) for p in range(parts)]
    std_l = lax.ppermute(std[columns - HALO :, :], "pencil", right)
    std_r = lax.ppermute(std[:HALO, :], "pencil", left)

    size = min(columns, WIDE - 2 * HALO)
    row_size = min(rows_block, LANES)
    lat2, lon2, lat1, lon1 = pl.pallas_call(
        functools.partial(bands_kernel, rows_block=row_size),
        out_shape=[
            jax.ShapeDtypeStruct((2, 3, 2 * WIDE, WIDE), BF),
            jax.ShapeDtypeStruct((2, size, size + 2 * HALO), BF),
            jax.ShapeDtypeStruct((2, row_size, row_size + 2 * PAD), BF),
            jax.ShapeDtypeStruct((2, 2 * WIDE, WIDE), BF),
        ],
        in_specs=[smem(), smem()],
        out_specs=[vmem()] * 4,
        compiler_params=params(),
        name="bands",
    )(x_kernel[0], y_kernel[0])

    meta = jnp.reshape(me, (1,)).astype(I32)
    ints, floats, own_lines, own = pl.pallas_call(
        functools.partial(
            unpack_kernel,
            layout=layout,
            parts=parts,
            columns=columns,
            height=height,
            capacity=capacity,
            stencil=stencil,
            group=group,
        ),
        out_shape=[
            jax.ShapeDtypeStruct((layout.int_rows, LANES), I32),
            jax.ShapeDtypeStruct((layout.float_rows, LANES), F32),
            jax.ShapeDtypeStruct((slots // LANES * (stencil + 8), LANES), I32),
            jax.ShapeDtypeStruct((slots, LANES), F32),
        ],
        in_specs=[smem(), vmem()],
        out_specs=[vmem()] * 4,
        scratch_shapes=[
            pltpu.VMEM((slots // LANES, LANES, LANES), F32),
            pltpu.VMEM((slots // LANES, stencil, LANES), F32),
            pltpu.VMEM((slots // LANES, stencil, LANES), F32),
        ],
        compiler_params=params(),
        name="unpack",
    )(meta, recv)
    ints = ints.reshape(-1)
    floats = floats.reshape(-1)
    own_lines = own_lines.reshape(-1)

    acc = pltpu.VMEM((blocks * wide + 8, LANES), F32)
    column_slots = pltpu.VMEM((slots, LANES), F32)
    static = dict(
        layout=layout,
        columns=columns,
        height=height,
        hold=hold,
        stencil=stencil,
        capacity=capacity,
        senders=senders,
        parts=parts,
        levels=levels,
    )
    per = group * stencil * hold
    line = group * hold
    index_scratch = [
        pltpu.SMEM((per,), I32),
        pltpu.SMEM((per,), F32),
        pltpu.SMEM((group * layout.table,), I32),
        pltpu.SMEM((slots * (stencil + 8),), I32),
    ]
    work = (
        [column_slots, pltpu.VMEM((stencil * slots, LANES), F32), column_slots]
        + [pltpu.VMEM((wide, height), BF)] * 2
        + [
            pltpu.VMEM((columns, height), F32),
            pltpu.VMEM((HALO, height), F32),
            pltpu.VMEM((HALO, height), F32),
            pltpu.VMEM(lat2.shape, BF),
            pltpu.VMEM(lon2.shape, BF),
            pltpu.VMEM((columns, height), F32),
        ]
        + [acc] * PAIR
        + [
            pltpu.SemaphoreType.DMA((4,)),
            pltpu.SemaphoreType.DMA((7,)),
            pltpu.SemaphoreType.DMA((height // WIDE,)),
            pltpu.SemaphoreType.DMA((parts,)),
        ]
    )
    field_shape = jax.ShapeDtypeStruct((columns, height), F32)
    reply_rows = 8 + stencil * slots // LANES
    field0, message, info, merged = pl.pallas_call(
        functools.partial(apply_kernel, first=True, **static),
        out_shape=[
            field_shape,
            jax.ShapeDtypeStruct((parts, reply_rows, LANES), F32),
            jax.ShapeDtypeStruct((slots, LANES), F32),
            jax.ShapeDtypeStruct((stencil * slots, LANES), F32),
        ],
        in_specs=[smem()] + [hbm()] * 3 + [vmem()] + [hbm()] * 5,
        out_specs=[hbm()] + [vmem()] * 2 + [hbm()],
        scratch_shapes=index_scratch
        + [
            pltpu.SMEM((line,), F32),
            acc,
            pltpu.VMEM((stencil * slots, LANES), F32),
            column_slots,
        ]
        + work,
        compiler_params=params(),
        name="apply_first",
    )(meta, ints, floats, own_lines, own, std, std_l, std_r, lat2, lon2)

    replies = lax.all_to_all(message, "pencil", split_axis=0, concat_axis=0, tiled=True)
    back = replies.reshape(-1)

    field1, sums = pl.pallas_call(
        functools.partial(apply_kernel, first=False, **static),
        out_shape=[
            field_shape,
            jax.ShapeDtypeStruct((parts * levels, 8, LANES), F32),
        ],
        in_specs=[smem()] + [hbm()] * 3 + [vmem(), hbm(), vmem()] + [hbm()] * 6,
        out_specs=[hbm(), vmem()],
        scratch_shapes=index_scratch + [pltpu.SMEM((parts * slots,), F32)] + work,
        compiler_params=params(),
        name="apply_second",
    )(
        meta,
        ints,
        floats,
        own_lines,
        info,
        back,
        replies,
        std,
        std_l,
        std_r,
        lat2,
        lon2,
        merged,
    )

    totals = lax.all_to_all(sums, ("pencil", "lev"), split_axis=0, concat_axis=0, tiled=True)
    totals = totals.reshape(parts, levels, 8, LANES)

    by_chunk = back
    if chunks > 1:
        by_chunk = jnp.concatenate(
            [replies[:, : slots // LANES, :], replies[:, 8:, :]], axis=1
        ).reshape(parts, stencil + 1, chunks, group * capacity)
        by_chunk = jnp.transpose(by_chunk, (2, 0, 1, 3)).reshape(-1)
    owner_words = by_chunk.shape[0] // (chunks * parts)
    high_rows = rows_block + 2 * PAD
    acc_rows = pltpu.VMEM(((length // LANES) * high_rows + 8, LANES), F32)
    control, increment = pl.pallas_call(
        functools.partial(
            final_kernel,
            layout=layout,
            hold=hold,
            stencil=stencil,
            capacity=capacity,
            senders=senders,
            parts=parts,
            length=length,
        ),
        out_shape=[
            jax.ShapeDtypeStruct((rows_block, length), F32),
            field_shape,
        ],
        in_specs=[hbm()] * 3 + [vmem()] + [hbm()] * 3 + [vmem()] * 2,
        out_specs=[hbm()] * 2,
        scratch_shapes=[
            pltpu.SMEM((per,), I32),
            pltpu.SMEM((line,), I32),
            pltpu.SMEM((group * layout.table,), I32),
            pltpu.SMEM((line,), I32),
            pltpu.SMEM((line,), F32),
            pltpu.SMEM((parts * owner_words,), F32),
            pltpu.VMEM((columns, height), F32),
            pltpu.VMEM((columns, height), F32),
            pltpu.VMEM((columns, height), F32),
            pltpu.VMEM((rows_block, length), F32),
            pltpu.VMEM((rows_block, length), BF),
            pltpu.VMEM((rows_block, length), BF),
        ]
        + [acc_rows] * COPIES
        + [
            pltpu.SemaphoreType.DMA((7,)),
            pltpu.SemaphoreType.DMA((3,)),
            pltpu.SemaphoreType.DMA((1 + length // WIDE,)),
        ],
        compiler_params=params(),
        name="outputs",
    )(ints, floats, by_chunk, totals, std, field0, field1, lat1, lon1)
    return control[None], increment[None]


def solution(mesh):
    return jax.shard_map(
        body,
        mesh=mesh,
        in_specs=(
            P("lev", "pencil", None),
            P("lev", None),
            P("lev", None),
            P(("pencil", "lev"), None),
            P(("pencil", "lev"), None),
            P(("pencil", "lev"), None),
            P(("pencil", "lev")),
            P(("pencil", "lev")),
            P(("pencil", "lev")),
        ),
        out_specs=(P("lev", "pencil", None), P("lev", "pencil", None)),
        check_vma=False,
    )
```

```python
import functools

import jax
import jax.numpy as jnp
import numpy as np
from jax import lax
from jax.experimental import pallas as pl
from jax.experimental.pallas import tpu as pltpu
from jax.sharding import PartitionSpec as P


BF = jnp.bfloat16
F32 = jnp.float32
I32 = jnp.int32
LANES = 128
WIDE = 256
HALO = 32
PAD = 16
PACK = 40
GROUP = 8
COPIES = 4
PAIR = 2
BATCH = 4
BLOCK = 32
CODES = 40
VMEM_LIMIT = 58 * 1024 * 1024


def vmem():
    return pl.BlockSpec(memory_space=pltpu.VMEM)


def smem():
    return pl.BlockSpec(memory_space=pltpu.SMEM)


def hbm():
    return pl.BlockSpec(memory_space=pl.ANY)


def cost(nanoseconds):
    return pl.CostEstimate(flops=0, bytes_accessed=3690 * nanoseconds, transcendentals=0)


def params():
    return pltpu.CompilerParams(vmem_limit_bytes=VMEM_LIMIT)


def split2(x):
    high = x.astype(BF)
    return high, (x - high.astype(F32)).astype(BF)


def split3(x):
    high = x.astype(BF)
    rest = x - high.astype(F32)
    mid = rest.astype(BF)
    return high, mid, (rest - mid.astype(F32)).astype(BF)


def mm(a, b):
    return jnp.dot(a, b, preferred_element_type=F32)


def mm_parts(a_parts, b_parts):
    (ah, al), (bh, bl) = a_parts, b_parts
    return mm(jnp.concatenate([ah, al, ah], axis=1), jnp.concatenate([bh, bh, bl], axis=0))


def iota(shape, dim):
    return lax.broadcasted_iota(I32, shape, dim)


def pack_kernel(
    counts, owner, cells, weights, depart, prec, out, *, parts, columns, height, margin
):
    stencil, hold = cells.shape
    shift = height.bit_length() - 1
    block = height // parts
    reach = 2 * margin
    row_id = iota((hold, hold), 0)
    col_id = iota((hold, hold), 1)
    eye = row_id == col_id
    col_f = col_id.astype(F32)
    live = iota((1, hold), 1) < counts[0]
    cell = cells[...]
    column = lax.shift_right_logical(cell, jnp.full(cell.shape, shift, I32))
    row = cell & (height - 1)

    def any_of(mask):
        return jnp.max(jnp.where(mask, 1.0, 0.0), axis=0, keepdims=True)

    def turn(line):
        return jnp.sum(jnp.where(eye, line, 0.0), axis=1, keepdims=True)

    left = any_of(column < reach)
    right = any_of(column >= columns - reach)
    side = left + 3.0 * right - 2.0 * left * right
    base = jnp.where(live, owner[...].astype(F32) * 4.0, 4.0 * parts)
    key = jnp.where(live, base + side, base)
    key_col = turn(key)
    before = (key_col < key) | ((key_col == key) & (row_id < col_id))
    rank = jnp.sum(jnp.where(before, 1.0, 0.0), axis=0, keepdims=True)
    begin = jnp.sum(jnp.where(key_col < base, 1.0, 0.0), axis=0, keepdims=True)
    rank_col = turn(rank)
    perm = jnp.where(rank_col == col_f, 1.0, 0.0).astype(BF)

    def sort(values):
        total = None
        for part in split3(values):
            term = mm(part, perm)
            total = term if total is None else total + term
        return total

    weight = jnp.where(live, prec[...], 0.0)
    rest = [weight * depart[...], weight, key, rank - begin, jnp.zeros((4, hold), F32)]
    values = [cell.astype(F32), weights[...]] + rest
    ordered = sort(jnp.concatenate(values, axis=0))
    line = iota((8, hold), 0)
    tail = ordered[2 * stencil : 2 * stencil + 8, :]
    first_half = col_f < float(LANES)
    fourfold = 4.0 * jnp.where(first_half, col_f, col_f - float(LANES))
    for i, (low, high) in enumerate(((0.0, 4.0), (1.0, 3.0), (2.0, 2.0))):
        bound = fourfold + jnp.where(first_half, low, high)
        begins = jnp.sum(jnp.where(key_col < bound, 1.0, 0.0), axis=0, keepdims=True)
        tail = jnp.where(line == 5 + i, begins, tail)
    last = (line == 7) & (iota((8, hold), 1) == hold - 1)

    def per_part(part, carry):
        low = part * block - margin
        high = (part + 1) * block + margin
        flag = jnp.where(live, any_of((row >= low) & (row < high)), 0.0)
        place = jnp.sum(jnp.where(col_id < row_id, flag, 0.0), axis=1, keepdims=True)
        chosen = (place == col_f) & (turn(flag) > 0.0)
        listed = jnp.sum(jnp.where(chosen, rank_col, 0.0), axis=0, keepdims=True)
        amount = jnp.sum(flag, axis=1, keepdims=True)
        out[part, 0 : 2 * stencil, :] = ordered[0 : 2 * stencil, :]
        out[part, 2 * stencil : 2 * stencil + 8, :] = jnp.where(
            line == 4, listed, jnp.where(last, amount, tail)
        )
        return carry

    lax.fori_loop(0, parts, per_part, 0, unroll=parts <= GROUP)


class Layout:
    def __init__(self, senders, hold, stencil, parts):
        lines = hold // LANES
        self.table = 3 * hold
        sizes = dict(
            addr=stencil * lines, rows=stencil * lines, listed=lines, slot=lines, start=3 * lines
        )
        self.ints = {}
        at = 0
        for name, size in sizes.items():
            self.ints[name] = (at, size)
            at += senders * size
        self.int_rows = at
        self.floats = {}
        at = 0
        for name, size in dict(wgt=stencil * lines, val=lines).items():
            self.floats[name] = (at, size)
            at += senders * size
        self.float_rows = at


def unpack_kernel(
    meta,
    recv,
    ints,
    floats,
    own_lines,
    own,
    own_sum,
    line_sum,
    lane_sum,
    *,
    layout,
    parts,
    columns,
    height,
    capacity,
    stencil,
    group,
):
    senders, _, hold = recv.shape
    lines = hold // LANES
    me = meta[0]
    shift = height.bit_length() - 1
    wide = columns + 2 * HALO
    block = height // parts
    high_rows = block + 2 * PAD
    length = columns * parts
    slots = senders * capacity

    def put(ref, place, sender, value):
        begin, size = place
        count = value.shape[0]
        for i in range(lines):
            part = value[:, i * LANES : (i + 1) * LANES]
            if count % 8 == 0:
                at = pl.multiple_of(begin + sender * size + i * count, 8)
                ref[pl.ds(at, count), :] = part
            else:
                for j in range(count):
                    ref[pl.ds(begin + sender * size + i + j * lines, 1), :] = part[j : j + 1]

    def right(x, by):
        return lax.shift_right_logical(x, jnp.full(x.shape, by, I32))

    def nt(a, b):
        return lax.dot_general(a, b, (((1,), (1,)), ((), ())), preferred_element_type=F32)

    own_sum[...] = jnp.zeros(own_sum.shape, F32)
    line_sum[...] = jnp.zeros(line_sum.shape, F32)
    lane_sum[...] = jnp.zeros(lane_sum.shape, F32)
    place = iota((LANES, hold), 0)
    index = iota((LANES, hold), 1)

    def per_sender(sender, carry):
        cell = recv[sender, 0:stencil, :].astype(I32)
        tail = recv[sender, 2 * stencil : 2 * stencil + 8, :]
        whole = tail.astype(I32)
        key = whole[2:3, :]
        pos = whole[3:4, :]
        owner = right(key, 2)
        offset = owner - me
        offset = jnp.where(offset > parts // 2, offset - parts, offset)
        offset = jnp.where(offset < -(parts // 2), offset + parts, offset)
        column = right(cell, shift)
        row = cell & (height - 1)
        at = offset * columns + column + HALO
        addr = jnp.where(
            (at >= 0) & (at < wide),
            (right(row, 7) * wide + at) * LANES + (row & (LANES - 1)),
            (height // LANES) * wide * LANES,
        )
        at_row = row - (block * me - PAD)
        across = owner * columns + column
        rows = jnp.where(
            (at_row >= 0) & (at_row < high_rows) & (owner < parts),
            (right(across, 7) * high_rows + at_row) * LANES + (across & (LANES - 1)),
            (length // LANES) * high_rows * LANES,
        )
        within = lax.rem(sender, group) * capacity + pos
        owner = jnp.minimum(owner, parts - 1)
        put(ints, layout.ints["addr"], sender, addr)
        put(ints, layout.ints["rows"], sender, rows)
        put(ints, layout.ints["listed"], sender, whole[4:5, :])
        put(ints, layout.ints["slot"], sender, owner * (group * capacity) + within)
        put(ints, layout.ints["start"], sender, whole[5:8, :])
        put(floats, layout.floats["wgt"], sender, recv[sender, stencil : 2 * stencil, :])
        put(floats, layout.floats["val"], sender, tail[0:1, :])

        here = iota((1, LANES), 1) == me
        begin = jnp.sum(jnp.where(here, whole[5:6, :LANES], 0), axis=1, keepdims=True)
        end = jnp.sum(jnp.where(here, whole[5:6, LANES : 2 * LANES], 0), axis=1, keepdims=True)
        first_slot = sender * capacity
        block_of = first_slot // LANES
        within = place - (first_slot - block_of * LANES)
        chosen = (within >= 0) & (index == begin + within) & (index < end)
        select = jnp.where(chosen, 1.0, 0.0).astype(BF)
        at_lane = (addr & (LANES - 1)).astype(F32)
        fields = jnp.concatenate([at_lane, recv[sender, stencil : 2 * stencil + 8, :]], axis=0)
        total = None
        for part in split3(fields):
            term = nt(select, part)
            total = term if total is None else total + term
        own_sum[block_of, :, 0:CODES] += total
        lane_sum[block_of] += nt(at_lane.astype(BF), select)
        total = None
        for part in split2(right(addr, 7).astype(F32)):
            term = nt(part, select)
            total = term if total is None else total + term
        line_sum[block_of] += total
        return carry

    lax.fori_loop(0, senders, per_sender, 0, unroll=senders <= GROUP)

    number = iota((stencil, LANES), 0).astype(F32)
    nowhere = float((height // LANES) * wide)
    for i in range(slots // LANES):
        line = line_sum[i]
        leader = jnp.zeros(line.shape, F32)
        for k in reversed(range(stencil)):
            leader = jnp.where(line == line[k : k + 1, :], float(k), leader)
        leads = jnp.where(leader == number, 1.0, 0.0)
        count = jnp.zeros((1, LANES), F32)
        ranks = []
        for k in range(stencil):
            ranks.append(count)
            count = count + leads[k : k + 1, :]
        place = jnp.zeros(line.shape, F32)
        for k in range(stencil):
            place = jnp.where(leader == float(k), ranks[k], place)
        lists = []
        for k in range(stencil):
            found = jnp.where((leads > 0.0) & (place == float(k)), line, 0.0)
            found = jnp.sum(found, axis=0, keepdims=True)
            lists.append(jnp.where(count > float(k), found, nowhere))
        batches = lax.shift_right_logical(
            count.astype(I32) + (BATCH - 1), jnp.full(count.shape, BATCH.bit_length() - 1, I32)
        )
        lists = jnp.concatenate(lists, axis=0).astype(I32)
        top = i * (stencil + 8)
        own_lines[top : top + stencil, :] = lists
        batches = batches.astype(F32)
        most = jnp.zeros((1, LANES), F32)
        slot = iota((1, LANES), 1)
        for begin in range(0, LANES, BLOCK):
            here = (slot >= begin) & (slot < begin + BLOCK)
            found = jnp.max(jnp.where(here, batches, 0.0), axis=1, keepdims=True)
            most = jnp.where(here, found, most)
        own_lines[top + stencil : top + stencil + 8, :] = jnp.where(
            iota((8, LANES), 0) == 0, batches, most
        ).astype(I32)
        codes = jnp.concatenate(
            [
                jnp.zeros((CODES, LANES), F32),
                place * float(LANES) + lane_sum[i],
                jnp.zeros((LANES - CODES - stencil, LANES), F32),
            ],
            axis=0,
        )
        own[i * LANES : (i + 1) * LANES, :] = own_sum[i] + codes.T


def band(shape, taps, shift):
    distance = iota(shape, 1) - iota(shape, 0) + shift
    result = jnp.zeros(shape, F32)
    for tap in range(taps.shape[0]):
        result = jnp.where(distance == tap, taps[tap], result)
    return result


def band_rev(shape, taps, shift):
    distance = iota(shape, 0) - iota(shape, 1) + shift
    result = jnp.zeros(shape, F32)
    for tap in range(taps.shape[0]):
        result = jnp.where(distance == tap, taps[tap], result)
    return result


def exact_nt(a, b):
    return lax.dot_general(
        a,
        b,
        (((1,), (1,)), ((), ())),
        precision=lax.Precision.HIGHEST,
        preferred_element_type=F32,
    )


def store_split(ref, index, value):
    high, low = split2(value)
    ref[(0,) + index] = high
    ref[(1,) + index] = low


def bands_kernel(kx, ky, lat2, lon2, lat1, lon1, *, rows_block):
    margin = kx.shape[0] // 2
    window = lat2.shape[2]
    first = band((window, window), ky, margin)
    reach = first[LANES : LANES + WIDE, :]
    place = iota((window, window), 1)
    for variant in range(3):
        kept = first
        if variant == 0:
            kept = jnp.where(place >= LANES, first, 0.0)
        if variant == 2:
            kept = jnp.where(place < LANES + WIDE, first, 0.0)
        store_split(lat2, (variant,), exact_nt(kept, reach))
    size = lon2.shape[1]
    wide = size + 2 * HALO
    depth = (wide + 32 + LANES - 1) // LANES * LANES
    second = band((wide, depth), kx, -(16 - margin))
    store_split(lon2, (), exact_nt(second[HALO : HALO + size, :], second))
    store_split(lat1, (), band_rev((rows_block, rows_block + 2 * PAD), ky, PAD + margin))
    store_split(lon1, (), band((2 * WIDE, WIDE), kx, LANES + margin))


def pairs(low, high, action):
    def step(i, carry):
        one = low + 2 * i
        action(one, jnp.minimum(one + 1, high - 1), one + 1 < high)
        return carry

    lax.fori_loop(0, lax.shift_right_logical(high - low + 1, 1), step, 0)


def zero_all(refs):
    rows = refs[0].shape[0]
    step = 256

    def clear(i, carry):
        for ref in refs:
            ref[pl.ds(pl.multiple_of(i * step, 8), step), :] = jnp.zeros((step, LANES), F32)
        return carry

    whole = rows // step
    lax.fori_loop(0, whole, clear, 0)
    if rows % step:
        for ref in refs:
            ref[whole * step : rows, :] = jnp.zeros((rows % step, LANES), F32)


def scatter_entries(copies, entries, lane):
    for start in range(0, len(entries), len(copies)):
        group = []
        for ref, (address, value) in zip(copies, entries[start : start + len(copies)]):
            line = lax.shift_right_logical(address, 7)
            spread = jnp.where(lane == (address & (LANES - 1)), value, 0.0)
            group.append((ref, line, ref[pl.ds(line, 1), :] + spread))
        for ref, line, value in group:
            ref[pl.ds(line, 1), :] = value


def spot(sender, idx, per, stencil):
    return sender * per + idx + lax.shift_right_logical(idx, 7) * ((stencil - 1) * LANES)


def copy_parts(layout, source, target, place, chunk, chunks, group, sem):
    begin, size = place
    words = group * size * LANES
    at = begin * LANES + chunk * words
    return pltpu.make_async_copy(source.at[pl.ds(at, words)], target, sem)


def apply_kernel(
    *refs, first, layout, columns, height, hold, stencil, capacity, senders, parts, levels
):
    refs = list(refs)

    def take(count):
        taken = refs[:count]
        del refs[:count]
        return taken

    meta, ints, floats, own_lines, own = take(5)
    if not first:
        replies_h, replies = take(2)
    std_h, std_l_h, std_r_h, lat2_h, lon2_h = take(5)
    if not first:
        merged_h = take(1)[0]
    field_h, send = take(2)
    if first:
        info_out, merged_h = take(2)
    addr, wgt, start, lines_s, val = take(5)
    if first:
        std_flat, picked, chosen = take(3)
    scale, merged, sums, high_s, low_s, std, std_l, std_r, lat2, lon2, field = take(11)
    copies = take(PAIR)
    sems, in_sems, out_sems, val_sem = take(4)

    me = meta[0]
    wide = columns + 2 * HALO
    blocks = height // LANES
    group = min(GROUP, senders)
    chunks = senders // group
    slots = senders * capacity
    lane = iota((1, LANES), 1)
    per = stencil * hold
    table = layout.table

    def chunk_copies(chunk):
        todo = [
            (ints, addr, layout.ints["addr"]),
            (floats, wgt, layout.floats["wgt"]),
            (ints, start, layout.ints["start"]),
        ]
        if first:
            todo.append((floats, val, layout.floats["val"]))
        return [
            copy_parts(layout, source, target, place, chunk, chunks, group, sems.at[i])
            for i, (source, target, place) in enumerate(todo)
        ]

    def load_chunk(chunk):
        for copy in chunk_copies(chunk):
            copy.start()
        for copy in chunk_copies(chunk):
            copy.wait()

    pending = []
    if chunks == 1:
        pending = chunk_copies(0)
        for copy in pending:
            copy.start()
    operands = [
        pltpu.make_async_copy(source, target, in_sems.at[i])
        for i, (source, target) in enumerate(
            (
                (std_h, std),
                (std_l_h, std_l),
                (std_r_h, std_r),
                (lat2_h, lat2),
                (lon2_h, lon2),
            )
        )
    ]
    own_copy = pltpu.make_async_copy(own_lines, lines_s, in_sems.at[5])
    own_copy.start()
    merged_copy = pltpu.make_async_copy(
        *((merged, merged_h) if first else (merged_h, merged)), in_sems.at[6]
    )
    if not first:
        merged_copy.start()
    for copy in operands:
        copy.start()

    def value_copy(owner):
        at = pl.multiple_of(owner * (replies.shape[1] * LANES), 1024)
        return pltpu.make_async_copy(
            replies_h.at[pl.ds(at, slots)], val.at[pl.ds(owner * slots, slots)], val_sem.at[owner]
        )

    def each_owner(action):
        def step(owner, carry):
            action(value_copy(owner))
            return carry

        lax.fori_loop(0, parts, step, 0)

    if not first:
        each_owner(lambda copy: copy.start())
    zero_all(copies)
    zero_all([sums])

    lane_of = iota((slots, LANES), 1)
    known = own[...]
    column = 2 * stencil if first else 2 * stencil + 2
    scale[...] = jnp.broadcast_to(known[:, column : column + 1], (slots, LANES))
    own_copy.wait()
    if pending:
        pending.pop(2).wait()
    if not first:
        merged_copy.wait()

    after = lax.rem(me + 1, parts)
    ahead = lax.rem(me + parts - 1, parts)

    def start_of(sender, owner, row, half):
        return start[sender * table + row * hold + half * LANES + owner]

    def entries_of(sender, idx, value):
        base = spot(sender, idx, per, stencil)
        return [
            (addr[base + k * LANES], wgt[base + k * LANES] * value) for k in range(stencil)
        ]

    def own_line(slot, k):
        at = lax.shift_right_logical(slot, 7) * ((stencil + 7) * LANES) + slot
        return lines_s[at + k * LANES]

    def batches_of(one, two):
        return jnp.maximum(own_line(one, stencil), own_line(two, stencil))

    def own_groups(action):
        def group_at(top):
            top = pl.multiple_of(top, 8)
            most = own_line(top, stencil + 1)

            @pl.when(most <= 2)
            def _():
                action(top, 2 * BATCH)

            @pl.when(most > 2)
            def _():
                action(top, stencil)

        if capacity % BLOCK or chunks > 1:

            def step(i, carry):
                group_at(i * BLOCK)
                return carry

            lax.fori_loop(0, slots // BLOCK, step, 0)
        else:

            def per_sender(sender, carry):
                amount = start_of(sender, me, 0, 1) - start_of(sender, me, 0, 0)

                def step(i, inner):
                    group_at(sender * capacity + i * BLOCK)
                    return inner

                lax.fori_loop(0, lax.div(amount + (BLOCK - 1), BLOCK), step, 0)
                return carry

            lax.fori_loop(0, senders, per_sender, 0)

    lane_f = iota((BLOCK, LANES), 1).astype(F32)

    def columns_of(info, begin):
        return [
            jnp.broadcast_to(info[:, begin + k : begin + k + 1], (BLOCK, LANES))
            for k in range(stencil)
        ]

    def build(top, places):
        info = own[pl.ds(top, BLOCK), :]
        codes = columns_of(info, CODES)
        weights = columns_of(info, stencil)
        for place in range(stencil):
            row = jnp.zeros((BLOCK, LANES), F32)
            if place < places:
                at = lane_f + float(LANES * place)
                for k in range(place, stencil):
                    row = row + jnp.where(at == codes[k], weights[k], 0.0)
            merged[pl.ds(place * slots + top, BLOCK), :] = row

    if first:
        own_groups(build)
        merged_copy.start()

    def own_pairs(chunk, action):
        def per_sender(sender, carry):
            amount = start_of(sender, me, 0, 1) - start_of(sender, me, 0, 0)
            base = (chunk * group + sender) * capacity
            pairs(base, base + amount, action)
            return carry

        lax.fori_loop(0, group, per_sender, 0)

    def scatter_own(chunk):
        def action(one, two, has_two):
            second = jnp.where(has_two, 1.0, 0.0)
            values = (scale[pl.ds(one, 1), :], scale[pl.ds(two, 1), :] * second)

            def batch(begin):
                todo = []
                for slot, value, ref in zip((one, two), values, copies):
                    for j in range(BATCH):
                        line = own_line(slot, begin + j)
                        row = merged[pl.ds((begin + j) * slots + slot, 1), :] * value
                        todo.append((ref, line, ref[pl.ds(line, 1), :] + row))
                for ref, line, row in todo:
                    ref[pl.ds(line, 1), :] = row

            def more(i, carry):
                batch(i * BATCH)
                return carry

            batch(0)
            lax.fori_loop(1, batches_of(one, two), more, 0)

        own_pairs(chunk, action)

    def scatter_halo(chunk):
        def per_sender(sender, carry):
            for owner, low, high in ((after, (1, 0), (1, 1)), (ahead, (2, 0), (0, 1))):
                begin = start_of(sender, owner, 0, 0)

                def value_of(idx, owner=owner, begin=begin):
                    if first:
                        return val[sender * hold + idx]
                    place = (chunk * group + sender) * capacity + idx - begin
                    return val[owner * slots + place]

                def action(one, two, has_two, value_of=value_of):
                    second = jnp.where(has_two, value_of(two), 0.0)
                    scatter_entries(
                        copies,
                        entries_of(sender, one, value_of(one)) + entries_of(sender, two, second),
                        lane,
                    )

                pairs(start_of(sender, owner, *low), start_of(sender, owner, *high), action)
            return carry

        lax.fori_loop(0, group, per_sender, 0)

    def scatter_chunk(chunk):
        scatter_own(chunk)
        for copy in pending:
            copy.wait()
        scatter_halo(chunk)

    def over_chunks(work):
        if chunks == 1:
            work(0)
        else:

            def step(chunk, carry):
                load_chunk(chunk)
                work(chunk)
                return carry

            lax.fori_loop(0, chunks, step, 0)

    if not first:
        each_owner(lambda copy: copy.wait())
    over_chunks(scatter_chunk)
    for copy in operands:
        copy.wait()

    for jb in range(blocks):
        lanes = slice(jb * LANES, (jb + 1) * LANES)
        for low, size, source in (
            (0, HALO, std_l),
            (HALO, columns, std),
            (HALO + columns, HALO, std_r),
        ):
            rows = slice(jb * wide + low, jb * wide + low + size)
            total = copies[0][rows, :]
            for ref in copies[1:]:
                total = total + ref[rows, :]
            high, lo = split2(total * source[:, lanes])
            high_s[low : low + size, lanes] = high
            low_s[low : low + size, lanes] = lo
        if first:
            std_flat[jb * wide + HALO : jb * wide + HALO + columns, :] = std[:, lanes]

    smoothed = copies[0]
    size = lon2.shape[1]
    count = height // WIDE
    outgoing = [merged_copy] if first else []
    for block in range(count):
        variant = 0 if block == 0 else (2 if block == count - 1 else 1)
        low = max(block * WIDE - LANES, 0)
        high = min(block * WIDE + WIDE + LANES, height)
        inner = slice(low - (block * WIDE - LANES), high - (block * WIDE - LANES))
        matrix = (lat2[0, variant, inner, :], lat2[1, variant, inner, :])
        along = mm_parts((high_s[:, low:high], low_s[:, low:high]), matrix)
        parts_y = split2(along)
        lanes = slice(block * WIDE, (block + 1) * WIDE)
        for begin in range(0, columns, size):
            some = min(size, columns - begin)
            rows = slice(begin, begin + some)
            window = slice(begin, begin + some + 2 * HALO)
            matrix = tuple(lon2[i, 0:some, 0 : some + 2 * HALO] for i in range(2))
            result = mm_parts(matrix, (parts_y[0][window, :], parts_y[1][window, :]))
            field[rows, lanes] = result
            scaled = result * std[rows, lanes]
            for half in range(WIDE // LANES):
                top = (block * (WIDE // LANES) + half) * wide + HALO + begin
                smoothed[top : top + some, :] = scaled[:, half * LANES : (half + 1) * LANES]
        outgoing.append(
            pltpu.make_async_copy(field.at[:, lanes], field_h.at[:, lanes], out_sems.at[block])
        )
        outgoing[-1].start()

    def gather_chunk(chunk):
        def action(one, two, has_two):
            def batch(begin, totals):
                result = []
                for slot, total in zip((one, two), totals):
                    terms = []
                    for j in range(BATCH):
                        line = own_line(slot, begin + j)
                        row = merged[pl.ds((begin + j) * slots + slot, 1), :]
                        terms.append(row * smoothed[pl.ds(line, 1), :])
                        if first:
                            picked[pl.ds((begin + j) * slots + slot, 1), :] = std_flat[
                                pl.ds(line, 1), :
                            ]
                    result.append(total + ((terms[0] + terms[1]) + (terms[2] + terms[3])))
                return tuple(result)

            zero = jnp.zeros((1, LANES), F32)
            totals = lax.fori_loop(
                1,
                batches_of(one, two),
                lambda i, totals: batch(i * BATCH, totals),
                batch(0, (zero, zero)),
            )
            for slot, total in zip((one, two), totals):
                sums[pl.ds(slot, 1), :] = total

        own_pairs(chunk, action)

    over_chunks(gather_chunk)

    def pick(top, places):
        info = own[pl.ds(top, BLOCK), :]
        codes = columns_of(info, CODES)
        rows = [picked[pl.ds(place * slots + top, BLOCK), :] for place in range(places)]
        result = jnp.zeros((BLOCK, LANES), F32)
        for k in range(stencil):
            cell = jnp.zeros((BLOCK, LANES), F32)
            for place in range(min(k + 1, places)):
                at = lane_f + float(LANES * place)
                cell = jnp.where(at == codes[k], rows[place], cell)
            cell = jnp.sum(cell, axis=1, keepdims=True)
            result = jnp.where(lane_f == float(stencil + k), cell, result)
        chosen[pl.ds(top, BLOCK), :] = result * info

    if first:
        own_groups(pick)

    def whole(x):
        return jnp.sum(x, axis=0, keepdims=True)

    total = jnp.sum(sums[...], axis=1, keepdims=True)
    lines = slots // LANES
    known = own[...]
    source, weight, reply, image0 = (
        known[:, 2 * stencil + i : 2 * stencil + i + 1] for i in range(4)
    )
    if first:
        reply = weight * total
        known = jnp.where(lane_of == 2 * stencil + 2, reply, known)
        known = jnp.where(lane_of == 2 * stencil + 3, total, known)
        info_out[...] = known
        turned = known.T[2 * stencil + 2 : 2 * stencil + 3, :]
        message = [turned[:, i * LANES : (i + 1) * LANES] for i in range(lines)]
        message.append(
            jnp.where(
                lane == 0, whole(source * total), jnp.where(lane == 1, whole(reply * total), 0.0)
            )
        )
        message.append(jnp.zeros((8 - len(message), LANES), F32))
        factors = chosen[...].T
        for k in range(stencil):
            row = factors[stencil + k : stencil + k + 1, :]
            message += [row[:, i * LANES : (i + 1) * LANES] for i in range(lines)]
        message = jnp.concatenate(message, axis=0)
    else:
        slab = jnp.sum(replies[:, 0:8, :], axis=0)[lines : lines + 1, :]
        length = slab[:, 0:1] / (slab[:, 0:1] + slab[:, 1:2])
        both = source + reply
        s_both = image0 + total
        resid = source - length * both
        s_resid = image0 - length * s_both
        values = [
            resid * s_resid,
            resid * s_both,
            both * s_both,
            resid * image0,
            both * image0,
            weight * s_resid * s_resid,
            weight * s_resid * s_both,
            weight * s_both * s_both,
            weight * s_resid * image0,
            weight * s_both * image0,
            source * image0,
            reply * image0,
        ]
        message = jnp.where(lane == len(values), length, 0.0)
        for i, value in enumerate(values):
            message = jnp.where(lane == i, whole(value), message)
        message = jnp.concatenate([message, jnp.zeros((7, LANES), F32)], axis=0)

    def send_to(i, carry):
        send[i] = message
        return carry

    lax.fori_loop(0, send.shape[0], send_to, 0)
    for copy in outgoing:
        copy.wait()


def final_kernel(
    ints,
    floats,
    replies_h,
    totals,
    std_h,
    field0_h,
    field1_h,
    lat1,
    lon1,
    control_h,
    increment_h,
    addr,
    listed,
    start,
    slot,
    val,
    factors,
    std,
    field0,
    field1,
    control,
    high_s,
    low_s,
    *rest,
    layout,
    hold,
    stencil,
    capacity,
    senders,
    parts,
    length,
):
    copies = rest[:COPIES]
    sems, in_sems, out_sems = rest[COPIES:]
    group = min(GROUP, senders)
    chunks = senders // group
    per = stencil * hold
    rows_block = control.shape[0]
    high_rows = rows_block + 2 * PAD
    lane = iota((1, LANES), 1)
    stride = group * capacity
    owner_words = factors.shape[0] // parts
    to_factors = owner_words - stencil * stride

    def chunk_copies(chunk):
        todo = [
            (ints, addr, layout.ints["rows"]),
            (ints, listed, layout.ints["listed"]),
            (ints, start, layout.ints["start"]),
            (ints, slot, layout.ints["slot"]),
            (floats, val, layout.floats["val"]),
        ]
        result = [
            copy_parts(layout, source, target, place, chunk, chunks, group, sems.at[i])
            for i, (source, target, place) in enumerate(todo)
        ]
        words = parts * owner_words
        result.append(
            pltpu.make_async_copy(
                replies_h.at[pl.ds(chunk * words, words)], factors, sems.at[len(todo)]
            )
        )
        return result

    pending = []
    if chunks == 1:
        pending = chunk_copies(0)
        for copy in pending:
            copy.start()
    operands = [
        pltpu.make_async_copy(source, target, in_sems.at[i])
        for i, (source, target) in enumerate(
            ((std_h, std), (field0_h, field0), (field1_h, field1))
        )
    ]
    for copy in operands:
        copy.start()

    slabs = totals.shape[1]
    every = jnp.sum(totals[...], axis=0)
    norm0 = quad0 = None
    for i in range(slabs):
        line = every[i, 0:1, :]
        a, b = line[:, 10:11], line[:, 11:12]
        norm0 = a if norm0 is None else norm0 + a
        quad0 = b if quad0 is None else quad0 + b
    step0 = norm0 / (norm0 + quad0)
    norm1 = cross = quad1 = quad01 = jnp.zeros((1, 1), F32)
    for i in range(slabs):
        line = every[i, 0:1, :]
        v = [line[:, j : j + 1] for j in range(10)]
        shift = totals[0, i, 0:1, 12:13] - step0
        norm1 = norm1 + (v[0] + shift * (2.0 * v[1] + shift * v[2]))
        cross = cross + (v[3] + shift * v[4])
        quad1 = quad1 + (v[5] + shift * (2.0 * v[6] + shift * v[7]))
        quad01 = quad01 + (v[8] + shift * v[9])
    ratio = norm1 / norm0
    curvature = norm1 + quad1 + ratio * (
        2.0 * (cross + quad01) + ratio * (norm0 + quad0)
    )
    step1 = norm1 / curvature
    first = step0 + step1 * (1.0 - step0 + ratio)
    second = -step0 * step1
    first_line = jnp.broadcast_to(first, (1, LANES))
    second_line = jnp.broadcast_to(second, (1, LANES))

    zero_all(copies)

    def scatter_chunk():
        def per_sender(sender, carry):
            def entries_of(at, scale):
                idx = listed[sender * hold + at]
                place = slot[sender * hold + idx]
                place = place + lax.div(place, stride) * (owner_words - stride)
                base = spot(sender, idx, per, stencil)
                z0 = val[sender * hold + idx] * scale
                u = factors[place] * scale
                value = first_line * z0 + second_line * u
                return [
                    (addr[base + k * LANES], factors[place + to_factors + k * stride] * value)
                    for k in range(stencil)
                ]

            def action(one, two, has_two):
                scale = jnp.where(has_two, 1.0, 0.0)
                scatter_entries(copies, entries_of(one, 1.0) + entries_of(two, scale), lane)

            pairs(0, start[sender * layout.table + layout.table - 1], action)
            return carry

        lax.fori_loop(0, group, per_sender, 0)

    if chunks == 1:
        for copy in pending:
            copy.wait()
        scatter_chunk()
    else:

        def step(chunk, carry):
            for copy in chunk_copies(chunk):
                copy.start()
            for copy in chunk_copies(chunk):
                copy.wait()
            scatter_chunk()
            return carry

        lax.fori_loop(0, chunks, step, 0)

    for copy in operands:
        copy.wait()
    increment = field0
    increment[...] = std[...] * (first * field0[...] + second * field1[...])
    outgoing = [pltpu.make_async_copy(increment, increment_h, out_sems.at[0])]
    outgoing[0].start()

    pair = WIDE // LANES
    count = length // WIDE
    for block in range(count):
        pieces = []
        for half in range(pair):
            rows = slice((block * pair + half) * high_rows, (block * pair + half + 1) * high_rows)
            total = copies[0][rows, :]
            for ref in copies[1:]:
                total = total + ref[rows, :]
            pieces.append(total)
        whole = split2(jnp.concatenate(pieces, axis=1))
        size = lat1.shape[1]
        for top in range(0, rows_block, size):
            window = slice(top, top + size + 2 * PAD)
            along = mm_parts((lat1[0], lat1[1]), (whole[0][window, :], whole[1][window, :]))
            high, low = split2(along)
            high_s[top : top + size, block * WIDE : (block + 1) * WIDE] = high
            low_s[top : top + size, block * WIDE : (block + 1) * WIDE] = low

    def window(ref, block):
        low, high = block * WIDE - LANES, (block + 1) * WIDE + LANES
        if low < 0:
            return jnp.concatenate([ref[:, length + low : length], ref[:, 0:high]], axis=1)
        if high > length:
            return jnp.concatenate([ref[:, low:length], ref[:, 0 : high - length]], axis=1)
        return ref[:, low:high]

    every_lanes = 4
    for block in range(count):
        control[:, block * WIDE : (block + 1) * WIDE] = mm_parts(
            (window(high_s, block), window(low_s, block)), (lon1[0], lon1[1])
        )
        if block % every_lanes == every_lanes - 1:
            lanes = slice((block + 1 - every_lanes) * WIDE, (block + 1) * WIDE)
            outgoing.append(
                pltpu.make_async_copy(
                    control.at[:, lanes], control_h.at[:, lanes], out_sems.at[len(outgoing)]
                )
            )
            outgoing[-1].start()
    for copy in outgoing:
        copy.wait()


def body(
    background_std,
    x_kernel,
    y_kernel,
    obs_owner,
    obs_cells,
    obs_weights,
    innovation,
    obs_precision,
    obs_counts,
):
    parts = lax.axis_size("pencil")
    levels = lax.axis_size("lev")
    me = lax.axis_index("pencil")
    _, columns, height = background_std.shape
    hold, stencil = obs_cells.shape
    margin = x_kernel.shape[1] // 2
    capacity = 2 * hold // parts
    senders = parts
    slots = senders * capacity
    rows_block = height // parts
    length = columns * parts
    blocks = height // LANES
    wide = columns + 2 * HALO
    group = min(GROUP, senders)
    chunks = senders // group
    layout = Layout(senders, hold, stencil, parts)
    std = background_std[0]

    packed = pl.pallas_call(
        functools.partial(
            pack_kernel, parts=parts, columns=columns, height=height, margin=margin
        ),
        out_shape=jax.ShapeDtypeStruct((parts, PACK, hold), F32),
        in_specs=[smem()] + [vmem()] * 5,
        out_specs=vmem(),
        compiler_params=params(),
        cost_estimate=cost(12000),
        name="pack",
    )(
        obs_counts,
        obs_owner.T,
        obs_cells.T,
        obs_weights.T,
        innovation[None, :],
        obs_precision[None, :],
    )
    recv = lax.all_to_all(packed, "pencil", split_axis=0, concat_axis=0, tiled=True)

    right = [(p, (p + 1) % parts) for p in range(parts)]
    left = [(p, (p - 1) % parts) for p in range(parts)]
    std_l = lax.ppermute(std[columns - HALO :, :], "pencil", right)
    std_r = lax.ppermute(std[:HALO, :], "pencil", left)

    size = min(columns, WIDE - 2 * HALO)
    row_size = min(rows_block, LANES)
    lat2, lon2, lat1, lon1 = pl.pallas_call(
        functools.partial(bands_kernel, rows_block=row_size),
        out_shape=[
            jax.ShapeDtypeStruct((2, 3, 2 * WIDE, WIDE), BF),
            jax.ShapeDtypeStruct((2, size, size + 2 * HALO), BF),
            jax.ShapeDtypeStruct((2, row_size, row_size + 2 * PAD), BF),
            jax.ShapeDtypeStruct((2, 2 * WIDE, WIDE), BF),
        ],
        in_specs=[smem(), smem()],
        out_specs=[vmem()] * 4,
        compiler_params=params(),
        cost_estimate=cost(6000),
        name="bands",
    )(x_kernel[0], y_kernel[0])

    meta = jnp.reshape(me, (1,)).astype(I32)
    ints, floats, own_lines, own = pl.pallas_call(
        functools.partial(
            unpack_kernel,
            layout=layout,
            parts=parts,
            columns=columns,
            height=height,
            capacity=capacity,
            stencil=stencil,
            group=group,
        ),
        out_shape=[
            jax.ShapeDtypeStruct((layout.int_rows, LANES), I32),
            jax.ShapeDtypeStruct((layout.float_rows, LANES), F32),
            jax.ShapeDtypeStruct((slots // LANES * (stencil + 8), LANES), I32),
            jax.ShapeDtypeStruct((slots, LANES), F32),
        ],
        in_specs=[smem(), vmem()],
        out_specs=[vmem()] * 4,
        scratch_shapes=[
            pltpu.VMEM((slots // LANES, LANES, LANES), F32),
            pltpu.VMEM((slots // LANES, stencil, LANES), F32),
            pltpu.VMEM((slots // LANES, stencil, LANES), F32),
        ],
        compiler_params=params(),
        cost_estimate=cost(100),
        name="unpack",
    )(meta, recv)
    ints = ints.reshape(-1)
    floats = floats.reshape(-1)
    own_lines = own_lines.reshape(-1)

    acc = pltpu.VMEM((blocks * wide + 8, LANES), F32)
    column_slots = pltpu.VMEM((slots, LANES), F32)
    static = dict(
        layout=layout,
        columns=columns,
        height=height,
        hold=hold,
        stencil=stencil,
        capacity=capacity,
        senders=senders,
        parts=parts,
        levels=levels,
    )
    per = group * stencil * hold
    line = group * hold
    index_scratch = [
        pltpu.SMEM((per,), I32),
        pltpu.SMEM((per,), F32),
        pltpu.SMEM((group * layout.table,), I32),
        pltpu.SMEM((slots * (stencil + 8),), I32),
    ]
    work = (
        [column_slots, pltpu.VMEM((stencil * slots, LANES), F32), column_slots]
        + [pltpu.VMEM((wide, height), BF)] * 2
        + [
            pltpu.VMEM((columns, height), F32),
            pltpu.VMEM((HALO, height), F32),
            pltpu.VMEM((HALO, height), F32),
            pltpu.VMEM(lat2.shape, BF),
            pltpu.VMEM(lon2.shape, BF),
            pltpu.VMEM((columns, height), F32),
        ]
        + [acc] * PAIR
        + [
            pltpu.SemaphoreType.DMA((4,)),
            pltpu.SemaphoreType.DMA((7,)),
            pltpu.SemaphoreType.DMA((height // WIDE,)),
            pltpu.SemaphoreType.DMA((parts,)),
        ]
    )
    field_shape = jax.ShapeDtypeStruct((columns, height), F32)
    reply_rows = 8 + stencil * slots // LANES
    field0, message, info, merged = pl.pallas_call(
        functools.partial(apply_kernel, first=True, **static),
        out_shape=[
            field_shape,
            jax.ShapeDtypeStruct((parts, reply_rows, LANES), F32),
            jax.ShapeDtypeStruct((slots, LANES), F32),
            jax.ShapeDtypeStruct((stencil * slots, LANES), F32),
        ],
        in_specs=[smem()] + [hbm()] * 3 + [vmem()] + [hbm()] * 5,
        out_specs=[hbm()] + [vmem()] * 2 + [hbm()],
        scratch_shapes=index_scratch
        + [
            pltpu.SMEM((line,), F32),
            acc,
            pltpu.VMEM((stencil * slots, LANES), F32),
            column_slots,
        ]
        + work,
        compiler_params=params(),
        name="apply_first",
    )(meta, ints, floats, own_lines, own, std, std_l, std_r, lat2, lon2)

    replies = lax.all_to_all(message, "pencil", split_axis=0, concat_axis=0, tiled=True)
    back = replies.reshape(-1)

    field1, sums = pl.pallas_call(
        functools.partial(apply_kernel, first=False, **static),
        out_shape=[
            field_shape,
            jax.ShapeDtypeStruct((parts * levels, 8, LANES), F32),
        ],
        in_specs=[smem()] + [hbm()] * 3 + [vmem(), hbm(), vmem()] + [hbm()] * 6,
        out_specs=[hbm(), vmem()],
        scratch_shapes=index_scratch + [pltpu.SMEM((parts * slots,), F32)] + work,
        compiler_params=params(),
        name="apply_second",
    )(
        meta,
        ints,
        floats,
        own_lines,
        info,
        back,
        replies,
        std,
        std_l,
        std_r,
        lat2,
        lon2,
        merged,
    )

    totals = lax.all_to_all(sums, ("pencil", "lev"), split_axis=0, concat_axis=0, tiled=True)
    totals = totals.reshape(parts, levels, 8, LANES)

    by_chunk = back
    if chunks > 1:
        by_chunk = jnp.concatenate(
            [replies[:, : slots // LANES, :], replies[:, 8:, :]], axis=1
        ).reshape(parts, stencil + 1, chunks, group * capacity)
        by_chunk = jnp.transpose(by_chunk, (2, 0, 1, 3)).reshape(-1)
    owner_words = by_chunk.shape[0] // (chunks * parts)
    high_rows = rows_block + 2 * PAD
    acc_rows = pltpu.VMEM(((length // LANES) * high_rows + 8, LANES), F32)
    control, increment = pl.pallas_call(
        functools.partial(
            final_kernel,
            layout=layout,
            hold=hold,
            stencil=stencil,
            capacity=capacity,
            senders=senders,
            parts=parts,
            length=length,
        ),
        out_shape=[
            jax.ShapeDtypeStruct((rows_block, length), F32),
            field_shape,
        ],
        in_specs=[hbm()] * 3 + [vmem()] + [hbm()] * 3 + [vmem()] * 2,
        out_specs=[hbm()] * 2,
        scratch_shapes=[
            pltpu.SMEM((per,), I32),
            pltpu.SMEM((line,), I32),
            pltpu.SMEM((group * layout.table,), I32),
            pltpu.SMEM((line,), I32),
            pltpu.SMEM((line,), F32),
            pltpu.SMEM((parts * owner_words,), F32),
            pltpu.VMEM((columns, height), F32),
            pltpu.VMEM((columns, height), F32),
            pltpu.VMEM((columns, height), F32),
            pltpu.VMEM((rows_block, length), F32),
            pltpu.VMEM((rows_block, length), BF),
            pltpu.VMEM((rows_block, length), BF),
        ]
        + [acc_rows] * COPIES
        + [
            pltpu.SemaphoreType.DMA((7,)),
            pltpu.SemaphoreType.DMA((3,)),
            pltpu.SemaphoreType.DMA((1 + length // WIDE,)),
        ],
        compiler_params=params(),
        name="outputs",
    )(ints, floats, by_chunk, totals, std, field0, field1, lat1, lon1)
    return control[None], increment[None]


def solution(mesh):
    return jax.shard_map(
        body,
        mesh=mesh,
        in_specs=(
            P("lev", "pencil", None),
            P("lev", None),
            P("lev", None),
            P(("pencil", "lev"), None),
            P(("pencil", "lev"), None),
            P(("pencil", "lev"), None),
            P(("pencil", "lev")),
            P(("pencil", "lev")),
            P(("pencil", "lev")),
        ),
        out_specs=(P("lev", "pencil", None), P("lev", "pencil", None)),
        check_vma=False,
    )
```

```python
import functools

import jax
import jax.numpy as jnp
import numpy as np
from jax import lax
from jax.experimental import pallas as pl
from jax.experimental.pallas import tpu as pltpu
from jax.sharding import PartitionSpec as P


BF = jnp.bfloat16
F32 = jnp.float32
I32 = jnp.int32
LANES = 128
WIDE = 256
HALO = 32
PAD = 16
PACK = 40
GROUP = 8
COPIES = 4
PAIR = 2
BATCH = 4
BLOCK = 32
CODES = 40
VMEM_LIMIT = 58 * 1024 * 1024


def vmem():
    return pl.BlockSpec(memory_space=pltpu.VMEM)


def smem():
    return pl.BlockSpec(memory_space=pltpu.SMEM)


def hbm():
    return pl.BlockSpec(memory_space=pl.ANY)


def cost(nanoseconds):
    return pl.CostEstimate(flops=0, bytes_accessed=3690 * nanoseconds, transcendentals=0)


def params():
    return pltpu.CompilerParams(vmem_limit_bytes=VMEM_LIMIT)


def split2(x):
    high = x.astype(BF)
    return high, (x - high.astype(F32)).astype(BF)


def split3(x):
    high = x.astype(BF)
    rest = x - high.astype(F32)
    mid = rest.astype(BF)
    return high, mid, (rest - mid.astype(F32)).astype(BF)


def mm(a, b):
    return jnp.dot(a, b, preferred_element_type=F32)


def mm_parts(a_parts, b_parts):
    (ah, al), (bh, bl) = a_parts, b_parts
    return mm(jnp.concatenate([ah, al, ah], axis=1), jnp.concatenate([bh, bh, bl], axis=0))


def iota(shape, dim):
    return lax.broadcasted_iota(I32, shape, dim)


def pack_kernel(
    counts, owner, cells, weights, depart, prec, out, *, parts, columns, height, margin
):
    stencil, hold = cells.shape
    shift = height.bit_length() - 1
    block = height // parts
    reach = 2 * margin
    row_id = iota((hold, hold), 0)
    col_id = iota((hold, hold), 1)
    eye = row_id == col_id
    col_f = col_id.astype(F32)
    live = iota((1, hold), 1) < counts[0]
    cell = cells[...]
    column = lax.shift_right_logical(cell, jnp.full(cell.shape, shift, I32))
    row = cell & (height - 1)

    def any_of(mask):
        return jnp.max(jnp.where(mask, 1.0, 0.0), axis=0, keepdims=True)

    def turn(line):
        return jnp.sum(jnp.where(eye, line, 0.0), axis=1, keepdims=True)

    left = any_of(column < reach)
    right = any_of(column >= columns - reach)
    side = left + 3.0 * right - 2.0 * left * right
    base = jnp.where(live, owner[...].astype(F32) * 4.0, 4.0 * parts)
    key = jnp.where(live, base + side, base)
    key_col = turn(key)
    before = (key_col < key) | ((key_col == key) & (row_id < col_id))
    rank = jnp.sum(jnp.where(before, 1.0, 0.0), axis=0, keepdims=True)
    begin = jnp.sum(jnp.where(key_col < base, 1.0, 0.0), axis=0, keepdims=True)
    rank_col = turn(rank)
    perm = jnp.where(rank_col == col_f, 1.0, 0.0).astype(BF)

    def sort(values):
        total = None
        for part in split3(values):
            term = mm(part, perm)
            total = term if total is None else total + term
        return total

    weight = jnp.where(live, prec[...], 0.0)
    rest = [weight * depart[...], weight, key, rank - begin, jnp.zeros((4, hold), F32)]
    values = [cell.astype(F32), weights[...]] + rest
    ordered = sort(jnp.concatenate(values, axis=0))
    line = iota((8, hold), 0)
    tail = ordered[2 * stencil : 2 * stencil + 8, :]
    first_half = col_f < float(LANES)
    fourfold = 4.0 * jnp.where(first_half, col_f, col_f - float(LANES))
    for i, (low, high) in enumerate(((0.0, 4.0), (1.0, 3.0), (2.0, 2.0))):
        bound = fourfold + jnp.where(first_half, low, high)
        begins = jnp.sum(jnp.where(key_col < bound, 1.0, 0.0), axis=0, keepdims=True)
        tail = jnp.where(line == 5 + i, begins, tail)
    last = (line == 7) & (iota((8, hold), 1) == hold - 1)

    def per_part(part, carry):
        low = part * block - margin
        high = (part + 1) * block + margin
        flag = jnp.where(live, any_of((row >= low) & (row < high)), 0.0)
        place = jnp.sum(jnp.where(col_id < row_id, flag, 0.0), axis=1, keepdims=True)
        chosen = (place == col_f) & (turn(flag) > 0.0)
        listed = jnp.sum(jnp.where(chosen, rank_col, 0.0), axis=0, keepdims=True)
        amount = jnp.sum(flag, axis=1, keepdims=True)
        out[part, 0 : 2 * stencil, :] = ordered[0 : 2 * stencil, :]
        out[part, 2 * stencil : 2 * stencil + 8, :] = jnp.where(
            line == 4, listed, jnp.where(last, amount, tail)
        )
        return carry

    lax.fori_loop(0, parts, per_part, 0, unroll=parts <= GROUP)


class Layout:
    def __init__(self, senders, hold, stencil, parts):
        lines = hold // LANES
        self.table = 3 * hold
        sizes = dict(
            addr=stencil * lines, rows=stencil * lines, listed=lines, slot=lines, start=3 * lines
        )
        self.ints = {}
        at = 0
        for name, size in sizes.items():
            self.ints[name] = (at, size)
            at += senders * size
        self.int_rows = at
        self.floats = {}
        at = 0
        for name, size in dict(wgt=stencil * lines, val=lines).items():
            self.floats[name] = (at, size)
            at += senders * size
        self.float_rows = at


def unpack_kernel(
    meta,
    recv,
    ints,
    floats,
    own_lines,
    own,
    own_sum,
    line_sum,
    lane_sum,
    *,
    layout,
    parts,
    columns,
    height,
    capacity,
    stencil,
    group,
):
    senders, _, hold = recv.shape
    lines = hold // LANES
    me = meta[0]
    shift = height.bit_length() - 1
    wide = columns + 2 * HALO
    block = height // parts
    high_rows = block + 2 * PAD
    length = columns * parts
    slots = senders * capacity

    def put(ref, place, sender, value):
        begin, size = place
        count = value.shape[0]
        for i in range(lines):
            part = value[:, i * LANES : (i + 1) * LANES]
            if count % 8 == 0:
                at = pl.multiple_of(begin + sender * size + i * count, 8)
                ref[pl.ds(at, count), :] = part
            else:
                for j in range(count):
                    ref[pl.ds(begin + sender * size + i + j * lines, 1), :] = part[j : j + 1]

    def right(x, by):
        return lax.shift_right_logical(x, jnp.full(x.shape, by, I32))

    def nt(a, b):
        return lax.dot_general(a, b, (((1,), (1,)), ((), ())), preferred_element_type=F32)

    own_sum[...] = jnp.zeros(own_sum.shape, F32)
    line_sum[...] = jnp.zeros(line_sum.shape, F32)
    lane_sum[...] = jnp.zeros(lane_sum.shape, F32)
    place = iota((LANES, hold), 0)
    index = iota((LANES, hold), 1)
    lane = iota((1, LANES), 1)
    halo_block = slots // LANES
    after = lax.rem(me + 1, parts)
    ahead = lax.rem(me + parts - 1, parts)

    def per_sender(sender, carry):
        halo_before, amounts = carry
        cell = recv[sender, 0:stencil, :].astype(I32)
        tail = recv[sender, 2 * stencil : 2 * stencil + 8, :]
        whole = tail.astype(I32)
        key = whole[2:3, :]
        pos = whole[3:4, :]
        owner = right(key, 2)
        offset = owner - me
        offset = jnp.where(offset > parts // 2, offset - parts, offset)
        offset = jnp.where(offset < -(parts // 2), offset + parts, offset)
        column = right(cell, shift)
        row = cell & (height - 1)
        at = offset * columns + column + HALO
        addr = jnp.where(
            (at >= 0) & (at < wide),
            (right(row, 7) * wide + at) * LANES + (row & (LANES - 1)),
            (height // LANES) * wide * LANES,
        )
        at_row = row - (block * me - PAD)
        across = owner * columns + column
        rows = jnp.where(
            (at_row >= 0) & (at_row < high_rows) & (owner < parts),
            (right(across, 7) * high_rows + at_row) * LANES + (across & (LANES - 1)),
            (length // LANES) * high_rows * LANES,
        )
        within = lax.rem(sender, group) * capacity + pos
        owner = jnp.minimum(owner, parts - 1)
        put(ints, layout.ints["addr"], sender, addr)
        put(ints, layout.ints["rows"], sender, rows)
        put(ints, layout.ints["listed"], sender, whole[4:5, :])
        put(ints, layout.ints["slot"], sender, owner * (group * capacity) + within)
        put(ints, layout.ints["start"], sender, whole[5:8, :])
        put(floats, layout.floats["wgt"], sender, recv[sender, stencil : 2 * stencil, :])
        put(floats, layout.floats["val"], sender, tail[0:1, :])

        def bound(line, half, owner):
            part = whole[5 + line : 6 + line, half * LANES : (half + 1) * LANES]
            return jnp.sum(jnp.where(lane == owner, part, 0), axis=1, keepdims=True)

        at_lane = (addr & (LANES - 1)).astype(F32)
        fields = jnp.concatenate([at_lane, recv[sender, stencil : 2 * stencil + 8, :]], axis=0)
        fields = split3(fields)
        back = owner * slots + sender * capacity + pos
        lines_of = jnp.concatenate([right(addr, 7), back, jnp.zeros((7, hold), I32)], axis=0)
        lines_of = split3(lines_of.astype(F32))

        def gather_into(block_of, chosen):
            select = jnp.where(chosen, 1.0, 0.0).astype(BF)
            total = None
            for part in fields:
                term = nt(select, part)
                total = term if total is None else total + term
            own_sum[block_of, :, 0:CODES] += total
            lane_sum[block_of] += nt(at_lane.astype(BF), select)
            total = None
            for part in lines_of:
                term = nt(part, select)
                total = term if total is None else total + term
            line_sum[block_of] += total

        begin, end = bound(0, 0, me), bound(0, 1, me)
        first_slot = sender * capacity
        block_of = first_slot // LANES
        within = place - (first_slot - block_of * LANES)
        gather_into(block_of, (within >= 0) & (index == begin + within) & (index < end))
        amounts = jnp.where(lane == sender, end - begin, amounts)

        first_r, last_r = bound(1, 0, after), bound(1, 1, after)
        first_l, last_l = bound(2, 0, ahead), bound(0, 1, ahead)
        middle = halo_before + (last_r - first_r)
        chosen_r = (index >= first_r) & (index < last_r) & (index - first_r + halo_before == place)
        chosen_l = (index >= first_l) & (index < last_l) & (index - first_l + middle == place)
        gather_into(halo_block, chosen_r | chosen_l)
        return middle + (last_l - first_l), amounts

    halo_count, amounts = lax.fori_loop(
        0,
        senders,
        per_sender,
        (jnp.zeros((1, 1), I32), jnp.zeros((1, LANES), I32)),
        unroll=senders <= GROUP,
    )

    number = iota((stencil, LANES), 0).astype(F32)
    nowhere = float((height // LANES) * wide)
    for i in range(slots // LANES + 1):
        line = line_sum[i, 0:stencil, :]
        leader = jnp.zeros(line.shape, F32)
        for k in reversed(range(stencil)):
            leader = jnp.where(line == line[k : k + 1, :], float(k), leader)
        leads = jnp.where(leader == number, 1.0, 0.0)
        count = jnp.zeros((1, LANES), F32)
        ranks = []
        for k in range(stencil):
            ranks.append(count)
            count = count + leads[k : k + 1, :]
        place = jnp.zeros(line.shape, F32)
        for k in range(stencil):
            place = jnp.where(leader == float(k), ranks[k], place)
        lists = []
        for k in range(stencil):
            found = jnp.where((leads > 0.0) & (place == float(k)), line, 0.0)
            found = jnp.sum(found, axis=0, keepdims=True)
            lists.append(jnp.where(count > float(k), found, nowhere))
        batches = lax.shift_right_logical(
            count.astype(I32) + (BATCH - 1), jnp.full(count.shape, BATCH.bit_length() - 1, I32)
        )
        lists = jnp.concatenate(lists, axis=0).astype(I32)
        top = i * (stencil + 8)
        own_lines[top : top + stencil, :] = lists
        batches = batches.astype(F32)
        most = jnp.zeros((1, LANES), F32)
        slot = iota((1, LANES), 1)
        for begin in range(0, LANES, BLOCK):
            here = (slot >= begin) & (slot < begin + BLOCK)
            found = jnp.max(jnp.where(here, batches, 0.0), axis=1, keepdims=True)
            most = jnp.where(here, found, most)
        own_lines[top + stencil : top + stencil + 8, :] = jnp.concatenate(
            [
                batches.astype(I32),
                most.astype(I32),
                line_sum[i, stencil : stencil + 1, :].astype(I32),
                amounts,
                jnp.broadcast_to(halo_count, (1, LANES)),
                jnp.zeros((3, LANES), I32),
            ],
            axis=0,
        )
        codes = jnp.concatenate(
            [
                jnp.zeros((CODES, LANES), F32),
                place * float(LANES) + lane_sum[i],
                jnp.zeros((LANES - CODES - stencil, LANES), F32),
            ],
            axis=0,
        )
        own[i * LANES : (i + 1) * LANES, :] = own_sum[i] + codes.T


def band(shape, taps, shift):
    distance = iota(shape, 1) - iota(shape, 0) + shift
    result = jnp.zeros(shape, F32)
    for tap in range(taps.shape[0]):
        result = jnp.where(distance == tap, taps[tap], result)
    return result


def band_rev(shape, taps, shift):
    distance = iota(shape, 0) - iota(shape, 1) + shift
    result = jnp.zeros(shape, F32)
    for tap in range(taps.shape[0]):
        result = jnp.where(distance == tap, taps[tap], result)
    return result


def exact_nt(a, b):
    return lax.dot_general(
        a,
        b,
        (((1,), (1,)), ((), ())),
        precision=lax.Precision.HIGHEST,
        preferred_element_type=F32,
    )


def store_split(ref, index, value):
    high, low = split2(value)
    ref[(0,) + index] = high
    ref[(1,) + index] = low


def bands_kernel(kx, ky, lat2, lon2, lat1, lon1, *, rows_block):
    margin = kx.shape[0] // 2
    window = lat2.shape[2]
    first = band((window, window), ky, margin)
    reach = first[LANES : LANES + WIDE, :]
    place = iota((window, window), 1)
    for variant in range(3):
        kept = first
        if variant == 0:
            kept = jnp.where(place >= LANES, first, 0.0)
        if variant == 2:
            kept = jnp.where(place < LANES + WIDE, first, 0.0)
        store_split(lat2, (variant,), exact_nt(kept, reach))
    size = lon2.shape[1]
    wide = size + 2 * HALO
    depth = (wide + 32 + LANES - 1) // LANES * LANES
    second = band((wide, depth), kx, -(16 - margin))
    store_split(lon2, (), exact_nt(second[HALO : HALO + size, :], second))
    store_split(lat1, (), band_rev((rows_block, rows_block + 2 * PAD), ky, PAD + margin))
    store_split(lon1, (), band((2 * WIDE, WIDE), kx, LANES + margin))


def pairs(low, high, action):
    def step(i, carry):
        one = low + 2 * i
        action(one, jnp.minimum(one + 1, high - 1), one + 1 < high)
        return carry

    lax.fori_loop(0, lax.shift_right_logical(high - low + 1, 1), step, 0)


def zero_all(refs):
    rows = refs[0].shape[0]
    step = 256

    def clear(i, carry):
        for ref in refs:
            ref[pl.ds(pl.multiple_of(i * step, 8), step), :] = jnp.zeros((step, LANES), F32)
        return carry

    whole = rows // step
    lax.fori_loop(0, whole, clear, 0)
    if rows % step:
        for ref in refs:
            ref[whole * step : rows, :] = jnp.zeros((rows % step, LANES), F32)


def scatter_entries(copies, entries, lane):
    for start in range(0, len(entries), len(copies)):
        group = []
        for ref, (address, value) in zip(copies, entries[start : start + len(copies)]):
            line = lax.shift_right_logical(address, 7)
            spread = jnp.where(lane == (address & (LANES - 1)), value, 0.0)
            group.append((ref, line, ref[pl.ds(line, 1), :] + spread))
        for ref, line, value in group:
            ref[pl.ds(line, 1), :] = value


def spot(sender, idx, per, stencil):
    return sender * per + idx + lax.shift_right_logical(idx, 7) * ((stencil - 1) * LANES)


def copy_parts(layout, source, target, place, chunk, chunks, group, sem):
    begin, size = place
    words = group * size * LANES
    at = begin * LANES + chunk * words
    return pltpu.make_async_copy(source.at[pl.ds(at, words)], target, sem)


def apply_kernel(
    *refs, first, layout, columns, height, hold, stencil, capacity, senders, parts, levels
):
    refs = list(refs)

    def take(count):
        taken = refs[:count]
        del refs[:count]
        return taken

    meta, ints, floats, own_lines, own = take(5)
    if not first:
        replies_h, replies = take(2)
    std_h, std_l_h, std_r_h, lat2_h, lon2_h = take(5)
    if not first:
        merged_h = take(1)[0]
    field_h, send = take(2)
    if first:
        info_out, merged_h = take(2)
    addr, wgt, start, lines_s, val = take(5)
    if first:
        std_flat, picked, chosen = take(3)
    scale, merged, sums, high_s, low_s, std, std_l, std_r, lat2, lon2, field = take(11)
    copies = take(PAIR)
    sems, in_sems, out_sems, val_sem = take(4)

    me = meta[0]
    wide = columns + 2 * HALO
    blocks = height // LANES
    group = min(GROUP, senders)
    chunks = senders // group
    slots = senders * capacity
    lane = iota((1, LANES), 1)
    per = stencil * hold
    table = layout.table

    def chunk_copies(chunk):
        todo = [
            (ints, addr, layout.ints["addr"]),
            (floats, wgt, layout.floats["wgt"]),
            (ints, start, layout.ints["start"]),
        ]
        if first:
            todo.append((floats, val, layout.floats["val"]))
        return [
            copy_parts(layout, source, target, place, chunk, chunks, group, sems.at[i])
            for i, (source, target, place) in enumerate(todo)
        ]

    def load_chunk(chunk):
        for copy in chunk_copies(chunk):
            copy.start()
        for copy in chunk_copies(chunk):
            copy.wait()

    operands = [
        pltpu.make_async_copy(source, target, in_sems.at[i])
        for i, (source, target) in enumerate(
            (
                (std_h, std),
                (std_l_h, std_l),
                (std_r_h, std_r),
                (lat2_h, lat2),
                (lon2_h, lon2),
            )
        )
    ]
    own_copy = pltpu.make_async_copy(own_lines, lines_s, in_sems.at[5])
    own_copy.start()
    merged_copy = pltpu.make_async_copy(
        *((merged, merged_h) if first else (merged_h, merged)), in_sems.at[6]
    )
    if not first:
        merged_copy.start()
    for copy in operands:
        copy.start()

    def value_copy(owner):
        at = pl.multiple_of(owner * (replies.shape[1] * LANES), 1024)
        return pltpu.make_async_copy(
            replies_h.at[pl.ds(at, slots)], val.at[pl.ds(owner * slots, slots)], val_sem.at[owner]
        )

    def each_owner(action):
        def step(owner, carry):
            action(value_copy(owner))
            return carry

        lax.fori_loop(0, parts, step, 0)

    if not first:
        each_owner(lambda copy: copy.start())
    zero_all(copies)
    zero_all([sums])

    lane_of = iota((slots, LANES), 1)
    room = slots + LANES
    column = 2 * stencil if first else 2 * stencil + 2
    scale[...] = jnp.broadcast_to(own[:, column : column + 1], (room, LANES))
    known = own[0:slots, :]
    own_copy.wait()
    if not first:
        merged_copy.wait()

    after = lax.rem(me + 1, parts)
    ahead = lax.rem(me + parts - 1, parts)

    def start_of(sender, owner, row, half):
        return start[sender * table + row * hold + half * LANES + owner]

    def entries_of(sender, idx, value):
        base = spot(sender, idx, per, stencil)
        return [
            (addr[base + k * LANES], wgt[base + k * LANES] * value) for k in range(stencil)
        ]

    def own_line(slot, k):
        at = lax.shift_right_logical(slot, 7) * ((stencil + 7) * LANES) + slot
        return lines_s[at + k * LANES]

    def amount_of(sender):
        return lines_s[(stencil + 3) * LANES + sender]

    halo_count = lines_s[(stencil + 4) * LANES]
    halo_fits = halo_count <= LANES

    def batches_of(one, two):
        return jnp.maximum(own_line(one, stencil), own_line(two, stencil))

    def own_groups(action, halo):
        def group_at(top):
            top = pl.multiple_of(top, 8)
            most = own_line(top, stencil + 1)

            @pl.when(most <= 2)
            def _():
                action(top, 2 * BATCH)

            @pl.when(most > 2)
            def _():
                action(top, stencil)

        def blocks_of(top, amount):
            def step(i, inner):
                group_at(top + i * BLOCK)
                return inner

            lax.fori_loop(0, lax.div(amount + (BLOCK - 1), BLOCK), step, 0)

        if capacity % BLOCK:
            blocks_of(0, slots)
        else:

            def per_sender(sender, carry):
                blocks_of(sender * capacity, amount_of(sender))
                return carry

            lax.fori_loop(0, senders, per_sender, 0)
        if halo:
            blocks_of(slots, jnp.minimum(halo_count, LANES))

    lane_f = iota((BLOCK, LANES), 1).astype(F32)

    def columns_of(info, begin):
        return [
            jnp.broadcast_to(info[:, begin + k : begin + k + 1], (BLOCK, LANES))
            for k in range(stencil)
        ]

    def build(top, places):
        info = own[pl.ds(top, BLOCK), :]
        codes = columns_of(info, CODES)
        weights = columns_of(info, stencil)
        for place in range(stencil):
            row = jnp.zeros((BLOCK, LANES), F32)
            if place < places:
                at = lane_f + float(LANES * place)
                for k in range(place, stencil):
                    row = row + jnp.where(at == codes[k], weights[k], 0.0)
            merged[pl.ds(place * room + top, BLOCK), :] = row

    if first:
        own_groups(build, True)
        merged_copy.start()

    def own_pairs(action):
        def per_sender(sender, carry):
            base = sender * capacity
            pairs(base, base + amount_of(sender), action)
            return carry

        lax.fori_loop(0, senders, per_sender, 0)

    def scatter_pair(one, two, values):
        def batch(begin):
            todo = []
            for slot, value, ref in zip((one, two), values, copies):
                for j in range(BATCH):
                    line = own_line(slot, begin + j)
                    row = merged[pl.ds((begin + j) * room + slot, 1), :] * value
                    todo.append((ref, line, ref[pl.ds(line, 1), :] + row))
            for ref, line, row in todo:
                ref[pl.ds(line, 1), :] = row

        def more(i, carry):
            batch(i * BATCH)
            return carry

        batch(0)
        lax.fori_loop(1, batches_of(one, two), more, 0)

    def scatter_known(one, two, has_two):
        second = jnp.where(has_two, 1.0, 0.0)
        scatter_pair(one, two, (scale[pl.ds(one, 1), :], scale[pl.ds(two, 1), :] * second))

    def scatter_sent(one, two, has_two):
        second = jnp.where(has_two, val[own_line(two, stencil + 2)], 0.0)
        scatter_pair(one, two, (val[own_line(one, stencil + 2)], second))

    def scatter_halo(chunk):
        def per_sender(sender, carry):
            for owner, low, high in ((after, (1, 0), (1, 1)), (ahead, (2, 0), (0, 1))):
                begin = start_of(sender, owner, 0, 0)

                def value_of(idx, owner=owner, begin=begin):
                    if first:
                        return val[sender * hold + idx]
                    place = (chunk * group + sender) * capacity + idx - begin
                    return val[owner * slots + place]

                def action(one, two, has_two, value_of=value_of):
                    second = jnp.where(has_two, value_of(two), 0.0)
                    scatter_entries(
                        copies,
                        entries_of(sender, one, value_of(one)) + entries_of(sender, two, second),
                        lane,
                    )

                pairs(start_of(sender, owner, *low), start_of(sender, owner, *high), action)
            return carry

        lax.fori_loop(0, group, per_sender, 0)

    own_pairs(scatter_known)
    if not first:
        each_owner(lambda copy: copy.wait())

    @pl.when(halo_fits)
    def _():
        pairs(slots, slots + halo_count, scatter_known if first else scatter_sent)

    @pl.when(jnp.logical_not(halo_fits))
    def _():
        def step(chunk, carry):
            load_chunk(chunk)
            scatter_halo(chunk)
            return carry

        lax.fori_loop(0, chunks, step, 0)

    for copy in operands:
        copy.wait()

    for jb in range(blocks):
        lanes = slice(jb * LANES, (jb + 1) * LANES)
        for low, size, source in (
            (0, HALO, std_l),
            (HALO, columns, std),
            (HALO + columns, HALO, std_r),
        ):
            rows = slice(jb * wide + low, jb * wide + low + size)
            total = copies[0][rows, :]
            for ref in copies[1:]:
                total = total + ref[rows, :]
            high, lo = split2(total * source[:, lanes])
            high_s[low : low + size, lanes] = high
            low_s[low : low + size, lanes] = lo
        if first:
            std_flat[jb * wide + HALO : jb * wide + HALO + columns, :] = std[:, lanes]

    smoothed = copies[0]
    size = lon2.shape[1]
    count = height // WIDE
    outgoing = [merged_copy] if first else []
    for block in range(count):
        variant = 0 if block == 0 else (2 if block == count - 1 else 1)
        low = max(block * WIDE - LANES, 0)
        high = min(block * WIDE + WIDE + LANES, height)
        inner = slice(low - (block * WIDE - LANES), high - (block * WIDE - LANES))
        matrix = (lat2[0, variant, inner, :], lat2[1, variant, inner, :])
        along = mm_parts((high_s[:, low:high], low_s[:, low:high]), matrix)
        parts_y = split2(along)
        lanes = slice(block * WIDE, (block + 1) * WIDE)
        for begin in range(0, columns, size):
            some = min(size, columns - begin)
            rows = slice(begin, begin + some)
            window = slice(begin, begin + some + 2 * HALO)
            matrix = tuple(lon2[i, 0:some, 0 : some + 2 * HALO] for i in range(2))
            result = mm_parts(matrix, (parts_y[0][window, :], parts_y[1][window, :]))
            field[rows, lanes] = result
            scaled = result * std[rows, lanes]
            for half in range(WIDE // LANES):
                top = (block * (WIDE // LANES) + half) * wide + HALO + begin
                smoothed[top : top + some, :] = scaled[:, half * LANES : (half + 1) * LANES]
        outgoing.append(
            pltpu.make_async_copy(field.at[:, lanes], field_h.at[:, lanes], out_sems.at[block])
        )
        outgoing[-1].start()

    def gather_pair(one, two, has_two):
        def batch(begin, totals):
            result = []
            for slot, total in zip((one, two), totals):
                terms = []
                for j in range(BATCH):
                    line = own_line(slot, begin + j)
                    row = merged[pl.ds((begin + j) * room + slot, 1), :]
                    terms.append(row * smoothed[pl.ds(line, 1), :])
                    if first:
                        picked[pl.ds((begin + j) * room + slot, 1), :] = std_flat[
                            pl.ds(line, 1), :
                        ]
                result.append(total + ((terms[0] + terms[1]) + (terms[2] + terms[3])))
            return tuple(result)

        zero = jnp.zeros((1, LANES), F32)
        totals = lax.fori_loop(
            1,
            batches_of(one, two),
            lambda i, totals: batch(i * BATCH, totals),
            batch(0, (zero, zero)),
        )
        for slot, total in zip((one, two), totals):
            sums[pl.ds(slot, 1), :] = total

    own_pairs(gather_pair)

    def pick(top, places):
        info = own[pl.ds(top, BLOCK), :]
        codes = columns_of(info, CODES)
        rows = [picked[pl.ds(place * room + top, BLOCK), :] for place in range(places)]
        result = jnp.zeros((BLOCK, LANES), F32)
        for k in range(stencil):
            cell = jnp.zeros((BLOCK, LANES), F32)
            for place in range(min(k + 1, places)):
                at = lane_f + float(LANES * place)
                cell = jnp.where(at == codes[k], rows[place], cell)
            cell = jnp.sum(cell, axis=1, keepdims=True)
            result = jnp.where(lane_f == float(stencil + k), cell, result)
        chosen[pl.ds(top, BLOCK), :] = result * info

    if first:
        own_groups(pick, False)

    def whole(x):
        return jnp.sum(x, axis=0, keepdims=True)

    total = jnp.sum(sums[...], axis=1, keepdims=True)
    lines = slots // LANES
    known = own[0:slots, :]
    source, weight, reply, image0 = (
        known[:, 2 * stencil + i : 2 * stencil + i + 1] for i in range(4)
    )
    if first:
        reply = weight * total
        known = jnp.where(lane_of == 2 * stencil + 2, reply, known)
        known = jnp.where(lane_of == 2 * stencil + 3, total, known)
        info_out[0:slots, :] = known
        info_out[slots:room, :] = own[slots:room, :]
        turned = known.T[2 * stencil + 2 : 2 * stencil + 3, :]
        message = [turned[:, i * LANES : (i + 1) * LANES] for i in range(lines)]
        message.append(
            jnp.where(
                lane == 0, whole(source * total), jnp.where(lane == 1, whole(reply * total), 0.0)
            )
        )
        message.append(jnp.zeros((8 - len(message), LANES), F32))
        factors = chosen[...].T
        for k in range(stencil):
            row = factors[stencil + k : stencil + k + 1, :]
            message += [row[:, i * LANES : (i + 1) * LANES] for i in range(lines)]
        message = jnp.concatenate(message, axis=0)
    else:
        slab = jnp.sum(replies[:, 0:8, :], axis=0)[lines : lines + 1, :]
        length = slab[:, 0:1] / (slab[:, 0:1] + slab[:, 1:2])
        both = source + reply
        s_both = image0 + total
        resid = source - length * both
        s_resid = image0 - length * s_both
        values = [
            resid * s_resid,
            resid * s_both,
            both * s_both,
            resid * image0,
            both * image0,
            weight * s_resid * s_resid,
            weight * s_resid * s_both,
            weight * s_both * s_both,
            weight * s_resid * image0,
            weight * s_both * image0,
            source * image0,
            reply * image0,
        ]
        message = jnp.where(lane == len(values), length, 0.0)
        for i, value in enumerate(values):
            message = jnp.where(lane == i, whole(value), message)
        message = jnp.concatenate([message, jnp.zeros((7, LANES), F32)], axis=0)

    def send_to(i, carry):
        send[i] = message
        return carry

    lax.fori_loop(0, send.shape[0], send_to, 0)
    for copy in outgoing:
        copy.wait()


def final_kernel(
    ints,
    floats,
    replies_h,
    totals,
    std_h,
    field0_h,
    field1_h,
    lat1,
    lon1,
    control_h,
    increment_h,
    addr,
    listed,
    start,
    slot,
    val,
    factors,
    std,
    field0,
    field1,
    control,
    high_s,
    low_s,
    *rest,
    layout,
    hold,
    stencil,
    capacity,
    senders,
    parts,
    length,
):
    copies = rest[:COPIES]
    sems, in_sems, out_sems = rest[COPIES:]
    group = min(GROUP, senders)
    chunks = senders // group
    per = stencil * hold
    rows_block = control.shape[0]
    high_rows = rows_block + 2 * PAD
    lane = iota((1, LANES), 1)
    stride = group * capacity
    owner_words = factors.shape[0] // parts
    to_factors = owner_words - stencil * stride

    def chunk_copies(chunk):
        todo = [
            (ints, addr, layout.ints["rows"]),
            (ints, listed, layout.ints["listed"]),
            (ints, start, layout.ints["start"]),
            (ints, slot, layout.ints["slot"]),
            (floats, val, layout.floats["val"]),
        ]
        result = [
            copy_parts(layout, source, target, place, chunk, chunks, group, sems.at[i])
            for i, (source, target, place) in enumerate(todo)
        ]
        words = parts * owner_words
        result.append(
            pltpu.make_async_copy(
                replies_h.at[pl.ds(chunk * words, words)], factors, sems.at[len(todo)]
            )
        )
        return result

    pending = []
    if chunks == 1:
        pending = chunk_copies(0)
        for copy in pending:
            copy.start()
    operands = [
        pltpu.make_async_copy(source, target, in_sems.at[i])
        for i, (source, target) in enumerate(
            ((std_h, std), (field0_h, field0), (field1_h, field1))
        )
    ]
    for copy in operands:
        copy.start()

    slabs = totals.shape[1]
    every = jnp.sum(totals[...], axis=0)
    norm0 = quad0 = None
    for i in range(slabs):
        line = every[i, 0:1, :]
        a, b = line[:, 10:11], line[:, 11:12]
        norm0 = a if norm0 is None else norm0 + a
        quad0 = b if quad0 is None else quad0 + b
    step0 = norm0 / (norm0 + quad0)
    norm1 = cross = quad1 = quad01 = jnp.zeros((1, 1), F32)
    for i in range(slabs):
        line = every[i, 0:1, :]
        v = [line[:, j : j + 1] for j in range(10)]
        shift = totals[0, i, 0:1, 12:13] - step0
        norm1 = norm1 + (v[0] + shift * (2.0 * v[1] + shift * v[2]))
        cross = cross + (v[3] + shift * v[4])
        quad1 = quad1 + (v[5] + shift * (2.0 * v[6] + shift * v[7]))
        quad01 = quad01 + (v[8] + shift * v[9])
    ratio = norm1 / norm0
    curvature = norm1 + quad1 + ratio * (
        2.0 * (cross + quad01) + ratio * (norm0 + quad0)
    )
    step1 = norm1 / curvature
    first = step0 + step1 * (1.0 - step0 + ratio)
    second = -step0 * step1
    first_line = jnp.broadcast_to(first, (1, LANES))
    second_line = jnp.broadcast_to(second, (1, LANES))

    zero_all(copies)

    def scatter_chunk():
        def per_sender(sender, carry):
            def entries_of(at, scale):
                idx = listed[sender * hold + at]
                place = slot[sender * hold + idx]
                place = place + lax.div(place, stride) * (owner_words - stride)
                base = spot(sender, idx, per, stencil)
                z0 = val[sender * hold + idx] * scale
                u = factors[place] * scale
                value = first_line * z0 + second_line * u
                return [
                    (addr[base + k * LANES], factors[place + to_factors + k * stride] * value)
                    for k in range(stencil)
                ]

            def action(one, two, has_two):
                scale = jnp.where(has_two, 1.0, 0.0)
                scatter_entries(copies, entries_of(one, 1.0) + entries_of(two, scale), lane)

            pairs(0, start[sender * layout.table + layout.table - 1], action)
            return carry

        lax.fori_loop(0, group, per_sender, 0)

    if chunks == 1:
        for copy in pending:
            copy.wait()
        scatter_chunk()
    else:

        def step(chunk, carry):
            for copy in chunk_copies(chunk):
                copy.start()
            for copy in chunk_copies(chunk):
                copy.wait()
            scatter_chunk()
            return carry

        lax.fori_loop(0, chunks, step, 0)

    for copy in operands:
        copy.wait()
    increment = field0
    increment[...] = std[...] * (first * field0[...] + second * field1[...])
    outgoing = [pltpu.make_async_copy(increment, increment_h, out_sems.at[0])]
    outgoing[0].start()

    pair = WIDE // LANES
    count = length // WIDE
    for block in range(count):
        pieces = []
        for half in range(pair):
            rows = slice((block * pair + half) * high_rows, (block * pair + half + 1) * high_rows)
            total = copies[0][rows, :]
            for ref in copies[1:]:
                total = total + ref[rows, :]
            pieces.append(total)
        whole = split2(jnp.concatenate(pieces, axis=1))
        size = lat1.shape[1]
        for top in range(0, rows_block, size):
            window = slice(top, top + size + 2 * PAD)
            along = mm_parts((lat1[0], lat1[1]), (whole[0][window, :], whole[1][window, :]))
            high, low = split2(along)
            high_s[top : top + size, block * WIDE : (block + 1) * WIDE] = high
            low_s[top : top + size, block * WIDE : (block + 1) * WIDE] = low

    def window(ref, block):
        low, high = block * WIDE - LANES, (block + 1) * WIDE + LANES
        if low < 0:
            return jnp.concatenate([ref[:, length + low : length], ref[:, 0:high]], axis=1)
        if high > length:
            return jnp.concatenate([ref[:, low:length], ref[:, 0 : high - length]], axis=1)
        return ref[:, low:high]

    every_lanes = 4
    for block in range(count):
        control[:, block * WIDE : (block + 1) * WIDE] = mm_parts(
            (window(high_s, block), window(low_s, block)), (lon1[0], lon1[1])
        )
        if block % every_lanes == every_lanes - 1:
            lanes = slice((block + 1 - every_lanes) * WIDE, (block + 1) * WIDE)
            outgoing.append(
                pltpu.make_async_copy(
                    control.at[:, lanes], control_h.at[:, lanes], out_sems.at[len(outgoing)]
                )
            )
            outgoing[-1].start()
    for copy in outgoing:
        copy.wait()


def body(
    background_std,
    x_kernel,
    y_kernel,
    obs_owner,
    obs_cells,
    obs_weights,
    innovation,
    obs_precision,
    obs_counts,
):
    parts = lax.axis_size("pencil")
    levels = lax.axis_size("lev")
    me = lax.axis_index("pencil")
    _, columns, height = background_std.shape
    hold, stencil = obs_cells.shape
    margin = x_kernel.shape[1] // 2
    capacity = 2 * hold // parts
    senders = parts
    slots = senders * capacity
    room = slots + LANES
    rows_block = height // parts
    length = columns * parts
    blocks = height // LANES
    wide = columns + 2 * HALO
    group = min(GROUP, senders)
    chunks = senders // group
    layout = Layout(senders, hold, stencil, parts)
    std = background_std[0]

    packed = pl.pallas_call(
        functools.partial(
            pack_kernel, parts=parts, columns=columns, height=height, margin=margin
        ),
        out_shape=jax.ShapeDtypeStruct((parts, PACK, hold), F32),
        in_specs=[smem()] + [vmem()] * 5,
        out_specs=vmem(),
        compiler_params=params(),
        cost_estimate=cost(12000),
        name="pack",
    )(
        obs_counts,
        obs_owner.T,
        obs_cells.T,
        obs_weights.T,
        innovation[None, :],
        obs_precision[None, :],
    )
    recv = lax.all_to_all(packed, "pencil", split_axis=0, concat_axis=0, tiled=True)

    right = [(p, (p + 1) % parts) for p in range(parts)]
    left = [(p, (p - 1) % parts) for p in range(parts)]
    std_l = lax.ppermute(std[columns - HALO :, :], "pencil", right)
    std_r = lax.ppermute(std[:HALO, :], "pencil", left)

    size = min(columns, WIDE - 2 * HALO)
    row_size = min(rows_block, LANES)
    lat2, lon2, lat1, lon1 = pl.pallas_call(
        functools.partial(bands_kernel, rows_block=row_size),
        out_shape=[
            jax.ShapeDtypeStruct((2, 3, 2 * WIDE, WIDE), BF),
            jax.ShapeDtypeStruct((2, size, size + 2 * HALO), BF),
            jax.ShapeDtypeStruct((2, row_size, row_size + 2 * PAD), BF),
            jax.ShapeDtypeStruct((2, 2 * WIDE, WIDE), BF),
        ],
        in_specs=[smem(), smem()],
        out_specs=[vmem()] * 4,
        compiler_params=params(),
        cost_estimate=cost(6000),
        name="bands",
    )(x_kernel[0], y_kernel[0])

    meta = jnp.reshape(me, (1,)).astype(I32)
    ints, floats, own_lines, own = pl.pallas_call(
        functools.partial(
            unpack_kernel,
            layout=layout,
            parts=parts,
            columns=columns,
            height=height,
            capacity=capacity,
            stencil=stencil,
            group=group,
        ),
        out_shape=[
            jax.ShapeDtypeStruct((layout.int_rows, LANES), I32),
            jax.ShapeDtypeStruct((layout.float_rows, LANES), F32),
            jax.ShapeDtypeStruct((room // LANES * (stencil + 8), LANES), I32),
            jax.ShapeDtypeStruct((room, LANES), F32),
        ],
        in_specs=[smem(), vmem()],
        out_specs=[vmem()] * 4,
        scratch_shapes=[
            pltpu.VMEM((room // LANES, LANES, LANES), F32),
            pltpu.VMEM((room // LANES, stencil + 8, LANES), F32),
            pltpu.VMEM((room // LANES, stencil, LANES), F32),
        ],
        compiler_params=params(),
        cost_estimate=cost(100),
        name="unpack",
    )(meta, recv)
    ints = ints.reshape(-1)
    floats = floats.reshape(-1)
    own_lines = own_lines.reshape(-1)

    acc = pltpu.VMEM((blocks * wide + 8, LANES), F32)
    column_slots = pltpu.VMEM((slots, LANES), F32)
    static = dict(
        layout=layout,
        columns=columns,
        height=height,
        hold=hold,
        stencil=stencil,
        capacity=capacity,
        senders=senders,
        parts=parts,
        levels=levels,
    )
    per = group * stencil * hold
    line = group * hold
    index_scratch = [
        pltpu.SMEM((per,), I32),
        pltpu.SMEM((per,), F32),
        pltpu.SMEM((group * layout.table,), I32),
        pltpu.SMEM((room * (stencil + 8),), I32),
    ]
    work = (
        [
            pltpu.VMEM((room, LANES), F32),
            pltpu.VMEM((stencil * room, LANES), F32),
            column_slots,
        ]
        + [pltpu.VMEM((wide, height), BF)] * 2
        + [
            pltpu.VMEM((columns, height), F32),
            pltpu.VMEM((HALO, height), F32),
            pltpu.VMEM((HALO, height), F32),
            pltpu.VMEM(lat2.shape, BF),
            pltpu.VMEM(lon2.shape, BF),
            pltpu.VMEM((columns, height), F32),
        ]
        + [acc] * PAIR
        + [
            pltpu.SemaphoreType.DMA((4,)),
            pltpu.SemaphoreType.DMA((7,)),
            pltpu.SemaphoreType.DMA((height // WIDE,)),
            pltpu.SemaphoreType.DMA((parts,)),
        ]
    )
    field_shape = jax.ShapeDtypeStruct((columns, height), F32)
    reply_rows = 8 + stencil * slots // LANES
    field0, message, info, merged = pl.pallas_call(
        functools.partial(apply_kernel, first=True, **static),
        out_shape=[
            field_shape,
            jax.ShapeDtypeStruct((parts, reply_rows, LANES), F32),
            jax.ShapeDtypeStruct((room, LANES), F32),
            jax.ShapeDtypeStruct((stencil * room, LANES), F32),
        ],
        in_specs=[smem()] + [hbm()] * 3 + [vmem()] + [hbm()] * 5,
        out_specs=[hbm()] + [vmem()] * 2 + [hbm()],
        scratch_shapes=index_scratch
        + [
            pltpu.SMEM((line,), F32),
            acc,
            pltpu.VMEM((stencil * room, LANES), F32),
            column_slots,
        ]
        + work,
        compiler_params=params(),
        name="apply_first",
    )(meta, ints, floats, own_lines, own, std, std_l, std_r, lat2, lon2)

    replies = lax.all_to_all(message, "pencil", split_axis=0, concat_axis=0, tiled=True)
    back = replies.reshape(-1)

    field1, sums = pl.pallas_call(
        functools.partial(apply_kernel, first=False, **static),
        out_shape=[
            field_shape,
            jax.ShapeDtypeStruct((parts * levels, 8, LANES), F32),
        ],
        in_specs=[smem()] + [hbm()] * 3 + [vmem(), hbm(), vmem()] + [hbm()] * 6,
        out_specs=[hbm(), vmem()],
        scratch_shapes=index_scratch + [pltpu.SMEM((parts * slots,), F32)] + work,
        compiler_params=params(),
        name="apply_second",
    )(
        meta,
        ints,
        floats,
        own_lines,
        info,
        back,
        replies,
        std,
        std_l,
        std_r,
        lat2,
        lon2,
        merged,
    )

    totals = lax.all_to_all(sums, ("pencil", "lev"), split_axis=0, concat_axis=0, tiled=True)
    totals = totals.reshape(parts, levels, 8, LANES)

    by_chunk = back
    if chunks > 1:
        by_chunk = jnp.concatenate(
            [replies[:, : slots // LANES, :], replies[:, 8:, :]], axis=1
        ).reshape(parts, stencil + 1, chunks, group * capacity)
        by_chunk = jnp.transpose(by_chunk, (2, 0, 1, 3)).reshape(-1)
    owner_words = by_chunk.shape[0] // (chunks * parts)
    high_rows = rows_block + 2 * PAD
    acc_rows = pltpu.VMEM(((length // LANES) * high_rows + 8, LANES), F32)
    control, increment = pl.pallas_call(
        functools.partial(
            final_kernel,
            layout=layout,
            hold=hold,
            stencil=stencil,
            capacity=capacity,
            senders=senders,
            parts=parts,
            length=length,
        ),
        out_shape=[
            jax.ShapeDtypeStruct((rows_block, length), F32),
            field_shape,
        ],
        in_specs=[hbm()] * 3 + [vmem()] + [hbm()] * 3 + [vmem()] * 2,
        out_specs=[hbm()] * 2,
        scratch_shapes=[
            pltpu.SMEM((per,), I32),
            pltpu.SMEM((line,), I32),
            pltpu.SMEM((group * layout.table,), I32),
            pltpu.SMEM((line,), I32),
            pltpu.SMEM((line,), F32),
            pltpu.SMEM((parts * owner_words,), F32),
            pltpu.VMEM((columns, height), F32),
            pltpu.VMEM((columns, height), F32),
            pltpu.VMEM((columns, height), F32),
            pltpu.VMEM((rows_block, length), F32),
            pltpu.VMEM((rows_block, length), BF),
            pltpu.VMEM((rows_block, length), BF),
        ]
        + [acc_rows] * COPIES
        + [
            pltpu.SemaphoreType.DMA((7,)),
            pltpu.SemaphoreType.DMA((3,)),
            pltpu.SemaphoreType.DMA((1 + length // WIDE,)),
        ],
        compiler_params=params(),
        name="outputs",
    )(ints, floats, by_chunk, totals, std, field0, field1, lat1, lon1)
    return control[None], increment[None]


def solution(mesh):
    return jax.shard_map(
        body,
        mesh=mesh,
        in_specs=(
            P("lev", "pencil", None),
            P("lev", None),
            P("lev", None),
            P(("pencil", "lev"), None),
            P(("pencil", "lev"), None),
            P(("pencil", "lev"), None),
            P(("pencil", "lev")),
            P(("pencil", "lev")),
            P(("pencil", "lev")),
        ),
        out_specs=(P("lev", "pencil", None), P("lev", "pencil", None)),
        check_vma=False,
    )
```

```python
import functools

import jax
import jax.numpy as jnp
import numpy as np
from jax import lax
from jax.experimental import pallas as pl
from jax.experimental.pallas import tpu as pltpu
from jax.sharding import PartitionSpec as P


BF = jnp.bfloat16
F32 = jnp.float32
I32 = jnp.int32
LANES = 128
WIDE = 256
HALO = 32
PAD = 16
PACK = 40
GROUP = 8
PAIR = 2
BATCH = 4
BLOCK = 32
CODES = 40
STACK = 64
LISTED = 512
VMEM_LIMIT = 58 * 1024 * 1024


def vmem():
    return pl.BlockSpec(memory_space=pltpu.VMEM)


def smem():
    return pl.BlockSpec(memory_space=pltpu.SMEM)


def hbm():
    return pl.BlockSpec(memory_space=pl.ANY)


def cost(nanoseconds):
    return pl.CostEstimate(flops=0, bytes_accessed=3690 * nanoseconds, transcendentals=0)


def params():
    return pltpu.CompilerParams(vmem_limit_bytes=VMEM_LIMIT)


def split2(x):
    high = x.astype(BF)
    return high, (x - high.astype(F32)).astype(BF)


def split3(x):
    high = x.astype(BF)
    rest = x - high.astype(F32)
    mid = rest.astype(BF)
    return high, mid, (rest - mid.astype(F32)).astype(BF)


def mm(a, b):
    return jnp.dot(a, b, preferred_element_type=F32)


def mm_parts(a_parts, b_parts):
    (ah, al), (bh, bl) = a_parts, b_parts
    return mm(jnp.concatenate([ah, al, ah], axis=1), jnp.concatenate([bh, bh, bl], axis=0))


def iota(shape, dim):
    return lax.broadcasted_iota(I32, shape, dim)


def pack_kernel(
    counts, owner, cells, weights, depart, prec, out, marks, *, parts, columns, height, margin
):
    stencil, hold = cells.shape
    shift = height.bit_length() - 1
    block = height // parts
    reach = 2 * margin
    row_id = iota((hold, hold), 0)
    col_id = iota((hold, hold), 1)
    eye = row_id == col_id
    col_f = col_id.astype(F32)
    live = iota((1, hold), 1) < counts[0]
    cell = cells[...]
    column = lax.shift_right_logical(cell, jnp.full(cell.shape, shift, I32))
    row = cell & (height - 1)

    def any_of(mask):
        return jnp.max(jnp.where(mask, 1.0, 0.0), axis=0, keepdims=True)

    def turn(line):
        return jnp.sum(jnp.where(eye, line, 0.0), axis=1, keepdims=True)

    left = any_of(column < reach)
    right = any_of(column >= columns - reach)
    side = left + 3.0 * right - 2.0 * left * right
    base = jnp.where(live, owner[...].astype(F32) * 4.0, 4.0 * parts)
    key = jnp.where(live, base + side, base)
    key_col = turn(key)
    before = (key_col < key) | ((key_col == key) & (row_id < col_id))
    rank = jnp.sum(jnp.where(before, 1.0, 0.0), axis=0, keepdims=True)
    begin = jnp.sum(jnp.where(key_col < base, 1.0, 0.0), axis=0, keepdims=True)
    rank_col = turn(rank)
    perm = jnp.where(rank_col == col_f, 1.0, 0.0).astype(BF)

    def sort(values):
        total = None
        for part in split3(values):
            term = mm(part, perm)
            total = term if total is None else total + term
        return total

    weight = jnp.where(live, prec[...], 0.0)
    rest = [weight * depart[...], weight, key, rank - begin, jnp.zeros((4, hold), F32)]
    values = [cell.astype(F32), weights[...]] + rest
    ordered = sort(jnp.concatenate(values, axis=0))
    line = iota((8, hold), 0)
    tail = ordered[2 * stencil : 2 * stencil + 8, :]
    first_half = col_f < float(LANES)
    fourfold = 4.0 * jnp.where(first_half, col_f, col_f - float(LANES))
    for i, (low, high) in enumerate(((0.0, 4.0), (1.0, 3.0), (2.0, 2.0))):
        bound = fourfold + jnp.where(first_half, low, high)
        begins = jnp.sum(jnp.where(key_col < bound, 1.0, 0.0), axis=0, keepdims=True)
        tail = jnp.where(line == 5 + i, begins, tail)
    last = (line == 7) & (iota((8, hold), 1) == hold - 1)

    def mark(part, carry):
        low = part * block - margin
        high = (part + 1) * block + margin
        flag = jnp.where(live, any_of((row >= low) & (row < high)), 0.0)
        place = jnp.sum(jnp.where(row_id < col_id, turn(flag), 0.0), axis=0, keepdims=True)
        marks[pl.ds(part, 1), :] = flag * (place + 1.0)
        return carry

    lax.fori_loop(0, parts, mark, 0, unroll=parts <= GROUP)
    listed = marks[...]
    amounts = jnp.max(listed, axis=1, keepdims=True)
    listed = mm(listed.astype(BF), perm)
    for part in range(parts):
        out[part, 0 : 2 * stencil, :] = ordered[0 : 2 * stencil, :]
        out[part, 2 * stencil : 2 * stencil + 8, :] = jnp.where(
            line == 4,
            listed[part : part + 1, :],
            jnp.where(last, amounts[part : part + 1, :], tail),
        )


class Layout:
    def __init__(self, senders, hold, stencil, parts):
        lines = hold // LANES
        self.table = 3 * hold
        sizes = dict(
            addr=stencil * lines, rows=stencil * lines, listed=lines, slot=lines, start=3 * lines
        )
        self.ints = {}
        at = 0
        for name, size in sizes.items():
            self.ints[name] = (at, size)
            at += senders * size
        self.int_rows = at
        self.floats = {}
        at = 0
        for name, size in dict(wgt=stencil * lines, val=lines).items():
            self.floats[name] = (at, size)
            at += senders * size
        self.float_rows = at


def right(x, by):
    return lax.shift_right_logical(x, jnp.full(x.shape, by, I32))


def nt(a, b):
    return lax.dot_general(a, b, (((1,), (1,)), ((), ())), preferred_element_type=F32)


class Received:
    def __init__(self, recv, sender, me, *, parts, columns, height, capacity, stencil):
        senders, _, hold = recv.shape
        wide = columns + 2 * HALO
        block = height // parts
        high_rows = block + 2 * PAD
        cell = recv[sender, 0:stencil, :].astype(I32)
        self.tail = recv[sender, 2 * stencil : 2 * stencil + 8, :]
        self.whole = self.tail.astype(I32)
        self.pos = self.whole[3:4, :]
        owner = right(self.whole[2:3, :], 2)
        offset = owner - me
        offset = jnp.where(offset > parts // 2, offset - parts, offset)
        offset = jnp.where(offset < -(parts // 2), offset + parts, offset)
        column = right(cell, height.bit_length() - 1)
        row = cell & (height - 1)
        at = offset * columns + column + HALO
        self.addr = jnp.where(
            (at >= 0) & (at < wide),
            (right(row, 7) * wide + at) * LANES + (row & (LANES - 1)),
            (height // LANES) * wide * LANES,
        )
        at_row = row - (block * me - PAD)
        across = owner * columns + column
        self.rows = jnp.where(
            (at_row >= 0) & (at_row < high_rows) & (owner < parts),
            (right(across, 7) * high_rows + at_row) * LANES + (across & (LANES - 1)),
            (columns * parts // LANES) * high_rows * LANES,
        )
        self.owner = jnp.minimum(owner, parts - 1)
        self.back = self.owner * (senders * capacity) + sender * capacity + self.pos


def stack_of(addr, weights, tail, back):
    hold = addr.shape[1]
    rows = [
        (addr & (LANES - 1)).astype(F32),
        weights,
        tail,
        right(addr, 7).astype(F32),
        back.astype(F32),
        jnp.zeros((7, hold), F32),
    ]
    return jnp.concatenate(split3(jnp.concatenate(rows, axis=0)), axis=1)


def gathered(stack, chosen):
    select = jnp.where(chosen, 1.0, 0.0).astype(BF)
    return nt(stack, jnp.concatenate([select] * 3, axis=1))


def merge_lines(block, nowhere, stencil, extra):
    number = iota((stencil, LANES), 0).astype(F32)
    line = block[CODES : CODES + stencil, :]
    leader = jnp.zeros(line.shape, F32)
    for k in reversed(range(stencil)):
        leader = jnp.where(line == line[k : k + 1, :], float(k), leader)
    leads = jnp.where(leader == number, 1.0, 0.0)
    count = jnp.zeros((1, LANES), F32)
    ranks = []
    for k in range(stencil):
        ranks.append(count)
        count = count + leads[k : k + 1, :]
    place = jnp.zeros(line.shape, F32)
    for k in range(stencil):
        place = jnp.where(leader == float(k), ranks[k], place)
    lists = []
    for k in range(stencil):
        found = jnp.where((leads > 0.0) & (place == float(k)), line, 0.0)
        found = jnp.sum(found, axis=0, keepdims=True)
        lists.append(jnp.where(count > float(k), found, nowhere))
    batches = right(count.astype(I32) + (BATCH - 1), BATCH.bit_length() - 1)
    most = jnp.zeros((1, LANES), F32)
    slot = iota((1, LANES), 1)
    for begin in range(0, LANES, BLOCK):
        here = (slot >= begin) & (slot < begin + BLOCK)
        found = jnp.max(jnp.where(here, batches.astype(F32), 0.0), axis=1, keepdims=True)
        most = jnp.where(here, found, most)
    back = block[CODES + stencil : CODES + stencil + 1, :]
    ints = [jnp.concatenate(lists, axis=0).astype(I32), batches]
    ints += [most.astype(I32), back.astype(I32)] + extra
    ints = jnp.concatenate(ints, axis=0)
    ints = jnp.concatenate([ints, jnp.zeros((stencil + 8 - ints.shape[0], LANES), I32)], axis=0)
    rows = [
        block[0:CODES, :],
        place * float(LANES) + block[0:stencil, :],
        jnp.zeros((LANES - CODES - stencil, LANES), F32),
    ]
    return ints, jnp.concatenate(rows, axis=0).T


def unpack_kernel(
    meta, recv, ints, floats, own_lines, own, total, *, layout, group, **sizes
):
    senders, _, hold = recv.shape
    lines = hold // LANES
    me = meta[0]
    parts, stencil, capacity = sizes["parts"], sizes["stencil"], sizes["capacity"]
    wide = sizes["columns"] + 2 * HALO
    slots = senders * capacity

    def put(ref, place, sender, value):
        begin, size = place
        count = value.shape[0]
        for i in range(lines):
            part = value[:, i * LANES : (i + 1) * LANES]
            if count % 8 == 0:
                at = pl.multiple_of(begin + sender * size + i * count, 8)
                ref[pl.ds(at, count), :] = part
            else:
                for j in range(count):
                    ref[pl.ds(begin + sender * size + i + j * lines, 1), :] = part[j : j + 1]

    total[...] = jnp.zeros(total.shape, F32)
    place = iota((LANES, hold), 0)
    index = iota((LANES, hold), 1)
    lane = iota((1, LANES), 1)
    halo_block = slots // LANES
    after = lax.rem(me + 1, parts)
    ahead = lax.rem(me + parts - 1, parts)

    def per_sender(sender, carry):
        halo_before, amounts = carry
        got = Received(recv, sender, me, **sizes)
        weights = recv[sender, stencil : 2 * stencil, :]
        within = lax.rem(sender, group) * capacity + got.pos
        put(ints, layout.ints["addr"], sender, got.addr)
        put(ints, layout.ints["rows"], sender, got.rows)
        put(ints, layout.ints["listed"], sender, got.whole[4:5, :])
        put(ints, layout.ints["slot"], sender, got.owner * (group * capacity) + within)
        put(ints, layout.ints["start"], sender, got.whole[5:8, :])
        put(floats, layout.floats["wgt"], sender, weights)
        put(floats, layout.floats["val"], sender, got.tail[0:1, :])

        def bound(line, half, owner):
            part = got.whole[5 + line : 6 + line, half * LANES : (half + 1) * LANES]
            return jnp.sum(jnp.where(lane == owner, part, 0), axis=1, keepdims=True)

        stack = stack_of(got.addr, weights, got.tail, got.back)

        begin, end = bound(0, 0, me), bound(0, 1, me)
        first_slot = sender * capacity
        block_of = first_slot // LANES
        within = place - (first_slot - block_of * LANES)
        chosen = (within >= 0) & (index == begin + within) & (index < end)
        shift = first_slot - block_of * LANES
        here = (lane >= shift) & (lane < shift + (end - begin))
        total[block_of] = jnp.where(here, gathered(stack, chosen), total[block_of])
        amounts = jnp.where(lane == sender, end - begin, amounts)

        first_r, last_r = bound(1, 0, after), bound(1, 1, after)
        first_l, last_l = bound(2, 0, ahead), bound(0, 1, ahead)
        middle = halo_before + (last_r - first_r)
        chosen_r = (index >= first_r) & (index < last_r) & (index - first_r + halo_before == place)
        chosen_l = (index >= first_l) & (index < last_l) & (index - first_l + middle == place)
        halo_after = middle + (last_l - first_l)
        here = (lane >= halo_before) & (lane < halo_after)
        values = gathered(stack, chosen_r | chosen_l)
        total[halo_block] = jnp.where(here, values, total[halo_block])
        return halo_after, amounts

    halo_count, amounts = lax.fori_loop(
        0,
        senders,
        per_sender,
        (jnp.zeros((1, 1), I32), jnp.zeros((1, LANES), I32)),
        unroll=senders <= GROUP,
    )
    extra = [amounts, jnp.broadcast_to(halo_count, (1, LANES))]
    nowhere = float((sizes["height"] // LANES) * wide)
    for i in range(slots // LANES + 1):
        top = i * (stencil + 8)
        own_lines[top : top + stencil + 8, :], own[i * LANES : (i + 1) * LANES, :] = merge_lines(
            total[i], nowhere, stencil, extra
        )


def list_kernel(meta, recv, _, row_lines, row_data, total, **sizes):
    senders, _, hold = recv.shape
    stencil = sizes["stencil"]
    high_rows = sizes["height"] // sizes["parts"] + 2 * PAD
    place = iota((LISTED, hold), 0)
    total[...] = jnp.zeros(total.shape, F32)

    def per_sender(sender, before):
        got = Received(recv, sender, meta[0], **sizes)
        marks = got.whole[4:5, :]
        zeros = jnp.zeros((stencil, hold), F32)
        tail = jnp.concatenate([got.tail[0:1, :], zeros[0:7, :]], axis=0)
        stack = stack_of(got.rows, zeros, tail, got.back)
        values = gathered(stack, (marks > 0) & (marks - 1 + before == place))
        after = before + got.whole[7:8, hold - 1 : hold]
        slot = iota((1, LISTED), 1)
        total[...] = jnp.where((slot >= before) & (slot < after), values, total[...])
        return after

    count = lax.fori_loop(
        0, senders, per_sender, jnp.zeros((1, 1), I32), unroll=senders <= GROUP
    )
    nowhere = float((sizes["columns"] * sizes["parts"] // LANES) * high_rows)
    for i in range(LISTED // LANES):
        top = i * (stencil + 8)
        block = total[:, i * LANES : (i + 1) * LANES]
        (
            row_lines[top : top + stencil + 8, :],
            row_data[i * LANES : (i + 1) * LANES, :],
        ) = merge_lines(block, nowhere, stencil, [jnp.broadcast_to(count, (1, LANES))])


def word_of(table, slot, k, stencil):
    at = lax.shift_right_logical(slot, 7) * ((stencil + 7) * LANES) + slot
    return table[at + k * LANES]


def columns_of(info, begin, stencil):
    return [jnp.broadcast_to(info[:, begin + k : begin + k + 1], info.shape) for k in range(stencil)]


def weight_rows(info, places, stencil):
    lane_f = iota(info.shape, 1).astype(F32)
    codes = columns_of(info, CODES, stencil)
    weights = columns_of(info, stencil, stencil)
    rows = []
    for place in range(stencil):
        row = jnp.zeros(info.shape, F32)
        if place < places:
            at = lane_f + float(LANES * place)
            for k in range(place, stencil):
                row = row + jnp.where(at == codes[k], weights[k], 0.0)
        rows.append(row)
    return rows


def block_at(table, top, stencil, action):
    top = pl.multiple_of(top, 8)
    most = word_of(table, top, stencil + 1, stencil)

    @pl.when(most <= 2)
    def _():
        action(top, 2 * BATCH)

    @pl.when(most > 2)
    def _():
        action(top, stencil)


def blocks_of(table, top, amount, stencil, action):
    def step(i, carry):
        block_at(table, top + i * BLOCK, stencil, action)
        return carry

    lax.fori_loop(0, lax.div(amount + (BLOCK - 1), BLOCK), step, 0)


def factor_kernel(
    lines_h, data, replies, _, merged_h, mixed, lines_s, table, merged, sems, *, stencil, slots
):
    parts = replies.shape[0]
    lines = slots // LANES
    lines_copy = pltpu.make_async_copy(lines_h, lines_s, sems.at[0])
    lines_copy.start()

    def per_owner(owner, carry):
        for i in range(lines):
            rows = [
                jnp.zeros((stencil, LANES), F32),
                replies[owner, pl.ds(8 + i, stencil, stride=lines), :],
                jnp.zeros((1, LANES), F32),
                replies[owner, i : i + 1, :],
                jnp.zeros((LANES - 2 * stencil - 2, LANES), F32),
            ]
            at = pl.multiple_of(owner * slots + i * LANES, LANES)
            table[pl.ds(at, LANES), :] = jnp.concatenate(rows, axis=0).T
        return carry

    lax.fori_loop(0, parts, per_owner, 0)
    lines_copy.wait()
    count = jnp.minimum(lines_s[(stencil + 3) * LANES], LISTED)

    def mix(one, two, has_two):
        for slot in (one, two):
            back = word_of(lines_s, slot, stencil + 2, stencil)
            mixed[pl.ds(slot, 1), :] = data[pl.ds(slot, 1), :] + table[pl.ds(back, 1), :]

    pairs(0, count, mix)

    def build(top, places):
        rows = weight_rows(mixed[pl.ds(top, BLOCK), :], places, stencil)
        for place, row in enumerate(rows):
            merged[pl.ds(place * LISTED + top, BLOCK), :] = row

    blocks_of(lines_s, 0, count, stencil, build)
    merged_copy = pltpu.make_async_copy(merged, merged_h, sems.at[1])
    merged_copy.start()
    merged_copy.wait()


def scatter_pair(table, merged, room, copies, one, two, values, stencil):
    def batch(begin):
        todo = []
        for slot, value, ref in zip((one, two), values, copies):
            for j in range(BATCH):
                line = word_of(table, slot, begin + j, stencil)
                row = merged[pl.ds((begin + j) * room + slot, 1), :] * value
                todo.append((ref, line, ref[pl.ds(line, 1), :] + row))
        for ref, line, row in todo:
            ref[pl.ds(line, 1), :] = row

    def more(i, carry):
        batch(i * BATCH)
        return carry

    batch(0)
    most = jnp.maximum(
        word_of(table, one, stencil, stencil), word_of(table, two, stencil, stencil)
    )
    lax.fori_loop(1, most, more, 0)


def band(shape, taps, shift):
    distance = iota(shape, 1) - iota(shape, 0) + shift
    result = jnp.zeros(shape, F32)
    for tap in range(taps.shape[0]):
        result = jnp.where(distance == tap, taps[tap], result)
    return result


def band_rev(shape, taps, shift):
    distance = iota(shape, 0) - iota(shape, 1) + shift
    result = jnp.zeros(shape, F32)
    for tap in range(taps.shape[0]):
        result = jnp.where(distance == tap, taps[tap], result)
    return result


def exact_nt(a, b):
    return lax.dot_general(
        a,
        b,
        (((1,), (1,)), ((), ())),
        precision=lax.Precision.HIGHEST,
        preferred_element_type=F32,
    )


def store_split(ref, index, value):
    high, low = split2(value)
    ref[(0,) + index] = high
    ref[(1,) + index] = low


def bands_kernel(kx, ky, lat2, lon2, lat1, lon1, *, rows_block):
    margin = kx.shape[0] // 2
    window = lat2.shape[2]
    first = band((window, window), ky, margin)
    reach = first[LANES : LANES + WIDE, :]
    place = iota((window, window), 1)
    for variant in range(3):
        kept = first
        if variant == 0:
            kept = jnp.where(place >= LANES, first, 0.0)
        if variant == 2:
            kept = jnp.where(place < LANES + WIDE, first, 0.0)
        store_split(lat2, (variant,), exact_nt(kept, reach))
    size = lon2.shape[1]
    wide = size + 2 * HALO
    depth = (wide + 32 + LANES - 1) // LANES * LANES
    second = band((wide, depth), kx, -(16 - margin))
    store_split(lon2, (), exact_nt(second[HALO : HALO + size, :], second))
    store_split(lat1, (), band_rev((rows_block, rows_block + 2 * PAD), ky, PAD + margin))
    store_split(lon1, (), band((2 * WIDE, WIDE), kx, LANES + margin))


def pairs(low, high, action):
    def step(i, carry):
        one = low + 2 * i
        action(one, jnp.minimum(one + 1, high - 1), one + 1 < high)
        return carry

    lax.fori_loop(0, lax.shift_right_logical(high - low + 1, 1), step, 0)


def zero_all(refs):
    rows = refs[0].shape[0]
    step = 256

    def clear(i, carry):
        for ref in refs:
            ref[pl.ds(pl.multiple_of(i * step, 8), step), :] = jnp.zeros((step, LANES), F32)
        return carry

    whole = rows // step
    lax.fori_loop(0, whole, clear, 0)
    if rows % step:
        for ref in refs:
            ref[whole * step : rows, :] = jnp.zeros((rows % step, LANES), F32)


def scatter_entries(copies, entries, lane):
    for start in range(0, len(entries), len(copies)):
        group = []
        for ref, (address, value) in zip(copies, entries[start : start + len(copies)]):
            line = lax.shift_right_logical(address, 7)
            spread = jnp.where(lane == (address & (LANES - 1)), value, 0.0)
            group.append((ref, line, ref[pl.ds(line, 1), :] + spread))
        for ref, line, value in group:
            ref[pl.ds(line, 1), :] = value


def spot(sender, idx, per, stencil):
    return sender * per + idx + lax.shift_right_logical(idx, 7) * ((stencil - 1) * LANES)


def copy_parts(layout, source, target, place, chunk, chunks, group, sem):
    begin, size = place
    words = group * size * LANES
    at = begin * LANES + chunk * words
    return pltpu.make_async_copy(source.at[pl.ds(at, words)], target, sem)


def apply_kernel(
    *refs, first, layout, columns, height, hold, stencil, capacity, senders, parts, levels
):
    refs = list(refs)

    def take(count):
        taken = refs[:count]
        del refs[:count]
        return taken

    meta, ints, floats, own_lines, own = take(5)
    if not first:
        replies_h, replies = take(2)
    std_h, std_l_h, std_r_h, lat2_h, lon2_h = take(5)
    if not first:
        merged_h = take(1)[0]
    field_h, send = take(2)
    if first:
        info_out, merged_h = take(2)
    addr, wgt, start, lines_s, val = take(5)
    if first:
        std_flat, picked, chosen = take(3)
    scale, merged, sums, high_s, low_s, std, std_l, std_r, lat2, lon2, field = take(11)
    copies = take(PAIR)
    sems, in_sems, out_sems, val_sem = take(4)

    me = meta[0]
    wide = columns + 2 * HALO
    blocks = height // LANES
    group = min(GROUP, senders)
    chunks = senders // group
    slots = senders * capacity
    lane = iota((1, LANES), 1)
    per = stencil * hold
    table = layout.table

    def chunk_copies(chunk):
        todo = [
            (ints, addr, layout.ints["addr"]),
            (floats, wgt, layout.floats["wgt"]),
            (ints, start, layout.ints["start"]),
        ]
        if first:
            todo.append((floats, val, layout.floats["val"]))
        return [
            copy_parts(layout, source, target, place, chunk, chunks, group, sems.at[i])
            for i, (source, target, place) in enumerate(todo)
        ]

    def load_chunk(chunk):
        for copy in chunk_copies(chunk):
            copy.start()
        for copy in chunk_copies(chunk):
            copy.wait()

    operands = [
        pltpu.make_async_copy(source, target, in_sems.at[i])
        for i, (source, target) in enumerate(
            (
                (std_h, std),
                (std_l_h, std_l),
                (std_r_h, std_r),
                (lat2_h, lat2),
                (lon2_h, lon2),
            )
        )
    ]
    own_copy = pltpu.make_async_copy(own_lines, lines_s, in_sems.at[5])
    own_copy.start()
    merged_copy = pltpu.make_async_copy(
        *((merged, merged_h) if first else (merged_h, merged)), in_sems.at[6]
    )
    if not first:
        merged_copy.start()
    for copy in operands:
        copy.start()

    def value_copy(owner):
        at = pl.multiple_of(owner * (replies.shape[1] * LANES), 1024)
        return pltpu.make_async_copy(
            replies_h.at[pl.ds(at, slots)], val.at[pl.ds(owner * slots, slots)], val_sem.at[owner]
        )

    def each_owner(action):
        def step(owner, carry):
            action(value_copy(owner))
            return carry

        lax.fori_loop(0, parts, step, 0)

    if not first:
        each_owner(lambda copy: copy.start())
    zero_all(copies)
    zero_all([sums])

    lane_of = iota((slots, LANES), 1)
    room = slots + LANES
    column = 2 * stencil if first else 2 * stencil + 2
    scale[...] = jnp.broadcast_to(own[:, column : column + 1], (room, LANES))
    known = own[0:slots, :]
    own_copy.wait()
    if not first:
        merged_copy.wait()

    after = lax.rem(me + 1, parts)
    ahead = lax.rem(me + parts - 1, parts)

    def start_of(sender, owner, row, half):
        return start[sender * table + row * hold + half * LANES + owner]

    def entries_of(sender, idx, value):
        base = spot(sender, idx, per, stencil)
        return [
            (addr[base + k * LANES], wgt[base + k * LANES] * value) for k in range(stencil)
        ]

    def own_line(slot, k):
        return word_of(lines_s, slot, k, stencil)

    def amount_of(sender):
        return lines_s[(stencil + 3) * LANES + sender]

    halo_count = lines_s[(stencil + 4) * LANES]
    halo_fits = halo_count <= LANES

    def batches_of(one, two):
        return jnp.maximum(own_line(one, stencil), own_line(two, stencil))

    def own_groups(action, halo):
        if capacity % BLOCK:
            blocks_of(lines_s, 0, slots, stencil, action)
        else:

            def per_sender(sender, carry):
                blocks_of(lines_s, sender * capacity, amount_of(sender), stencil, action)
                return carry

            lax.fori_loop(0, senders, per_sender, 0)
        if halo:
            blocks_of(lines_s, slots, jnp.minimum(halo_count, LANES), stencil, action)

    def build(top, places):
        rows = weight_rows(own[pl.ds(top, BLOCK), :], places, stencil)
        for place, row in enumerate(rows):
            merged[pl.ds(place * room + top, BLOCK), :] = row

    if first:
        own_groups(build, True)
        merged_copy.start()

    def own_pairs(action):
        def per_sender(sender, carry):
            base = sender * capacity
            pairs(base, base + amount_of(sender), action)
            return carry

        lax.fori_loop(0, senders, per_sender, 0)

    def scatter_known(one, two, has_two):
        second = jnp.where(has_two, 1.0, 0.0)
        values = (scale[pl.ds(one, 1), :], scale[pl.ds(two, 1), :] * second)
        scatter_pair(lines_s, merged, room, copies, one, two, values, stencil)

    def scatter_sent(one, two, has_two):
        second = jnp.where(has_two, val[own_line(two, stencil + 2)], 0.0)
        values = (val[own_line(one, stencil + 2)], second)
        scatter_pair(lines_s, merged, room, copies, one, two, values, stencil)

    def scatter_halo(chunk):
        def per_sender(sender, carry):
            for owner, low, high in ((after, (1, 0), (1, 1)), (ahead, (2, 0), (0, 1))):
                begin = start_of(sender, owner, 0, 0)

                def value_of(idx, owner=owner, begin=begin):
                    if first:
                        return val[sender * hold + idx]
                    place = (chunk * group + sender) * capacity + idx - begin
                    return val[owner * slots + place]

                def action(one, two, has_two, value_of=value_of):
                    second = jnp.where(has_two, value_of(two), 0.0)
                    scatter_entries(
                        copies,
                        entries_of(sender, one, value_of(one)) + entries_of(sender, two, second),
                        lane,
                    )

                pairs(start_of(sender, owner, *low), start_of(sender, owner, *high), action)
            return carry

        lax.fori_loop(0, group, per_sender, 0)

    own_pairs(scatter_known)
    if not first:
        each_owner(lambda copy: copy.wait())

    @pl.when(halo_fits)
    def _():
        pairs(slots, slots + halo_count, scatter_known if first else scatter_sent)

    @pl.when(jnp.logical_not(halo_fits))
    def _():
        def step(chunk, carry):
            load_chunk(chunk)
            scatter_halo(chunk)
            return carry

        lax.fori_loop(0, chunks, step, 0)

    for copy in operands:
        copy.wait()

    for jb in range(blocks):
        lanes = slice(jb * LANES, (jb + 1) * LANES)
        for low, size, source in (
            (0, HALO, std_l),
            (HALO, columns, std),
            (HALO + columns, HALO, std_r),
        ):
            rows = slice(jb * wide + low, jb * wide + low + size)
            total = copies[0][rows, :]
            for ref in copies[1:]:
                total = total + ref[rows, :]
            high, lo = split2(total * source[:, lanes])
            high_s[low : low + size, lanes] = high
            low_s[low : low + size, lanes] = lo
        if first:
            std_flat[jb * wide + HALO : jb * wide + HALO + columns, :] = std[:, lanes]

    smoothed = copies[0]
    size = lon2.shape[1]
    count = height // WIDE
    outgoing = [merged_copy] if first else []
    for block in range(count):
        variant = 0 if block == 0 else (2 if block == count - 1 else 1)
        low = max(block * WIDE - LANES, 0)
        high = min(block * WIDE + WIDE + LANES, height)
        inner = slice(low - (block * WIDE - LANES), high - (block * WIDE - LANES))
        matrix = (lat2[0, variant, inner, :], lat2[1, variant, inner, :])
        along = mm_parts((high_s[:, low:high], low_s[:, low:high]), matrix)
        parts_y = split2(along)
        lanes = slice(block * WIDE, (block + 1) * WIDE)
        for begin in range(0, columns, size):
            some = min(size, columns - begin)
            rows = slice(begin, begin + some)
            window = slice(begin, begin + some + 2 * HALO)
            matrix = tuple(lon2[i, 0:some, 0 : some + 2 * HALO] for i in range(2))
            result = mm_parts(matrix, (parts_y[0][window, :], parts_y[1][window, :]))
            field[rows, lanes] = result
            scaled = result * std[rows, lanes]
            for half in range(WIDE // LANES):
                top = (block * (WIDE // LANES) + half) * wide + HALO + begin
                smoothed[top : top + some, :] = scaled[:, half * LANES : (half + 1) * LANES]
        outgoing.append(
            pltpu.make_async_copy(field.at[:, lanes], field_h.at[:, lanes], out_sems.at[block])
        )
        outgoing[-1].start()

    def gather_pair(one, two, has_two):
        def batch(begin, totals):
            result = []
            for slot, total in zip((one, two), totals):
                terms = []
                for j in range(BATCH):
                    line = own_line(slot, begin + j)
                    row = merged[pl.ds((begin + j) * room + slot, 1), :]
                    terms.append(row * smoothed[pl.ds(line, 1), :])
                    if first:
                        picked[pl.ds((begin + j) * room + slot, 1), :] = std_flat[
                            pl.ds(line, 1), :
                        ]
                result.append(total + ((terms[0] + terms[1]) + (terms[2] + terms[3])))
            return tuple(result)

        zero = jnp.zeros((1, LANES), F32)
        totals = lax.fori_loop(
            1,
            batches_of(one, two),
            lambda i, totals: batch(i * BATCH, totals),
            batch(0, (zero, zero)),
        )
        for slot, total in zip((one, two), totals):
            sums[pl.ds(slot, 1), :] = total

    own_pairs(gather_pair)

    def pick(top, places):
        info = own[pl.ds(top, BLOCK), :]
        codes = columns_of(info, CODES, stencil)
        lane_f = iota(info.shape, 1).astype(F32)
        rows = [picked[pl.ds(place * room + top, BLOCK), :] for place in range(places)]
        result = jnp.zeros((BLOCK, LANES), F32)
        for k in range(stencil):
            cell = jnp.zeros((BLOCK, LANES), F32)
            for place in range(min(k + 1, places)):
                at = lane_f + float(LANES * place)
                cell = jnp.where(at == codes[k], rows[place], cell)
            cell = jnp.sum(cell, axis=1, keepdims=True)
            result = jnp.where(lane_f == float(stencil + k), cell, result)
        chosen[pl.ds(top, BLOCK), :] = result * info

    if first:
        own_groups(pick, False)

    def whole(x):
        return jnp.sum(x, axis=0, keepdims=True)

    total = jnp.sum(sums[...], axis=1, keepdims=True)
    lines = slots // LANES
    known = own[0:slots, :]
    source, weight, reply, image0 = (
        known[:, 2 * stencil + i : 2 * stencil + i + 1] for i in range(4)
    )
    if first:
        reply = weight * total
        known = jnp.where(lane_of == 2 * stencil + 2, reply, known)
        known = jnp.where(lane_of == 2 * stencil + 3, total, known)
        info_out[0:slots, :] = known
        info_out[slots:room, :] = own[slots:room, :]
        turned = known.T[2 * stencil + 2 : 2 * stencil + 3, :]
        message = [turned[:, i * LANES : (i + 1) * LANES] for i in range(lines)]
        message.append(
            jnp.where(
                lane == 0, whole(source * total), jnp.where(lane == 1, whole(reply * total), 0.0)
            )
        )
        message.append(jnp.zeros((8 - len(message), LANES), F32))
        factors = chosen[...].T
        for k in range(stencil):
            row = factors[stencil + k : stencil + k + 1, :]
            message += [row[:, i * LANES : (i + 1) * LANES] for i in range(lines)]
        message = jnp.concatenate(message, axis=0)
    else:
        slab = jnp.sum(replies[:, 0:8, :], axis=0)[lines : lines + 1, :]
        length = slab[:, 0:1] / (slab[:, 0:1] + slab[:, 1:2])
        both = source + reply
        s_both = image0 + total
        resid = source - length * both
        s_resid = image0 - length * s_both
        values = [
            resid * s_resid,
            resid * s_both,
            both * s_both,
            resid * image0,
            both * image0,
            weight * s_resid * s_resid,
            weight * s_resid * s_both,
            weight * s_both * s_both,
            weight * s_resid * image0,
            weight * s_both * image0,
            source * image0,
            reply * image0,
        ]
        message = jnp.where(lane == len(values), length, 0.0)
        for i, value in enumerate(values):
            message = jnp.where(lane == i, whole(value), message)
        message = jnp.concatenate([message, jnp.zeros((7, LANES), F32)], axis=0)

    def send_to(i, carry):
        send[i] = message
        return carry

    lax.fori_loop(0, send.shape[0], send_to, 0)
    for copy in outgoing:
        copy.wait()


def final_kernel(
    ints,
    floats,
    replies_h,
    lines_h,
    merged_h,
    mixed,
    totals,
    std_h,
    field0_h,
    field1_h,
    lat1,
    lon1,
    control_h,
    increment_h,
    addr,
    listed,
    slot,
    val,
    factors,
    std,
    field0,
    field1,
    control,
    high_s,
    low_s,
    lines_s,
    merged,
    scale,
    *rest,
    layout,
    hold,
    stencil,
    capacity,
    senders,
    parts,
    length,
):
    copies = rest[:PAIR]
    sems, in_sems, out_sems = rest[PAIR:]
    group = min(GROUP, senders)
    chunks = senders // group
    per = stencil * hold
    rows_block = control.shape[0]
    high_rows = rows_block + 2 * PAD
    lane = iota((1, LANES), 1)
    stride = group * capacity
    owner_words = factors.shape[0] // parts
    to_factors = owner_words - stencil * stride

    def chunk_copies(chunk):
        todo = [
            (ints, addr, layout.ints["rows"]),
            (ints, listed, layout.ints["listed"]),
            (ints, slot, layout.ints["slot"]),
            (floats, val, layout.floats["val"]),
        ]
        result = [
            copy_parts(layout, source, target, place, chunk, chunks, group, sems.at[i])
            for i, (source, target, place) in enumerate(todo)
        ]
        words = parts * owner_words
        result.append(
            pltpu.make_async_copy(
                replies_h.at[pl.ds(chunk * words, words)], factors, sems.at[len(todo)]
            )
        )
        return result

    listing = [
        pltpu.make_async_copy(lines_h, lines_s, in_sems.at[3]),
        pltpu.make_async_copy(merged_h, merged, in_sems.at[4]),
    ]
    for copy in listing:
        copy.start()
    operands = [
        pltpu.make_async_copy(source, target, in_sems.at[i])
        for i, (source, target) in enumerate(
            ((std_h, std), (field0_h, field0), (field1_h, field1))
        )
    ]
    for copy in operands:
        copy.start()

    slabs = totals.shape[1]
    every = jnp.sum(totals[...], axis=0)
    norm0 = quad0 = None
    for i in range(slabs):
        line = every[i, 0:1, :]
        a, b = line[:, 10:11], line[:, 11:12]
        norm0 = a if norm0 is None else norm0 + a
        quad0 = b if quad0 is None else quad0 + b
    step0 = norm0 / (norm0 + quad0)
    norm1 = cross = quad1 = quad01 = jnp.zeros((1, 1), F32)
    for i in range(slabs):
        line = every[i, 0:1, :]
        v = [line[:, j : j + 1] for j in range(10)]
        shift = totals[0, i, 0:1, 12:13] - step0
        norm1 = norm1 + (v[0] + shift * (2.0 * v[1] + shift * v[2]))
        cross = cross + (v[3] + shift * v[4])
        quad1 = quad1 + (v[5] + shift * (2.0 * v[6] + shift * v[7]))
        quad01 = quad01 + (v[8] + shift * v[9])
    ratio = norm1 / norm0
    curvature = norm1 + quad1 + ratio * (
        2.0 * (cross + quad01) + ratio * (norm0 + quad0)
    )
    step1 = norm1 / curvature
    first = step0 + step1 * (1.0 - step0 + ratio)
    second = -step0 * step1
    first_line = jnp.broadcast_to(first, (1, LANES))
    second_line = jnp.broadcast_to(second, (1, LANES))

    zero_all(copies)

    data = mixed[...]
    column = 2 * stencil
    scale[...] = first * data[:, column : column + 1] + second * jnp.broadcast_to(
        data[:, column + 1 : column + 2], data.shape
    )
    for copy in listing:
        copy.wait()
    count = lines_s[(stencil + 3) * LANES]

    def add(one, two, has_two):
        rest = jnp.where(has_two, 1.0, 0.0)
        values = (scale[pl.ds(one, 1), :], scale[pl.ds(two, 1), :] * rest)
        scatter_pair(lines_s, merged, LISTED, copies, one, two, values, stencil)

    def scatter_chunk():
        def per_sender(sender, carry):
            def step(idx, inner):
                @pl.when(listed[sender * hold + idx] > 0)
                def _():
                    place = slot[sender * hold + idx]
                    place = place + lax.div(place, stride) * (owner_words - stride)
                    base = spot(sender, idx, per, stencil)
                    z0 = val[sender * hold + idx]
                    value = first_line * z0 + second_line * factors[place]
                    entries = [
                        (addr[base + k * LANES], factors[place + to_factors + k * stride] * value)
                        for k in range(stencil)
                    ]
                    scatter_entries(copies, entries, lane)

                return inner

            lax.fori_loop(0, hold, step, 0)
            return carry

        lax.fori_loop(0, group, per_sender, 0)

    @pl.when(count <= LISTED)
    def _():
        pairs(0, count, add)

    @pl.when(count > LISTED)
    def _():
        def step(chunk, carry):
            for copy in chunk_copies(chunk):
                copy.start()
            for copy in chunk_copies(chunk):
                copy.wait()
            scatter_chunk()
            return carry

        lax.fori_loop(0, chunks, step, 0)

    for copy in operands:
        copy.wait()
    increment = field0
    increment[...] = std[...] * (first * field0[...] + second * field1[...])
    outgoing = [pltpu.make_async_copy(increment, increment_h, out_sems.at[0])]
    outgoing[0].start()

    pair = WIDE // LANES
    count = length // WIDE
    for block in range(count):
        pieces = []
        for half in range(pair):
            rows = slice((block * pair + half) * high_rows, (block * pair + half + 1) * high_rows)
            total = copies[0][rows, :]
            for ref in copies[1:]:
                total = total + ref[rows, :]
            pieces.append(total)
        whole = split2(jnp.concatenate(pieces, axis=1))
        size = lat1.shape[1]
        for top in range(0, rows_block, size):
            window = slice(top, top + size + 2 * PAD)
            along = mm_parts((lat1[0], lat1[1]), (whole[0][window, :], whole[1][window, :]))
            high, low = split2(along)
            high_s[top : top + size, block * WIDE : (block + 1) * WIDE] = high
            low_s[top : top + size, block * WIDE : (block + 1) * WIDE] = low

    def window(ref, block):
        low, high = block * WIDE - LANES, (block + 1) * WIDE + LANES
        if low < 0:
            return jnp.concatenate([ref[:, length + low : length], ref[:, 0:high]], axis=1)
        if high > length:
            return jnp.concatenate([ref[:, low:length], ref[:, 0 : high - length]], axis=1)
        return ref[:, low:high]

    every_lanes = 4
    for block in range(count):
        control[:, block * WIDE : (block + 1) * WIDE] = mm_parts(
            (window(high_s, block), window(low_s, block)), (lon1[0], lon1[1])
        )
        if block % every_lanes == every_lanes - 1:
            lanes = slice((block + 1 - every_lanes) * WIDE, (block + 1) * WIDE)
            outgoing.append(
                pltpu.make_async_copy(
                    control.at[:, lanes], control_h.at[:, lanes], out_sems.at[len(outgoing)]
                )
            )
            outgoing[-1].start()
    for copy in outgoing:
        copy.wait()


def body(
    background_std,
    x_kernel,
    y_kernel,
    obs_owner,
    obs_cells,
    obs_weights,
    innovation,
    obs_precision,
    obs_counts,
):
    parts = lax.axis_size("pencil")
    levels = lax.axis_size("lev")
    me = lax.axis_index("pencil")
    _, columns, height = background_std.shape
    hold, stencil = obs_cells.shape
    margin = x_kernel.shape[1] // 2
    capacity = 2 * hold // parts
    senders = parts
    slots = senders * capacity
    room = slots + LANES
    rows_block = height // parts
    length = columns * parts
    blocks = height // LANES
    wide = columns + 2 * HALO
    group = min(GROUP, senders)
    chunks = senders // group
    layout = Layout(senders, hold, stencil, parts)
    std = background_std[0]

    packed = pl.pallas_call(
        functools.partial(
            pack_kernel, parts=parts, columns=columns, height=height, margin=margin
        ),
        out_shape=jax.ShapeDtypeStruct((parts, PACK, hold), F32),
        in_specs=[smem()] + [vmem()] * 5,
        out_specs=vmem(),
        scratch_shapes=[pltpu.VMEM((parts, hold), F32)],
        compiler_params=params(),
        cost_estimate=cost(12000),
        name="pack",
    )(
        obs_counts,
        obs_owner.T,
        obs_cells.T,
        obs_weights.T,
        innovation[None, :],
        obs_precision[None, :],
    )
    recv = lax.all_to_all(packed, "pencil", split_axis=0, concat_axis=0, tiled=True)

    right = [(p, (p + 1) % parts) for p in range(parts)]
    left = [(p, (p - 1) % parts) for p in range(parts)]
    std_l = lax.ppermute(std[columns - HALO :, :], "pencil", right)
    std_r = lax.ppermute(std[:HALO, :], "pencil", left)

    size = min(columns, WIDE - 2 * HALO)
    row_size = min(rows_block, LANES)
    lat2, lon2, lat1, lon1 = pl.pallas_call(
        functools.partial(bands_kernel, rows_block=row_size),
        out_shape=[
            jax.ShapeDtypeStruct((2, 3, 2 * WIDE, WIDE), BF),
            jax.ShapeDtypeStruct((2, size, size + 2 * HALO), BF),
            jax.ShapeDtypeStruct((2, row_size, row_size + 2 * PAD), BF),
            jax.ShapeDtypeStruct((2, 2 * WIDE, WIDE), BF),
        ],
        in_specs=[smem(), smem()],
        out_specs=[vmem()] * 4,
        compiler_params=params(),
        cost_estimate=cost(6000),
        name="bands",
    )(x_kernel[0], y_kernel[0])

    meta = jnp.reshape(me, (1,)).astype(I32)
    place = dict(
        parts=parts, columns=columns, height=height, capacity=capacity, stencil=stencil
    )
    ints, floats, own_lines, own = pl.pallas_call(
        functools.partial(unpack_kernel, layout=layout, group=group, **place),
        out_shape=[
            jax.ShapeDtypeStruct((layout.int_rows, LANES), I32),
            jax.ShapeDtypeStruct((layout.float_rows, LANES), F32),
            jax.ShapeDtypeStruct((room // LANES * (stencil + 8), LANES), I32),
            jax.ShapeDtypeStruct((room, LANES), F32),
        ],
        in_specs=[smem(), vmem()],
        out_specs=[vmem()] * 4,
        scratch_shapes=[
            pltpu.VMEM((room // LANES, STACK, LANES), F32),
        ],
        compiler_params=params(),
        cost_estimate=cost(100),
        name="unpack",
    )(meta, recv)
    ints = ints.reshape(-1)
    floats = floats.reshape(-1)
    own_lines = own_lines.reshape(-1)

    acc = pltpu.VMEM((blocks * wide + 8, LANES), F32)
    column_slots = pltpu.VMEM((slots, LANES), F32)
    static = dict(
        layout=layout,
        columns=columns,
        height=height,
        hold=hold,
        stencil=stencil,
        capacity=capacity,
        senders=senders,
        parts=parts,
        levels=levels,
    )
    per = group * stencil * hold
    line = group * hold
    index_scratch = [
        pltpu.SMEM((per,), I32),
        pltpu.SMEM((per,), F32),
        pltpu.SMEM((group * layout.table,), I32),
        pltpu.SMEM((room * (stencil + 8),), I32),
    ]
    work = (
        [
            pltpu.VMEM((room, LANES), F32),
            pltpu.VMEM((stencil * room, LANES), F32),
            column_slots,
        ]
        + [pltpu.VMEM((wide, height), BF)] * 2
        + [
            pltpu.VMEM((columns, height), F32),
            pltpu.VMEM((HALO, height), F32),
            pltpu.VMEM((HALO, height), F32),
            pltpu.VMEM(lat2.shape, BF),
            pltpu.VMEM(lon2.shape, BF),
            pltpu.VMEM((columns, height), F32),
        ]
        + [acc] * PAIR
        + [
            pltpu.SemaphoreType.DMA((4,)),
            pltpu.SemaphoreType.DMA((7,)),
            pltpu.SemaphoreType.DMA((height // WIDE,)),
            pltpu.SemaphoreType.DMA((parts,)),
        ]
    )
    field_shape = jax.ShapeDtypeStruct((columns, height), F32)
    reply_rows = 8 + stencil * slots // LANES
    field0, message, info, merged = pl.pallas_call(
        functools.partial(apply_kernel, first=True, **static),
        out_shape=[
            field_shape,
            jax.ShapeDtypeStruct((parts, reply_rows, LANES), F32),
            jax.ShapeDtypeStruct((room, LANES), F32),
            jax.ShapeDtypeStruct((stencil * room, LANES), F32),
        ],
        in_specs=[smem()] + [hbm()] * 3 + [vmem()] + [hbm()] * 5,
        out_specs=[hbm()] + [vmem()] * 2 + [hbm()],
        scratch_shapes=index_scratch
        + [
            pltpu.SMEM((line,), F32),
            acc,
            pltpu.VMEM((stencil * room, LANES), F32),
            column_slots,
        ]
        + work,
        compiler_params=params(),
        name="apply_first",
    )(meta, ints, floats, own_lines, own, std, std_l, std_r, lat2, lon2)

    replies = lax.all_to_all(message, "pencil", split_axis=0, concat_axis=0, tiled=True)
    back = replies.reshape(-1)
    line_rows = LISTED // LANES * (stencil + 8)
    row_lines, row_data = pl.pallas_call(
        functools.partial(list_kernel, **place),
        out_shape=[
            jax.ShapeDtypeStruct((line_rows, LANES), I32),
            jax.ShapeDtypeStruct((LISTED, LANES), F32),
        ],
        in_specs=[smem(), vmem(), hbm()],
        out_specs=[vmem()] * 2,
        scratch_shapes=[pltpu.VMEM((STACK, LISTED), F32)],
        compiler_params=params(),
        cost_estimate=cost(4000),
        name="list_rows",
    )(meta, recv, info)
    row_lines = row_lines.reshape(-1)

    field1, sums = pl.pallas_call(
        functools.partial(apply_kernel, first=False, **static),
        out_shape=[
            field_shape,
            jax.ShapeDtypeStruct((parts * levels, 8, LANES), F32),
        ],
        in_specs=[smem()] + [hbm()] * 3 + [vmem(), hbm(), vmem()] + [hbm()] * 6,
        out_specs=[hbm(), vmem()],
        scratch_shapes=index_scratch + [pltpu.SMEM((parts * slots,), F32)] + work,
        compiler_params=params(),
        name="apply_second",
    )(
        meta,
        ints,
        floats,
        own_lines,
        info,
        back,
        replies,
        std,
        std_l,
        std_r,
        lat2,
        lon2,
        merged,
    )

    totals = lax.all_to_all(sums, ("pencil", "lev"), split_axis=0, concat_axis=0, tiled=True)
    totals = totals.reshape(parts, levels, 8, LANES)

    listed_rows, mixed = pl.pallas_call(
        functools.partial(factor_kernel, stencil=stencil, slots=slots),
        out_shape=[
            jax.ShapeDtypeStruct((stencil * LISTED, LANES), F32),
            jax.ShapeDtypeStruct((LISTED, LANES), F32),
        ],
        in_specs=[hbm(), vmem(), vmem(), hbm()],
        out_specs=[hbm(), vmem()],
        scratch_shapes=[
            pltpu.SMEM((line_rows * LANES,), I32),
            pltpu.VMEM((parts * slots, LANES), F32),
            pltpu.VMEM((stencil * LISTED, LANES), F32),
            pltpu.SemaphoreType.DMA((2,)),
        ],
        compiler_params=params(),
        cost_estimate=cost(8000),
        name="factor_rows",
    )(row_lines, row_data, replies, sums)

    by_chunk = back
    if chunks > 1:
        by_chunk = jnp.concatenate(
            [replies[:, : slots // LANES, :], replies[:, 8:, :]], axis=1
        ).reshape(parts, stencil + 1, chunks, group * capacity)
        by_chunk = jnp.transpose(by_chunk, (2, 0, 1, 3)).reshape(-1)
    owner_words = by_chunk.shape[0] // (chunks * parts)
    high_rows = rows_block + 2 * PAD
    acc_rows = pltpu.VMEM(((length // LANES) * high_rows + 8, LANES), F32)
    control, increment = pl.pallas_call(
        functools.partial(
            final_kernel,
            layout=layout,
            hold=hold,
            stencil=stencil,
            capacity=capacity,
            senders=senders,
            parts=parts,
            length=length,
        ),
        out_shape=[
            jax.ShapeDtypeStruct((rows_block, length), F32),
            field_shape,
        ],
        in_specs=[hbm()] * 5 + [vmem()] * 2 + [hbm()] * 3 + [vmem()] * 2,
        out_specs=[hbm()] * 2,
        scratch_shapes=[
            pltpu.SMEM((per,), I32),
            pltpu.SMEM((line,), I32),
            pltpu.SMEM((line,), I32),
            pltpu.SMEM((line,), F32),
            pltpu.SMEM((parts * owner_words,), F32),
            pltpu.VMEM((columns, height), F32),
            pltpu.VMEM((columns, height), F32),
            pltpu.VMEM((columns, height), F32),
            pltpu.VMEM((rows_block, length), F32),
            pltpu.VMEM((rows_block, length), BF),
            pltpu.VMEM((rows_block, length), BF),
            pltpu.SMEM((line_rows * LANES,), I32),
            pltpu.VMEM((stencil * LISTED, LANES), F32),
            pltpu.VMEM((LISTED, LANES), F32),
        ]
        + [acc_rows] * PAIR
        + [
            pltpu.SemaphoreType.DMA((5,)),
            pltpu.SemaphoreType.DMA((5,)),
            pltpu.SemaphoreType.DMA((1 + length // WIDE,)),
        ],
        compiler_params=params(),
        name="outputs",
    )(
        ints,
        floats,
        by_chunk,
        row_lines,
        listed_rows,
        mixed,
        totals,
        std,
        field0,
        field1,
        lat1,
        lon1,
    )
    return control[None], increment[None]


def solution(mesh):
    return jax.shard_map(
        body,
        mesh=mesh,
        in_specs=(
            P("lev", "pencil", None),
            P("lev", None),
            P("lev", None),
            P(("pencil", "lev"), None),
            P(("pencil", "lev"), None),
            P(("pencil", "lev"), None),
            P(("pencil", "lev")),
            P(("pencil", "lev")),
            P(("pencil", "lev")),
        ),
        out_specs=(P("lev", "pencil", None), P("lev", "pencil", None)),
        check_vma=False,
    )
```

```python
import functools

import jax
import jax.numpy as jnp
import numpy as np
from jax import lax
from jax.experimental import pallas as pl
from jax.experimental.pallas import tpu as pltpu
from jax.sharding import PartitionSpec as P


BF = jnp.bfloat16
F32 = jnp.float32
I32 = jnp.int32
LANES = 128
WIDE = 256
HALO = 32
PAD = 16
PACK = 40
GROUP = 8
PAIR = 2
BATCH = 4
BLOCK = 32
CODES = 40
STACK = 64
LISTED = 512
VMEM_LIMIT = 58 * 1024 * 1024


def vmem():
    return pl.BlockSpec(memory_space=pltpu.VMEM)


def smem():
    return pl.BlockSpec(memory_space=pltpu.SMEM)


def hbm():
    return pl.BlockSpec(memory_space=pl.ANY)


def cost(nanoseconds):
    return pl.CostEstimate(flops=0, bytes_accessed=3690 * nanoseconds, transcendentals=0)


def params():
    return pltpu.CompilerParams(vmem_limit_bytes=VMEM_LIMIT)


def split2(x):
    high = x.astype(BF)
    return high, (x - high.astype(F32)).astype(BF)


def split3(x):
    high = x.astype(BF)
    rest = x - high.astype(F32)
    mid = rest.astype(BF)
    return high, mid, (rest - mid.astype(F32)).astype(BF)


def mm(a, b):
    return jnp.dot(a, b, preferred_element_type=F32)


def mm_parts(a_parts, b_parts):
    (ah, al), (bh, bl) = a_parts, b_parts
    return mm(jnp.concatenate([ah, al, ah], axis=1), jnp.concatenate([bh, bh, bl], axis=0))


def iota(shape, dim):
    return lax.broadcasted_iota(I32, shape, dim)


def pack_kernel(
    counts, owner, cells, weights, depart, prec, out, marks, *, parts, columns, height, margin
):
    stencil, hold = cells.shape
    shift = height.bit_length() - 1
    block = height // parts
    reach = 2 * margin
    row_id = iota((hold, hold), 0)
    col_id = iota((hold, hold), 1)
    eye = row_id == col_id
    col_f = col_id.astype(F32)
    live = iota((1, hold), 1) < counts[0]
    cell = cells[...]
    column = lax.shift_right_logical(cell, jnp.full(cell.shape, shift, I32))
    row = cell & (height - 1)

    def any_of(mask):
        return jnp.max(jnp.where(mask, 1.0, 0.0), axis=0, keepdims=True)

    def turn(line):
        return jnp.sum(jnp.where(eye, line, 0.0), axis=1, keepdims=True)

    left = any_of(column < reach)
    right = any_of(column >= columns - reach)
    side = left + 3.0 * right - 2.0 * left * right
    base = jnp.where(live, owner[...].astype(F32) * 4.0, 4.0 * parts)
    key = jnp.where(live, base + side, base)
    key_col = turn(key)
    before = (key_col < key) | ((key_col == key) & (row_id < col_id))
    rank = jnp.sum(jnp.where(before, 1.0, 0.0), axis=0, keepdims=True)
    begin = jnp.sum(jnp.where(key_col < base, 1.0, 0.0), axis=0, keepdims=True)
    rank_col = turn(rank)
    perm = jnp.where(rank_col == col_f, 1.0, 0.0).astype(BF)

    def sort(values):
        total = None
        for part in split3(values):
            term = mm(part, perm)
            total = term if total is None else total + term
        return total

    weight = jnp.where(live, prec[...], 0.0)
    rest = [weight * depart[...], weight, key, rank - begin, jnp.zeros((4, hold), F32)]
    values = [cell.astype(F32), weights[...]] + rest
    ordered = sort(jnp.concatenate(values, axis=0))
    line = iota((8, hold), 0)
    tail = ordered[2 * stencil : 2 * stencil + 8, :]
    first_half = col_f < float(LANES)
    fourfold = 4.0 * jnp.where(first_half, col_f, col_f - float(LANES))
    for i, (low, high) in enumerate(((0.0, 4.0), (1.0, 3.0), (2.0, 2.0))):
        bound = fourfold + jnp.where(first_half, low, high)
        begins = jnp.sum(jnp.where(key_col < bound, 1.0, 0.0), axis=0, keepdims=True)
        tail = jnp.where(line == 5 + i, begins, tail)
    last = (line == 7) & (iota((8, hold), 1) == hold - 1)

    def mark(part, carry):
        low = part * block - margin
        high = (part + 1) * block + margin
        flag = jnp.where(live, any_of((row >= low) & (row < high)), 0.0)
        place = jnp.sum(jnp.where(row_id < col_id, turn(flag), 0.0), axis=0, keepdims=True)
        marks[pl.ds(part, 1), :] = flag * (place + 1.0)
        return carry

    lax.fori_loop(0, parts, mark, 0, unroll=parts <= GROUP)
    listed = marks[...]
    amounts = jnp.max(listed, axis=1, keepdims=True)
    listed = mm(listed.astype(BF), perm)
    for part in range(parts):
        out[part, 0 : 2 * stencil, :] = ordered[0 : 2 * stencil, :]
        out[part, 2 * stencil : 2 * stencil + 8, :] = jnp.where(
            line == 4,
            listed[part : part + 1, :],
            jnp.where(last, amounts[part : part + 1, :], tail),
        )


class Layout:
    def __init__(self, senders, hold, stencil, parts):
        lines = hold // LANES
        self.table = 3 * hold
        sizes = dict(
            addr=stencil * lines, rows=stencil * lines, listed=lines, slot=lines, start=3 * lines
        )
        self.ints = {}
        at = 0
        for name, size in sizes.items():
            self.ints[name] = (at, size)
            at += senders * size
        self.int_rows = at
        self.floats = {}
        at = 0
        for name, size in dict(wgt=stencil * lines, val=lines).items():
            self.floats[name] = (at, size)
            at += senders * size
        self.float_rows = at


def right(x, by):
    return lax.shift_right_logical(x, jnp.full(x.shape, by, I32))


def nt(a, b):
    return lax.dot_general(a, b, (((1,), (1,)), ((), ())), preferred_element_type=F32)


class Received:
    def __init__(self, recv, sender, me, *, parts, columns, height, capacity, stencil):
        senders, _, hold = recv.shape
        wide = columns + 2 * HALO
        block = height // parts
        high_rows = block + 2 * PAD
        cell = recv[sender, 0:stencil, :].astype(I32)
        self.tail = recv[sender, 2 * stencil : 2 * stencil + 8, :]
        self.whole = self.tail.astype(I32)
        self.pos = self.whole[3:4, :]
        owner = right(self.whole[2:3, :], 2)
        offset = owner - me
        offset = jnp.where(offset > parts // 2, offset - parts, offset)
        offset = jnp.where(offset < -(parts // 2), offset + parts, offset)
        column = right(cell, height.bit_length() - 1)
        row = cell & (height - 1)
        at = offset * columns + column + HALO
        self.addr = jnp.where(
            (at >= 0) & (at < wide),
            (right(row, 7) * wide + at) * LANES + (row & (LANES - 1)),
            (height // LANES) * wide * LANES,
        )
        at_row = row - (block * me - PAD)
        across = owner * columns + column
        self.rows = jnp.where(
            (at_row >= 0) & (at_row < high_rows) & (owner < parts),
            (right(across, 7) * high_rows + at_row) * LANES + (across & (LANES - 1)),
            (columns * parts // LANES) * high_rows * LANES,
        )
        self.owner = jnp.minimum(owner, parts - 1)
        self.back = self.owner * (senders * capacity) + sender * capacity + self.pos


def stack_of(addr, weights, tail, back):
    hold = addr.shape[1]
    rows = [
        (addr & (LANES - 1)).astype(F32),
        weights,
        tail,
        right(addr, 7).astype(F32),
        back.astype(F32),
        jnp.zeros((7, hold), F32),
    ]
    return jnp.concatenate(split3(jnp.concatenate(rows, axis=0)), axis=1)


def gathered(stack, chosen):
    select = jnp.where(chosen, 1.0, 0.0).astype(BF)
    return nt(stack, jnp.concatenate([select] * 3, axis=1))


def merge_lines(block, nowhere, stencil, extra):
    number = iota((stencil, LANES), 0).astype(F32)
    line = block[CODES : CODES + stencil, :]
    leader = jnp.zeros(line.shape, F32)
    for k in reversed(range(stencil)):
        leader = jnp.where(line == line[k : k + 1, :], float(k), leader)
    leads = jnp.where(leader == number, 1.0, 0.0)
    count = jnp.zeros((1, LANES), F32)
    ranks = []
    for k in range(stencil):
        ranks.append(count)
        count = count + leads[k : k + 1, :]
    place = jnp.zeros(line.shape, F32)
    for k in range(stencil):
        place = jnp.where(leader == float(k), ranks[k], place)
    lists = []
    for k in range(stencil):
        found = jnp.where((leads > 0.0) & (place == float(k)), line, 0.0)
        found = jnp.sum(found, axis=0, keepdims=True)
        lists.append(jnp.where(count > float(k), found, nowhere))
    batches = right(count.astype(I32) + (BATCH - 1), BATCH.bit_length() - 1)
    most = jnp.zeros((1, LANES), F32)
    slot = iota((1, LANES), 1)
    for begin in range(0, LANES, BLOCK):
        here = (slot >= begin) & (slot < begin + BLOCK)
        found = jnp.max(jnp.where(here, batches.astype(F32), 0.0), axis=1, keepdims=True)
        most = jnp.where(here, found, most)
    back = block[CODES + stencil : CODES + stencil + 1, :]
    ints = [jnp.concatenate(lists, axis=0).astype(I32), batches]
    ints += [most.astype(I32), back.astype(I32)] + extra
    ints = jnp.concatenate(ints, axis=0)
    ints = jnp.concatenate([ints, jnp.zeros((stencil + 8 - ints.shape[0], LANES), I32)], axis=0)
    rows = [
        block[0:CODES, :],
        place * float(LANES) + block[0:stencil, :],
        jnp.zeros((LANES - CODES - stencil, LANES), F32),
    ]
    return ints, jnp.concatenate(rows, axis=0).T


def unpack_kernel(
    meta, recv, ints, floats, own_lines, own, total, *, layout, group, **sizes
):
    senders, _, hold = recv.shape
    lines = hold // LANES
    me = meta[0]
    parts, stencil, capacity = sizes["parts"], sizes["stencil"], sizes["capacity"]
    wide = sizes["columns"] + 2 * HALO
    slots = senders * capacity

    def put(ref, place, sender, value):
        begin, size = place
        count = value.shape[0]
        for i in range(lines):
            part = value[:, i * LANES : (i + 1) * LANES]
            if count % 8 == 0:
                at = pl.multiple_of(begin + sender * size + i * count, 8)
                ref[pl.ds(at, count), :] = part
            else:
                for j in range(count):
                    ref[pl.ds(begin + sender * size + i + j * lines, 1), :] = part[j : j + 1]

    total[...] = jnp.zeros(total.shape, F32)
    place = iota((LANES, hold), 0)
    index = iota((LANES, hold), 1)
    lane = iota((1, LANES), 1)
    halo_block = slots // LANES
    after = lax.rem(me + 1, parts)
    ahead = lax.rem(me + parts - 1, parts)

    def per_sender(sender, carry):
        halo_before, amounts = carry
        got = Received(recv, sender, me, **sizes)
        weights = recv[sender, stencil : 2 * stencil, :]
        within = lax.rem(sender, group) * capacity + got.pos
        put(ints, layout.ints["addr"], sender, got.addr)
        put(ints, layout.ints["rows"], sender, got.rows)
        put(ints, layout.ints["listed"], sender, got.whole[4:5, :])
        put(ints, layout.ints["slot"], sender, got.owner * (group * capacity) + within)
        put(ints, layout.ints["start"], sender, got.whole[5:8, :])
        put(floats, layout.floats["wgt"], sender, weights)
        put(floats, layout.floats["val"], sender, got.tail[0:1, :])

        def bound(line, half, owner):
            part = got.whole[5 + line : 6 + line, half * LANES : (half + 1) * LANES]
            return jnp.sum(jnp.where(lane == owner, part, 0), axis=1, keepdims=True)

        stack = stack_of(got.addr, weights, got.tail, got.back)

        begin, end = bound(0, 0, me), bound(0, 1, me)
        first_slot = sender * capacity
        block_of = first_slot // LANES
        within = place - (first_slot - block_of * LANES)
        chosen = (within >= 0) & (index == begin + within) & (index < end)
        shift = first_slot - block_of * LANES
        here = (lane >= shift) & (lane < shift + (end - begin))
        total[block_of] = jnp.where(here, gathered(stack, chosen), total[block_of])
        amounts = jnp.where(lane == sender, end - begin, amounts)

        first_r, last_r = bound(1, 0, after), bound(1, 1, after)
        first_l, last_l = bound(2, 0, ahead), bound(0, 1, ahead)
        middle = halo_before + (last_r - first_r)
        chosen_r = (index >= first_r) & (index < last_r) & (index - first_r + halo_before == place)
        chosen_l = (index >= first_l) & (index < last_l) & (index - first_l + middle == place)
        halo_after = middle + (last_l - first_l)
        here = (lane >= halo_before) & (lane < halo_after)
        values = gathered(stack, chosen_r | chosen_l)
        total[halo_block] = jnp.where(here, values, total[halo_block])
        return halo_after, amounts

    halo_count, amounts = lax.fori_loop(
        0,
        senders,
        per_sender,
        (jnp.zeros((1, 1), I32), jnp.zeros((1, LANES), I32)),
        unroll=senders <= GROUP,
    )
    extra = [amounts, jnp.broadcast_to(halo_count, (1, LANES))]
    nowhere = float((sizes["height"] // LANES) * wide)
    for i in range(slots // LANES + 1):
        top = i * (stencil + 8)
        own_lines[top : top + stencil + 8, :], own[i * LANES : (i + 1) * LANES, :] = merge_lines(
            total[i], nowhere, stencil, extra
        )


def edges_kernel(std, _, __, low, high, sems):
    columns = std.shape[0]
    copies = [
        pltpu.make_async_copy(std.at[pl.ds(0, HALO), :], low, sems.at[0]),
        pltpu.make_async_copy(std.at[pl.ds(columns - HALO, HALO), :], high, sems.at[1]),
    ]
    for copy in copies:
        copy.start()
    for copy in copies:
        copy.wait()


def list_kernel(meta, recv, _, row_lines, row_data, total, **sizes):
    senders, _, hold = recv.shape
    stencil = sizes["stencil"]
    high_rows = sizes["height"] // sizes["parts"] + 2 * PAD
    place = iota((LISTED, hold), 0)
    total[...] = jnp.zeros(total.shape, F32)

    def per_sender(sender, before):
        got = Received(recv, sender, meta[0], **sizes)
        marks = got.whole[4:5, :]
        zeros = jnp.zeros((stencil, hold), F32)
        tail = jnp.concatenate([got.tail[0:1, :], zeros[0:7, :]], axis=0)
        stack = stack_of(got.rows, zeros, tail, got.back)
        values = gathered(stack, (marks > 0) & (marks - 1 + before == place))
        after = before + got.whole[7:8, hold - 1 : hold]
        slot = iota((1, LISTED), 1)
        total[...] = jnp.where((slot >= before) & (slot < after), values, total[...])
        return after

    count = lax.fori_loop(
        0, senders, per_sender, jnp.zeros((1, 1), I32), unroll=senders <= GROUP
    )
    nowhere = float((sizes["columns"] * sizes["parts"] // LANES) * high_rows)
    for i in range(LISTED // LANES):
        top = i * (stencil + 8)
        block = total[:, i * LANES : (i + 1) * LANES]
        (
            row_lines[top : top + stencil + 8, :],
            row_data[i * LANES : (i + 1) * LANES, :],
        ) = merge_lines(block, nowhere, stencil, [jnp.broadcast_to(count, (1, LANES))])


def word_of(table, slot, k, stencil):
    at = lax.shift_right_logical(slot, 7) * ((stencil + 7) * LANES) + slot
    return table[at + k * LANES]


def columns_of(info, begin, stencil):
    return [jnp.broadcast_to(info[:, begin + k : begin + k + 1], info.shape) for k in range(stencil)]


def weight_rows(info, places, stencil):
    lane_f = iota(info.shape, 1).astype(F32)
    codes = columns_of(info, CODES, stencil)
    weights = columns_of(info, stencil, stencil)
    rows = []
    for place in range(stencil):
        row = jnp.zeros(info.shape, F32)
        if place < places:
            at = lane_f + float(LANES * place)
            for k in range(place, stencil):
                row = row + jnp.where(at == codes[k], weights[k], 0.0)
        rows.append(row)
    return rows


def block_at(table, top, stencil, action):
    top = pl.multiple_of(top, 8)
    most = word_of(table, top, stencil + 1, stencil)

    @pl.when(most <= 1)
    def _():
        action(top, BATCH)

    @pl.when(most == 2)
    def _():
        action(top, 2 * BATCH)

    @pl.when(most > 2)
    def _():
        action(top, stencil)


def blocks_of(table, top, amount, stencil, action):
    def step(i, carry):
        block_at(table, top + i * BLOCK, stencil, action)
        return carry

    lax.fori_loop(0, lax.div(amount + (BLOCK - 1), BLOCK), step, 0)


def factor_kernel(
    lines_h, data, replies, _, merged_h, mixed, lines_s, table, merged, sems, *, stencil, slots
):
    parts = replies.shape[0]
    lines = slots // LANES
    lines_copy = pltpu.make_async_copy(lines_h, lines_s, sems.at[0])
    lines_copy.start()

    def per_owner(owner, carry):
        for i in range(lines):
            rows = [
                jnp.zeros((stencil, LANES), F32),
                replies[owner, pl.ds(8 + i, stencil, stride=lines), :],
                jnp.zeros((1, LANES), F32),
                replies[owner, i : i + 1, :],
                jnp.zeros((LANES - 2 * stencil - 2, LANES), F32),
            ]
            at = pl.multiple_of(owner * slots + i * LANES, LANES)
            table[pl.ds(at, LANES), :] = jnp.concatenate(rows, axis=0).T
        return carry

    lax.fori_loop(0, parts, per_owner, 0)
    lines_copy.wait()
    count = jnp.minimum(lines_s[(stencil + 3) * LANES], LISTED)

    def mix(one, two, has_two):
        for slot in (one, two):
            back = word_of(lines_s, slot, stencil + 2, stencil)
            mixed[pl.ds(slot, 1), :] = data[pl.ds(slot, 1), :] + table[pl.ds(back, 1), :]

    pairs(0, count, mix)

    def build(top, places):
        rows = weight_rows(mixed[pl.ds(top, BLOCK), :], places, stencil)
        for place, row in enumerate(rows):
            merged[pl.ds(place * LISTED + top, BLOCK), :] = row

    blocks_of(lines_s, 0, count, stencil, build)
    merged_copy = pltpu.make_async_copy(merged, merged_h, sems.at[1])
    merged_copy.start()
    merged_copy.wait()


def most_batches(table, slots, stencil):
    most = word_of(table, slots[0], stencil, stencil)
    for slot in slots[1:]:
        most = jnp.maximum(most, word_of(table, slot, stencil, stencil))
    return most


def scatter_slots(table, merged, room, copies, slots, values, stencil):
    def batch(begin):
        for first in range(0, len(slots), len(copies)):
            todo = []
            some = slice(first, first + len(copies))
            for slot, value, ref in zip(slots[some], values[some], copies):
                for j in range(BATCH):
                    line = word_of(table, slot, begin + j, stencil)
                    row = merged[pl.ds((begin + j) * room + slot, 1), :] * value
                    todo.append((ref, line, ref[pl.ds(line, 1), :] + row))
            for ref, line, row in todo:
                ref[pl.ds(line, 1), :] = row

    def more(i, carry):
        batch(i * BATCH)
        return carry

    batch(0)
    lax.fori_loop(1, most_batches(table, slots, stencil), more, 0)


def band(shape, taps, shift):
    distance = iota(shape, 1) - iota(shape, 0) + shift
    result = jnp.zeros(shape, F32)
    for tap in range(taps.shape[0]):
        result = jnp.where(distance == tap, taps[tap], result)
    return result


def band_rev(shape, taps, shift):
    distance = iota(shape, 0) - iota(shape, 1) + shift
    result = jnp.zeros(shape, F32)
    for tap in range(taps.shape[0]):
        result = jnp.where(distance == tap, taps[tap], result)
    return result


def exact_nt(a, b):
    return lax.dot_general(
        a,
        b,
        (((1,), (1,)), ((), ())),
        precision=lax.Precision.HIGHEST,
        preferred_element_type=F32,
    )


def store_split(ref, index, value):
    high, low = split2(value)
    ref[(0,) + index] = high
    ref[(1,) + index] = low


def bands_kernel(kx, ky, lat2, lon2, lat1, lon1, *, rows_block):
    margin = kx.shape[0] // 2
    window = lat2.shape[2]
    first = band((window, window), ky, margin)
    reach = first[LANES : LANES + WIDE, :]
    place = iota((window, window), 1)
    for variant in range(3):
        kept = first
        if variant == 0:
            kept = jnp.where(place >= LANES, first, 0.0)
        if variant == 2:
            kept = jnp.where(place < LANES + WIDE, first, 0.0)
        store_split(lat2, (variant,), exact_nt(kept, reach))
    size = lon2.shape[1]
    wide = size + 2 * HALO
    depth = (wide + 32 + LANES - 1) // LANES * LANES
    second = band((wide, depth), kx, -(16 - margin))
    store_split(lon2, (), exact_nt(second[HALO : HALO + size, :], second))
    store_split(lat1, (), band_rev((rows_block, rows_block + 2 * PAD), ky, PAD + margin))
    store_split(lon1, (), band((2 * WIDE, WIDE), kx, LANES + margin))


def pairs(low, high, action):
    def step(i, carry):
        one = low + 2 * i
        action(one, jnp.minimum(one + 1, high - 1), one + 1 < high)
        return carry

    lax.fori_loop(0, lax.shift_right_logical(high - low + 1, 1), step, 0)


def quads(low, high, action):
    def step(i, carry):
        one = low + 4 * i
        numbers = [one] + [jnp.minimum(one + j, high - 1) for j in range(1, 4)]
        weights = [None] + [jnp.where(one + j < high, 1.0, 0.0) for j in range(1, 4)]
        action(numbers, weights)
        return carry

    lax.fori_loop(0, lax.shift_right_logical(high - low + 3, 2), step, 0)


def weighted(value, weight):
    return value if weight is None else value * weight


def zero_all(refs):
    rows = refs[0].shape[0]
    step = 256

    def clear(i, carry):
        for ref in refs:
            ref[pl.ds(pl.multiple_of(i * step, 8), step), :] = jnp.zeros((step, LANES), F32)
        return carry

    whole = rows // step
    lax.fori_loop(0, whole, clear, 0)
    if rows % step:
        for ref in refs:
            ref[whole * step : rows, :] = jnp.zeros((rows % step, LANES), F32)


def scatter_entries(copies, entries, lane):
    for start in range(0, len(entries), len(copies)):
        group = []
        for ref, (address, value) in zip(copies, entries[start : start + len(copies)]):
            line = lax.shift_right_logical(address, 7)
            spread = jnp.where(lane == (address & (LANES - 1)), value, 0.0)
            group.append((ref, line, ref[pl.ds(line, 1), :] + spread))
        for ref, line, value in group:
            ref[pl.ds(line, 1), :] = value


def spot(sender, idx, per, stencil):
    return sender * per + idx + lax.shift_right_logical(idx, 7) * ((stencil - 1) * LANES)


def copy_parts(layout, source, target, place, chunk, chunks, group, sem):
    begin, size = place
    words = group * size * LANES
    at = begin * LANES + chunk * words
    return pltpu.make_async_copy(source.at[pl.ds(at, words)], target, sem)


def apply_kernel(
    *refs, first, layout, columns, height, hold, stencil, capacity, senders, parts, levels
):
    refs = list(refs)

    def take(count):
        taken = refs[:count]
        del refs[:count]
        return taken

    meta, ints, floats, own_lines, own = take(5)
    if not first:
        replies_h, replies = take(2)
    std_h, std_l_h, std_r_h, lat2_h, lon2_h = take(5)
    if not first:
        merged_h, _ = take(2)
    field_h, send = take(2)
    if first:
        info_out, merged_h = take(2)
    addr, wgt, start, lines_s, val = take(5)
    if first:
        std_flat, picked, chosen = take(3)
    scale, merged, sums, high_s, low_s, std, std_l, std_r, lat2, lon2, field = take(11)
    copies = take(PAIR)
    sems, in_sems, out_sems, val_sem = take(4)

    me = meta[0]
    wide = columns + 2 * HALO
    blocks = height // LANES
    group = min(GROUP, senders)
    chunks = senders // group
    slots = senders * capacity
    lane = iota((1, LANES), 1)
    per = stencil * hold
    table = layout.table

    def chunk_copies(chunk):
        todo = [
            (ints, addr, layout.ints["addr"]),
            (floats, wgt, layout.floats["wgt"]),
            (ints, start, layout.ints["start"]),
        ]
        if first:
            todo.append((floats, val, layout.floats["val"]))
        return [
            copy_parts(layout, source, target, place, chunk, chunks, group, sems.at[i])
            for i, (source, target, place) in enumerate(todo)
        ]

    def load_chunk(chunk):
        for copy in chunk_copies(chunk):
            copy.start()
        for copy in chunk_copies(chunk):
            copy.wait()

    operands = [
        pltpu.make_async_copy(source, target, in_sems.at[i])
        for i, (source, target) in enumerate(
            (
                (std_h, std),
                (std_l_h, std_l),
                (std_r_h, std_r),
                (lat2_h, lat2),
                (lon2_h, lon2),
            )
        )
    ]
    own_copy = pltpu.make_async_copy(own_lines, lines_s, in_sems.at[5])
    own_copy.start()
    merged_copy = pltpu.make_async_copy(
        *((merged, merged_h) if first else (merged_h, merged)), in_sems.at[6]
    )
    if not first:
        merged_copy.start()
    for copy in operands:
        copy.start()

    def value_copy(owner):
        at = pl.multiple_of(owner * (replies.shape[1] * LANES), 1024)
        return pltpu.make_async_copy(
            replies_h.at[pl.ds(at, slots)], val.at[pl.ds(owner * slots, slots)], val_sem.at[owner]
        )

    def each_owner(action):
        def step(owner, carry):
            action(value_copy(owner))
            return carry

        lax.fori_loop(0, parts, step, 0)

    if not first:
        each_owner(lambda copy: copy.start())
    zero_all(copies)
    zero_all([sums])

    lane_of = iota((slots, LANES), 1)
    room = slots + LANES
    column = 2 * stencil if first else 2 * stencil + 2
    scale[...] = jnp.broadcast_to(own[:, column : column + 1], (room, LANES))
    known = own[0:slots, :]
    own_copy.wait()
    if not first:
        merged_copy.wait()

    after = lax.rem(me + 1, parts)
    ahead = lax.rem(me + parts - 1, parts)

    def start_of(sender, owner, row, half):
        return start[sender * table + row * hold + half * LANES + owner]

    def entries_of(sender, idx, value):
        base = spot(sender, idx, per, stencil)
        return [
            (addr[base + k * LANES], wgt[base + k * LANES] * value) for k in range(stencil)
        ]

    def own_line(slot, k):
        return word_of(lines_s, slot, k, stencil)

    def amount_of(sender):
        return lines_s[(stencil + 3) * LANES + sender]

    halo_count = lines_s[(stencil + 4) * LANES]
    halo_fits = halo_count <= LANES

    def own_groups(action, halo):
        if capacity % BLOCK:
            blocks_of(lines_s, 0, slots, stencil, action)
        else:

            def per_sender(sender, carry):
                blocks_of(lines_s, sender * capacity, amount_of(sender), stencil, action)
                return carry

            lax.fori_loop(0, senders, per_sender, 0)
        if halo:
            blocks_of(lines_s, slots, jnp.minimum(halo_count, LANES), stencil, action)

    def build(top, places):
        rows = weight_rows(own[pl.ds(top, BLOCK), :], places, stencil)
        for place, row in enumerate(rows):
            merged[pl.ds(place * room + top, BLOCK), :] = row

    if first:
        own_groups(build, True)
        merged_copy.start()

    def own_quads(action):
        def per_sender(sender, carry):
            base = sender * capacity
            quads(base, base + amount_of(sender), action)
            return carry

        lax.fori_loop(0, senders, per_sender, 0)

    def scatter_known(numbers, weights):
        values = [weighted(scale[pl.ds(i, 1), :], w) for i, w in zip(numbers, weights)]
        scatter_slots(lines_s, merged, room, copies, numbers, values, stencil)

    def scatter_sent(numbers, weights):
        values = [weighted(val[own_line(i, stencil + 2)], w) for i, w in zip(numbers, weights)]
        scatter_slots(lines_s, merged, room, copies, numbers, values, stencil)

    def scatter_halo(chunk):
        def per_sender(sender, carry):
            for owner, low, high in ((after, (1, 0), (1, 1)), (ahead, (2, 0), (0, 1))):
                begin = start_of(sender, owner, 0, 0)

                def value_of(idx, owner=owner, begin=begin):
                    if first:
                        return val[sender * hold + idx]
                    place = (chunk * group + sender) * capacity + idx - begin
                    return val[owner * slots + place]

                def action(one, two, has_two, value_of=value_of):
                    second = jnp.where(has_two, value_of(two), 0.0)
                    scatter_entries(
                        copies,
                        entries_of(sender, one, value_of(one)) + entries_of(sender, two, second),
                        lane,
                    )

                pairs(start_of(sender, owner, *low), start_of(sender, owner, *high), action)
            return carry

        lax.fori_loop(0, group, per_sender, 0)

    own_quads(scatter_known)
    if not first:
        each_owner(lambda copy: copy.wait())

    @pl.when(halo_fits)
    def _():
        quads(slots, slots + halo_count, scatter_known if first else scatter_sent)

    @pl.when(jnp.logical_not(halo_fits))
    def _():
        def step(chunk, carry):
            load_chunk(chunk)
            scatter_halo(chunk)
            return carry

        lax.fori_loop(0, chunks, step, 0)

    for copy in operands:
        copy.wait()

    for jb in range(blocks):
        lanes = slice(jb * LANES, (jb + 1) * LANES)
        for low, size, source in (
            (0, HALO, std_l),
            (HALO, columns, std),
            (HALO + columns, HALO, std_r),
        ):
            rows = slice(jb * wide + low, jb * wide + low + size)
            total = copies[0][rows, :]
            for ref in copies[1:]:
                total = total + ref[rows, :]
            high, lo = split2(total * source[:, lanes])
            high_s[low : low + size, lanes] = high
            low_s[low : low + size, lanes] = lo
        if first:
            std_flat[jb * wide + HALO : jb * wide + HALO + columns, :] = std[:, lanes]

    smoothed = copies[0]
    size = lon2.shape[1]
    count = height // WIDE
    outgoing = [merged_copy] if first else []
    for block in range(count):
        variant = 0 if block == 0 else (2 if block == count - 1 else 1)
        low = max(block * WIDE - LANES, 0)
        high = min(block * WIDE + WIDE + LANES, height)
        inner = slice(low - (block * WIDE - LANES), high - (block * WIDE - LANES))
        matrix = (lat2[0, variant, inner, :], lat2[1, variant, inner, :])
        along = mm_parts((high_s[:, low:high], low_s[:, low:high]), matrix)
        parts_y = split2(along)
        lanes = slice(block * WIDE, (block + 1) * WIDE)
        for begin in range(0, columns, size):
            some = min(size, columns - begin)
            rows = slice(begin, begin + some)
            window = slice(begin, begin + some + 2 * HALO)
            matrix = tuple(lon2[i, 0:some, 0 : some + 2 * HALO] for i in range(2))
            result = mm_parts(matrix, (parts_y[0][window, :], parts_y[1][window, :]))
            field[rows, lanes] = result
            scaled = result * std[rows, lanes]
            for half in range(WIDE // LANES):
                top = (block * (WIDE // LANES) + half) * wide + HALO + begin
                smoothed[top : top + some, :] = scaled[:, half * LANES : (half + 1) * LANES]
        outgoing.append(
            pltpu.make_async_copy(field.at[:, lanes], field_h.at[:, lanes], out_sems.at[block])
        )
        outgoing[-1].start()

    def gather_quad(numbers, weights):
        def batch(begin, totals):
            result = []
            for slot, total in zip(numbers, totals):
                terms = []
                for j in range(BATCH):
                    line = own_line(slot, begin + j)
                    row = merged[pl.ds((begin + j) * room + slot, 1), :]
                    terms.append(row * smoothed[pl.ds(line, 1), :])
                    if first:
                        picked[pl.ds((begin + j) * room + slot, 1), :] = std_flat[
                            pl.ds(line, 1), :
                        ]
                result.append(total + ((terms[0] + terms[1]) + (terms[2] + terms[3])))
            return tuple(result)

        zero = jnp.zeros((1, LANES), F32)
        totals = lax.fori_loop(
            1,
            most_batches(lines_s, numbers, stencil),
            lambda i, totals: batch(i * BATCH, totals),
            batch(0, (zero,) * len(numbers)),
        )
        for slot, total in zip(numbers, totals):
            sums[pl.ds(slot, 1), :] = total

    own_quads(gather_quad)

    def pick(top, places):
        info = own[pl.ds(top, BLOCK), :]
        codes = columns_of(info, CODES, stencil)
        lane_f = iota(info.shape, 1).astype(F32)
        rows = [picked[pl.ds(place * room + top, BLOCK), :] for place in range(places)]
        result = jnp.zeros((BLOCK, LANES), F32)
        for k in range(stencil):
            cell = jnp.zeros((BLOCK, LANES), F32)
            for place in range(min(k + 1, places)):
                at = lane_f + float(LANES * place)
                cell = jnp.where(at == codes[k], rows[place], cell)
            cell = jnp.sum(cell, axis=1, keepdims=True)
            result = jnp.where(lane_f == float(stencil + k), cell, result)
        chosen[pl.ds(top, BLOCK), :] = result * info

    if first:
        own_groups(pick, False)

    def whole(x):
        return jnp.sum(x, axis=0, keepdims=True)

    total = jnp.sum(sums[...], axis=1, keepdims=True)
    lines = slots // LANES
    known = own[0:slots, :]
    source, weight, reply, image0 = (
        known[:, 2 * stencil + i : 2 * stencil + i + 1] for i in range(4)
    )
    if first:
        reply = weight * total
        known = jnp.where(lane_of == 2 * stencil + 2, reply, known)
        known = jnp.where(lane_of == 2 * stencil + 3, total, known)
        info_out[0:slots, :] = known
        info_out[slots:room, :] = own[slots:room, :]
        turned = known.T[2 * stencil + 2 : 2 * stencil + 3, :]
        message = [turned[:, i * LANES : (i + 1) * LANES] for i in range(lines)]
        message.append(
            jnp.where(
                lane == 0, whole(source * total), jnp.where(lane == 1, whole(reply * total), 0.0)
            )
        )
        message.append(jnp.zeros((8 - len(message), LANES), F32))
        factors = chosen[...].T
        for k in range(stencil):
            row = factors[stencil + k : stencil + k + 1, :]
            message += [row[:, i * LANES : (i + 1) * LANES] for i in range(lines)]
        message = jnp.concatenate(message, axis=0)
    else:
        slab = jnp.sum(replies[:, 0:8, :], axis=0)[lines : lines + 1, :]
        length = slab[:, 0:1] / (slab[:, 0:1] + slab[:, 1:2])
        both = source + reply
        s_both = image0 + total
        resid = source - length * both
        s_resid = image0 - length * s_both
        values = [
            resid * s_resid,
            resid * s_both,
            both * s_both,
            resid * image0,
            both * image0,
            weight * s_resid * s_resid,
            weight * s_resid * s_both,
            weight * s_both * s_both,
            weight * s_resid * image0,
            weight * s_both * image0,
            source * image0,
            reply * image0,
        ]
        message = jnp.where(lane == len(values), length, 0.0)
        for i, value in enumerate(values):
            message = jnp.where(lane == i, whole(value), message)
        message = jnp.concatenate([message, jnp.zeros((7, LANES), F32)], axis=0)

    def send_to(i, carry):
        send[i] = message
        return carry

    lax.fori_loop(0, send.shape[0], send_to, 0)
    for copy in outgoing:
        copy.wait()


def final_kernel(
    ints,
    floats,
    replies_h,
    lines_h,
    merged_h,
    mixed,
    totals,
    std_h,
    field0_h,
    field1_h,
    lat1,
    lon1,
    control_h,
    increment_h,
    addr,
    listed,
    slot,
    val,
    factors,
    std,
    field0,
    field1,
    control,
    high_s,
    low_s,
    lines_s,
    merged,
    scale,
    *rest,
    layout,
    hold,
    stencil,
    capacity,
    senders,
    parts,
    length,
):
    copies = rest[:PAIR]
    sems, in_sems, out_sems = rest[PAIR:]
    group = min(GROUP, senders)
    chunks = senders // group
    per = stencil * hold
    rows_block = control.shape[0]
    high_rows = rows_block + 2 * PAD
    lane = iota((1, LANES), 1)
    stride = group * capacity
    owner_words = factors.shape[0] // parts
    to_factors = owner_words - stencil * stride

    def chunk_copies(chunk):
        todo = [
            (ints, addr, layout.ints["rows"]),
            (ints, listed, layout.ints["listed"]),
            (ints, slot, layout.ints["slot"]),
            (floats, val, layout.floats["val"]),
        ]
        result = [
            copy_parts(layout, source, target, place, chunk, chunks, group, sems.at[i])
            for i, (source, target, place) in enumerate(todo)
        ]
        words = parts * owner_words
        result.append(
            pltpu.make_async_copy(
                replies_h.at[pl.ds(chunk * words, words)], factors, sems.at[len(todo)]
            )
        )
        return result

    listing = [
        pltpu.make_async_copy(lines_h, lines_s, in_sems.at[3]),
        pltpu.make_async_copy(merged_h, merged, in_sems.at[4]),
    ]
    for copy in listing:
        copy.start()
    operands = [
        pltpu.make_async_copy(source, target, in_sems.at[i])
        for i, (source, target) in enumerate(
            ((std_h, std), (field0_h, field0), (field1_h, field1))
        )
    ]
    for copy in operands:
        copy.start()

    slabs = totals.shape[1]
    every = jnp.sum(totals[...], axis=0)
    norm0 = quad0 = None
    for i in range(slabs):
        line = every[i, 0:1, :]
        a, b = line[:, 10:11], line[:, 11:12]
        norm0 = a if norm0 is None else norm0 + a
        quad0 = b if quad0 is None else quad0 + b
    step0 = norm0 / (norm0 + quad0)
    norm1 = cross = quad1 = quad01 = jnp.zeros((1, 1), F32)
    for i in range(slabs):
        line = every[i, 0:1, :]
        v = [line[:, j : j + 1] for j in range(10)]
        shift = totals[0, i, 0:1, 12:13] - step0
        norm1 = norm1 + (v[0] + shift * (2.0 * v[1] + shift * v[2]))
        cross = cross + (v[3] + shift * v[4])
        quad1 = quad1 + (v[5] + shift * (2.0 * v[6] + shift * v[7]))
        quad01 = quad01 + (v[8] + shift * v[9])
    ratio = norm1 / norm0
    curvature = norm1 + quad1 + ratio * (
        2.0 * (cross + quad01) + ratio * (norm0 + quad0)
    )
    step1 = norm1 / curvature
    first = step0 + step1 * (1.0 - step0 + ratio)
    second = -step0 * step1
    first_line = jnp.broadcast_to(first, (1, LANES))
    second_line = jnp.broadcast_to(second, (1, LANES))

    zero_all(copies)

    data = mixed[...]
    column = 2 * stencil
    scale[...] = first * data[:, column : column + 1] + second * jnp.broadcast_to(
        data[:, column + 1 : column + 2], data.shape
    )
    for copy in listing:
        copy.wait()
    count = lines_s[(stencil + 3) * LANES]

    def add(numbers, weights):
        values = [weighted(scale[pl.ds(i, 1), :], w) for i, w in zip(numbers, weights)]
        scatter_slots(lines_s, merged, LISTED, copies, numbers, values, stencil)

    def scatter_chunk():
        def per_sender(sender, carry):
            def step(idx, inner):
                @pl.when(listed[sender * hold + idx] > 0)
                def _():
                    place = slot[sender * hold + idx]
                    place = place + lax.div(place, stride) * (owner_words - stride)
                    base = spot(sender, idx, per, stencil)
                    z0 = val[sender * hold + idx]
                    value = first_line * z0 + second_line * factors[place]
                    entries = [
                        (addr[base + k * LANES], factors[place + to_factors + k * stride] * value)
                        for k in range(stencil)
                    ]
                    scatter_entries(copies, entries, lane)

                return inner

            lax.fori_loop(0, hold, step, 0)
            return carry

        lax.fori_loop(0, group, per_sender, 0)

    @pl.when(count <= LISTED)
    def _():
        quads(0, count, add)

    @pl.when(count > LISTED)
    def _():
        def step(chunk, carry):
            for copy in chunk_copies(chunk):
                copy.start()
            for copy in chunk_copies(chunk):
                copy.wait()
            scatter_chunk()
            return carry

        lax.fori_loop(0, chunks, step, 0)

    for copy in operands:
        copy.wait()
    increment = field0
    increment[...] = std[...] * (first * field0[...] + second * field1[...])
    outgoing = [pltpu.make_async_copy(increment, increment_h, out_sems.at[0])]
    outgoing[0].start()

    pair = WIDE // LANES
    count = length // WIDE
    for block in range(count):
        pieces = []
        for half in range(pair):
            rows = slice((block * pair + half) * high_rows, (block * pair + half + 1) * high_rows)
            total = copies[0][rows, :]
            for ref in copies[1:]:
                total = total + ref[rows, :]
            pieces.append(total)
        whole = split2(jnp.concatenate(pieces, axis=1))
        size = lat1.shape[1]
        for top in range(0, rows_block, size):
            window = slice(top, top + size + 2 * PAD)
            along = mm_parts((lat1[0], lat1[1]), (whole[0][window, :], whole[1][window, :]))
            high, low = split2(along)
            high_s[top : top + size, block * WIDE : (block + 1) * WIDE] = high
            low_s[top : top + size, block * WIDE : (block + 1) * WIDE] = low

    def window(ref, block):
        low, high = block * WIDE - LANES, (block + 1) * WIDE + LANES
        if low < 0:
            return jnp.concatenate([ref[:, length + low : length], ref[:, 0:high]], axis=1)
        if high > length:
            return jnp.concatenate([ref[:, low:length], ref[:, 0 : high - length]], axis=1)
        return ref[:, low:high]

    every_lanes = 4
    for block in range(count):
        control[:, block * WIDE : (block + 1) * WIDE] = mm_parts(
            (window(high_s, block), window(low_s, block)), (lon1[0], lon1[1])
        )
        if block % every_lanes == every_lanes - 1:
            lanes = slice((block + 1 - every_lanes) * WIDE, (block + 1) * WIDE)
            outgoing.append(
                pltpu.make_async_copy(
                    control.at[:, lanes], control_h.at[:, lanes], out_sems.at[len(outgoing)]
                )
            )
            outgoing[-1].start()
    for copy in outgoing:
        copy.wait()


def body(
    background_std,
    x_kernel,
    y_kernel,
    obs_owner,
    obs_cells,
    obs_weights,
    innovation,
    obs_precision,
    obs_counts,
):
    parts = lax.axis_size("pencil")
    levels = lax.axis_size("lev")
    me = lax.axis_index("pencil")
    _, columns, height = background_std.shape
    hold, stencil = obs_cells.shape
    margin = x_kernel.shape[1] // 2
    capacity = 2 * hold // parts
    senders = parts
    slots = senders * capacity
    room = slots + LANES
    rows_block = height // parts
    length = columns * parts
    blocks = height // LANES
    wide = columns + 2 * HALO
    group = min(GROUP, senders)
    chunks = senders // group
    layout = Layout(senders, hold, stencil, parts)
    std = background_std[0]

    packed = pl.pallas_call(
        functools.partial(
            pack_kernel, parts=parts, columns=columns, height=height, margin=margin
        ),
        out_shape=jax.ShapeDtypeStruct((parts, PACK, hold), F32),
        in_specs=[smem()] + [vmem()] * 5,
        out_specs=vmem(),
        scratch_shapes=[pltpu.VMEM((parts, hold), F32)],
        compiler_params=params(),
        cost_estimate=cost(2000),
        name="pack",
    )(
        obs_counts,
        obs_owner.T,
        obs_cells.T,
        obs_weights.T,
        innovation[None, :],
        obs_precision[None, :],
    )
    recv = lax.all_to_all(packed, "pencil", split_axis=0, concat_axis=0, tiled=True)

    right_of = [(p, (p + 1) % parts) for p in range(parts)]
    left_of = [(p, (p - 1) % parts) for p in range(parts)]
    size = min(columns, WIDE - 2 * HALO)
    row_size = min(rows_block, LANES)
    lat2, lon2, lat1, lon1 = pl.pallas_call(
        functools.partial(bands_kernel, rows_block=row_size),
        out_shape=[
            jax.ShapeDtypeStruct((2, 3, 2 * WIDE, WIDE), BF),
            jax.ShapeDtypeStruct((2, size, size + 2 * HALO), BF),
            jax.ShapeDtypeStruct((2, row_size, row_size + 2 * PAD), BF),
            jax.ShapeDtypeStruct((2, 2 * WIDE, WIDE), BF),
        ],
        in_specs=[smem(), smem()],
        out_specs=[vmem()] * 4,
        compiler_params=params(),
        cost_estimate=cost(6000),
        name="bands",
    )(x_kernel[0], y_kernel[0])

    edge = jax.ShapeDtypeStruct((HALO, height), F32)
    low_edge, high_edge = pl.pallas_call(
        edges_kernel,
        out_shape=[edge, edge],
        in_specs=[hbm()] * 3,
        out_specs=[hbm()] * 2,
        scratch_shapes=[pltpu.SemaphoreType.DMA((2,))],
        compiler_params=params(),
        cost_estimate=cost(500),
        name="edges",
    )(std, recv, lat1)
    std_l = lax.ppermute(high_edge, "pencil", right_of)
    std_r = lax.ppermute(low_edge, "pencil", left_of)

    meta = jnp.reshape(me, (1,)).astype(I32)
    place = dict(
        parts=parts, columns=columns, height=height, capacity=capacity, stencil=stencil
    )
    ints, floats, own_lines, own = pl.pallas_call(
        functools.partial(unpack_kernel, layout=layout, group=group, **place),
        out_shape=[
            jax.ShapeDtypeStruct((layout.int_rows, LANES), I32),
            jax.ShapeDtypeStruct((layout.float_rows, LANES), F32),
            jax.ShapeDtypeStruct((room // LANES * (stencil + 8), LANES), I32),
            jax.ShapeDtypeStruct((room, LANES), F32),
        ],
        in_specs=[smem(), vmem()],
        out_specs=[vmem()] * 4,
        scratch_shapes=[
            pltpu.VMEM((room // LANES, STACK, LANES), F32),
        ],
        compiler_params=params(),
        cost_estimate=cost(3500),
        name="unpack",
    )(meta, recv)
    ints = ints.reshape(-1)
    floats = floats.reshape(-1)
    own_lines = own_lines.reshape(-1)

    acc = pltpu.VMEM((blocks * wide + 8, LANES), F32)
    column_slots = pltpu.VMEM((slots, LANES), F32)
    static = dict(
        layout=layout,
        columns=columns,
        height=height,
        hold=hold,
        stencil=stencil,
        capacity=capacity,
        senders=senders,
        parts=parts,
        levels=levels,
    )
    per = group * stencil * hold
    line = group * hold
    index_scratch = [
        pltpu.SMEM((per,), I32),
        pltpu.SMEM((per,), F32),
        pltpu.SMEM((group * layout.table,), I32),
        pltpu.SMEM((room * (stencil + 8),), I32),
    ]
    work = (
        [
            pltpu.VMEM((room, LANES), F32),
            pltpu.VMEM((stencil * room, LANES), F32),
            column_slots,
        ]
        + [pltpu.VMEM((wide, height), BF)] * 2
        + [
            pltpu.VMEM((columns, height), F32),
            pltpu.VMEM((HALO, height), F32),
            pltpu.VMEM((HALO, height), F32),
            pltpu.VMEM(lat2.shape, BF),
            pltpu.VMEM(lon2.shape, BF),
            pltpu.VMEM((columns, height), F32),
        ]
        + [acc] * PAIR
        + [
            pltpu.SemaphoreType.DMA((4,)),
            pltpu.SemaphoreType.DMA((7,)),
            pltpu.SemaphoreType.DMA((height // WIDE,)),
            pltpu.SemaphoreType.DMA((parts,)),
        ]
    )
    field_shape = jax.ShapeDtypeStruct((columns, height), F32)
    reply_rows = 8 + stencil * slots // LANES
    field0, message, info, merged = pl.pallas_call(
        functools.partial(apply_kernel, first=True, **static),
        out_shape=[
            field_shape,
            jax.ShapeDtypeStruct((parts, reply_rows, LANES), F32),
            jax.ShapeDtypeStruct((room, LANES), F32),
            jax.ShapeDtypeStruct((stencil * room, LANES), F32),
        ],
        in_specs=[smem()] + [hbm()] * 3 + [vmem()] + [hbm()] * 5,
        out_specs=[hbm()] + [vmem()] * 2 + [hbm()],
        scratch_shapes=index_scratch
        + [
            pltpu.SMEM((line,), F32),
            acc,
            pltpu.VMEM((stencil * room, LANES), F32),
            column_slots,
        ]
        + work,
        compiler_params=params(),
        name="apply_first",
    )(meta, ints, floats, own_lines, own, std, std_l, std_r, lat2, lon2)

    replies = lax.all_to_all(message, "pencil", split_axis=0, concat_axis=0, tiled=True)
    back = replies.reshape(-1)
    line_rows = LISTED // LANES * (stencil + 8)
    row_lines, row_data = pl.pallas_call(
        functools.partial(list_kernel, **place),
        out_shape=[
            jax.ShapeDtypeStruct((line_rows, LANES), I32),
            jax.ShapeDtypeStruct((LISTED, LANES), F32),
        ],
        in_specs=[smem(), vmem(), hbm()],
        out_specs=[vmem()] * 2,
        scratch_shapes=[pltpu.VMEM((STACK, LISTED), F32)],
        compiler_params=params(),
        cost_estimate=cost(4000),
        name="list_rows",
    )(meta, recv, info)
    row_lines = row_lines.reshape(-1)

    field1, sums = pl.pallas_call(
        functools.partial(apply_kernel, first=False, **static),
        out_shape=[
            field_shape,
            jax.ShapeDtypeStruct((parts * levels, 8, LANES), F32),
        ],
        in_specs=[smem()] + [hbm()] * 3 + [vmem(), hbm(), vmem()] + [hbm()] * 7,
        out_specs=[hbm(), vmem()],
        scratch_shapes=index_scratch + [pltpu.SMEM((parts * slots,), F32)] + work,
        compiler_params=params(),
        name="apply_second",
    )(
        meta,
        ints,
        floats,
        own_lines,
        info,
        back,
        replies,
        std,
        std_l,
        std_r,
        lat2,
        lon2,
        merged,
        row_data,
    )

    totals = lax.all_to_all(sums, ("pencil", "lev"), split_axis=0, concat_axis=0, tiled=True)
    totals = totals.reshape(parts, levels, 8, LANES)

    listed_rows, mixed = pl.pallas_call(
        functools.partial(factor_kernel, stencil=stencil, slots=slots),
        out_shape=[
            jax.ShapeDtypeStruct((stencil * LISTED, LANES), F32),
            jax.ShapeDtypeStruct((LISTED, LANES), F32),
        ],
        in_specs=[hbm(), vmem(), vmem(), hbm()],
        out_specs=[hbm(), vmem()],
        scratch_shapes=[
            pltpu.SMEM((line_rows * LANES,), I32),
            pltpu.VMEM((parts * slots, LANES), F32),
            pltpu.VMEM((stencil * LISTED, LANES), F32),
            pltpu.SemaphoreType.DMA((2,)),
        ],
        compiler_params=params(),
        cost_estimate=cost(8000),
        name="factor_rows",
    )(row_lines, row_data, replies, sums)

    by_chunk = back
    if chunks > 1:
        by_chunk = jnp.concatenate(
            [replies[:, : slots // LANES, :], replies[:, 8:, :]], axis=1
        ).reshape(parts, stencil + 1, chunks, group * capacity)
        by_chunk = jnp.transpose(by_chunk, (2, 0, 1, 3)).reshape(-1)
    owner_words = by_chunk.shape[0] // (chunks * parts)
    high_rows = rows_block + 2 * PAD
    acc_rows = pltpu.VMEM(((length // LANES) * high_rows + 8, LANES), F32)
    control, increment = pl.pallas_call(
        functools.partial(
            final_kernel,
            layout=layout,
            hold=hold,
            stencil=stencil,
            capacity=capacity,
            senders=senders,
            parts=parts,
            length=length,
        ),
        out_shape=[
            jax.ShapeDtypeStruct((rows_block, length), F32),
            field_shape,
        ],
        in_specs=[hbm()] * 5 + [vmem()] * 2 + [hbm()] * 3 + [vmem()] * 2,
        out_specs=[hbm()] * 2,
        scratch_shapes=[
            pltpu.SMEM((per,), I32),
            pltpu.SMEM((line,), I32),
            pltpu.SMEM((line,), I32),
            pltpu.SMEM((line,), F32),
            pltpu.SMEM((parts * owner_words,), F32),
            pltpu.VMEM((columns, height), F32),
            pltpu.VMEM((columns, height), F32),
            pltpu.VMEM((columns, height), F32),
            pltpu.VMEM((rows_block, length), F32),
            pltpu.VMEM((rows_block, length), BF),
            pltpu.VMEM((rows_block, length), BF),
            pltpu.SMEM((line_rows * LANES,), I32),
            pltpu.VMEM((stencil * LISTED, LANES), F32),
            pltpu.VMEM((LISTED, LANES), F32),
        ]
        + [acc_rows] * PAIR
        + [
            pltpu.SemaphoreType.DMA((5,)),
            pltpu.SemaphoreType.DMA((5,)),
            pltpu.SemaphoreType.DMA((1 + length // WIDE,)),
        ],
        compiler_params=params(),
        name="outputs",
    )(
        ints,
        floats,
        by_chunk,
        row_lines,
        listed_rows,
        mixed,
        totals,
        std,
        field0,
        field1,
        lat1,
        lon1,
    )
    return control[None], increment[None]


def solution(mesh):
    return jax.shard_map(
        body,
        mesh=mesh,
        in_specs=(
            P("lev", "pencil", None),
            P("lev", None),
            P("lev", None),
            P(("pencil", "lev"), None),
            P(("pencil", "lev"), None),
            P(("pencil", "lev"), None),
            P(("pencil", "lev")),
            P(("pencil", "lev")),
            P(("pencil", "lev")),
        ),
        out_specs=(P("lev", "pencil", None), P("lev", "pencil", None)),
        check_vma=False,
    )
```

```python
import functools

import jax
import jax.numpy as jnp
import numpy as np
from jax import lax
from jax.experimental import pallas as pl
from jax.experimental.pallas import tpu as pltpu
from jax.sharding import PartitionSpec as P


BF = jnp.bfloat16
F32 = jnp.float32
I32 = jnp.int32
LANES = 128
WIDE = 256
HALO = 32
PAD = 16
PACK = 40
GROUP = 8
PAIR = 2
BATCH = 4
BLOCK = 32
CODES = 40
STACK = 64
LISTED = 512
VMEM_LIMIT = 58 * 1024 * 1024


def vmem():
    return pl.BlockSpec(memory_space=pltpu.VMEM)


def smem():
    return pl.BlockSpec(memory_space=pltpu.SMEM)


def hbm():
    return pl.BlockSpec(memory_space=pl.ANY)


def cost(nanoseconds):
    return pl.CostEstimate(flops=0, bytes_accessed=3690 * nanoseconds, transcendentals=0)


def params():
    return pltpu.CompilerParams(vmem_limit_bytes=VMEM_LIMIT)


def split2(x):
    high = x.astype(BF)
    return high, (x - high.astype(F32)).astype(BF)


def split3(x):
    high = x.astype(BF)
    rest = x - high.astype(F32)
    mid = rest.astype(BF)
    return high, mid, (rest - mid.astype(F32)).astype(BF)


def mm(a, b):
    return jnp.dot(a, b, preferred_element_type=F32)


def mm_parts(a_parts, b_parts):
    (ah, al), (bh, bl) = a_parts, b_parts
    return mm(jnp.concatenate([ah, al, ah], axis=1), jnp.concatenate([bh, bh, bl], axis=0))


def iota(shape, dim):
    return lax.broadcasted_iota(I32, shape, dim)


def pack_kernel(
    counts, owner, cells, weights, depart, prec, out, marks, *, parts, columns, height, margin
):
    stencil, hold = cells.shape
    shift = height.bit_length() - 1
    block = height // parts
    reach = 2 * margin
    row_id = iota((hold, hold), 0)
    col_id = iota((hold, hold), 1)
    eye = row_id == col_id
    col_f = col_id.astype(F32)
    live = iota((1, hold), 1) < counts[0]
    cell = cells[...]
    column = lax.shift_right_logical(cell, jnp.full(cell.shape, shift, I32))
    row = cell & (height - 1)

    def any_of(mask):
        return jnp.max(jnp.where(mask, 1.0, 0.0), axis=0, keepdims=True)

    def turn(line):
        return jnp.sum(jnp.where(eye, line, 0.0), axis=1, keepdims=True)

    left = any_of(column < reach)
    right = any_of(column >= columns - reach)
    side = left + 3.0 * right - 2.0 * left * right
    base = jnp.where(live, owner[...].astype(F32) * 4.0, 4.0 * parts)
    key = jnp.where(live, base + side, base)
    key_col = turn(key)
    before = (key_col < key) | ((key_col == key) & (row_id < col_id))
    rank = jnp.sum(jnp.where(before, 1.0, 0.0), axis=0, keepdims=True)
    begin = jnp.sum(jnp.where(key_col < base, 1.0, 0.0), axis=0, keepdims=True)
    rank_col = turn(rank)
    perm = jnp.where(rank_col == col_f, 1.0, 0.0).astype(BF)

    def sort(values):
        total = None
        for part in split3(values):
            term = mm(part, perm)
            total = term if total is None else total + term
        return total

    weight = jnp.where(live, prec[...], 0.0)
    rest = [weight * depart[...], weight, key, rank - begin, jnp.zeros((4, hold), F32)]
    values = [cell.astype(F32), weights[...]] + rest
    ordered = sort(jnp.concatenate(values, axis=0))
    line = iota((8, hold), 0)
    tail = ordered[2 * stencil : 2 * stencil + 8, :]
    first_half = col_f < float(LANES)
    fourfold = 4.0 * jnp.where(first_half, col_f, col_f - float(LANES))
    for i, (low, high) in enumerate(((0.0, 4.0), (1.0, 3.0), (2.0, 2.0))):
        bound = fourfold + jnp.where(first_half, low, high)
        begins = jnp.sum(jnp.where(key_col < bound, 1.0, 0.0), axis=0, keepdims=True)
        tail = jnp.where(line == 5 + i, begins, tail)
    last = (line == 7) & (iota((8, hold), 1) == hold - 1)

    def mark(part, carry):
        low = part * block - margin
        high = (part + 1) * block + margin
        flag = jnp.where(live, any_of((row >= low) & (row < high)), 0.0)
        place = jnp.sum(jnp.where(row_id < col_id, turn(flag), 0.0), axis=0, keepdims=True)
        marks[pl.ds(part, 1), :] = flag * (place + 1.0)
        return carry

    lax.fori_loop(0, parts, mark, 0, unroll=parts <= GROUP)
    listed = marks[...]
    amounts = jnp.max(listed, axis=1, keepdims=True)
    listed = mm(listed.astype(BF), perm)
    for part in range(parts):
        out[part, 0 : 2 * stencil, :] = ordered[0 : 2 * stencil, :]
        out[part, 2 * stencil : 2 * stencil + 8, :] = jnp.where(
            line == 4,
            listed[part : part + 1, :],
            jnp.where(last, amounts[part : part + 1, :], tail),
        )


class Layout:
    def __init__(self, senders, hold, stencil, parts):
        lines = hold // LANES
        self.table = 3 * hold
        sizes = dict(
            addr=stencil * lines, rows=stencil * lines, listed=lines, slot=lines, start=3 * lines
        )
        self.ints = {}
        at = 0
        for name, size in sizes.items():
            self.ints[name] = (at, size)
            at += senders * size
        self.int_rows = at
        self.floats = {}
        at = 0
        for name, size in dict(wgt=stencil * lines, val=lines).items():
            self.floats[name] = (at, size)
            at += senders * size
        self.float_rows = at


def right(x, by):
    return lax.shift_right_logical(x, jnp.full(x.shape, by, I32))


def nt(a, b):
    return lax.dot_general(a, b, (((1,), (1,)), ((), ())), preferred_element_type=F32)


class Received:
    def __init__(self, recv, sender, me, *, parts, columns, height, capacity, stencil):
        senders, _, hold = recv.shape
        wide = columns + 2 * HALO
        block = height // parts
        high_rows = block + 2 * PAD
        cell = recv[sender, 0:stencil, :].astype(I32)
        self.tail = recv[sender, 2 * stencil : 2 * stencil + 8, :]
        self.whole = self.tail.astype(I32)
        self.pos = self.whole[3:4, :]
        owner = right(self.whole[2:3, :], 2)
        offset = owner - me
        offset = jnp.where(offset > parts // 2, offset - parts, offset)
        offset = jnp.where(offset < -(parts // 2), offset + parts, offset)
        column = right(cell, height.bit_length() - 1)
        row = cell & (height - 1)
        at = offset * columns + column + HALO
        self.addr = jnp.where(
            (at >= 0) & (at < wide),
            (right(row, 7) * wide + at) * LANES + (row & (LANES - 1)),
            (height // LANES) * wide * LANES,
        )
        at_row = row - (block * me - PAD)
        across = owner * columns + column
        self.rows = jnp.where(
            (at_row >= 0) & (at_row < high_rows) & (owner < parts),
            (right(across, 7) * high_rows + at_row) * LANES + (across & (LANES - 1)),
            (columns * parts // LANES) * high_rows * LANES,
        )
        self.owner = jnp.minimum(owner, parts - 1)
        self.back = self.owner * (senders * capacity) + sender * capacity + self.pos


def stack_of(addr, weights, tail, back):
    hold = addr.shape[1]
    rows = [
        (addr & (LANES - 1)).astype(F32),
        weights,
        tail,
        right(addr, 7).astype(F32),
        back.astype(F32),
        jnp.zeros((7, hold), F32),
    ]
    return jnp.concatenate(split3(jnp.concatenate(rows, axis=0)), axis=1)


def gathered(stack, chosen):
    select = jnp.where(chosen, 1.0, 0.0).astype(BF)
    return nt(stack, jnp.concatenate([select] * 3, axis=1))


def merge_lines(block, nowhere, stencil, extra):
    number = iota((stencil, LANES), 0).astype(F32)
    line = block[CODES : CODES + stencil, :]
    leader = jnp.zeros(line.shape, F32)
    for k in reversed(range(stencil)):
        leader = jnp.where(line == line[k : k + 1, :], float(k), leader)
    leads = jnp.where(leader == number, 1.0, 0.0)
    count = jnp.zeros((1, LANES), F32)
    ranks = []
    for k in range(stencil):
        ranks.append(count)
        count = count + leads[k : k + 1, :]
    place = jnp.zeros(line.shape, F32)
    for k in range(stencil):
        place = jnp.where(leader == float(k), ranks[k], place)
    lists = []
    for k in range(stencil):
        found = jnp.where((leads > 0.0) & (place == float(k)), line, 0.0)
        found = jnp.sum(found, axis=0, keepdims=True)
        lists.append(jnp.where(count > float(k), found, nowhere))
    batches = right(count.astype(I32) + (BATCH - 1), BATCH.bit_length() - 1)
    most = jnp.zeros((1, LANES), F32)
    slot = iota((1, LANES), 1)
    for begin in range(0, LANES, BLOCK):
        here = (slot >= begin) & (slot < begin + BLOCK)
        found = jnp.max(jnp.where(here, batches.astype(F32), 0.0), axis=1, keepdims=True)
        most = jnp.where(here, found, most)
    back = block[CODES + stencil : CODES + stencil + 1, :]
    ints = [jnp.concatenate(lists, axis=0).astype(I32), batches]
    ints += [most.astype(I32), back.astype(I32)] + extra
    ints = jnp.concatenate(ints, axis=0)
    ints = jnp.concatenate([ints, jnp.zeros((stencil + 8 - ints.shape[0], LANES), I32)], axis=0)
    rows = [
        block[0:CODES, :],
        place * float(LANES) + block[0:stencil, :],
        jnp.zeros((LANES - CODES - stencil, LANES), F32),
    ]
    return ints, jnp.concatenate(rows, axis=0).T


def unpack_kernel(
    meta, recv, _, ints, floats, own_lines, own, total, *, layout, group, **sizes
):
    senders, _, hold = recv.shape
    lines = hold // LANES
    me = meta[0]
    parts, stencil, capacity = sizes["parts"], sizes["stencil"], sizes["capacity"]
    wide = sizes["columns"] + 2 * HALO
    slots = senders * capacity

    def put(ref, place, sender, value):
        begin, size = place
        count = value.shape[0]
        for i in range(lines):
            part = value[:, i * LANES : (i + 1) * LANES]
            if count % 8 == 0:
                at = pl.multiple_of(begin + sender * size + i * count, 8)
                ref[pl.ds(at, count), :] = part
            else:
                for j in range(count):
                    ref[pl.ds(begin + sender * size + i + j * lines, 1), :] = part[j : j + 1]

    total[...] = jnp.zeros(total.shape, F32)
    place = iota((LANES, hold), 0)
    index = iota((LANES, hold), 1)
    lane = iota((1, LANES), 1)
    halo_block = slots // LANES
    after = lax.rem(me + 1, parts)
    ahead = lax.rem(me + parts - 1, parts)

    def per_sender(sender, carry):
        halo_before, amounts = carry
        got = Received(recv, sender, me, **sizes)
        weights = recv[sender, stencil : 2 * stencil, :]
        within = lax.rem(sender, group) * capacity + got.pos
        put(ints, layout.ints["addr"], sender, got.addr)
        put(ints, layout.ints["rows"], sender, got.rows)
        put(ints, layout.ints["listed"], sender, got.whole[4:5, :])
        put(ints, layout.ints["slot"], sender, got.owner * (group * capacity) + within)
        put(ints, layout.ints["start"], sender, got.whole[5:8, :])
        put(floats, layout.floats["wgt"], sender, weights)
        put(floats, layout.floats["val"], sender, got.tail[0:1, :])

        def bound(line, half, owner):
            part = got.whole[5 + line : 6 + line, half * LANES : (half + 1) * LANES]
            return jnp.sum(jnp.where(lane == owner, part, 0), axis=1, keepdims=True)

        stack = stack_of(got.addr, weights, got.tail, got.back)

        begin, end = bound(0, 0, me), bound(0, 1, me)
        first_slot = sender * capacity
        block_of = first_slot // LANES
        within = place - (first_slot - block_of * LANES)
        chosen = (within >= 0) & (index == begin + within) & (index < end)
        shift = first_slot - block_of * LANES
        here = (lane >= shift) & (lane < shift + (end - begin))
        total[block_of] = jnp.where(here, gathered(stack, chosen), total[block_of])
        amounts = jnp.where(lane == sender, end - begin, amounts)

        first_r, last_r = bound(1, 0, after), bound(1, 1, after)
        first_l, last_l = bound(2, 0, ahead), bound(0, 1, ahead)
        middle = halo_before + (last_r - first_r)
        chosen_r = (index >= first_r) & (index < last_r) & (index - first_r + halo_before == place)
        chosen_l = (index >= first_l) & (index < last_l) & (index - first_l + middle == place)
        halo_after = middle + (last_l - first_l)
        here = (lane >= halo_before) & (lane < halo_after)
        values = gathered(stack, chosen_r | chosen_l)
        total[halo_block] = jnp.where(here, values, total[halo_block])
        return halo_after, amounts

    halo_count, amounts = lax.fori_loop(
        0,
        senders,
        per_sender,
        (jnp.zeros((1, 1), I32), jnp.zeros((1, LANES), I32)),
        unroll=senders <= GROUP,
    )
    extra = [amounts, jnp.broadcast_to(halo_count, (1, LANES))]
    nowhere = float((sizes["height"] // LANES) * wide)
    for i in range(slots // LANES + 1):
        top = i * (stencil + 8)
        own_lines[top : top + stencil + 8, :], own[i * LANES : (i + 1) * LANES, :] = merge_lines(
            total[i], nowhere, stencil, extra
        )


def list_kernel(meta, recv, _, row_lines, row_data, total, **sizes):
    senders, _, hold = recv.shape
    stencil = sizes["stencil"]
    high_rows = sizes["height"] // sizes["parts"] + 2 * PAD
    place = iota((LISTED, hold), 0)
    total[...] = jnp.zeros(total.shape, F32)

    def per_sender(sender, before):
        got = Received(recv, sender, meta[0], **sizes)
        marks = got.whole[4:5, :]
        zeros = jnp.zeros((stencil, hold), F32)
        tail = jnp.concatenate([got.tail[0:1, :], zeros[0:7, :]], axis=0)
        stack = stack_of(got.rows, zeros, tail, got.back)
        values = gathered(stack, (marks > 0) & (marks - 1 + before == place))
        after = before + got.whole[7:8, hold - 1 : hold]
        slot = iota((1, LISTED), 1)
        total[...] = jnp.where((slot >= before) & (slot < after), values, total[...])
        return after

    count = lax.fori_loop(
        0, senders, per_sender, jnp.zeros((1, 1), I32), unroll=senders <= GROUP
    )
    nowhere = float((sizes["columns"] * sizes["parts"] // LANES) * high_rows)
    for i in range(LISTED // LANES):
        top = i * (stencil + 8)
        block = total[:, i * LANES : (i + 1) * LANES]
        (
            row_lines[top : top + stencil + 8, :],
            row_data[i * LANES : (i + 1) * LANES, :],
        ) = merge_lines(block, nowhere, stencil, [jnp.broadcast_to(count, (1, LANES))])


class RowCopies:
    def __init__(self, source, target, room, table, sems, stencil):
        half = 2 * BATCH * room
        self.always = pltpu.make_async_copy(
            source.at[pl.ds(0, half), :], target.at[pl.ds(0, half), :], sems[0]
        )
        size = source.shape[0] - half
        self.seldom = pltpu.make_async_copy(
            source.at[pl.ds(half, size), :], target.at[pl.ds(half, size), :], sems[1]
        )
        self.table, self.room, self.stencil = table, room, stencil

    def rest(self):
        most = word_of(self.table, 0, self.stencil + 1, self.stencil)
        for top in range(BLOCK, self.room, BLOCK):
            most = jnp.maximum(most, word_of(self.table, top, self.stencil + 1, self.stencil))
        return most > 2

    def run_rest(self):
        @pl.when(self.rest())
        def _():
            self.seldom.start()
            self.seldom.wait()


def word_of(table, slot, k, stencil):
    at = lax.shift_right_logical(slot, 7) * ((stencil + 7) * LANES) + slot
    return table[at + k * LANES]


def columns_of(info, begin, stencil):
    return [jnp.broadcast_to(info[:, begin + k : begin + k + 1], info.shape) for k in range(stencil)]


def weight_rows(info, places, stencil):
    lane_f = iota(info.shape, 1).astype(F32)
    codes = columns_of(info, CODES, stencil)
    weights = columns_of(info, stencil, stencil)
    rows = []
    for place in range(stencil):
        row = jnp.zeros(info.shape, F32)
        if place < places:
            at = lane_f + float(LANES * place)
            for k in range(place, stencil):
                row = row + jnp.where(at == codes[k], weights[k], 0.0)
        rows.append(row)
    return rows


def block_at(table, top, stencil, action):
    top = pl.multiple_of(top, 8)
    most = word_of(table, top, stencil + 1, stencil)

    @pl.when(most <= 1)
    def _():
        action(top, BATCH)

    @pl.when(most == 2)
    def _():
        action(top, 2 * BATCH)

    @pl.when(most > 2)
    def _():
        action(top, stencil)


def blocks_of(table, top, amount, stencil, action):
    def step(i, carry):
        block_at(table, top + i * BLOCK, stencil, action)
        return carry

    lax.fori_loop(0, lax.div(amount + (BLOCK - 1), BLOCK), step, 0)


def factor_kernel(
    lines_h, data, replies, _, merged_h, mixed, lines_s, table, merged, sems, *, stencil, slots
):
    parts = replies.shape[0]
    lines = slots // LANES
    lines_copy = pltpu.make_async_copy(lines_h, lines_s, sems.at[0])
    lines_copy.start()

    def per_owner(owner, carry):
        for i in range(lines):
            rows = [
                jnp.zeros((stencil, LANES), F32),
                replies[owner, pl.ds(8 + i, stencil, stride=lines), :],
                jnp.zeros((1, LANES), F32),
                replies[owner, i : i + 1, :],
                jnp.zeros((LANES - 2 * stencil - 2, LANES), F32),
            ]
            at = pl.multiple_of(owner * slots + i * LANES, LANES)
            table[pl.ds(at, LANES), :] = jnp.concatenate(rows, axis=0).T
        return carry

    lax.fori_loop(0, parts, per_owner, 0)
    lines_copy.wait()
    count = jnp.minimum(lines_s[(stencil + 3) * LANES], LISTED)

    def mix(one, two, has_two):
        for slot in (one, two):
            back = word_of(lines_s, slot, stencil + 2, stencil)
            mixed[pl.ds(slot, 1), :] = data[pl.ds(slot, 1), :] + table[pl.ds(back, 1), :]

    pairs(0, count, mix)

    def build(top, places):
        rows = weight_rows(mixed[pl.ds(top, BLOCK), :], places, stencil)
        for place, row in enumerate(rows):
            merged[pl.ds(place * LISTED + top, BLOCK), :] = row

    blocks_of(lines_s, 0, count, stencil, build)
    copies = RowCopies(
        merged, merged_h, LISTED, lines_s, (sems.at[1], sems.at[2]), stencil
    )
    copies.always.start()
    copies.run_rest()
    copies.always.wait()


def most_batches(table, slots, stencil):
    most = word_of(table, slots[0], stencil, stencil)
    for slot in slots[1:]:
        most = jnp.maximum(most, word_of(table, slot, stencil, stencil))
    return most


def scatter_slots(table, merged, room, copies, slots, values, stencil):
    def batch(begin):
        for first in range(0, len(slots), len(copies)):
            todo = []
            some = slice(first, first + len(copies))
            for slot, value, ref in zip(slots[some], values[some], copies):
                for j in range(BATCH):
                    line = word_of(table, slot, begin + j, stencil)
                    row = merged[pl.ds((begin + j) * room + slot, 1), :] * value
                    todo.append((ref, line, ref[pl.ds(line, 1), :] + row))
            for ref, line, row in todo:
                ref[pl.ds(line, 1), :] = row

    def more(i, carry):
        batch(i * BATCH)
        return carry

    batch(0)
    lax.fori_loop(1, most_batches(table, slots, stencil), more, 0)


def band(shape, taps, shift):
    distance = iota(shape, 1) - iota(shape, 0) + shift
    result = jnp.zeros(shape, F32)
    for tap in range(taps.shape[0]):
        result = jnp.where(distance == tap, taps[tap], result)
    return result


def band_rev(shape, taps, shift):
    distance = iota(shape, 0) - iota(shape, 1) + shift
    result = jnp.zeros(shape, F32)
    for tap in range(taps.shape[0]):
        result = jnp.where(distance == tap, taps[tap], result)
    return result


def exact_nt(a, b):
    return lax.dot_general(
        a,
        b,
        (((1,), (1,)), ((), ())),
        precision=lax.Precision.HIGHEST,
        preferred_element_type=F32,
    )


def store_split(ref, index, value):
    high, low = split2(value)
    ref[(0,) + index] = high
    ref[(1,) + index] = low


def bands_kernel(kx, ky, lat2, lon2, lat1, lon1, *, rows_block):
    margin = kx.shape[0] // 2
    window = lat2.shape[2]
    first = band((window, window), ky, margin)
    reach = first[LANES : LANES + WIDE, :]
    place = iota((window, window), 1)
    for variant in range(3):
        kept = first
        if variant == 0:
            kept = jnp.where(place >= LANES, first, 0.0)
        if variant == 2:
            kept = jnp.where(place < LANES + WIDE, first, 0.0)
        store_split(lat2, (variant,), exact_nt(kept, reach))
    size = lon2.shape[1]
    wide = size + 2 * HALO
    depth = (wide + 32 + LANES - 1) // LANES * LANES
    second = band((wide, depth), kx, -(16 - margin))
    store_split(lon2, (), exact_nt(second[HALO : HALO + size, :], second))
    store_split(lat1, (), band_rev((rows_block, rows_block + 2 * PAD), ky, PAD + margin))
    store_split(lon1, (), band((2 * WIDE, WIDE), kx, LANES + margin))


def pairs(low, high, action):
    def step(i, carry):
        one = low + 2 * i
        action(one, jnp.minimum(one + 1, high - 1), one + 1 < high)
        return carry

    lax.fori_loop(0, lax.shift_right_logical(high - low + 1, 1), step, 0)


def quads(low, high, action):
    def step(i, carry):
        one = low + 4 * i
        numbers = [one] + [jnp.minimum(one + j, high - 1) for j in range(1, 4)]
        weights = [None] + [jnp.where(one + j < high, 1.0, 0.0) for j in range(1, 4)]
        action(numbers, weights)
        return carry

    lax.fori_loop(0, lax.shift_right_logical(high - low + 3, 2), step, 0)


def weighted(value, weight):
    return value if weight is None else value * weight


def zero_all(refs):
    rows = refs[0].shape[0]
    step = 256

    def clear(i, carry):
        for ref in refs:
            ref[pl.ds(pl.multiple_of(i * step, 8), step), :] = jnp.zeros((step, LANES), F32)
        return carry

    whole = rows // step
    lax.fori_loop(0, whole, clear, 0)
    if rows % step:
        for ref in refs:
            ref[whole * step : rows, :] = jnp.zeros((rows % step, LANES), F32)


def scatter_entries(copies, entries, lane):
    for start in range(0, len(entries), len(copies)):
        group = []
        for ref, (address, value) in zip(copies, entries[start : start + len(copies)]):
            line = lax.shift_right_logical(address, 7)
            spread = jnp.where(lane == (address & (LANES - 1)), value, 0.0)
            group.append((ref, line, ref[pl.ds(line, 1), :] + spread))
        for ref, line, value in group:
            ref[pl.ds(line, 1), :] = value


def spot(sender, idx, per, stencil):
    return sender * per + idx + lax.shift_right_logical(idx, 7) * ((stencil - 1) * LANES)


def copy_parts(layout, source, target, place, chunk, chunks, group, sem):
    begin, size = place
    words = group * size * LANES
    at = begin * LANES + chunk * words
    return pltpu.make_async_copy(source.at[pl.ds(at, words)], target, sem)


def apply_kernel(
    *refs, first, layout, columns, height, hold, stencil, capacity, senders, parts, levels
):
    refs = list(refs)

    def take(count):
        taken = refs[:count]
        del refs[:count]
        return taken

    meta, ints, floats, own_lines, own = take(5)
    if not first:
        replies_h, replies = take(2)
    std_h, std_l_h, std_r_h, lat2_h, lon2_h = take(5)
    if not first:
        merged_h, _ = take(2)
    field_h, send = take(2)
    if first:
        info_out, merged_h = take(2)
    addr, wgt, start, lines_s, val = take(5)
    if first:
        std_flat, picked, chosen = take(3)
    scale, merged, sums, high_s, low_s, std, std_l, std_r, lat2, lon2, field = take(11)
    copies = take(PAIR)
    sems, in_sems, out_sems, val_sem = take(4)

    me = meta[0]
    wide = columns + 2 * HALO
    blocks = height // LANES
    group = min(GROUP, senders)
    chunks = senders // group
    slots = senders * capacity
    lane = iota((1, LANES), 1)
    per = stencil * hold
    table = layout.table

    def chunk_copies(chunk):
        todo = [
            (ints, addr, layout.ints["addr"]),
            (floats, wgt, layout.floats["wgt"]),
            (ints, start, layout.ints["start"]),
        ]
        if first:
            todo.append((floats, val, layout.floats["val"]))
        return [
            copy_parts(layout, source, target, place, chunk, chunks, group, sems.at[i])
            for i, (source, target, place) in enumerate(todo)
        ]

    def load_chunk(chunk):
        for copy in chunk_copies(chunk):
            copy.start()
        for copy in chunk_copies(chunk):
            copy.wait()

    operands = [
        pltpu.make_async_copy(source, target, in_sems.at[i])
        for i, (source, target) in enumerate(
            (
                (std_h, std),
                (std_l_h, std_l),
                (std_r_h, std_r),
                (lat2_h, lat2),
                (lon2_h, lon2),
            )
        )
    ]
    own_copy = pltpu.make_async_copy(own_lines, lines_s, in_sems.at[5])
    own_copy.start()
    merged_copies = RowCopies(
        *((merged, merged_h) if first else (merged_h, merged)),
        slots + LANES,
        lines_s,
        (in_sems.at[6], in_sems.at[7]),
        stencil,
    )
    if not first:
        merged_copies.always.start()
    for copy in operands:
        copy.start()

    def value_copy(owner):
        at = pl.multiple_of(owner * (replies_h.shape[0] // parts), 1024)
        return pltpu.make_async_copy(
            replies_h.at[pl.ds(at, slots)], val.at[pl.ds(owner * slots, slots)], val_sem.at[owner]
        )

    def each_owner(action):
        def step(owner, carry):
            action(value_copy(owner))
            return carry

        lax.fori_loop(0, parts, step, 0)

    if not first:
        each_owner(lambda copy: copy.start())
    zero_all(copies)
    zero_all([sums])

    lane_of = iota((slots, LANES), 1)
    room = slots + LANES
    column = 2 * stencil if first else 2 * stencil + 2
    scale[...] = jnp.broadcast_to(own[:, column : column + 1], (room, LANES))
    known = own[0:slots, :]
    own_copy.wait()
    if not first:
        merged_copies.always.wait()
        merged_copies.run_rest()

    after = lax.rem(me + 1, parts)
    ahead = lax.rem(me + parts - 1, parts)

    def start_of(sender, owner, row, half):
        return start[sender * table + row * hold + half * LANES + owner]

    def entries_of(sender, idx, value):
        base = spot(sender, idx, per, stencil)
        return [
            (addr[base + k * LANES], wgt[base + k * LANES] * value) for k in range(stencil)
        ]

    def own_line(slot, k):
        return word_of(lines_s, slot, k, stencil)

    def amount_of(sender):
        return lines_s[(stencil + 3) * LANES + sender]

    halo_count = lines_s[(stencil + 4) * LANES]
    halo_fits = halo_count <= LANES

    def own_groups(action, halo):
        if capacity % BLOCK:
            blocks_of(lines_s, 0, slots, stencil, action)
        else:

            def per_sender(sender, carry):
                blocks_of(lines_s, sender * capacity, amount_of(sender), stencil, action)
                return carry

            lax.fori_loop(0, senders, per_sender, 0)
        if halo:
            blocks_of(lines_s, slots, jnp.minimum(halo_count, LANES), stencil, action)

    def build(top, places):
        rows = weight_rows(own[pl.ds(top, BLOCK), :], places, stencil)
        for place, row in enumerate(rows):
            merged[pl.ds(place * room + top, BLOCK), :] = row

    if first:
        own_groups(build, True)
        merged_copies.always.start()
        merged_copies.run_rest()

    def own_quads(action):
        def per_sender(sender, carry):
            base = sender * capacity
            quads(base, base + amount_of(sender), action)
            return carry

        lax.fori_loop(0, senders, per_sender, 0)

    def scatter_known(numbers, weights):
        values = [weighted(scale[pl.ds(i, 1), :], w) for i, w in zip(numbers, weights)]
        scatter_slots(lines_s, merged, room, copies, numbers, values, stencil)

    def scatter_sent(numbers, weights):
        values = [weighted(val[own_line(i, stencil + 2)], w) for i, w in zip(numbers, weights)]
        scatter_slots(lines_s, merged, room, copies, numbers, values, stencil)

    def scatter_halo(chunk):
        def per_sender(sender, carry):
            for owner, low, high in ((after, (1, 0), (1, 1)), (ahead, (2, 0), (0, 1))):
                begin = start_of(sender, owner, 0, 0)

                def value_of(idx, owner=owner, begin=begin):
                    if first:
                        return val[sender * hold + idx]
                    place = (chunk * group + sender) * capacity + idx - begin
                    return val[owner * slots + place]

                def action(one, two, has_two, value_of=value_of):
                    second = jnp.where(has_two, value_of(two), 0.0)
                    scatter_entries(
                        copies,
                        entries_of(sender, one, value_of(one)) + entries_of(sender, two, second),
                        lane,
                    )

                pairs(start_of(sender, owner, *low), start_of(sender, owner, *high), action)
            return carry

        lax.fori_loop(0, group, per_sender, 0)

    own_quads(scatter_known)
    if not first:
        each_owner(lambda copy: copy.wait())

    @pl.when(halo_fits)
    def _():
        quads(slots, slots + halo_count, scatter_known if first else scatter_sent)

    @pl.when(jnp.logical_not(halo_fits))
    def _():
        def step(chunk, carry):
            load_chunk(chunk)
            scatter_halo(chunk)
            return carry

        lax.fori_loop(0, chunks, step, 0)

    for copy in operands:
        copy.wait()

    for jb in range(blocks):
        lanes = slice(jb * LANES, (jb + 1) * LANES)
        for low, size, source in (
            (0, HALO, std_l),
            (HALO, columns, std),
            (HALO + columns, HALO, std_r),
        ):
            rows = slice(jb * wide + low, jb * wide + low + size)
            total = copies[0][rows, :]
            for ref in copies[1:]:
                total = total + ref[rows, :]
            high, lo = split2(total * source[:, lanes])
            high_s[low : low + size, lanes] = high
            low_s[low : low + size, lanes] = lo
        if first:
            std_flat[jb * wide + HALO : jb * wide + HALO + columns, :] = std[:, lanes]

    smoothed = copies[0]
    size = lon2.shape[1]
    count = height // WIDE
    outgoing = [merged_copies.always] if first else []
    for block in range(count):
        variant = 0 if block == 0 else (2 if block == count - 1 else 1)
        low = max(block * WIDE - LANES, 0)
        high = min(block * WIDE + WIDE + LANES, height)
        inner = slice(low - (block * WIDE - LANES), high - (block * WIDE - LANES))
        matrix = (lat2[0, variant, inner, :], lat2[1, variant, inner, :])
        along = mm_parts((high_s[:, low:high], low_s[:, low:high]), matrix)
        parts_y = split2(along)
        lanes = slice(block * WIDE, (block + 1) * WIDE)
        for begin in range(0, columns, size):
            some = min(size, columns - begin)
            rows = slice(begin, begin + some)
            window = slice(begin, begin + some + 2 * HALO)
            matrix = tuple(lon2[i, 0:some, 0 : some + 2 * HALO] for i in range(2))
            result = mm_parts(matrix, (parts_y[0][window, :], parts_y[1][window, :]))
            scaled = result * std[rows, lanes]
            field[rows, lanes] = scaled
            for half in range(WIDE // LANES):
                top = (block * (WIDE // LANES) + half) * wide + HALO + begin
                smoothed[top : top + some, :] = scaled[:, half * LANES : (half + 1) * LANES]
        outgoing.append(
            pltpu.make_async_copy(field.at[:, lanes], field_h.at[:, lanes], out_sems.at[block])
        )
        outgoing[-1].start()

    def gather_quad(numbers, weights):
        def batch(begin, totals):
            result = []
            for slot, total in zip(numbers, totals):
                terms = []
                for j in range(BATCH):
                    line = own_line(slot, begin + j)
                    row = merged[pl.ds((begin + j) * room + slot, 1), :]
                    terms.append(row * smoothed[pl.ds(line, 1), :])
                    if first:
                        picked[pl.ds((begin + j) * room + slot, 1), :] = std_flat[
                            pl.ds(line, 1), :
                        ]
                result.append(total + ((terms[0] + terms[1]) + (terms[2] + terms[3])))
            return tuple(result)

        zero = jnp.zeros((1, LANES), F32)
        totals = lax.fori_loop(
            1,
            most_batches(lines_s, numbers, stencil),
            lambda i, totals: batch(i * BATCH, totals),
            batch(0, (zero,) * len(numbers)),
        )
        for slot, total in zip(numbers, totals):
            sums[pl.ds(slot, 1), :] = total

    own_quads(gather_quad)

    def pick(top, places):
        info = own[pl.ds(top, BLOCK), :]
        codes = columns_of(info, CODES, stencil)
        lane_f = iota(info.shape, 1).astype(F32)
        rows = [picked[pl.ds(place * room + top, BLOCK), :] for place in range(places)]
        result = jnp.zeros((BLOCK, LANES), F32)
        for k in range(stencil):
            cell = jnp.zeros((BLOCK, LANES), F32)
            for place in range(min(k + 1, places)):
                at = lane_f + float(LANES * place)
                cell = jnp.where(at == codes[k], rows[place], cell)
            cell = jnp.sum(cell, axis=1, keepdims=True)
            result = jnp.where(lane_f == float(stencil + k), cell, result)
        chosen[pl.ds(top, BLOCK), :] = result * info

    if first:
        own_groups(pick, False)

    def whole(x):
        return jnp.sum(x, axis=0, keepdims=True)

    total = jnp.sum(sums[...], axis=1, keepdims=True)
    lines = slots // LANES
    known = own[0:slots, :]
    source, weight, reply, image0 = (
        known[:, 2 * stencil + i : 2 * stencil + i + 1] for i in range(4)
    )
    if first:
        reply = weight * total
        known = jnp.where(lane_of == 2 * stencil + 2, reply, known)
        known = jnp.where(lane_of == 2 * stencil + 3, total, known)
        info_out[0:slots, :] = known
        info_out[slots:room, :] = own[slots:room, :]
        turned = known.T[2 * stencil + 2 : 2 * stencil + 3, :]
        message = [turned[:, i * LANES : (i + 1) * LANES] for i in range(lines)]
        message.append(
            jnp.where(
                lane == 0, whole(source * total), jnp.where(lane == 1, whole(reply * total), 0.0)
            )
        )
        message.append(jnp.zeros((8 - len(message), LANES), F32))
        factors = chosen[...].T
        for k in range(stencil):
            row = factors[stencil + k : stencil + k + 1, :]
            message += [row[:, i * LANES : (i + 1) * LANES] for i in range(lines)]
        message = jnp.concatenate(message, axis=0)
    else:
        slab = jnp.sum(replies[:, 0:8, :], axis=0)[lines : lines + 1, :]
        length = slab[:, 0:1] / (slab[:, 0:1] + slab[:, 1:2])
        both = source + reply
        s_both = image0 + total
        resid = source - length * both
        s_resid = image0 - length * s_both
        values = [
            resid * s_resid,
            resid * s_both,
            both * s_both,
            resid * image0,
            both * image0,
            weight * s_resid * s_resid,
            weight * s_resid * s_both,
            weight * s_both * s_both,
            weight * s_resid * image0,
            weight * s_both * image0,
            source * image0,
            reply * image0,
        ]
        message = jnp.where(lane == len(values), length, 0.0)
        for i, value in enumerate(values):
            message = jnp.where(lane == i, whole(value), message)
        message = jnp.concatenate([message, jnp.zeros((7, LANES), F32)], axis=0)

    def send_to(i, carry):
        send[i] = message
        return carry

    lax.fori_loop(0, send.shape[0], send_to, 0)
    for copy in outgoing:
        copy.wait()


def final_kernel(
    ints,
    floats,
    replies_h,
    lines_h,
    merged_h,
    mixed,
    totals,
    field0_h,
    field1_h,
    lat1,
    lon1,
    control_h,
    increment_h,
    addr,
    listed,
    slot,
    val,
    factors,
    field0,
    field1,
    control,
    high_s,
    low_s,
    lines_s,
    merged,
    scale,
    *rest,
    layout,
    hold,
    stencil,
    capacity,
    senders,
    parts,
    length,
):
    copies = rest[:PAIR]
    sems, in_sems, out_sems = rest[PAIR:]
    group = min(GROUP, senders)
    chunks = senders // group
    per = stencil * hold
    rows_block = control.shape[0]
    high_rows = rows_block + 2 * PAD
    lane = iota((1, LANES), 1)
    stride = group * capacity
    owner_words = factors.shape[0] // parts
    to_factors = owner_words - stencil * stride

    def chunk_copies(chunk):
        todo = [
            (ints, addr, layout.ints["rows"]),
            (ints, listed, layout.ints["listed"]),
            (ints, slot, layout.ints["slot"]),
            (floats, val, layout.floats["val"]),
        ]
        result = [
            copy_parts(layout, source, target, place, chunk, chunks, group, sems.at[i])
            for i, (source, target, place) in enumerate(todo)
        ]
        words = parts * owner_words
        result.append(
            pltpu.make_async_copy(
                replies_h.at[pl.ds(chunk * words, words)], factors, sems.at[len(todo)]
            )
        )
        return result

    row_copies = RowCopies(
        merged_h, merged, LISTED, lines_s, (in_sems.at[3], in_sems.at[4]), stencil
    )
    listing = [pltpu.make_async_copy(lines_h, lines_s, in_sems.at[2]), row_copies.always]
    for copy in listing:
        copy.start()
    operands = [
        pltpu.make_async_copy(source, target, in_sems.at[i])
        for i, (source, target) in enumerate(
            ((field0_h, field0), (field1_h, field1))
        )
    ]
    for copy in operands:
        copy.start()

    slabs = totals.shape[1]
    every = jnp.sum(totals[...], axis=0)
    norm0 = quad0 = None
    for i in range(slabs):
        line = every[i, 0:1, :]
        a, b = line[:, 10:11], line[:, 11:12]
        norm0 = a if norm0 is None else norm0 + a
        quad0 = b if quad0 is None else quad0 + b
    step0 = norm0 / (norm0 + quad0)
    norm1 = cross = quad1 = quad01 = jnp.zeros((1, 1), F32)
    for i in range(slabs):
        line = every[i, 0:1, :]
        v = [line[:, j : j + 1] for j in range(10)]
        shift = totals[0, i, 0:1, 12:13] - step0
        norm1 = norm1 + (v[0] + shift * (2.0 * v[1] + shift * v[2]))
        cross = cross + (v[3] + shift * v[4])
        quad1 = quad1 + (v[5] + shift * (2.0 * v[6] + shift * v[7]))
        quad01 = quad01 + (v[8] + shift * v[9])
    ratio = norm1 / norm0
    curvature = norm1 + quad1 + ratio * (
        2.0 * (cross + quad01) + ratio * (norm0 + quad0)
    )
    step1 = norm1 / curvature
    first = step0 + step1 * (1.0 - step0 + ratio)
    second = -step0 * step1
    first_line = jnp.broadcast_to(first, (1, LANES))
    second_line = jnp.broadcast_to(second, (1, LANES))

    zero_all(copies)

    data = mixed[...]
    column = 2 * stencil
    scale[...] = first * data[:, column : column + 1] + second * jnp.broadcast_to(
        data[:, column + 1 : column + 2], data.shape
    )
    for copy in listing:
        copy.wait()
    row_copies.run_rest()
    count = lines_s[(stencil + 3) * LANES]

    def add(numbers, weights):
        values = [weighted(scale[pl.ds(i, 1), :], w) for i, w in zip(numbers, weights)]
        scatter_slots(lines_s, merged, LISTED, copies, numbers, values, stencil)

    def scatter_chunk():
        def per_sender(sender, carry):
            def step(idx, inner):
                @pl.when(listed[sender * hold + idx] > 0)
                def _():
                    place = slot[sender * hold + idx]
                    place = place + lax.div(place, stride) * (owner_words - stride)
                    base = spot(sender, idx, per, stencil)
                    z0 = val[sender * hold + idx]
                    value = first_line * z0 + second_line * factors[place]
                    entries = [
                        (addr[base + k * LANES], factors[place + to_factors + k * stride] * value)
                        for k in range(stencil)
                    ]
                    scatter_entries(copies, entries, lane)

                return inner

            lax.fori_loop(0, hold, step, 0)
            return carry

        lax.fori_loop(0, group, per_sender, 0)

    @pl.when(count <= LISTED)
    def _():
        quads(0, count, add)

    @pl.when(count > LISTED)
    def _():
        def step(chunk, carry):
            for copy in chunk_copies(chunk):
                copy.start()
            for copy in chunk_copies(chunk):
                copy.wait()
            scatter_chunk()
            return carry

        lax.fori_loop(0, chunks, step, 0)

    for copy in operands:
        copy.wait()
    increment = field0
    increment[...] = first * field0[...] + second * field1[...]
    outgoing = [pltpu.make_async_copy(increment, increment_h, out_sems.at[0])]
    outgoing[0].start()

    pair = WIDE // LANES
    count = length // WIDE
    for block in range(count):
        pieces = []
        for half in range(pair):
            rows = slice((block * pair + half) * high_rows, (block * pair + half + 1) * high_rows)
            total = copies[0][rows, :]
            for ref in copies[1:]:
                total = total + ref[rows, :]
            pieces.append(total)
        whole = split2(jnp.concatenate(pieces, axis=1))
        size = lat1.shape[1]
        for top in range(0, rows_block, size):
            window = slice(top, top + size + 2 * PAD)
            along = mm_parts((lat1[0], lat1[1]), (whole[0][window, :], whole[1][window, :]))
            high, low = split2(along)
            high_s[top : top + size, block * WIDE : (block + 1) * WIDE] = high
            low_s[top : top + size, block * WIDE : (block + 1) * WIDE] = low

    def window(ref, block):
        low, high = block * WIDE - LANES, (block + 1) * WIDE + LANES
        if low < 0:
            return jnp.concatenate([ref[:, length + low : length], ref[:, 0:high]], axis=1)
        if high > length:
            return jnp.concatenate([ref[:, low:length], ref[:, 0 : high - length]], axis=1)
        return ref[:, low:high]

    every_lanes = 4
    for block in range(count):
        control[:, block * WIDE : (block + 1) * WIDE] = mm_parts(
            (window(high_s, block), window(low_s, block)), (lon1[0], lon1[1])
        )
        if block % every_lanes == every_lanes - 1:
            lanes = slice((block + 1 - every_lanes) * WIDE, (block + 1) * WIDE)
            outgoing.append(
                pltpu.make_async_copy(
                    control.at[:, lanes], control_h.at[:, lanes], out_sems.at[len(outgoing)]
                )
            )
            outgoing[-1].start()
    for copy in outgoing:
        copy.wait()


def body(
    background_std,
    x_kernel,
    y_kernel,
    obs_owner,
    obs_cells,
    obs_weights,
    innovation,
    obs_precision,
    obs_counts,
):
    parts = lax.axis_size("pencil")
    levels = lax.axis_size("lev")
    me = lax.axis_index("pencil")
    _, columns, height = background_std.shape
    hold, stencil = obs_cells.shape
    margin = x_kernel.shape[1] // 2
    capacity = 2 * hold // parts
    senders = parts
    slots = senders * capacity
    room = slots + LANES
    rows_block = height // parts
    length = columns * parts
    blocks = height // LANES
    wide = columns + 2 * HALO
    group = min(GROUP, senders)
    chunks = senders // group
    layout = Layout(senders, hold, stencil, parts)
    std = background_std[0]

    packed = pl.pallas_call(
        functools.partial(
            pack_kernel, parts=parts, columns=columns, height=height, margin=margin
        ),
        out_shape=jax.ShapeDtypeStruct((parts, PACK, hold), F32),
        in_specs=[smem()] + [vmem()] * 5,
        out_specs=vmem(),
        scratch_shapes=[pltpu.VMEM((parts, hold), F32)],
        compiler_params=params(),
        cost_estimate=cost(12000),
        name="pack",
    )(
        obs_counts,
        obs_owner.T,
        obs_cells.T,
        obs_weights.T,
        innovation[None, :],
        obs_precision[None, :],
    )
    recv = lax.all_to_all(packed, "pencil", split_axis=0, concat_axis=0, tiled=True)

    right_of = [(p, (p + 1) % parts) for p in range(parts)]
    left_of = [(p, (p - 1) % parts) for p in range(parts)]
    std_l = lax.ppermute(std[columns - HALO :, :], "pencil", right_of)
    std_r = lax.ppermute(std[:HALO, :], "pencil", left_of)

    size = min(columns, WIDE - 2 * HALO)
    row_size = min(rows_block, LANES)
    lat2, lon2, lat1, lon1 = pl.pallas_call(
        functools.partial(bands_kernel, rows_block=row_size),
        out_shape=[
            jax.ShapeDtypeStruct((2, 3, 2 * WIDE, WIDE), BF),
            jax.ShapeDtypeStruct((2, size, size + 2 * HALO), BF),
            jax.ShapeDtypeStruct((2, row_size, row_size + 2 * PAD), BF),
            jax.ShapeDtypeStruct((2, 2 * WIDE, WIDE), BF),
        ],
        in_specs=[smem(), smem()],
        out_specs=[vmem()] * 4,
        compiler_params=params(),
        cost_estimate=cost(100),
        name="bands",
    )(x_kernel[0], y_kernel[0])

    meta = jnp.reshape(me, (1,)).astype(I32)
    place = dict(
        parts=parts, columns=columns, height=height, capacity=capacity, stencil=stencil
    )
    ints, floats, own_lines, own = pl.pallas_call(
        functools.partial(unpack_kernel, layout=layout, group=group, **place),
        out_shape=[
            jax.ShapeDtypeStruct((layout.int_rows, LANES), I32),
            jax.ShapeDtypeStruct((layout.float_rows, LANES), F32),
            jax.ShapeDtypeStruct((room // LANES * (stencil + 8), LANES), I32),
            jax.ShapeDtypeStruct((room, LANES), F32),
        ],
        in_specs=[smem(), vmem(), hbm()],
        out_specs=[vmem()] * 4,
        scratch_shapes=[
            pltpu.VMEM((room // LANES, STACK, LANES), F32),
        ],
        compiler_params=params(),
        cost_estimate=cost(100),
        name="unpack",
    )(meta, recv, lat1)
    ints = ints.reshape(-1)
    floats = floats.reshape(-1)
    own_lines = own_lines.reshape(-1)

    acc = pltpu.VMEM((blocks * wide + 8, LANES), F32)
    column_slots = pltpu.VMEM((slots, LANES), F32)
    static = dict(
        layout=layout,
        columns=columns,
        height=height,
        hold=hold,
        stencil=stencil,
        capacity=capacity,
        senders=senders,
        parts=parts,
        levels=levels,
    )
    per = group * stencil * hold
    line = group * hold
    index_scratch = [
        pltpu.SMEM((per,), I32),
        pltpu.SMEM((per,), F32),
        pltpu.SMEM((group * layout.table,), I32),
        pltpu.SMEM((room * (stencil + 8),), I32),
    ]
    work = (
        [
            pltpu.VMEM((room, LANES), F32),
            pltpu.VMEM((stencil * room, LANES), F32),
            column_slots,
        ]
        + [pltpu.VMEM((wide, height), BF)] * 2
        + [
            pltpu.VMEM((columns, height), F32),
            pltpu.VMEM((HALO, height), F32),
            pltpu.VMEM((HALO, height), F32),
            pltpu.VMEM(lat2.shape, BF),
            pltpu.VMEM(lon2.shape, BF),
            pltpu.VMEM((columns, height), F32),
        ]
        + [acc] * PAIR
        + [
            pltpu.SemaphoreType.DMA((4,)),
            pltpu.SemaphoreType.DMA((8,)),
            pltpu.SemaphoreType.DMA((height // WIDE,)),
            pltpu.SemaphoreType.DMA((parts,)),
        ]
    )
    field_shape = jax.ShapeDtypeStruct((columns, height), F32)
    reply_rows = 8 + stencil * slots // LANES
    field0, message, info, merged = pl.pallas_call(
        functools.partial(apply_kernel, first=True, **static),
        out_shape=[
            field_shape,
            jax.ShapeDtypeStruct((parts, reply_rows, LANES), F32),
            jax.ShapeDtypeStruct((room, LANES), F32),
            jax.ShapeDtypeStruct((stencil * room, LANES), F32),
        ],
        in_specs=[smem()] + [hbm()] * 3 + [vmem()] + [hbm()] * 5,
        out_specs=[hbm()] + [vmem()] * 2 + [hbm()],
        scratch_shapes=index_scratch
        + [
            pltpu.SMEM((line,), F32),
            acc,
            pltpu.VMEM((stencil * room, LANES), F32),
            column_slots,
        ]
        + work,
        compiler_params=params(),
        name="apply_first",
    )(meta, ints, floats, own_lines, own, std, std_l, std_r, lat2, lon2)

    replies = lax.all_to_all(message, "pencil", split_axis=0, concat_axis=0, tiled=True)
    back = replies.reshape(-1)
    line_rows = LISTED // LANES * (stencil + 8)
    row_lines, row_data = pl.pallas_call(
        functools.partial(list_kernel, **place),
        out_shape=[
            jax.ShapeDtypeStruct((line_rows, LANES), I32),
            jax.ShapeDtypeStruct((LISTED, LANES), F32),
        ],
        in_specs=[smem(), vmem(), hbm()],
        out_specs=[vmem()] * 2,
        scratch_shapes=[pltpu.VMEM((STACK, LISTED), F32)],
        compiler_params=params(),
        cost_estimate=cost(4000),
        name="list_rows",
    )(meta, recv, info)
    row_lines = row_lines.reshape(-1)

    field1, sums = pl.pallas_call(
        functools.partial(apply_kernel, first=False, **static),
        out_shape=[
            field_shape,
            jax.ShapeDtypeStruct((parts * levels, 8, LANES), F32),
        ],
        in_specs=[smem()] + [hbm()] * 3 + [vmem(), hbm(), vmem()] + [hbm()] * 7,
        out_specs=[hbm(), vmem()],
        scratch_shapes=index_scratch + [pltpu.SMEM((parts * slots,), F32)] + work,
        compiler_params=params(),
        name="apply_second",
    )(
        meta,
        ints,
        floats,
        own_lines,
        info,
        back,
        replies,
        std,
        std_l,
        std_r,
        lat2,
        lon2,
        merged,
        row_data,
    )

    totals = lax.all_to_all(sums, ("pencil", "lev"), split_axis=0, concat_axis=0, tiled=True)
    totals = totals.reshape(parts, levels, 8, LANES)

    listed_rows, mixed = pl.pallas_call(
        functools.partial(factor_kernel, stencil=stencil, slots=slots),
        out_shape=[
            jax.ShapeDtypeStruct((stencil * LISTED, LANES), F32),
            jax.ShapeDtypeStruct((LISTED, LANES), F32),
        ],
        in_specs=[hbm(), vmem(), vmem(), hbm()],
        out_specs=[hbm(), vmem()],
        scratch_shapes=[
            pltpu.SMEM((line_rows * LANES,), I32),
            pltpu.VMEM((parts * slots, LANES), F32),
            pltpu.VMEM((stencil * LISTED, LANES), F32),
            pltpu.SemaphoreType.DMA((3,)),
        ],
        compiler_params=params(),
        cost_estimate=cost(8000),
        name="factor_rows",
    )(row_lines, row_data, replies, sums)

    by_chunk = back
    if chunks > 1:
        by_chunk = jnp.concatenate(
            [replies[:, : slots // LANES, :], replies[:, 8:, :]], axis=1
        ).reshape(parts, stencil + 1, chunks, group * capacity)
        by_chunk = jnp.transpose(by_chunk, (2, 0, 1, 3)).reshape(-1)
    owner_words = by_chunk.shape[0] // (chunks * parts)
    high_rows = rows_block + 2 * PAD
    acc_rows = pltpu.VMEM(((length // LANES) * high_rows + 8, LANES), F32)
    control, increment = pl.pallas_call(
        functools.partial(
            final_kernel,
            layout=layout,
            hold=hold,
            stencil=stencil,
            capacity=capacity,
            senders=senders,
            parts=parts,
            length=length,
        ),
        out_shape=[
            jax.ShapeDtypeStruct((rows_block, length), F32),
            field_shape,
        ],
        in_specs=[hbm()] * 5 + [vmem()] * 2 + [hbm()] * 2 + [vmem()] * 2,
        out_specs=[hbm()] * 2,
        scratch_shapes=[
            pltpu.SMEM((per,), I32),
            pltpu.SMEM((line,), I32),
            pltpu.SMEM((line,), I32),
            pltpu.SMEM((line,), F32),
            pltpu.SMEM((parts * owner_words,), F32),
            pltpu.VMEM((columns, height), F32),
            pltpu.VMEM((columns, height), F32),
            pltpu.VMEM((rows_block, length), F32),
            pltpu.VMEM((rows_block, length), BF),
            pltpu.VMEM((rows_block, length), BF),
            pltpu.SMEM((line_rows * LANES,), I32),
            pltpu.VMEM((stencil * LISTED, LANES), F32),
            pltpu.VMEM((LISTED, LANES), F32),
        ]
        + [acc_rows] * PAIR
        + [
            pltpu.SemaphoreType.DMA((5,)),
            pltpu.SemaphoreType.DMA((5,)),
            pltpu.SemaphoreType.DMA((1 + length // WIDE,)),
        ],
        compiler_params=params(),
        name="outputs",
    )(
        ints,
        floats,
        by_chunk,
        row_lines,
        listed_rows,
        mixed,
        totals,
        field0,
        field1,
        lat1,
        lon1,
    )
    return control[None], increment[None]


def solution(mesh):
    return jax.shard_map(
        body,
        mesh=mesh,
        in_specs=(
            P("lev", "pencil", None),
            P("lev", None),
            P("lev", None),
            P(("pencil", "lev"), None),
            P(("pencil", "lev"), None),
            P(("pencil", "lev"), None),
            P(("pencil", "lev")),
            P(("pencil", "lev")),
            P(("pencil", "lev")),
        ),
        out_specs=(P("lev", "pencil", None), P("lev", "pencil", None)),
        check_vma=False,
    )
```

```python
import functools

import jax
import jax.numpy as jnp
import numpy as np
from jax import lax
from jax.experimental import pallas as pl
from jax.experimental.pallas import tpu as pltpu
from jax.sharding import PartitionSpec as P


BF = jnp.bfloat16
F32 = jnp.float32
I32 = jnp.int32
LANES = 128
WIDE = 256
HALO = 32
PAD = 16
PACK = 40
GROUP = 8
PAIR = 2
BATCH = 4
BLOCK = 32
CODES = 40
STACK = 64
LISTED = 512
VMEM_LIMIT = 58 * 1024 * 1024


def vmem():
    return pl.BlockSpec(memory_space=pltpu.VMEM)


def smem():
    return pl.BlockSpec(memory_space=pltpu.SMEM)


def hbm():
    return pl.BlockSpec(memory_space=pltpu.HBM)


def cost(nanoseconds):
    return pl.CostEstimate(flops=0, bytes_accessed=3690 * nanoseconds, transcendentals=0)


def params():
    return pltpu.CompilerParams(vmem_limit_bytes=VMEM_LIMIT)


def split2(x):
    high = x.astype(BF)
    return high, (x - high.astype(F32)).astype(BF)


def split3(x):
    high = x.astype(BF)
    rest = x - high.astype(F32)
    mid = rest.astype(BF)
    return high, mid, (rest - mid.astype(F32)).astype(BF)


def mm(a, b):
    return jnp.dot(a, b, preferred_element_type=F32)


def mm_parts(a_parts, b_parts):
    (ah, al), (bh, bl) = a_parts, b_parts
    return mm(jnp.concatenate([ah, al, ah], axis=1), jnp.concatenate([bh, bh, bl], axis=0))


def iota(shape, dim):
    return lax.broadcasted_iota(I32, shape, dim)


def pack_kernel(
    counts,
    owner,
    cells,
    weights,
    depart,
    prec,
    std,
    out,
    low_edge,
    high_edge,
    marks,
    sems,
    *,
    parts,
    columns,
    height,
    margin,
):
    stencil, hold = cells.shape
    edges = [
        pltpu.make_async_copy(std.at[pl.ds(0, HALO), :], low_edge, sems.at[0]),
        pltpu.make_async_copy(std.at[pl.ds(columns - HALO, HALO), :], high_edge, sems.at[1]),
    ]
    for copy in edges:
        copy.start()
    shift = height.bit_length() - 1
    block = height // parts
    reach = 2 * margin
    row_id = iota((hold, hold), 0)
    col_id = iota((hold, hold), 1)
    eye = row_id == col_id
    col_f = col_id.astype(F32)
    live = iota((1, hold), 1) < counts[0]
    cell = cells[...]
    column = lax.shift_right_logical(cell, jnp.full(cell.shape, shift, I32))
    row = cell & (height - 1)

    def any_of(mask):
        return jnp.max(jnp.where(mask, 1.0, 0.0), axis=0, keepdims=True)

    def turn(line):
        return jnp.sum(jnp.where(eye, line, 0.0), axis=1, keepdims=True)

    left = any_of(column < reach)
    right = any_of(column >= columns - reach)
    side = left + 3.0 * right - 2.0 * left * right
    base = jnp.where(live, owner[...].astype(F32) * 4.0, 4.0 * parts)
    key = jnp.where(live, base + side, base)
    key_col = turn(key)
    before = (key_col < key) | ((key_col == key) & (row_id < col_id))
    rank = jnp.sum(jnp.where(before, 1.0, 0.0), axis=0, keepdims=True)
    begin = jnp.sum(jnp.where(key_col < base, 1.0, 0.0), axis=0, keepdims=True)
    rank_col = turn(rank)
    perm = jnp.where(rank_col == col_f, 1.0, 0.0).astype(BF)

    def sort(values):
        total = None
        for part in split3(values):
            term = mm(part, perm)
            total = term if total is None else total + term
        return total

    weight = jnp.where(live, prec[...], 0.0)
    rest = [weight * depart[...], weight, key, rank - begin, jnp.zeros((4, hold), F32)]
    values = [cell.astype(F32), weights[...]] + rest
    ordered = sort(jnp.concatenate(values, axis=0))
    line = iota((8, hold), 0)
    tail = ordered[2 * stencil : 2 * stencil + 8, :]
    first_half = col_f < float(LANES)
    fourfold = 4.0 * jnp.where(first_half, col_f, col_f - float(LANES))
    for i, (low, high) in enumerate(((0.0, 4.0), (1.0, 3.0), (2.0, 2.0))):
        bound = fourfold + jnp.where(first_half, low, high)
        begins = jnp.sum(jnp.where(key_col < bound, 1.0, 0.0), axis=0, keepdims=True)
        tail = jnp.where(line == 5 + i, begins, tail)
    last = (line == 7) & (iota((8, hold), 1) == hold - 1)

    def mark(part, carry):
        low = part * block - margin
        high = (part + 1) * block + margin
        flag = jnp.where(live, any_of((row >= low) & (row < high)), 0.0)
        place = jnp.sum(jnp.where(row_id < col_id, turn(flag), 0.0), axis=0, keepdims=True)
        marks[pl.ds(part, 1), :] = flag * (place + 1.0)
        return carry

    lax.fori_loop(0, parts, mark, 0, unroll=parts <= GROUP)
    listed = marks[...]
    amounts = jnp.max(listed, axis=1, keepdims=True)
    listed = mm(listed.astype(BF), perm)
    for part in range(parts):
        out[part, 0 : 2 * stencil, :] = ordered[0 : 2 * stencil, :]
        out[part, 2 * stencil : 2 * stencil + 8, :] = jnp.where(
            line == 4,
            listed[part : part + 1, :],
            jnp.where(last, amounts[part : part + 1, :], tail),
        )
    for copy in edges:
        copy.wait()


class Layout:
    def __init__(self, senders, hold, stencil, parts):
        lines = hold // LANES
        self.table = 3 * hold
        sizes = dict(
            addr=stencil * lines, rows=stencil * lines, listed=lines, slot=lines, start=3 * lines
        )
        self.ints = {}
        at = 0
        for name, size in sizes.items():
            self.ints[name] = (at, size)
            at += senders * size
        self.int_rows = at
        self.floats = {}
        at = 0
        for name, size in dict(wgt=stencil * lines, val=lines).items():
            self.floats[name] = (at, size)
            at += senders * size
        self.float_rows = at


def right(x, by):
    return lax.shift_right_logical(x, jnp.full(x.shape, by, I32))


def nt(a, b):
    return lax.dot_general(a, b, (((1,), (1,)), ((), ())), preferred_element_type=F32)


class Received:
    def __init__(self, recv, sender, me, *, parts, columns, height, capacity, stencil):
        senders, _, hold = recv.shape
        wide = columns + 2 * HALO
        block = height // parts
        high_rows = block + 2 * PAD
        cell = recv[sender, 0:stencil, :].astype(I32)
        self.tail = recv[sender, 2 * stencil : 2 * stencil + 8, :]
        self.whole = self.tail.astype(I32)
        self.pos = self.whole[3:4, :]
        owner = right(self.whole[2:3, :], 2)
        offset = owner - me
        offset = jnp.where(offset > parts // 2, offset - parts, offset)
        offset = jnp.where(offset < -(parts // 2), offset + parts, offset)
        column = right(cell, height.bit_length() - 1)
        row = cell & (height - 1)
        at = offset * columns + column + HALO
        self.addr = jnp.where(
            (at >= 0) & (at < wide),
            (right(row, 7) * wide + at) * LANES + (row & (LANES - 1)),
            (height // LANES) * wide * LANES,
        )
        at_row = row - (block * me - PAD)
        across = owner * columns + column
        self.rows = jnp.where(
            (at_row >= 0) & (at_row < high_rows) & (owner < parts),
            (right(across, 7) * high_rows + at_row) * LANES + (across & (LANES - 1)),
            (columns * parts // LANES) * high_rows * LANES,
        )
        self.owner = jnp.minimum(owner, parts - 1)
        self.back = self.owner * (senders * capacity) + sender * capacity + self.pos


def stack_of(addr, weights, tail, back):
    hold = addr.shape[1]
    rows = [
        (addr & (LANES - 1)).astype(F32),
        weights,
        tail,
        right(addr, 7).astype(F32),
        back.astype(F32),
        jnp.zeros((7, hold), F32),
    ]
    return jnp.concatenate(split3(jnp.concatenate(rows, axis=0)), axis=1)


def gathered(stack, chosen):
    select = jnp.where(chosen, 1.0, 0.0).astype(BF)
    return nt(stack, jnp.concatenate([select] * 3, axis=1))


def merge_lines(block, nowhere, stencil, extra):
    number = iota((stencil, LANES), 0).astype(F32)
    line = block[CODES : CODES + stencil, :]
    leader = jnp.zeros(line.shape, F32)
    for k in reversed(range(stencil)):
        leader = jnp.where(line == line[k : k + 1, :], float(k), leader)
    leads = jnp.where(leader == number, 1.0, 0.0)
    count = jnp.zeros((1, LANES), F32)
    ranks = []
    for k in range(stencil):
        ranks.append(count)
        count = count + leads[k : k + 1, :]
    place = jnp.zeros(line.shape, F32)
    for k in range(stencil):
        place = jnp.where(leader == float(k), ranks[k], place)
    lists = []
    for k in range(stencil):
        found = jnp.where((leads > 0.0) & (place == float(k)), line, 0.0)
        found = jnp.sum(found, axis=0, keepdims=True)
        lists.append(jnp.where(count > float(k), found, nowhere))
    batches = right(count.astype(I32) + (BATCH - 1), BATCH.bit_length() - 1)
    most = jnp.zeros((1, LANES), F32)
    slot = iota((1, LANES), 1)
    for begin in range(0, LANES, BLOCK):
        here = (slot >= begin) & (slot < begin + BLOCK)
        found = jnp.max(jnp.where(here, batches.astype(F32), 0.0), axis=1, keepdims=True)
        most = jnp.where(here, found, most)
    back = block[CODES + stencil : CODES + stencil + 1, :]
    ints = [jnp.concatenate(lists, axis=0).astype(I32), batches]
    ints += [most.astype(I32), back.astype(I32)] + extra
    ints = jnp.concatenate(ints, axis=0)
    ints = jnp.concatenate([ints, jnp.zeros((stencil + 8 - ints.shape[0], LANES), I32)], axis=0)
    rows = [
        block[0:CODES, :],
        place * float(LANES) + block[0:stencil, :],
        jnp.zeros((LANES - CODES - stencil, LANES), F32),
    ]
    return ints, jnp.concatenate(rows, axis=0).T


def unpack_kernel(
    meta, recv, _, ints, floats, own_lines, own, total, *, layout, group, **sizes
):
    senders, _, hold = recv.shape
    lines = hold // LANES
    me = meta[0]
    parts, stencil, capacity = sizes["parts"], sizes["stencil"], sizes["capacity"]
    wide = sizes["columns"] + 2 * HALO
    slots = senders * capacity

    def put(ref, place, sender, value):
        begin, size = place
        count = value.shape[0]
        for i in range(lines):
            part = value[:, i * LANES : (i + 1) * LANES]
            if count % 8 == 0:
                at = pl.multiple_of(begin + sender * size + i * count, 8)
                ref[pl.ds(at, count), :] = part
            else:
                for j in range(count):
                    ref[pl.ds(begin + sender * size + i + j * lines, 1), :] = part[j : j + 1]

    total[...] = jnp.zeros(total.shape, F32)
    place = iota((LANES, hold), 0)
    index = iota((LANES, hold), 1)
    lane = iota((1, LANES), 1)
    halo_block = slots // LANES
    after = lax.rem(me + 1, parts)
    ahead = lax.rem(me + parts - 1, parts)

    def per_sender(sender, carry):
        halo_before, amounts = carry
        got = Received(recv, sender, me, **sizes)
        weights = recv[sender, stencil : 2 * stencil, :]
        within = lax.rem(sender, group) * capacity + got.pos
        put(ints, layout.ints["addr"], sender, got.addr)
        put(ints, layout.ints["rows"], sender, got.rows)
        put(ints, layout.ints["listed"], sender, got.whole[4:5, :])
        put(ints, layout.ints["slot"], sender, got.owner * (group * capacity) + within)
        put(ints, layout.ints["start"], sender, got.whole[5:8, :])
        put(floats, layout.floats["wgt"], sender, weights)
        put(floats, layout.floats["val"], sender, got.tail[0:1, :])

        def bound(line, half, owner):
            part = got.whole[5 + line : 6 + line, half * LANES : (half + 1) * LANES]
            return jnp.sum(jnp.where(lane == owner, part, 0), axis=1, keepdims=True)

        stack = stack_of(got.addr, weights, got.tail, got.back)

        begin, end = bound(0, 0, me), bound(0, 1, me)
        first_slot = sender * capacity
        block_of = first_slot // LANES
        within = place - (first_slot - block_of * LANES)
        chosen = (within >= 0) & (index == begin + within) & (index < end)
        shift = first_slot - block_of * LANES
        here = (lane >= shift) & (lane < shift + (end - begin))
        total[block_of] = jnp.where(here, gathered(stack, chosen), total[block_of])
        amounts = jnp.where(lane == sender, end - begin, amounts)

        first_r, last_r = bound(1, 0, after), bound(1, 1, after)
        first_l, last_l = bound(2, 0, ahead), bound(0, 1, ahead)
        middle = halo_before + (last_r - first_r)
        chosen_r = (index >= first_r) & (index < last_r) & (index - first_r + halo_before == place)
        chosen_l = (index >= first_l) & (index < last_l) & (index - first_l + middle == place)
        halo_after = middle + (last_l - first_l)
        here = (lane >= halo_before) & (lane < halo_after)
        values = gathered(stack, chosen_r | chosen_l)
        total[halo_block] = jnp.where(here, values, total[halo_block])
        return halo_after, amounts

    halo_count, amounts = lax.fori_loop(
        0,
        senders,
        per_sender,
        (jnp.zeros((1, 1), I32), jnp.zeros((1, LANES), I32)),
        unroll=senders <= GROUP,
    )
    extra = [amounts, jnp.broadcast_to(halo_count, (1, LANES))]
    nowhere = float((sizes["height"] // LANES) * wide)
    for i in range(slots // LANES + 1):
        top = i * (stencil + 8)
        own_lines[top : top + stencil + 8, :], own[i * LANES : (i + 1) * LANES, :] = merge_lines(
            total[i], nowhere, stencil, extra
        )


def list_kernel(meta, recv, _, row_lines, row_data, total, **sizes):
    senders, _, hold = recv.shape
    stencil = sizes["stencil"]
    high_rows = sizes["height"] // sizes["parts"] + 2 * PAD
    place = iota((LISTED, hold), 0)
    total[...] = jnp.zeros(total.shape, F32)

    def per_sender(sender, before):
        got = Received(recv, sender, meta[0], **sizes)
        marks = got.whole[4:5, :]
        zeros = jnp.zeros((stencil, hold), F32)
        tail = jnp.concatenate([got.tail[0:1, :], zeros[0:7, :]], axis=0)
        stack = stack_of(got.rows, zeros, tail, got.back)
        values = gathered(stack, (marks > 0) & (marks - 1 + before == place))
        after = before + got.whole[7:8, hold - 1 : hold]
        slot = iota((1, LISTED), 1)
        total[...] = jnp.where((slot >= before) & (slot < after), values, total[...])
        return after

    count = lax.fori_loop(
        0, senders, per_sender, jnp.zeros((1, 1), I32), unroll=senders <= GROUP
    )
    nowhere = float((sizes["columns"] * sizes["parts"] // LANES) * high_rows)
    for i in range(LISTED // LANES):
        top = i * (stencil + 8)
        block = total[:, i * LANES : (i + 1) * LANES]
        (
            row_lines[top : top + stencil + 8, :],
            row_data[i * LANES : (i + 1) * LANES, :],
        ) = merge_lines(block, nowhere, stencil, [jnp.broadcast_to(count, (1, LANES))])


class RowCopies:
    def __init__(self, source, target, room, table, sems, stencil):
        half = 2 * BATCH * room
        self.always = pltpu.make_async_copy(
            source.at[pl.ds(0, half), :], target.at[pl.ds(0, half), :], sems[0]
        )
        size = source.shape[0] - half
        self.seldom = pltpu.make_async_copy(
            source.at[pl.ds(half, size), :], target.at[pl.ds(half, size), :], sems[1]
        )
        self.table, self.room, self.stencil = table, room, stencil

    def rest(self):
        most = word_of(self.table, 0, self.stencil + 1, self.stencil)
        for top in range(BLOCK, self.room, BLOCK):
            most = jnp.maximum(most, word_of(self.table, top, self.stencil + 1, self.stencil))
        return most > 2

    def run_rest(self):
        @pl.when(self.rest())
        def _():
            self.seldom.start()
            self.seldom.wait()


def word_of(table, slot, k, stencil):
    at = lax.shift_right_logical(slot, 7) * ((stencil + 7) * LANES) + slot
    return table[at + k * LANES]


def columns_of(info, begin, stencil):
    return [jnp.broadcast_to(info[:, begin + k : begin + k + 1], info.shape) for k in range(stencil)]


def weight_rows(info, places, stencil):
    lane_f = iota(info.shape, 1).astype(F32)
    codes = columns_of(info, CODES, stencil)
    weights = columns_of(info, stencil, stencil)
    rows = []
    for place in range(stencil):
        row = jnp.zeros(info.shape, F32)
        if place < places:
            at = lane_f + float(LANES * place)
            for k in range(place, stencil):
                row = row + jnp.where(at == codes[k], weights[k], 0.0)
        rows.append(row)
    return rows


def block_at(table, top, stencil, action):
    top = pl.multiple_of(top, 8)
    most = word_of(table, top, stencil + 1, stencil)

    @pl.when(most <= 1)
    def _():
        action(top, BATCH)

    @pl.when(most == 2)
    def _():
        action(top, 2 * BATCH)

    @pl.when(most > 2)
    def _():
        action(top, stencil)


def blocks_of(table, top, amount, stencil, action):
    def step(i, carry):
        block_at(table, top + i * BLOCK, stencil, action)
        return carry

    lax.fori_loop(0, lax.div(amount + (BLOCK - 1), BLOCK), step, 0)


def factor_kernel(
    lines_h, data, replies, _, merged_h, mixed, lines_s, table, merged, sems, *, stencil, slots
):
    parts = replies.shape[0]
    lines = slots // LANES
    lines_copy = pltpu.make_async_copy(lines_h, lines_s, sems.at[0])
    lines_copy.start()

    def per_owner(owner, carry):
        for i in range(lines):
            rows = [
                jnp.zeros((stencil, LANES), F32),
                replies[owner, pl.ds(8 + i, stencil, stride=lines), :],
                jnp.zeros((1, LANES), F32),
                replies[owner, i : i + 1, :],
                jnp.zeros((LANES - 2 * stencil - 2, LANES), F32),
            ]
            at = pl.multiple_of(owner * slots + i * LANES, LANES)
            table[pl.ds(at, LANES), :] = jnp.concatenate(rows, axis=0).T
        return carry

    lax.fori_loop(0, parts, per_owner, 0)
    lines_copy.wait()
    count = jnp.minimum(lines_s[(stencil + 3) * LANES], LISTED)

    def mix(one, two, has_two):
        for slot in (one, two):
            back = word_of(lines_s, slot, stencil + 2, stencil)
            mixed[pl.ds(slot, 1), :] = data[pl.ds(slot, 1), :] + table[pl.ds(back, 1), :]

    pairs(0, count, mix)

    def build(top, places):
        rows = weight_rows(mixed[pl.ds(top, BLOCK), :], places, stencil)
        for place, row in enumerate(rows):
            merged[pl.ds(place * LISTED + top, BLOCK), :] = row

    blocks_of(lines_s, 0, count, stencil, build)
    copies = RowCopies(
        merged, merged_h, LISTED, lines_s, (sems.at[1], sems.at[2]), stencil
    )
    copies.always.start()
    copies.run_rest()
    copies.always.wait()


def most_batches(table, slots, stencil):
    most = word_of(table, slots[0], stencil, stencil)
    for slot in slots[1:]:
        most = jnp.maximum(most, word_of(table, slot, stencil, stencil))
    return most


def scatter_slots(table, merged, room, copies, slots, values, stencil):
    def batch(begin):
        for first in range(0, len(slots), len(copies)):
            todo = []
            some = slice(first, first + len(copies))
            for slot, value, ref in zip(slots[some], values[some], copies):
                for j in range(BATCH):
                    line = word_of(table, slot, begin + j, stencil)
                    row = merged[pl.ds((begin + j) * room + slot, 1), :] * value
                    todo.append((ref, line, ref[pl.ds(line, 1), :] + row))
            for ref, line, row in todo:
                ref[pl.ds(line, 1), :] = row

    def more(i, carry):
        batch(i * BATCH)
        return carry

    batch(0)
    lax.fori_loop(1, most_batches(table, slots, stencil), more, 0)


def band(shape, taps, shift):
    distance = iota(shape, 1) - iota(shape, 0) + shift
    result = jnp.zeros(shape, F32)
    for tap in range(taps.shape[0]):
        result = jnp.where(distance == tap, taps[tap], result)
    return result


def band_rev(shape, taps, shift):
    distance = iota(shape, 0) - iota(shape, 1) + shift
    result = jnp.zeros(shape, F32)
    for tap in range(taps.shape[0]):
        result = jnp.where(distance == tap, taps[tap], result)
    return result


def exact_nt(a, b):
    return lax.dot_general(
        a,
        b,
        (((1,), (1,)), ((), ())),
        precision=lax.Precision.HIGHEST,
        preferred_element_type=F32,
    )


def store_split(ref, index, value):
    high, low = split2(value)
    ref[(0,) + index] = high
    ref[(1,) + index] = low


def bands_kernel(kx, ky, lat2, lon2, lat1, lon1, *, rows_block):
    margin = kx.shape[0] // 2
    window = lat2.shape[2]
    first = band((window, window), ky, margin)
    reach = first[LANES : LANES + WIDE, :]
    place = iota((window, window), 1)
    for variant in range(3):
        kept = first
        if variant == 0:
            kept = jnp.where(place >= LANES, first, 0.0)
        if variant == 2:
            kept = jnp.where(place < LANES + WIDE, first, 0.0)
        store_split(lat2, (variant,), exact_nt(kept, reach))
    size = lon2.shape[1]
    wide = size + 2 * HALO
    depth = (wide + 32 + LANES - 1) // LANES * LANES
    second = band((wide, depth), kx, -(16 - margin))
    store_split(lon2, (), exact_nt(second[HALO : HALO + size, :], second))
    store_split(lat1, (), band_rev((rows_block, rows_block + 2 * PAD), ky, PAD + margin))
    store_split(lon1, (), band((2 * WIDE, WIDE), kx, LANES + margin))


def pairs(low, high, action):
    def step(i, carry):
        one = low + 2 * i
        action(one, jnp.minimum(one + 1, high - 1), one + 1 < high)
        return carry

    lax.fori_loop(0, lax.shift_right_logical(high - low + 1, 1), step, 0)


def quads(low, high, action):
    def step(i, carry):
        one = low + 4 * i
        numbers = [one] + [jnp.minimum(one + j, high - 1) for j in range(1, 4)]
        weights = [None] + [jnp.where(one + j < high, 1.0, 0.0) for j in range(1, 4)]
        action(numbers, weights)
        return carry

    lax.fori_loop(0, lax.shift_right_logical(high - low + 3, 2), step, 0)


def weighted(value, weight):
    return value if weight is None else value * weight


def zero_all(refs):
    rows = refs[0].shape[0]
    step = 256

    def clear(i, carry):
        for ref in refs:
            ref[pl.ds(pl.multiple_of(i * step, 8), step), :] = jnp.zeros((step, LANES), F32)
        return carry

    whole = rows // step
    lax.fori_loop(0, whole, clear, 0)
    if rows % step:
        for ref in refs:
            ref[whole * step : rows, :] = jnp.zeros((rows % step, LANES), F32)


def scatter_entries(copies, entries, lane):
    for start in range(0, len(entries), len(copies)):
        group = []
        for ref, (address, value) in zip(copies, entries[start : start + len(copies)]):
            line = lax.shift_right_logical(address, 7)
            spread = jnp.where(lane == (address & (LANES - 1)), value, 0.0)
            group.append((ref, line, ref[pl.ds(line, 1), :] + spread))
        for ref, line, value in group:
            ref[pl.ds(line, 1), :] = value


def spot(sender, idx, per, stencil):
    return sender * per + idx + lax.shift_right_logical(idx, 7) * ((stencil - 1) * LANES)


def copy_parts(layout, source, target, place, chunk, chunks, group, sem):
    begin, size = place
    words = group * size * LANES
    at = begin * LANES + chunk * words
    return pltpu.make_async_copy(source.at[pl.ds(at, words)], target, sem)


def apply_kernel(
    *refs, first, layout, columns, height, hold, stencil, capacity, senders, parts, levels
):
    refs = list(refs)

    def take(count):
        taken = refs[:count]
        del refs[:count]
        return taken

    meta, ints, floats, own_lines, own = take(5)
    if not first:
        replies_h, moments_h = take(2)
    std_h, std_l_h, std_r_h, lat2_h, lon2_h = take(5)
    if not first:
        merged_h, _ = take(2)
    field_h, send = take(2)
    if first:
        info_out, merged_h = take(2)
    addr, wgt, start, lines_s, val = take(5)
    if not first:
        moments = take(1)[0]
    if first:
        picked, chosen = take(2)
    scale, merged, sums, high_s, low_s, std, lat2, lon2, field = take(9)
    copies = take(PAIR)
    sems, in_sems, out_sems, val_sem, std_sems = take(5)

    me = meta[0]
    wide = columns + 2 * HALO
    blocks = height // LANES
    group = min(GROUP, senders)
    chunks = senders // group
    slots = senders * capacity
    lane = iota((1, LANES), 1)
    per = stencil * hold
    table = layout.table

    def chunk_copies(chunk):
        todo = [
            (ints, addr, layout.ints["addr"]),
            (floats, wgt, layout.floats["wgt"]),
            (ints, start, layout.ints["start"]),
        ]
        if first:
            todo.append((floats, val, layout.floats["val"]))
        return [
            copy_parts(layout, source, target, place, chunk, chunks, group, sems.at[i])
            for i, (source, target, place) in enumerate(todo)
        ]

    def load_chunk(chunk):
        for copy in chunk_copies(chunk):
            copy.start()
        for copy in chunk_copies(chunk):
            copy.wait()

    operands = [
        pltpu.make_async_copy(lat2_h, lat2, in_sems.at[0]),
        pltpu.make_async_copy(lon2_h, lon2, in_sems.at[1]),
    ]

    def std_copies(block):
        lanes = pl.ds(pl.multiple_of(block * LANES, LANES), LANES)
        top = pl.multiple_of(block * wide, 8)
        result = []
        for source, begin, size, sem in (
            (std_l_h, 0, HALO, 2),
            (std_h, HALO, columns, 3),
            (std_r_h, HALO + columns, HALO, 4),
        ):
            target = std.at[pl.ds(pl.multiple_of(top + begin, 8), size), :]
            result.append(
                pltpu.make_async_copy(source.at[:, lanes], target, std_sems.at[sem - 2, block])
            )
        return result

    def each_block(action):
        def step(block, carry):
            for copy in std_copies(block):
                action(copy)
            return carry

        lax.fori_loop(0, blocks, step, 0)

    own_copy = pltpu.make_async_copy(own_lines, lines_s, in_sems.at[5])
    own_copy.start()
    merged_copies = RowCopies(
        *((merged, merged_h) if first else (merged_h, merged)),
        slots + LANES,
        lines_s,
        (in_sems.at[6], in_sems.at[7]),
        stencil,
    )
    if not first:
        merged_copies.always.start()
    each_block(lambda copy: copy.start())
    for copy in operands:
        copy.start()

    def value_copy(owner):
        at = pl.multiple_of(owner * (replies_h.shape[0] // parts), 1024)
        return pltpu.make_async_copy(
            replies_h.at[pl.ds(at, slots)], val.at[pl.ds(owner * slots, slots)], val_sem.at[owner]
        )

    def each_owner(action):
        def step(owner, carry):
            action(value_copy(owner))
            return carry

        lax.fori_loop(0, parts, step, 0)

    if not first:
        each_owner(lambda copy: copy.start())
        moments_copy = pltpu.make_async_copy(
            moments_h.at[:, pl.ds(0, 8), :], moments, in_sems.at[2]
        )
        moments_copy.start()
    zero_all(copies)
    zero_all([sums])

    lane_of = iota((slots, LANES), 1)
    room = slots + LANES
    column = 2 * stencil if first else 2 * stencil + 2
    scale[...] = jnp.broadcast_to(own[:, column : column + 1], (room, LANES))
    known = own[0:slots, :]
    own_copy.wait()
    if not first:
        merged_copies.always.wait()
        merged_copies.run_rest()

    after = lax.rem(me + 1, parts)
    ahead = lax.rem(me + parts - 1, parts)

    def start_of(sender, owner, row, half):
        return start[sender * table + row * hold + half * LANES + owner]

    def entries_of(sender, idx, value):
        base = spot(sender, idx, per, stencil)
        return [
            (addr[base + k * LANES], wgt[base + k * LANES] * value) for k in range(stencil)
        ]

    def own_line(slot, k):
        return word_of(lines_s, slot, k, stencil)

    def amount_of(sender):
        return lines_s[(stencil + 3) * LANES + sender]

    halo_count = lines_s[(stencil + 4) * LANES]
    halo_fits = halo_count <= LANES

    def own_groups(action, halo):
        if capacity % BLOCK:
            blocks_of(lines_s, 0, slots, stencil, action)
        else:

            def per_sender(sender, carry):
                blocks_of(lines_s, sender * capacity, amount_of(sender), stencil, action)
                return carry

            lax.fori_loop(0, senders, per_sender, 0)
        if halo:
            blocks_of(lines_s, slots, jnp.minimum(halo_count, LANES), stencil, action)

    def build(top, places):
        rows = weight_rows(own[pl.ds(top, BLOCK), :], places, stencil)
        for place, row in enumerate(rows):
            merged[pl.ds(place * room + top, BLOCK), :] = row

    if first:
        own_groups(build, True)
        merged_copies.always.start()
        merged_copies.run_rest()

    def own_quads(action):
        def per_sender(sender, carry):
            base = sender * capacity
            quads(base, base + amount_of(sender), action)
            return carry

        lax.fori_loop(0, senders, per_sender, 0)

    def scatter_known(numbers, weights):
        values = [weighted(scale[pl.ds(i, 1), :], w) for i, w in zip(numbers, weights)]
        scatter_slots(lines_s, merged, room, copies, numbers, values, stencil)

    def scatter_sent(numbers, weights):
        values = [weighted(val[own_line(i, stencil + 2)], w) for i, w in zip(numbers, weights)]
        scatter_slots(lines_s, merged, room, copies, numbers, values, stencil)

    def scatter_halo(chunk):
        def per_sender(sender, carry):
            for owner, low, high in ((after, (1, 0), (1, 1)), (ahead, (2, 0), (0, 1))):
                begin = start_of(sender, owner, 0, 0)

                def value_of(idx, owner=owner, begin=begin):
                    if first:
                        return val[sender * hold + idx]
                    place = (chunk * group + sender) * capacity + idx - begin
                    return val[owner * slots + place]

                def action(one, two, has_two, value_of=value_of):
                    second = jnp.where(has_two, value_of(two), 0.0)
                    scatter_entries(
                        copies,
                        entries_of(sender, one, value_of(one)) + entries_of(sender, two, second),
                        lane,
                    )

                pairs(start_of(sender, owner, *low), start_of(sender, owner, *high), action)
            return carry

        lax.fori_loop(0, group, per_sender, 0)

    own_quads(scatter_known)
    if not first:
        each_owner(lambda copy: copy.wait())

    @pl.when(halo_fits)
    def _():
        quads(slots, slots + halo_count, scatter_known if first else scatter_sent)

    @pl.when(jnp.logical_not(halo_fits))
    def _():
        def step(chunk, carry):
            load_chunk(chunk)
            scatter_halo(chunk)
            return carry

        lax.fori_loop(0, chunks, step, 0)

    each_block(lambda copy: copy.wait())
    for copy in operands:
        copy.wait()

    for jb in range(blocks):
        lanes = slice(jb * LANES, (jb + 1) * LANES)
        rows = slice(jb * wide, (jb + 1) * wide)
        total = copies[0][rows, :]
        for ref in copies[1:]:
            total = total + ref[rows, :]
        high_s[:, lanes], low_s[:, lanes] = split2(total * std[rows, :])

    smoothed = copies[0]
    size = lon2.shape[1]
    count = height // WIDE
    outgoing = [merged_copies.always] if first else []
    for block in range(count):
        variant = 0 if block == 0 else (2 if block == count - 1 else 1)
        low = max(block * WIDE - LANES, 0)
        high = min(block * WIDE + WIDE + LANES, height)
        inner = slice(low - (block * WIDE - LANES), high - (block * WIDE - LANES))
        matrix = (lat2[0, variant, inner, :], lat2[1, variant, inner, :])
        along = mm_parts((high_s[:, low:high], low_s[:, low:high]), matrix)
        parts_y = split2(along)
        lanes = slice(block * WIDE, (block + 1) * WIDE)
        for begin in range(0, columns, size):
            some = min(size, columns - begin)
            rows = slice(begin, begin + some)
            window = slice(begin, begin + some + 2 * HALO)
            matrix = tuple(lon2[i, 0:some, 0 : some + 2 * HALO] for i in range(2))
            result = mm_parts(matrix, (parts_y[0][window, :], parts_y[1][window, :]))
            for half in range(WIDE // LANES):
                top = (block * (WIDE // LANES) + half) * wide + HALO + begin
                across = slice(half * LANES, (half + 1) * LANES)
                scaled = result[:, across] * std[top : top + some, :]
                smoothed[top : top + some, :] = scaled
                first_lane = block * WIDE + half * LANES
                field[rows, first_lane : first_lane + LANES] = scaled
        outgoing.append(
            pltpu.make_async_copy(field.at[:, lanes], field_h.at[:, lanes], out_sems.at[block])
        )
        outgoing[-1].start()

    def gather_quad(numbers, weights):
        def batch(begin, totals):
            result = []
            for slot, total in zip(numbers, totals):
                terms = []
                for j in range(BATCH):
                    line = own_line(slot, begin + j)
                    row = merged[pl.ds((begin + j) * room + slot, 1), :]
                    terms.append(row * smoothed[pl.ds(line, 1), :])
                    if first:
                        picked[pl.ds((begin + j) * room + slot, 1), :] = std[
                            pl.ds(line, 1), :
                        ]
                result.append(total + ((terms[0] + terms[1]) + (terms[2] + terms[3])))
            return tuple(result)

        zero = jnp.zeros((1, LANES), F32)
        totals = lax.fori_loop(
            1,
            most_batches(lines_s, numbers, stencil),
            lambda i, totals: batch(i * BATCH, totals),
            batch(0, (zero,) * len(numbers)),
        )
        for slot, total in zip(numbers, totals):
            sums[pl.ds(slot, 1), :] = total

    own_quads(gather_quad)

    def pick(top, places):
        info = own[pl.ds(top, BLOCK), :]
        codes = columns_of(info, CODES, stencil)
        lane_f = iota(info.shape, 1).astype(F32)
        rows = [picked[pl.ds(place * room + top, BLOCK), :] for place in range(places)]
        result = jnp.zeros((BLOCK, LANES), F32)
        for k in range(stencil):
            cell = jnp.zeros((BLOCK, LANES), F32)
            for place in range(min(k + 1, places)):
                at = lane_f + float(LANES * place)
                cell = jnp.where(at == codes[k], rows[place], cell)
            cell = jnp.sum(cell, axis=1, keepdims=True)
            result = jnp.where(lane_f == float(stencil + k), cell, result)
        chosen[pl.ds(top, BLOCK), :] = result * info

    if first:
        own_groups(pick, False)

    def whole(x):
        return jnp.sum(x, axis=0, keepdims=True)

    total = jnp.sum(sums[...], axis=1, keepdims=True)
    lines = slots // LANES
    known = own[0:slots, :]
    source, weight, reply, image0 = (
        known[:, 2 * stencil + i : 2 * stencil + i + 1] for i in range(4)
    )
    if first:
        reply = weight * total
        known = jnp.where(lane_of == 2 * stencil + 2, reply, known)
        known = jnp.where(lane_of == 2 * stencil + 3, total, known)
        info_out[0:slots, :] = known
        info_out[slots:room, :] = own[slots:room, :]
        turned = known.T[2 * stencil + 2 : 2 * stencil + 3, :]
        message = [turned[:, i * LANES : (i + 1) * LANES] for i in range(lines)]
        message.append(
            jnp.where(
                lane == 0, whole(source * total), jnp.where(lane == 1, whole(reply * total), 0.0)
            )
        )
        message.append(jnp.zeros((8 - len(message), LANES), F32))
        factors = chosen[...].T
        for k in range(stencil):
            row = factors[stencil + k : stencil + k + 1, :]
            message += [row[:, i * LANES : (i + 1) * LANES] for i in range(lines)]
        message = jnp.concatenate(message, axis=0)
    else:
        moments_copy.wait()
        slab = jnp.sum(moments[...], axis=0)[lines : lines + 1, :]
        length = slab[:, 0:1] / (slab[:, 0:1] + slab[:, 1:2])
        both = source + reply
        s_both = image0 + total
        resid = source - length * both
        s_resid = image0 - length * s_both
        values = [
            resid * s_resid,
            resid * s_both,
            both * s_both,
            resid * image0,
            both * image0,
            weight * s_resid * s_resid,
            weight * s_resid * s_both,
            weight * s_both * s_both,
            weight * s_resid * image0,
            weight * s_both * image0,
            source * image0,
            reply * image0,
        ]
        message = jnp.where(lane == len(values), length, 0.0)
        for i, value in enumerate(values):
            message = jnp.where(lane == i, whole(value), message)
        message = jnp.concatenate([message, jnp.zeros((7, LANES), F32)], axis=0)

    def send_to(i, carry):
        send[i] = message
        return carry

    lax.fori_loop(0, send.shape[0], send_to, 0)
    for copy in outgoing:
        copy.wait()


def final_kernel(
    ints,
    floats,
    replies_h,
    lines_h,
    merged_h,
    mixed,
    totals,
    field0_h,
    field1_h,
    lat1,
    lon1,
    control_h,
    increment_h,
    addr,
    listed,
    slot,
    val,
    factors,
    field0,
    field1,
    control,
    high_s,
    low_s,
    lines_s,
    merged,
    scale,
    *rest,
    layout,
    hold,
    stencil,
    capacity,
    senders,
    parts,
    length,
):
    copies = rest[:PAIR]
    sems, in_sems, out_sems = rest[PAIR:]
    group = min(GROUP, senders)
    chunks = senders // group
    per = stencil * hold
    rows_block = control.shape[0]
    high_rows = rows_block + 2 * PAD
    lane = iota((1, LANES), 1)
    stride = group * capacity
    owner_words = factors.shape[0] // parts
    to_factors = owner_words - stencil * stride

    def chunk_copies(chunk):
        todo = [
            (ints, addr, layout.ints["rows"]),
            (ints, listed, layout.ints["listed"]),
            (ints, slot, layout.ints["slot"]),
            (floats, val, layout.floats["val"]),
        ]
        result = [
            copy_parts(layout, source, target, place, chunk, chunks, group, sems.at[i])
            for i, (source, target, place) in enumerate(todo)
        ]
        words = parts * owner_words
        result.append(
            pltpu.make_async_copy(
                replies_h.at[pl.ds(chunk * words, words)], factors, sems.at[len(todo)]
            )
        )
        return result

    row_copies = RowCopies(
        merged_h, merged, LISTED, lines_s, (in_sems.at[3], in_sems.at[4]), stencil
    )
    listing = [pltpu.make_async_copy(lines_h, lines_s, in_sems.at[2]), row_copies.always]
    for copy in listing:
        copy.start()
    operands = [
        pltpu.make_async_copy(source, target, in_sems.at[i])
        for i, (source, target) in enumerate(
            ((field0_h, field0), (field1_h, field1))
        )
    ]
    for copy in operands:
        copy.start()

    slabs = totals.shape[1]
    every = jnp.sum(totals[...], axis=0)
    norm0 = quad0 = None
    for i in range(slabs):
        line = every[i, 0:1, :]
        a, b = line[:, 10:11], line[:, 11:12]
        norm0 = a if norm0 is None else norm0 + a
        quad0 = b if quad0 is None else quad0 + b
    step0 = norm0 / (norm0 + quad0)
    norm1 = cross = quad1 = quad01 = jnp.zeros((1, 1), F32)
    for i in range(slabs):
        line = every[i, 0:1, :]
        v = [line[:, j : j + 1] for j in range(10)]
        shift = totals[0, i, 0:1, 12:13] - step0
        norm1 = norm1 + (v[0] + shift * (2.0 * v[1] + shift * v[2]))
        cross = cross + (v[3] + shift * v[4])
        quad1 = quad1 + (v[5] + shift * (2.0 * v[6] + shift * v[7]))
        quad01 = quad01 + (v[8] + shift * v[9])
    ratio = norm1 / norm0
    curvature = norm1 + quad1 + ratio * (
        2.0 * (cross + quad01) + ratio * (norm0 + quad0)
    )
    step1 = norm1 / curvature
    first = step0 + step1 * (1.0 - step0 + ratio)
    second = -step0 * step1
    first_line = jnp.broadcast_to(first, (1, LANES))
    second_line = jnp.broadcast_to(second, (1, LANES))

    zero_all(copies)

    data = mixed[...]
    column = 2 * stencil
    scale[...] = first * data[:, column : column + 1] + second * jnp.broadcast_to(
        data[:, column + 1 : column + 2], data.shape
    )
    for copy in listing:
        copy.wait()
    row_copies.run_rest()
    count = lines_s[(stencil + 3) * LANES]

    def add(numbers, weights):
        values = [weighted(scale[pl.ds(i, 1), :], w) for i, w in zip(numbers, weights)]
        scatter_slots(lines_s, merged, LISTED, copies, numbers, values, stencil)

    def scatter_chunk():
        def per_sender(sender, carry):
            def step(idx, inner):
                @pl.when(listed[sender * hold + idx] > 0)
                def _():
                    place = slot[sender * hold + idx]
                    place = place + lax.div(place, stride) * (owner_words - stride)
                    base = spot(sender, idx, per, stencil)
                    z0 = val[sender * hold + idx]
                    value = first_line * z0 + second_line * factors[place]
                    entries = [
                        (addr[base + k * LANES], factors[place + to_factors + k * stride] * value)
                        for k in range(stencil)
                    ]
                    scatter_entries(copies, entries, lane)

                return inner

            lax.fori_loop(0, hold, step, 0)
            return carry

        lax.fori_loop(0, group, per_sender, 0)

    @pl.when(count <= LISTED)
    def _():
        quads(0, count, add)

    @pl.when(count > LISTED)
    def _():
        def step(chunk, carry):
            for copy in chunk_copies(chunk):
                copy.start()
            for copy in chunk_copies(chunk):
                copy.wait()
            scatter_chunk()
            return carry

        lax.fori_loop(0, chunks, step, 0)

    for copy in operands:
        copy.wait()
    increment = field0
    increment[...] = first * field0[...] + second * field1[...]
    outgoing = [pltpu.make_async_copy(increment, increment_h, out_sems.at[0])]
    outgoing[0].start()

    pair = WIDE // LANES
    count = length // WIDE
    for block in range(count):
        pieces = []
        for half in range(pair):
            rows = slice((block * pair + half) * high_rows, (block * pair + half + 1) * high_rows)
            total = copies[0][rows, :]
            for ref in copies[1:]:
                total = total + ref[rows, :]
            pieces.append(total)
        whole = split2(jnp.concatenate(pieces, axis=1))
        size = lat1.shape[1]
        for top in range(0, rows_block, size):
            window = slice(top, top + size + 2 * PAD)
            along = mm_parts((lat1[0], lat1[1]), (whole[0][window, :], whole[1][window, :]))
            high, low = split2(along)
            high_s[top : top + size, block * WIDE : (block + 1) * WIDE] = high
            low_s[top : top + size, block * WIDE : (block + 1) * WIDE] = low

    def window(ref, block):
        low, high = block * WIDE - LANES, (block + 1) * WIDE + LANES
        if low < 0:
            return jnp.concatenate([ref[:, length + low : length], ref[:, 0:high]], axis=1)
        if high > length:
            return jnp.concatenate([ref[:, low:length], ref[:, 0 : high - length]], axis=1)
        return ref[:, low:high]

    every_lanes = 4
    for block in range(count):
        control[:, block * WIDE : (block + 1) * WIDE] = mm_parts(
            (window(high_s, block), window(low_s, block)), (lon1[0], lon1[1])
        )
        if block % every_lanes == every_lanes - 1:
            lanes = slice((block + 1 - every_lanes) * WIDE, (block + 1) * WIDE)
            outgoing.append(
                pltpu.make_async_copy(
                    control.at[:, lanes], control_h.at[:, lanes], out_sems.at[len(outgoing)]
                )
            )
            outgoing[-1].start()
    for copy in outgoing:
        copy.wait()


def body(
    background_std,
    x_kernel,
    y_kernel,
    obs_owner,
    obs_cells,
    obs_weights,
    innovation,
    obs_precision,
    obs_counts,
):
    parts = lax.axis_size("pencil")
    levels = lax.axis_size("lev")
    me = lax.axis_index("pencil")
    _, columns, height = background_std.shape
    hold, stencil = obs_cells.shape
    margin = x_kernel.shape[1] // 2
    capacity = 2 * hold // parts
    senders = parts
    slots = senders * capacity
    room = slots + LANES
    rows_block = height // parts
    length = columns * parts
    blocks = height // LANES
    wide = columns + 2 * HALO
    group = min(GROUP, senders)
    chunks = senders // group
    layout = Layout(senders, hold, stencil, parts)
    std = background_std[0]

    edge = jax.ShapeDtypeStruct((HALO, height), F32)
    packed, low_edge, high_edge = pl.pallas_call(
        functools.partial(
            pack_kernel, parts=parts, columns=columns, height=height, margin=margin
        ),
        out_shape=[jax.ShapeDtypeStruct((parts, PACK, hold), F32), edge, edge],
        in_specs=[smem()] + [vmem()] * 5 + [hbm()],
        out_specs=[vmem()] * 3,
        scratch_shapes=[pltpu.VMEM((parts, hold), F32), pltpu.SemaphoreType.DMA((2,))],
        compiler_params=params(),
        cost_estimate=cost(12000),
        name="pack",
    )(
        obs_counts,
        obs_owner.T,
        obs_cells.T,
        obs_weights.T,
        innovation[None, :],
        obs_precision[None, :],
        std,
    )
    recv = lax.all_to_all(packed, "pencil", split_axis=0, concat_axis=0, tiled=True)

    right_of = [(p, (p + 1) % parts) for p in range(parts)]
    left_of = [(p, (p - 1) % parts) for p in range(parts)]
    std_l = lax.ppermute(high_edge, "pencil", right_of)
    std_r = lax.ppermute(low_edge, "pencil", left_of)

    size = min(columns, WIDE - 2 * HALO)
    row_size = min(rows_block, LANES)
    lat2, lon2, lat1, lon1 = pl.pallas_call(
        functools.partial(bands_kernel, rows_block=row_size),
        out_shape=[
            jax.ShapeDtypeStruct((2, 3, 2 * WIDE, WIDE), BF),
            jax.ShapeDtypeStruct((2, size, size + 2 * HALO), BF),
            jax.ShapeDtypeStruct((2, row_size, row_size + 2 * PAD), BF),
            jax.ShapeDtypeStruct((2, 2 * WIDE, WIDE), BF),
        ],
        in_specs=[smem(), smem()],
        out_specs=[vmem()] * 4,
        compiler_params=params(),
        cost_estimate=cost(100),
        name="bands",
    )(x_kernel[0], y_kernel[0])

    meta = jnp.reshape(me, (1,)).astype(I32)
    place = dict(
        parts=parts, columns=columns, height=height, capacity=capacity, stencil=stencil
    )
    ints, floats, own_lines, own = pl.pallas_call(
        functools.partial(unpack_kernel, layout=layout, group=group, **place),
        out_shape=[
            jax.ShapeDtypeStruct((layout.int_rows, LANES), I32),
            jax.ShapeDtypeStruct((layout.float_rows, LANES), F32),
            jax.ShapeDtypeStruct((room // LANES * (stencil + 8), LANES), I32),
            jax.ShapeDtypeStruct((room, LANES), F32),
        ],
        in_specs=[smem(), vmem(), hbm()],
        out_specs=[vmem()] * 4,
        scratch_shapes=[
            pltpu.VMEM((room // LANES, STACK, LANES), F32),
        ],
        compiler_params=params(),
        cost_estimate=cost(100),
        name="unpack",
    )(meta, recv, lat1)
    ints = ints.reshape(-1)
    floats = floats.reshape(-1)
    own_lines = own_lines.reshape(-1)

    acc = pltpu.VMEM((blocks * wide + 8, LANES), F32)
    column_slots = pltpu.VMEM((slots, LANES), F32)
    static = dict(
        layout=layout,
        columns=columns,
        height=height,
        hold=hold,
        stencil=stencil,
        capacity=capacity,
        senders=senders,
        parts=parts,
        levels=levels,
    )
    per = group * stencil * hold
    line = group * hold
    index_scratch = [
        pltpu.SMEM((per,), I32),
        pltpu.SMEM((per,), F32),
        pltpu.SMEM((group * layout.table,), I32),
        pltpu.SMEM((room * (stencil + 8),), I32),
    ]
    work = (
        [
            pltpu.VMEM((room, LANES), F32),
            pltpu.VMEM((stencil * room, LANES), F32),
            column_slots,
        ]
        + [pltpu.VMEM((wide, height), BF)] * 2
        + [
            acc,
            pltpu.VMEM(lat2.shape, BF),
            pltpu.VMEM(lon2.shape, BF),
            pltpu.VMEM((columns, height), F32),
        ]
        + [acc] * PAIR
        + [
            pltpu.SemaphoreType.DMA((4,)),
            pltpu.SemaphoreType.DMA((8,)),
            pltpu.SemaphoreType.DMA((height // WIDE,)),
            pltpu.SemaphoreType.DMA((parts,)),
            pltpu.SemaphoreType.DMA((3, blocks)),
        ]
    )
    field_shape = jax.ShapeDtypeStruct((columns, height), F32)
    reply_rows = 8 + stencil * slots // LANES
    field0, message, info, merged = pl.pallas_call(
        functools.partial(apply_kernel, first=True, **static),
        out_shape=[
            field_shape,
            jax.ShapeDtypeStruct((parts, reply_rows, LANES), F32),
            jax.ShapeDtypeStruct((room, LANES), F32),
            jax.ShapeDtypeStruct((stencil * room, LANES), F32),
        ],
        in_specs=[smem()] + [hbm()] * 3 + [vmem()] + [hbm()] * 5,
        out_specs=[hbm()] + [vmem()] * 2 + [hbm()],
        scratch_shapes=index_scratch
        + [
            pltpu.SMEM((line,), F32),
            pltpu.VMEM((stencil * room, LANES), F32),
            column_slots,
        ]
        + work,
        compiler_params=params(),
        name="apply_first",
    )(meta, ints, floats, own_lines, own, std, std_l, std_r, lat2, lon2)

    replies = lax.all_to_all(message, "pencil", split_axis=0, concat_axis=0, tiled=True)
    back = replies.reshape(-1)
    line_rows = LISTED // LANES * (stencil + 8)
    row_lines, row_data = pl.pallas_call(
        functools.partial(list_kernel, **place),
        out_shape=[
            jax.ShapeDtypeStruct((line_rows, LANES), I32),
            jax.ShapeDtypeStruct((LISTED, LANES), F32),
        ],
        in_specs=[smem(), vmem(), hbm()],
        out_specs=[vmem()] * 2,
        scratch_shapes=[pltpu.VMEM((STACK, LISTED), F32)],
        compiler_params=params(),
        cost_estimate=cost(4000),
        name="list_rows",
    )(meta, recv, info)
    row_lines = row_lines.reshape(-1)

    field1, sums = pl.pallas_call(
        functools.partial(apply_kernel, first=False, **static),
        out_shape=[
            field_shape,
            jax.ShapeDtypeStruct((parts * levels, 8, LANES), F32),
        ],
        in_specs=[smem()] + [hbm()] * 3 + [vmem()] + [hbm()] * 9,
        out_specs=[hbm(), vmem()],
        scratch_shapes=index_scratch
        + [pltpu.SMEM((parts * slots,), F32), pltpu.VMEM((parts, 8, LANES), F32)]
        + work,
        compiler_params=params(),
        name="apply_second",
    )(
        meta,
        ints,
        floats,
        own_lines,
        info,
        back,
        replies,
        std,
        std_l,
        std_r,
        lat2,
        lon2,
        merged,
        row_data,
    )

    totals = lax.all_to_all(sums, ("pencil", "lev"), split_axis=0, concat_axis=0, tiled=True)
    totals = totals.reshape(parts, levels, 8, LANES)

    listed_rows, mixed = pl.pallas_call(
        functools.partial(factor_kernel, stencil=stencil, slots=slots),
        out_shape=[
            jax.ShapeDtypeStruct((stencil * LISTED, LANES), F32),
            jax.ShapeDtypeStruct((LISTED, LANES), F32),
        ],
        in_specs=[hbm(), vmem(), vmem(), hbm()],
        out_specs=[hbm(), vmem()],
        scratch_shapes=[
            pltpu.SMEM((line_rows * LANES,), I32),
            pltpu.VMEM((parts * slots, LANES), F32),
            pltpu.VMEM((stencil * LISTED, LANES), F32),
            pltpu.SemaphoreType.DMA((3,)),
        ],
        compiler_params=params(),
        cost_estimate=cost(8000),
        name="factor_rows",
    )(row_lines, row_data, replies, sums)

    by_chunk = back
    if chunks > 1:
        by_chunk = jnp.concatenate(
            [replies[:, : slots // LANES, :], replies[:, 8:, :]], axis=1
        ).reshape(parts, stencil + 1, chunks, group * capacity)
        by_chunk = jnp.transpose(by_chunk, (2, 0, 1, 3)).reshape(-1)
    owner_words = by_chunk.shape[0] // (chunks * parts)
    high_rows = rows_block + 2 * PAD
    acc_rows = pltpu.VMEM(((length // LANES) * high_rows + 8, LANES), F32)
    control, increment = pl.pallas_call(
        functools.partial(
            final_kernel,
            layout=layout,
            hold=hold,
            stencil=stencil,
            capacity=capacity,
            senders=senders,
            parts=parts,
            length=length,
        ),
        out_shape=[
            jax.ShapeDtypeStruct((rows_block, length), F32),
            field_shape,
        ],
        in_specs=[hbm()] * 5 + [vmem()] * 2 + [hbm()] * 2 + [vmem()] * 2,
        out_specs=[hbm()] * 2,
        scratch_shapes=[
            pltpu.SMEM((per,), I32),
            pltpu.SMEM((line,), I32),
            pltpu.SMEM((line,), I32),
            pltpu.SMEM((line,), F32),
            pltpu.SMEM((parts * owner_words,), F32),
            pltpu.VMEM((columns, height), F32),
            pltpu.VMEM((columns, height), F32),
            pltpu.VMEM((rows_block, length), F32),
            pltpu.VMEM((rows_block, length), BF),
            pltpu.VMEM((rows_block, length), BF),
            pltpu.SMEM((line_rows * LANES,), I32),
            pltpu.VMEM((stencil * LISTED, LANES), F32),
            pltpu.VMEM((LISTED, LANES), F32),
        ]
        + [acc_rows] * PAIR
        + [
            pltpu.SemaphoreType.DMA((5,)),
            pltpu.SemaphoreType.DMA((5,)),
            pltpu.SemaphoreType.DMA((1 + length // WIDE,)),
        ],
        compiler_params=params(),
        name="outputs",
    )(
        ints,
        floats,
        by_chunk,
        row_lines,
        listed_rows,
        mixed,
        totals,
        field0,
        field1,
        lat1,
        lon1,
    )
    return control[None], increment[None]


def solution(mesh):
    return jax.shard_map(
        body,
        mesh=mesh,
        in_specs=(
            P("lev", "pencil", None),
            P("lev", None),
            P("lev", None),
            P(("pencil", "lev"), None),
            P(("pencil", "lev"), None),
            P(("pencil", "lev"), None),
            P(("pencil", "lev")),
            P(("pencil", "lev")),
            P(("pencil", "lev")),
        ),
        out_specs=(P("lev", "pencil", None), P("lev", "pencil", None)),
        check_vma=False,
    )
```

```python
import functools

import jax
import jax.numpy as jnp
import numpy as np
from jax import lax
from jax.experimental import pallas as pl
from jax.experimental.pallas import tpu as pltpu
from jax.sharding import PartitionSpec as P


BF = jnp.bfloat16
F32 = jnp.float32
I32 = jnp.int32
LANES = 128
WIDE = 256
HALO = 32
PAD = 16
PACK = 40
GROUP = 8
PAIR = 2
BATCH = 4
BLOCK = 32
CODES = 40
STACK = 64
LISTED = 512
VMEM_LIMIT = 58 * 1024 * 1024


def vmem():
    return pl.BlockSpec(memory_space=pltpu.VMEM)


def smem():
    return pl.BlockSpec(memory_space=pltpu.SMEM)


def hbm():
    return pl.BlockSpec(memory_space=pl.ANY)


def cost(nanoseconds):
    return pl.CostEstimate(flops=0, bytes_accessed=3690 * nanoseconds, transcendentals=0)


def params():
    return pltpu.CompilerParams(vmem_limit_bytes=VMEM_LIMIT)


def split2(x):
    high = x.astype(BF)
    return high, (x - high.astype(F32)).astype(BF)


def split3(x):
    high = x.astype(BF)
    rest = x - high.astype(F32)
    mid = rest.astype(BF)
    return high, mid, (rest - mid.astype(F32)).astype(BF)


def mm(a, b):
    return jnp.dot(a, b, preferred_element_type=F32)


def mm_parts(a_parts, b_parts):
    (ah, al), (bh, bl) = a_parts, b_parts
    return mm(jnp.concatenate([ah, al, ah], axis=1), jnp.concatenate([bh, bh, bl], axis=0))


def iota(shape, dim):
    return lax.broadcasted_iota(I32, shape, dim)


def pack_kernel(
    counts, owner, cells, weights, depart, prec, out, marks, *, parts, columns, height, margin
):
    stencil, hold = cells.shape
    shift = height.bit_length() - 1
    block = height // parts
    reach = 2 * margin
    row_id = iota((hold, hold), 0)
    col_id = iota((hold, hold), 1)
    eye = row_id == col_id
    col_f = col_id.astype(F32)
    live = iota((1, hold), 1) < counts[0]
    cell = cells[...]
    column = lax.shift_right_logical(cell, jnp.full(cell.shape, shift, I32))
    row = cell & (height - 1)

    def any_of(mask):
        return jnp.max(jnp.where(mask, 1.0, 0.0), axis=0, keepdims=True)

    def turn(line):
        return jnp.sum(jnp.where(eye, line, 0.0), axis=1, keepdims=True)

    left = any_of(column < reach)
    right = any_of(column >= columns - reach)
    side = left + 3.0 * right - 2.0 * left * right
    base = jnp.where(live, owner[...].astype(F32) * 4.0, 4.0 * parts)
    key = jnp.where(live, base + side, base)
    key_col = turn(key)
    before = (key_col < key) | ((key_col == key) & (row_id < col_id))
    rank = jnp.sum(jnp.where(before, 1.0, 0.0), axis=0, keepdims=True)
    begin = jnp.sum(jnp.where(key_col < base, 1.0, 0.0), axis=0, keepdims=True)
    rank_col = turn(rank)
    perm = jnp.where(rank_col == col_f, 1.0, 0.0).astype(BF)

    def sort(values):
        total = None
        for part in split3(values):
            term = mm(part, perm)
            total = term if total is None else total + term
        return total

    weight = jnp.where(live, prec[...], 0.0)
    rest = [weight * depart[...], weight, key, rank - begin, jnp.zeros((4, hold), F32)]
    values = [cell.astype(F32), weights[...]] + rest
    ordered = sort(jnp.concatenate(values, axis=0))
    line = iota((8, hold), 0)
    tail = ordered[2 * stencil : 2 * stencil + 8, :]
    first_half = col_f < float(LANES)
    fourfold = 4.0 * jnp.where(first_half, col_f, col_f - float(LANES))
    for i, (low, high) in enumerate(((0.0, 4.0), (1.0, 3.0), (2.0, 2.0))):
        bound = fourfold + jnp.where(first_half, low, high)
        begins = jnp.sum(jnp.where(key_col < bound, 1.0, 0.0), axis=0, keepdims=True)
        tail = jnp.where(line == 5 + i, begins, tail)
    last = (line == 7) & (iota((8, hold), 1) == hold - 1)

    def mark(part, carry):
        low = part * block - margin
        high = (part + 1) * block + margin
        flag = jnp.where(live, any_of((row >= low) & (row < high)), 0.0)
        place = jnp.sum(jnp.where(row_id < col_id, turn(flag), 0.0), axis=0, keepdims=True)
        marks[pl.ds(part, 1), :] = flag * (place + 1.0)
        return carry

    lax.fori_loop(0, parts, mark, 0, unroll=parts <= GROUP)
    listed = marks[...]
    amounts = jnp.max(listed, axis=1, keepdims=True)
    listed = mm(listed.astype(BF), perm)
    for part in range(parts):
        out[part, 0 : 2 * stencil, :] = ordered[0 : 2 * stencil, :]
        out[part, 2 * stencil : 2 * stencil + 8, :] = jnp.where(
            line == 4,
            listed[part : part + 1, :],
            jnp.where(last, amounts[part : part + 1, :], tail),
        )


class Layout:
    def __init__(self, senders, hold, stencil, parts):
        lines = hold // LANES
        self.table = 3 * hold
        sizes = dict(
            addr=stencil * lines, rows=stencil * lines, listed=lines, slot=lines, start=3 * lines
        )
        self.ints = {}
        at = 0
        for name, size in sizes.items():
            self.ints[name] = (at, size)
            at += senders * size
        self.int_rows = at
        self.floats = {}
        at = 0
        for name, size in dict(wgt=stencil * lines, val=lines).items():
            self.floats[name] = (at, size)
            at += senders * size
        self.float_rows = at


def right(x, by):
    return lax.shift_right_logical(x, jnp.full(x.shape, by, I32))


def nt(a, b):
    return lax.dot_general(a, b, (((1,), (1,)), ((), ())), preferred_element_type=F32)


class Received:
    def __init__(self, recv, sender, me, *, parts, columns, height, capacity, stencil):
        senders, _, hold = recv.shape
        wide = columns + 2 * HALO
        block = height // parts
        high_rows = block + 2 * PAD
        cell = recv[sender, 0:stencil, :].astype(I32)
        self.tail = recv[sender, 2 * stencil : 2 * stencil + 8, :]
        self.whole = self.tail.astype(I32)
        self.pos = self.whole[3:4, :]
        owner = right(self.whole[2:3, :], 2)
        offset = owner - me
        offset = jnp.where(offset > parts // 2, offset - parts, offset)
        offset = jnp.where(offset < -(parts // 2), offset + parts, offset)
        column = right(cell, height.bit_length() - 1)
        row = cell & (height - 1)
        at = offset * columns + column + HALO
        self.addr = jnp.where(
            (at >= 0) & (at < wide),
            (right(row, 7) * wide + at) * LANES + (row & (LANES - 1)),
            (height // LANES) * wide * LANES,
        )
        at_row = row - (block * me - PAD)
        across = owner * columns + column
        self.rows = jnp.where(
            (at_row >= 0) & (at_row < high_rows) & (owner < parts),
            (right(across, 7) * high_rows + at_row) * LANES + (across & (LANES - 1)),
            (columns * parts // LANES) * high_rows * LANES,
        )
        self.owner = jnp.minimum(owner, parts - 1)
        self.back = self.owner * (senders * capacity) + sender * capacity + self.pos


def stack_of(addr, weights, tail, back):
    hold = addr.shape[1]
    rows = [
        (addr & (LANES - 1)).astype(F32),
        weights,
        tail,
        right(addr, 7).astype(F32),
        back.astype(F32),
        jnp.zeros((7, hold), F32),
    ]
    return jnp.concatenate(split3(jnp.concatenate(rows, axis=0)), axis=1)


def gathered(stack, chosen):
    select = jnp.where(chosen, 1.0, 0.0).astype(BF)
    return nt(stack, jnp.concatenate([select] * 3, axis=1))


def merge_lines(block, nowhere, stencil, extra):
    number = iota((stencil, LANES), 0).astype(F32)
    line = block[CODES : CODES + stencil, :]
    leader = jnp.zeros(line.shape, F32)
    for k in reversed(range(stencil)):
        leader = jnp.where(line == line[k : k + 1, :], float(k), leader)
    leads = jnp.where(leader == number, 1.0, 0.0)
    count = jnp.zeros((1, LANES), F32)
    ranks = []
    for k in range(stencil):
        ranks.append(count)
        count = count + leads[k : k + 1, :]
    place = jnp.zeros(line.shape, F32)
    for k in range(stencil):
        place = jnp.where(leader == float(k), ranks[k], place)
    lists = []
    for k in range(stencil):
        found = jnp.where((leads > 0.0) & (place == float(k)), line, 0.0)
        found = jnp.sum(found, axis=0, keepdims=True)
        lists.append(jnp.where(count > float(k), found, nowhere))
    batches = right(count.astype(I32) + (BATCH - 1), BATCH.bit_length() - 1)
    most = jnp.zeros((1, LANES), F32)
    slot = iota((1, LANES), 1)
    for begin in range(0, LANES, BLOCK):
        here = (slot >= begin) & (slot < begin + BLOCK)
        found = jnp.max(jnp.where(here, batches.astype(F32), 0.0), axis=1, keepdims=True)
        most = jnp.where(here, found, most)
    back = block[CODES + stencil : CODES + stencil + 1, :]
    ints = [jnp.concatenate(lists, axis=0).astype(I32), batches]
    ints += [most.astype(I32), back.astype(I32)] + extra
    ints = jnp.concatenate(ints, axis=0)
    ints = jnp.concatenate([ints, jnp.zeros((stencil + 8 - ints.shape[0], LANES), I32)], axis=0)
    rows = [
        block[0:CODES, :],
        place * float(LANES) + block[0:stencil, :],
        jnp.zeros((LANES - CODES - stencil, LANES), F32),
    ]
    return ints, jnp.concatenate(rows, axis=0).T


def unpack_kernel(
    meta, recv, _, ints, floats, own_lines, own, total, *, layout, group, **sizes
):
    senders, _, hold = recv.shape
    lines = hold // LANES
    me = meta[0]
    parts, stencil, capacity = sizes["parts"], sizes["stencil"], sizes["capacity"]
    wide = sizes["columns"] + 2 * HALO
    slots = senders * capacity

    def put(ref, place, sender, value):
        begin, size = place
        count = value.shape[0]
        for i in range(lines):
            part = value[:, i * LANES : (i + 1) * LANES]
            if count % 8 == 0:
                at = pl.multiple_of(begin + sender * size + i * count, 8)
                ref[pl.ds(at, count), :] = part
            else:
                for j in range(count):
                    ref[pl.ds(begin + sender * size + i + j * lines, 1), :] = part[j : j + 1]

    total[...] = jnp.zeros(total.shape, F32)
    place = iota((LANES, hold), 0)
    index = iota((LANES, hold), 1)
    lane = iota((1, LANES), 1)
    halo_block = slots // LANES
    after = lax.rem(me + 1, parts)
    ahead = lax.rem(me + parts - 1, parts)

    def per_sender(sender, carry):
        halo_before, amounts = carry
        got = Received(recv, sender, me, **sizes)
        weights = recv[sender, stencil : 2 * stencil, :]
        within = lax.rem(sender, group) * capacity + got.pos
        put(ints, layout.ints["addr"], sender, got.addr)
        put(ints, layout.ints["rows"], sender, got.rows)
        put(ints, layout.ints["listed"], sender, got.whole[4:5, :])
        put(ints, layout.ints["slot"], sender, got.owner * (group * capacity) + within)
        put(ints, layout.ints["start"], sender, got.whole[5:8, :])
        put(floats, layout.floats["wgt"], sender, weights)
        put(floats, layout.floats["val"], sender, got.tail[0:1, :])

        def bound(line, half, owner):
            part = got.whole[5 + line : 6 + line, half * LANES : (half + 1) * LANES]
            return jnp.sum(jnp.where(lane == owner, part, 0), axis=1, keepdims=True)

        stack = stack_of(got.addr, weights, got.tail, got.back)

        begin, end = bound(0, 0, me), bound(0, 1, me)
        first_slot = sender * capacity
        block_of = first_slot // LANES
        within = place - (first_slot - block_of * LANES)
        chosen = (within >= 0) & (index == begin + within) & (index < end)
        shift = first_slot - block_of * LANES
        here = (lane >= shift) & (lane < shift + (end - begin))
        total[block_of] = jnp.where(here, gathered(stack, chosen), total[block_of])
        amounts = jnp.where(lane == sender, end - begin, amounts)

        first_r, last_r = bound(1, 0, after), bound(1, 1, after)
        first_l, last_l = bound(2, 0, ahead), bound(0, 1, ahead)
        middle = halo_before + (last_r - first_r)
        chosen_r = (index >= first_r) & (index < last_r) & (index - first_r + halo_before == place)
        chosen_l = (index >= first_l) & (index < last_l) & (index - first_l + middle == place)
        halo_after = middle + (last_l - first_l)
        here = (lane >= halo_before) & (lane < halo_after)
        values = gathered(stack, chosen_r | chosen_l)
        total[halo_block] = jnp.where(here, values, total[halo_block])
        return halo_after, amounts

    halo_count, amounts = lax.fori_loop(
        0,
        senders,
        per_sender,
        (jnp.zeros((1, 1), I32), jnp.zeros((1, LANES), I32)),
        unroll=senders <= GROUP,
    )
    extra = [amounts, jnp.broadcast_to(halo_count, (1, LANES))]
    nowhere = float((sizes["height"] // LANES) * wide)
    for i in range(slots // LANES + 1):
        top = i * (stencil + 8)
        own_lines[top : top + stencil + 8, :], own[i * LANES : (i + 1) * LANES, :] = merge_lines(
            total[i], nowhere, stencil, extra
        )


def list_kernel(meta, recv, _, row_lines, row_data, total, **sizes):
    senders, _, hold = recv.shape
    stencil = sizes["stencil"]
    high_rows = sizes["height"] // sizes["parts"] + 2 * PAD
    place = iota((LISTED, hold), 0)
    total[...] = jnp.zeros(total.shape, F32)

    def per_sender(sender, before):
        got = Received(recv, sender, meta[0], **sizes)
        marks = got.whole[4:5, :]
        zeros = jnp.zeros((stencil, hold), F32)
        tail = jnp.concatenate([got.tail[0:1, :], zeros[0:7, :]], axis=0)
        stack = stack_of(got.rows, zeros, tail, got.back)
        values = gathered(stack, (marks > 0) & (marks - 1 + before == place))
        after = before + got.whole[7:8, hold - 1 : hold]
        slot = iota((1, LISTED), 1)
        total[...] = jnp.where((slot >= before) & (slot < after), values, total[...])
        return after

    count = lax.fori_loop(
        0, senders, per_sender, jnp.zeros((1, 1), I32), unroll=senders <= GROUP
    )
    nowhere = float((sizes["columns"] * sizes["parts"] // LANES) * high_rows)
    for i in range(LISTED // LANES):
        top = i * (stencil + 8)
        block = total[:, i * LANES : (i + 1) * LANES]
        (
            row_lines[top : top + stencil + 8, :],
            row_data[i * LANES : (i + 1) * LANES, :],
        ) = merge_lines(block, nowhere, stencil, [jnp.broadcast_to(count, (1, LANES))])


class RowCopies:
    def __init__(self, source, target, room, table, sems, stencil):
        half = 2 * BATCH * room
        self.always = pltpu.make_async_copy(
            source.at[pl.ds(0, half), :], target.at[pl.ds(0, half), :], sems[0]
        )
        size = source.shape[0] - half
        self.seldom = pltpu.make_async_copy(
            source.at[pl.ds(half, size), :], target.at[pl.ds(half, size), :], sems[1]
        )
        self.table, self.room, self.stencil = table, room, stencil

    def rest(self):
        most = word_of(self.table, 0, self.stencil + 1, self.stencil)
        for top in range(BLOCK, self.room, BLOCK):
            most = jnp.maximum(most, word_of(self.table, top, self.stencil + 1, self.stencil))
        return most > 2

    def run_rest(self):
        @pl.when(self.rest())
        def _():
            self.seldom.start()
            self.seldom.wait()


def word_of(table, slot, k, stencil):
    at = lax.shift_right_logical(slot, 7) * ((stencil + 7) * LANES) + slot
    return table[at + k * LANES]


def columns_of(info, begin, stencil):
    return [jnp.broadcast_to(info[:, begin + k : begin + k + 1], info.shape) for k in range(stencil)]


def weight_rows(info, places, stencil):
    lane_f = iota(info.shape, 1).astype(F32)
    codes = columns_of(info, CODES, stencil)
    weights = columns_of(info, stencil, stencil)
    rows = []
    for place in range(stencil):
        row = jnp.zeros(info.shape, F32)
        if place < places:
            at = lane_f + float(LANES * place)
            for k in range(place, stencil):
                term = jnp.where(at == codes[k], weights[k], 0.0)
                row = term if k == place else row + term
        rows.append(row)
    return rows


def block_at(table, top, stencil, action):
    top = pl.multiple_of(top, 8)
    most = word_of(table, top, stencil + 1, stencil)

    @pl.when(most <= 1)
    def _():
        action(top, BATCH)

    @pl.when(most == 2)
    def _():
        action(top, 2 * BATCH)

    @pl.when(most > 2)
    def _():
        action(top, stencil)


def blocks_of(table, top, amount, stencil, action):
    def step(i, carry):
        block_at(table, top + i * BLOCK, stencil, action)
        return carry

    lax.fori_loop(0, lax.div(amount + (BLOCK - 1), BLOCK), step, 0)


def factor_kernel(
    lines_h, data, replies, _, merged_h, mixed, lines_s, table, merged, sems, *, stencil, slots
):
    parts = replies.shape[0]
    lines = slots // LANES
    lines_copy = pltpu.make_async_copy(lines_h, lines_s, sems.at[0])
    lines_copy.start()

    def per_owner(owner, carry):
        for i in range(lines):
            rows = [
                jnp.zeros((stencil, LANES), F32),
                replies[owner, pl.ds(8 + i, stencil, stride=lines), :],
                jnp.zeros((1, LANES), F32),
                replies[owner, i : i + 1, :],
                jnp.zeros((LANES - 2 * stencil - 2, LANES), F32),
            ]
            at = pl.multiple_of(owner * slots + i * LANES, LANES)
            table[pl.ds(at, LANES), :] = jnp.concatenate(rows, axis=0).T
        return carry

    lax.fori_loop(0, parts, per_owner, 0, unroll=parts <= GROUP)
    lines_copy.wait()
    count = jnp.minimum(lines_s[(stencil + 3) * LANES], LISTED)

    def mix(numbers, weights):
        for slot in numbers:
            back = word_of(lines_s, slot, stencil + 2, stencil)
            mixed[pl.ds(slot, 1), :] = data[pl.ds(slot, 1), :] + table[pl.ds(back, 1), :]

    quads(0, count, mix)

    def build(top, places):
        rows = weight_rows(mixed[pl.ds(top, BLOCK), :], places, stencil)
        for place, row in enumerate(rows):
            merged[pl.ds(place * LISTED + top, BLOCK), :] = row

    blocks_of(lines_s, 0, count, stencil, build)
    copies = RowCopies(
        merged, merged_h, LISTED, lines_s, (sems.at[1], sems.at[2]), stencil
    )
    copies.always.start()
    copies.run_rest()
    copies.always.wait()


def most_batches(table, slots, stencil):
    most = word_of(table, slots[0], stencil, stencil)
    for slot in slots[1:]:
        most = jnp.maximum(most, word_of(table, slot, stencil, stencil))
    return most


def scatter_slots(table, merged, room, copies, slots, values, stencil):
    def batch(begin):
        for first in range(0, len(slots), len(copies)):
            todo = []
            some = slice(first, first + len(copies))
            for slot, value, ref in zip(slots[some], values[some], copies):
                for j in range(BATCH):
                    line = word_of(table, slot, begin + j, stencil)
                    row = merged[pl.ds((begin + j) * room + slot, 1), :] * value
                    todo.append((ref, line, ref[pl.ds(line, 1), :] + row))
            for ref, line, row in todo:
                ref[pl.ds(line, 1), :] = row

    def more(i, carry):
        batch(i * BATCH)
        return carry

    batch(0)
    lax.fori_loop(1, most_batches(table, slots, stencil), more, 0)


def band(shape, taps, shift):
    distance = iota(shape, 1) - iota(shape, 0) + shift
    result = jnp.zeros(shape, F32)
    for tap in range(taps.shape[0]):
        result = jnp.where(distance == tap, taps[tap], result)
    return result


def band_rev(shape, taps, shift):
    distance = iota(shape, 0) - iota(shape, 1) + shift
    result = jnp.zeros(shape, F32)
    for tap in range(taps.shape[0]):
        result = jnp.where(distance == tap, taps[tap], result)
    return result


def exact_nt(a, b):
    return lax.dot_general(
        a,
        b,
        (((1,), (1,)), ((), ())),
        precision=lax.Precision.HIGHEST,
        preferred_element_type=F32,
    )


def store_split(ref, index, value):
    high, low = split2(value)
    ref[(0,) + index] = high
    ref[(1,) + index] = low


def bands_kernel(kx, ky, lat2, lon2, lat1, lon1, *, rows_block):
    margin = kx.shape[0] // 2
    window = lat2.shape[2]
    first = band((window, window), ky, margin)
    reach = first[LANES : LANES + WIDE, :]
    place = iota((window, window), 1)
    for variant in range(3):
        kept = first
        if variant == 0:
            kept = jnp.where(place >= LANES, first, 0.0)
        if variant == 2:
            kept = jnp.where(place < LANES + WIDE, first, 0.0)
        store_split(lat2, (variant,), exact_nt(kept, reach))
    size = lon2.shape[1]
    wide = size + 2 * HALO
    depth = (wide + 32 + LANES - 1) // LANES * LANES
    second = band((wide, depth), kx, -(16 - margin))
    store_split(lon2, (), exact_nt(second[HALO : HALO + size, :], second))
    store_split(lat1, (), band_rev((rows_block, rows_block + 2 * PAD), ky, PAD + margin))
    store_split(lon1, (), band((2 * WIDE, WIDE), kx, LANES + margin))


def pairs(low, high, action):
    def step(i, carry):
        one = low + 2 * i
        action(one, jnp.minimum(one + 1, high - 1), one + 1 < high)
        return carry

    lax.fori_loop(0, lax.shift_right_logical(high - low + 1, 1), step, 0)


def quads(low, high, action):
    def step(i, carry):
        one = low + 4 * i
        numbers = [one] + [jnp.minimum(one + j, high - 1) for j in range(1, 4)]
        weights = [None] + [jnp.where(one + j < high, 1.0, 0.0) for j in range(1, 4)]
        action(numbers, weights)
        return carry

    lax.fori_loop(0, lax.shift_right_logical(high - low + 3, 2), step, 0)


def weighted(value, weight):
    return value if weight is None else value * weight


def zero_all(refs):
    rows = refs[0].shape[0]
    step = 256

    def clear(i, carry):
        for ref in refs:
            ref[pl.ds(pl.multiple_of(i * step, 8), step), :] = jnp.zeros((step, LANES), F32)
        return carry

    whole = rows // step
    lax.fori_loop(0, whole, clear, 0)
    if rows % step:
        for ref in refs:
            ref[whole * step : rows, :] = jnp.zeros((rows % step, LANES), F32)


def scatter_entries(copies, entries, lane):
    for start in range(0, len(entries), len(copies)):
        group = []
        for ref, (address, value) in zip(copies, entries[start : start + len(copies)]):
            line = lax.shift_right_logical(address, 7)
            spread = jnp.where(lane == (address & (LANES - 1)), value, 0.0)
            group.append((ref, line, ref[pl.ds(line, 1), :] + spread))
        for ref, line, value in group:
            ref[pl.ds(line, 1), :] = value


def spot(sender, idx, per, stencil):
    return sender * per + idx + lax.shift_right_logical(idx, 7) * ((stencil - 1) * LANES)


def copy_parts(layout, source, target, place, chunk, chunks, group, sem):
    begin, size = place
    words = group * size * LANES
    at = begin * LANES + chunk * words
    return pltpu.make_async_copy(source.at[pl.ds(at, words)], target, sem)


def apply_kernel(
    *refs, first, layout, columns, height, hold, stencil, capacity, senders, parts, levels
):
    refs = list(refs)

    def take(count):
        taken = refs[:count]
        del refs[:count]
        return taken

    meta, ints, floats, own_lines, own = take(5)
    if not first:
        replies_h, replies = take(2)
    std_h, std_l_h, std_r_h, lat2_h, lon2_h = take(5)
    if not first:
        merged_h, _ = take(2)
    field_h, send = take(2)
    if first:
        info_out, merged_h = take(2)
    addr, wgt, start, lines_s, val = take(5)
    if first:
        std_flat, picked, chosen = take(3)
    scale, merged, sums, high_s, low_s, std, std_l, std_r, lat2, lon2, field = take(11)
    copies = take(PAIR)
    sems, in_sems, out_sems, val_sem = take(4)

    me = meta[0]
    wide = columns + 2 * HALO
    blocks = height // LANES
    group = min(GROUP, senders)
    chunks = senders // group
    slots = senders * capacity
    lane = iota((1, LANES), 1)
    per = stencil * hold
    table = layout.table

    def chunk_copies(chunk):
        todo = [
            (ints, addr, layout.ints["addr"]),
            (floats, wgt, layout.floats["wgt"]),
            (ints, start, layout.ints["start"]),
        ]
        if first:
            todo.append((floats, val, layout.floats["val"]))
        return [
            copy_parts(layout, source, target, place, chunk, chunks, group, sems.at[i])
            for i, (source, target, place) in enumerate(todo)
        ]

    def load_chunk(chunk):
        for copy in chunk_copies(chunk):
            copy.start()
        for copy in chunk_copies(chunk):
            copy.wait()

    operands = [
        pltpu.make_async_copy(source, target, in_sems.at[i])
        for i, (source, target) in enumerate(
            (
                (std_h, std),
                (std_l_h, std_l),
                (std_r_h, std_r),
                (lat2_h, lat2),
                (lon2_h, lon2),
            )
        )
    ]
    own_copy = pltpu.make_async_copy(own_lines, lines_s, in_sems.at[5])
    own_copy.start()
    merged_copies = RowCopies(
        *((merged, merged_h) if first else (merged_h, merged)),
        slots + LANES,
        lines_s,
        (in_sems.at[6], in_sems.at[7]),
        stencil,
    )
    if not first:
        merged_copies.always.start()
    for copy in operands:
        copy.start()

    def value_copy(owner):
        at = pl.multiple_of(owner * (replies_h.shape[0] // parts), 1024)
        return pltpu.make_async_copy(
            replies_h.at[pl.ds(at, slots)], val.at[pl.ds(owner * slots, slots)], val_sem.at[owner]
        )

    def each_owner(action):
        def step(owner, carry):
            action(value_copy(owner))
            return carry

        lax.fori_loop(0, parts, step, 0)

    if not first:
        each_owner(lambda copy: copy.start())
    zero_all(copies)
    zero_all([sums])

    lane_of = iota((slots, LANES), 1)
    room = slots + LANES
    column = 2 * stencil if first else 2 * stencil + 2
    scale[...] = jnp.broadcast_to(own[:, column : column + 1], (room, LANES))
    known = own[0:slots, :]
    own_copy.wait()
    if not first:
        merged_copies.always.wait()
        merged_copies.run_rest()

    after = lax.rem(me + 1, parts)
    ahead = lax.rem(me + parts - 1, parts)

    def start_of(sender, owner, row, half):
        return start[sender * table + row * hold + half * LANES + owner]

    def entries_of(sender, idx, value):
        base = spot(sender, idx, per, stencil)
        return [
            (addr[base + k * LANES], wgt[base + k * LANES] * value) for k in range(stencil)
        ]

    def own_line(slot, k):
        return word_of(lines_s, slot, k, stencil)

    def amount_of(sender):
        return lines_s[(stencil + 3) * LANES + sender]

    halo_count = lines_s[(stencil + 4) * LANES]
    halo_fits = halo_count <= LANES

    def own_groups(action, halo):
        if capacity % BLOCK:
            blocks_of(lines_s, 0, slots, stencil, action)
        else:

            def per_sender(sender, carry):
                blocks_of(lines_s, sender * capacity, amount_of(sender), stencil, action)
                return carry

            lax.fori_loop(0, senders, per_sender, 0)
        if halo:
            blocks_of(lines_s, slots, jnp.minimum(halo_count, LANES), stencil, action)

    def build(top, places):
        rows = weight_rows(own[pl.ds(top, BLOCK), :], places, stencil)
        for place, row in enumerate(rows):
            merged[pl.ds(place * room + top, BLOCK), :] = row

    if first:
        own_groups(build, True)
        merged_copies.always.start()
        merged_copies.run_rest()

    def own_quads(action):
        def per_sender(sender, carry):
            base = sender * capacity
            quads(base, base + amount_of(sender), action)
            return carry

        lax.fori_loop(0, senders, per_sender, 0)

    def scatter_known(numbers, weights):
        values = [weighted(scale[pl.ds(i, 1), :], w) for i, w in zip(numbers, weights)]
        scatter_slots(lines_s, merged, room, copies, numbers, values, stencil)

    def scatter_sent(numbers, weights):
        values = [weighted(val[own_line(i, stencil + 2)], w) for i, w in zip(numbers, weights)]
        scatter_slots(lines_s, merged, room, copies, numbers, values, stencil)

    def scatter_halo(chunk):
        def per_sender(sender, carry):
            for owner, low, high in ((after, (1, 0), (1, 1)), (ahead, (2, 0), (0, 1))):
                begin = start_of(sender, owner, 0, 0)

                def value_of(idx, owner=owner, begin=begin):
                    if first:
                        return val[sender * hold + idx]
                    place = (chunk * group + sender) * capacity + idx - begin
                    return val[owner * slots + place]

                def action(one, two, has_two, value_of=value_of):
                    second = jnp.where(has_two, value_of(two), 0.0)
                    scatter_entries(
                        copies,
                        entries_of(sender, one, value_of(one)) + entries_of(sender, two, second),
                        lane,
                    )

                pairs(start_of(sender, owner, *low), start_of(sender, owner, *high), action)
            return carry

        lax.fori_loop(0, group, per_sender, 0)

    own_quads(scatter_known)
    if not first:
        each_owner(lambda copy: copy.wait())

    @pl.when(halo_fits)
    def _():
        quads(slots, slots + halo_count, scatter_known if first else scatter_sent)

    @pl.when(jnp.logical_not(halo_fits))
    def _():
        def step(chunk, carry):
            load_chunk(chunk)
            scatter_halo(chunk)
            return carry

        lax.fori_loop(0, chunks, step, 0)

    for copy in operands:
        copy.wait()

    def prepare(jb):
        lanes = slice(jb * LANES, (jb + 1) * LANES)
        for low, size, source in (
            (0, HALO, std_l),
            (HALO, columns, std),
            (HALO + columns, HALO, std_r),
        ):
            rows = slice(jb * wide + low, jb * wide + low + size)
            total = copies[0][rows, :]
            for ref in copies[1:]:
                total = total + ref[rows, :]
            high, lo = split2(total * source[:, lanes])
            high_s[low : low + size, lanes] = high
            low_s[low : low + size, lanes] = lo
        if first:
            std_flat[jb * wide + HALO : jb * wide + HALO + columns, :] = std[:, lanes]

    smoothed = copies[0]
    size = lon2.shape[1]
    count = height // WIDE
    outgoing = [merged_copies.always] if first else []

    def along_latitude(block):
        variant = 0 if block == 0 else (2 if block == count - 1 else 1)
        low = max(block * WIDE - LANES, 0)
        high = min(block * WIDE + WIDE + LANES, height)
        inner = slice(low - (block * WIDE - LANES), high - (block * WIDE - LANES))
        matrix = (lat2[0, variant, inner, :], lat2[1, variant, inner, :])
        return split2(mm_parts((high_s[:, low:high], low_s[:, low:high]), matrix))

    def along_longitude(block, parts_y):
        lanes = slice(block * WIDE, (block + 1) * WIDE)
        for begin in range(0, columns, size):
            some = min(size, columns - begin)
            rows = slice(begin, begin + some)
            window = slice(begin, begin + some + 2 * HALO)
            matrix = tuple(lon2[i, 0:some, 0 : some + 2 * HALO] for i in range(2))
            result = mm_parts(matrix, (parts_y[0][window, :], parts_y[1][window, :]))
            scaled = result * std[rows, lanes]
            field[rows, lanes] = scaled
            for half in range(WIDE // LANES):
                top = (block * (WIDE // LANES) + half) * wide + HALO + begin
                smoothed[top : top + some, :] = scaled[:, half * LANES : (half + 1) * LANES]
        outgoing.append(
            pltpu.make_async_copy(field.at[:, lanes], field_h.at[:, lanes], out_sems.at[block])
        )
        outgoing[-1].start()

    ready = 0
    waiting = None
    for block in range(count + 1):
        upto = min((block + 1) * (WIDE // LANES) + 1, blocks)
        for jb in range(ready, upto):
            prepare(jb)
        ready = max(ready, upto)
        following = along_latitude(block) if block < count else None
        if block > 0:
            along_longitude(block - 1, waiting)
        waiting = following

    def gather_quad(numbers, weights):
        def batch(begin, totals):
            result = []
            for slot, total in zip(numbers, totals):
                terms = []
                for j in range(BATCH):
                    line = own_line(slot, begin + j)
                    row = merged[pl.ds((begin + j) * room + slot, 1), :]
                    terms.append(row * smoothed[pl.ds(line, 1), :])
                    if first:
                        picked[pl.ds((begin + j) * room + slot, 1), :] = std_flat[
                            pl.ds(line, 1), :
                        ]
                result.append(total + ((terms[0] + terms[1]) + (terms[2] + terms[3])))
            return tuple(result)

        zero = jnp.zeros((1, LANES), F32)
        totals = lax.fori_loop(
            1,
            most_batches(lines_s, numbers, stencil),
            lambda i, totals: batch(i * BATCH, totals),
            batch(0, (zero,) * len(numbers)),
        )
        for slot, total in zip(numbers, totals):
            sums[pl.ds(slot, 1), :] = total

    own_quads(gather_quad)

    def pick(top, places):
        info = own[pl.ds(top, BLOCK), :]
        codes = columns_of(info, CODES, stencil)
        lane_f = iota(info.shape, 1).astype(F32)
        rows = [picked[pl.ds(place * room + top, BLOCK), :] for place in range(places)]
        result = jnp.zeros((BLOCK, LANES), F32)
        for k in range(stencil):
            cell = jnp.zeros((BLOCK, LANES), F32)
            for place in range(min(k + 1, places)):
                at = lane_f + float(LANES * place)
                cell = jnp.where(at == codes[k], rows[place], cell)
            cell = jnp.sum(cell, axis=1, keepdims=True)
            result = jnp.where(lane_f == float(stencil + k), cell, result)
        chosen[pl.ds(top, BLOCK), :] = result * info

    if first:
        own_groups(pick, False)

    def whole(x):
        return jnp.sum(x, axis=0, keepdims=True)

    total = jnp.sum(sums[...], axis=1, keepdims=True)
    lines = slots // LANES
    known = own[0:slots, :]
    source, weight, reply, image0 = (
        known[:, 2 * stencil + i : 2 * stencil + i + 1] for i in range(4)
    )
    if first:
        reply = weight * total
        known = jnp.where(lane_of == 2 * stencil + 2, reply, known)
        known = jnp.where(lane_of == 2 * stencil + 3, total, known)
        info_out[0:slots, :] = known
        info_out[slots:room, :] = own[slots:room, :]
        turned = known.T[2 * stencil + 2 : 2 * stencil + 3, :]
        message = [turned[:, i * LANES : (i + 1) * LANES] for i in range(lines)]
        message.append(
            jnp.where(
                lane == 0, whole(source * total), jnp.where(lane == 1, whole(reply * total), 0.0)
            )
        )
        message.append(jnp.zeros((8 - len(message), LANES), F32))
        factors = chosen[...].T
        for k in range(stencil):
            row = factors[stencil + k : stencil + k + 1, :]
            message += [row[:, i * LANES : (i + 1) * LANES] for i in range(lines)]
        message = jnp.concatenate(message, axis=0)
    else:
        slab = jnp.sum(replies[:, 0:8, :], axis=0)[lines : lines + 1, :]
        length = slab[:, 0:1] / (slab[:, 0:1] + slab[:, 1:2])
        both = source + reply
        s_both = image0 + total
        resid = source - length * both
        s_resid = image0 - length * s_both
        values = [
            resid * s_resid,
            resid * s_both,
            both * s_both,
            resid * image0,
            both * image0,
            weight * s_resid * s_resid,
            weight * s_resid * s_both,
            weight * s_both * s_both,
            weight * s_resid * image0,
            weight * s_both * image0,
            source * image0,
            reply * image0,
        ]
        message = jnp.where(lane == len(values), length, 0.0)
        for i, value in enumerate(values):
            message = jnp.where(lane == i, whole(value), message)
        message = jnp.concatenate([message, jnp.zeros((7, LANES), F32)], axis=0)

    def send_to(i, carry):
        send[i] = message
        return carry

    lax.fori_loop(0, send.shape[0], send_to, 0)
    for copy in outgoing:
        copy.wait()


def final_kernel(
    ints,
    floats,
    replies_h,
    lines_h,
    merged_h,
    mixed,
    totals,
    field0_h,
    field1_h,
    lat1,
    lon1,
    control_h,
    increment_h,
    addr,
    listed,
    slot,
    val,
    factors,
    field0,
    field1,
    control,
    high_s,
    low_s,
    lines_s,
    merged,
    scale,
    *rest,
    layout,
    hold,
    stencil,
    capacity,
    senders,
    parts,
    length,
):
    copies = rest[:PAIR]
    sems, in_sems, out_sems = rest[PAIR:]
    group = min(GROUP, senders)
    chunks = senders // group
    per = stencil * hold
    rows_block = control.shape[0]
    high_rows = rows_block + 2 * PAD
    lane = iota((1, LANES), 1)
    stride = group * capacity
    owner_words = factors.shape[0] // parts
    to_factors = owner_words - stencil * stride

    def chunk_copies(chunk):
        todo = [
            (ints, addr, layout.ints["rows"]),
            (ints, listed, layout.ints["listed"]),
            (ints, slot, layout.ints["slot"]),
            (floats, val, layout.floats["val"]),
        ]
        result = [
            copy_parts(layout, source, target, place, chunk, chunks, group, sems.at[i])
            for i, (source, target, place) in enumerate(todo)
        ]
        words = parts * owner_words
        result.append(
            pltpu.make_async_copy(
                replies_h.at[pl.ds(chunk * words, words)], factors, sems.at[len(todo)]
            )
        )
        return result

    row_copies = RowCopies(
        merged_h, merged, LISTED, lines_s, (in_sems.at[3], in_sems.at[4]), stencil
    )
    listing = [pltpu.make_async_copy(lines_h, lines_s, in_sems.at[2]), row_copies.always]
    for copy in listing:
        copy.start()
    operands = [
        pltpu.make_async_copy(source, target, in_sems.at[i])
        for i, (source, target) in enumerate(
            ((field0_h, field0), (field1_h, field1))
        )
    ]
    for copy in operands:
        copy.start()

    slabs = totals.shape[1]
    every = jnp.sum(totals[...], axis=0)
    norm0 = quad0 = None
    for i in range(slabs):
        line = every[i, 0:1, :]
        a, b = line[:, 10:11], line[:, 11:12]
        norm0 = a if norm0 is None else norm0 + a
        quad0 = b if quad0 is None else quad0 + b
    step0 = norm0 / (norm0 + quad0)
    norm1 = cross = quad1 = quad01 = jnp.zeros((1, 1), F32)
    for i in range(slabs):
        line = every[i, 0:1, :]
        v = [line[:, j : j + 1] for j in range(10)]
        shift = totals[0, i, 0:1, 12:13] - step0
        norm1 = norm1 + (v[0] + shift * (2.0 * v[1] + shift * v[2]))
        cross = cross + (v[3] + shift * v[4])
        quad1 = quad1 + (v[5] + shift * (2.0 * v[6] + shift * v[7]))
        quad01 = quad01 + (v[8] + shift * v[9])
    ratio = norm1 / norm0
    curvature = norm1 + quad1 + ratio * (
        2.0 * (cross + quad01) + ratio * (norm0 + quad0)
    )
    step1 = norm1 / curvature
    first = step0 + step1 * (1.0 - step0 + ratio)
    second = -step0 * step1
    first_line = jnp.broadcast_to(first, (1, LANES))
    second_line = jnp.broadcast_to(second, (1, LANES))

    zero_all(copies)

    data = mixed[...]
    column = 2 * stencil
    scale[...] = first * data[:, column : column + 1] + second * jnp.broadcast_to(
        data[:, column + 1 : column + 2], data.shape
    )
    for copy in listing:
        copy.wait()
    row_copies.run_rest()
    count = lines_s[(stencil + 3) * LANES]

    def add(numbers, weights):
        values = [weighted(scale[pl.ds(i, 1), :], w) for i, w in zip(numbers, weights)]
        scatter_slots(lines_s, merged, LISTED, copies, numbers, values, stencil)

    def scatter_chunk():
        def per_sender(sender, carry):
            def step(idx, inner):
                @pl.when(listed[sender * hold + idx] > 0)
                def _():
                    place = slot[sender * hold + idx]
                    place = place + lax.div(place, stride) * (owner_words - stride)
                    base = spot(sender, idx, per, stencil)
                    z0 = val[sender * hold + idx]
                    value = first_line * z0 + second_line * factors[place]
                    entries = [
                        (addr[base + k * LANES], factors[place + to_factors + k * stride] * value)
                        for k in range(stencil)
                    ]
                    scatter_entries(copies, entries, lane)

                return inner

            lax.fori_loop(0, hold, step, 0)
            return carry

        lax.fori_loop(0, group, per_sender, 0)

    @pl.when(count <= LISTED)
    def _():
        quads(0, count, add)

    @pl.when(count > LISTED)
    def _():
        def step(chunk, carry):
            for copy in chunk_copies(chunk):
                copy.start()
            for copy in chunk_copies(chunk):
                copy.wait()
            scatter_chunk()
            return carry

        lax.fori_loop(0, chunks, step, 0)

    for copy in operands:
        copy.wait()
    increment = field0
    increment[...] = first * field0[...] + second * field1[...]
    outgoing = [pltpu.make_async_copy(increment, increment_h, out_sems.at[0])]
    outgoing[0].start()

    pair = WIDE // LANES
    count = length // WIDE

    def along_latitude(block):
        pieces = []
        for half in range(pair):
            rows = slice((block * pair + half) * high_rows, (block * pair + half + 1) * high_rows)
            total = copies[0][rows, :]
            for ref in copies[1:]:
                total = total + ref[rows, :]
            pieces.append(total)
        whole = split2(jnp.concatenate(pieces, axis=1))
        size = lat1.shape[1]
        for top in range(0, rows_block, size):
            window = slice(top, top + size + 2 * PAD)
            along = mm_parts((lat1[0], lat1[1]), (whole[0][window, :], whole[1][window, :]))
            high, low = split2(along)
            high_s[top : top + size, block * WIDE : (block + 1) * WIDE] = high
            low_s[top : top + size, block * WIDE : (block + 1) * WIDE] = low

    def window(ref, block):
        low, high = block * WIDE - LANES, (block + 1) * WIDE + LANES
        if low < 0:
            return jnp.concatenate([ref[:, length + low : length], ref[:, 0:high]], axis=1)
        if high > length:
            return jnp.concatenate([ref[:, low:length], ref[:, 0 : high - length]], axis=1)
        return ref[:, low:high]

    every_lanes = 4

    def along_longitude(block):
        control[:, block * WIDE : (block + 1) * WIDE] = mm_parts(
            (window(high_s, block), window(low_s, block)), (lon1[0], lon1[1])
        )
        if block % every_lanes == every_lanes - 1:
            lanes = slice((block + 1 - every_lanes) * WIDE, (block + 1) * WIDE)
            outgoing.append(
                pltpu.make_async_copy(
                    control.at[:, lanes], control_h.at[:, lanes], out_sems.at[len(outgoing)]
                )
            )
            outgoing[-1].start()

    along_latitude(count - 1)
    along_latitude(0)
    along_latitude(1)
    for block in range(count):
        if 2 <= block + 2 < count - 1:
            along_latitude(block + 2)
        along_longitude(block)
    for copy in outgoing:
        copy.wait()


def body(
    background_std,
    x_kernel,
    y_kernel,
    obs_owner,
    obs_cells,
    obs_weights,
    innovation,
    obs_precision,
    obs_counts,
):
    parts = lax.axis_size("pencil")
    levels = lax.axis_size("lev")
    me = lax.axis_index("pencil")
    _, columns, height = background_std.shape
    hold, stencil = obs_cells.shape
    margin = x_kernel.shape[1] // 2
    capacity = 2 * hold // parts
    senders = parts
    slots = senders * capacity
    room = slots + LANES
    rows_block = height // parts
    length = columns * parts
    blocks = height // LANES
    wide = columns + 2 * HALO
    group = min(GROUP, senders)
    chunks = senders // group
    layout = Layout(senders, hold, stencil, parts)
    std = background_std[0]

    packed = pl.pallas_call(
        functools.partial(
            pack_kernel, parts=parts, columns=columns, height=height, margin=margin
        ),
        out_shape=jax.ShapeDtypeStruct((parts, PACK, hold), F32),
        in_specs=[smem()] + [vmem()] * 5,
        out_specs=vmem(),
        scratch_shapes=[pltpu.VMEM((parts, hold), F32)],
        compiler_params=params(),
        cost_estimate=cost(12000),
        name="pack",
    )(
        obs_counts,
        obs_owner.T,
        obs_cells.T,
        obs_weights.T,
        innovation[None, :],
        obs_precision[None, :],
    )
    recv = lax.all_to_all(packed, "pencil", split_axis=0, concat_axis=0, tiled=True)

    right_of = [(p, (p + 1) % parts) for p in range(parts)]
    left_of = [(p, (p - 1) % parts) for p in range(parts)]
    std_l = lax.ppermute(std[columns - HALO :, :], "pencil", right_of)
    std_r = lax.ppermute(std[:HALO, :], "pencil", left_of)

    size = min(columns, WIDE - 2 * HALO)
    row_size = min(rows_block, LANES)
    lat2, lon2, lat1, lon1 = pl.pallas_call(
        functools.partial(bands_kernel, rows_block=row_size),
        out_shape=[
            jax.ShapeDtypeStruct((2, 3, 2 * WIDE, WIDE), BF),
            jax.ShapeDtypeStruct((2, size, size + 2 * HALO), BF),
            jax.ShapeDtypeStruct((2, row_size, row_size + 2 * PAD), BF),
            jax.ShapeDtypeStruct((2, 2 * WIDE, WIDE), BF),
        ],
        in_specs=[smem(), smem()],
        out_specs=[vmem()] * 4,
        compiler_params=params(),
        cost_estimate=cost(100),
        name="bands",
    )(x_kernel[0], y_kernel[0])

    meta = jnp.reshape(me, (1,)).astype(I32)
    place = dict(
        parts=parts, columns=columns, height=height, capacity=capacity, stencil=stencil
    )
    ints, floats, own_lines, own = pl.pallas_call(
        functools.partial(unpack_kernel, layout=layout, group=group, **place),
        out_shape=[
            jax.ShapeDtypeStruct((layout.int_rows, LANES), I32),
            jax.ShapeDtypeStruct((layout.float_rows, LANES), F32),
            jax.ShapeDtypeStruct((room // LANES * (stencil + 8), LANES), I32),
            jax.ShapeDtypeStruct((room, LANES), F32),
        ],
        in_specs=[smem(), vmem(), hbm()],
        out_specs=[vmem()] * 4,
        scratch_shapes=[
            pltpu.VMEM((room // LANES, STACK, LANES), F32),
        ],
        compiler_params=params(),
        cost_estimate=cost(100),
        name="unpack",
    )(meta, recv, lat1)
    ints = ints.reshape(-1)
    floats = floats.reshape(-1)
    own_lines = own_lines.reshape(-1)

    acc = pltpu.VMEM((blocks * wide + 8, LANES), F32)
    column_slots = pltpu.VMEM((slots, LANES), F32)
    static = dict(
        layout=layout,
        columns=columns,
        height=height,
        hold=hold,
        stencil=stencil,
        capacity=capacity,
        senders=senders,
        parts=parts,
        levels=levels,
    )
    per = group * stencil * hold
    line = group * hold
    index_scratch = [
        pltpu.SMEM((per,), I32),
        pltpu.SMEM((per,), F32),
        pltpu.SMEM((group * layout.table,), I32),
        pltpu.SMEM((room * (stencil + 8),), I32),
    ]
    work = (
        [
            pltpu.VMEM((room, LANES), F32),
            pltpu.VMEM((stencil * room, LANES), F32),
            column_slots,
        ]
        + [pltpu.VMEM((wide, height), BF)] * 2
        + [
            pltpu.VMEM((columns, height), F32),
            pltpu.VMEM((HALO, height), F32),
            pltpu.VMEM((HALO, height), F32),
            pltpu.VMEM(lat2.shape, BF),
            pltpu.VMEM(lon2.shape, BF),
            pltpu.VMEM((columns, height), F32),
        ]
        + [acc] * PAIR
        + [
            pltpu.SemaphoreType.DMA((4,)),
            pltpu.SemaphoreType.DMA((8,)),
            pltpu.SemaphoreType.DMA((height // WIDE,)),
            pltpu.SemaphoreType.DMA((parts,)),
        ]
    )
    field_shape = jax.ShapeDtypeStruct((columns, height), F32)
    reply_rows = 8 + stencil * slots // LANES
    field0, message, info, merged = pl.pallas_call(
        functools.partial(apply_kernel, first=True, **static),
        out_shape=[
            field_shape,
            jax.ShapeDtypeStruct((parts, reply_rows, LANES), F32),
            jax.ShapeDtypeStruct((room, LANES), F32),
            jax.ShapeDtypeStruct((stencil * room, LANES), F32),
        ],
        in_specs=[smem()] + [hbm()] * 3 + [vmem()] + [hbm()] * 5,
        out_specs=[hbm()] + [vmem()] * 2 + [hbm()],
        scratch_shapes=index_scratch
        + [
            pltpu.SMEM((line,), F32),
            acc,
            pltpu.VMEM((stencil * room, LANES), F32),
            column_slots,
        ]
        + work,
        compiler_params=params(),
        name="apply_first",
    )(meta, ints, floats, own_lines, own, std, std_l, std_r, lat2, lon2)

    replies = lax.all_to_all(message, "pencil", split_axis=0, concat_axis=0, tiled=True)
    back = replies.reshape(-1)
    line_rows = LISTED // LANES * (stencil + 8)
    row_lines, row_data = pl.pallas_call(
        functools.partial(list_kernel, **place),
        out_shape=[
            jax.ShapeDtypeStruct((line_rows, LANES), I32),
            jax.ShapeDtypeStruct((LISTED, LANES), F32),
        ],
        in_specs=[smem(), vmem(), hbm()],
        out_specs=[vmem()] * 2,
        scratch_shapes=[pltpu.VMEM((STACK, LISTED), F32)],
        compiler_params=params(),
        cost_estimate=cost(4000),
        name="list_rows",
    )(meta, recv, info)
    row_lines = row_lines.reshape(-1)

    field1, sums = pl.pallas_call(
        functools.partial(apply_kernel, first=False, **static),
        out_shape=[
            field_shape,
            jax.ShapeDtypeStruct((parts * levels, 8, LANES), F32),
        ],
        in_specs=[smem()] + [hbm()] * 3 + [vmem(), hbm(), vmem()] + [hbm()] * 7,
        out_specs=[hbm(), vmem()],
        scratch_shapes=index_scratch + [pltpu.SMEM((parts * slots,), F32)] + work,
        compiler_params=params(),
        name="apply_second",
    )(
        meta,
        ints,
        floats,
        own_lines,
        info,
        back,
        replies,
        std,
        std_l,
        std_r,
        lat2,
        lon2,
        merged,
        row_data,
    )

    totals = lax.all_to_all(sums, ("pencil", "lev"), split_axis=0, concat_axis=0, tiled=True)
    totals = totals.reshape(parts, levels, 8, LANES)

    listed_rows, mixed = pl.pallas_call(
        functools.partial(factor_kernel, stencil=stencil, slots=slots),
        out_shape=[
            jax.ShapeDtypeStruct((stencil * LISTED, LANES), F32),
            jax.ShapeDtypeStruct((LISTED, LANES), F32),
        ],
        in_specs=[hbm(), vmem(), vmem(), hbm()],
        out_specs=[hbm(), vmem()],
        scratch_shapes=[
            pltpu.SMEM((line_rows * LANES,), I32),
            pltpu.VMEM((parts * slots, LANES), F32),
            pltpu.VMEM((stencil * LISTED, LANES), F32),
            pltpu.SemaphoreType.DMA((3,)),
        ],
        compiler_params=params(),
        cost_estimate=cost(8000),
        name="factor_rows",
    )(row_lines, row_data, replies, sums)

    by_chunk = back
    if chunks > 1:
        by_chunk = jnp.concatenate(
            [replies[:, : slots // LANES, :], replies[:, 8:, :]], axis=1
        ).reshape(parts, stencil + 1, chunks, group * capacity)
        by_chunk = jnp.transpose(by_chunk, (2, 0, 1, 3)).reshape(-1)
    owner_words = by_chunk.shape[0] // (chunks * parts)
    high_rows = rows_block + 2 * PAD
    acc_rows = pltpu.VMEM(((length // LANES) * high_rows + 8, LANES), F32)
    control, increment = pl.pallas_call(
        functools.partial(
            final_kernel,
            layout=layout,
            hold=hold,
            stencil=stencil,
            capacity=capacity,
            senders=senders,
            parts=parts,
            length=length,
        ),
        out_shape=[
            jax.ShapeDtypeStruct((rows_block, length), F32),
            field_shape,
        ],
        in_specs=[hbm()] * 5 + [vmem()] * 2 + [hbm()] * 2 + [vmem()] * 2,
        out_specs=[hbm()] * 2,
        scratch_shapes=[
            pltpu.SMEM((per,), I32),
            pltpu.SMEM((line,), I32),
            pltpu.SMEM((line,), I32),
            pltpu.SMEM((line,), F32),
            pltpu.SMEM((parts * owner_words,), F32),
            pltpu.VMEM((columns, height), F32),
            pltpu.VMEM((columns, height), F32),
            pltpu.VMEM((rows_block, length), F32),
            pltpu.VMEM((rows_block, length), BF),
            pltpu.VMEM((rows_block, length), BF),
            pltpu.SMEM((line_rows * LANES,), I32),
            pltpu.VMEM((stencil * LISTED, LANES), F32),
            pltpu.VMEM((LISTED, LANES), F32),
        ]
        + [acc_rows] * PAIR
        + [
            pltpu.SemaphoreType.DMA((5,)),
            pltpu.SemaphoreType.DMA((5,)),
            pltpu.SemaphoreType.DMA((1 + length // WIDE,)),
        ],
        compiler_params=params(),
        name="outputs",
    )(
        ints,
        floats,
        by_chunk,
        row_lines,
        listed_rows,
        mixed,
        totals,
        field0,
        field1,
        lat1,
        lon1,
    )
    return control[None], increment[None]


def solution(mesh):
    return jax.shard_map(
        body,
        mesh=mesh,
        in_specs=(
            P("lev", "pencil", None),
            P("lev", None),
            P("lev", None),
            P(("pencil", "lev"), None),
            P(("pencil", "lev"), None),
            P(("pencil", "lev"), None),
            P(("pencil", "lev")),
            P(("pencil", "lev")),
            P(("pencil", "lev")),
        ),
        out_specs=(P("lev", "pencil", None), P("lev", "pencil", None)),
        check_vma=False,
    )
```

```python
import functools

import jax
import jax.numpy as jnp
import numpy as np
from jax import lax
from jax.experimental import pallas as pl
from jax.experimental.pallas import tpu as pltpu
from jax.sharding import PartitionSpec as P


BF = jnp.bfloat16
F32 = jnp.float32
I32 = jnp.int32
LANES = 128
WIDE = 256
HALO = 32
PAD = 16
PACK = 40
GROUP = 8
PAIR = 2
BATCH = 4
BLOCK = 32
CODES = 40
STACK = 64
LISTED = 512
VMEM_LIMIT = 58 * 1024 * 1024


def vmem():
    return pl.BlockSpec(memory_space=pltpu.VMEM)


def smem():
    return pl.BlockSpec(memory_space=pltpu.SMEM)


def hbm():
    return pl.BlockSpec(memory_space=pl.ANY)


def cost(nanoseconds):
    return pl.CostEstimate(flops=0, bytes_accessed=3690 * nanoseconds, transcendentals=0)


def params():
    return pltpu.CompilerParams(vmem_limit_bytes=VMEM_LIMIT)


def split2(x):
    high = x.astype(BF)
    return high, (x - high.astype(F32)).astype(BF)


def split3(x):
    high = x.astype(BF)
    rest = x - high.astype(F32)
    mid = rest.astype(BF)
    return high, mid, (rest - mid.astype(F32)).astype(BF)


def mm(a, b):
    return jnp.dot(a, b, preferred_element_type=F32)


def mm_parts(a_parts, b_parts):
    (ah, al), (bh, bl) = a_parts, b_parts
    return mm(jnp.concatenate([ah, al, ah], axis=1), jnp.concatenate([bh, bh, bl], axis=0))


def iota(shape, dim):
    return lax.broadcasted_iota(I32, shape, dim)


def pack_kernel(
    counts, owner, cells, weights, depart, prec, out, marks, *, parts, columns, height, margin
):
    stencil, hold = cells.shape
    shift = height.bit_length() - 1
    block = height // parts
    reach = 2 * margin
    row_id = iota((hold, hold), 0)
    col_id = iota((hold, hold), 1)
    eye = row_id == col_id
    col_f = col_id.astype(F32)
    live = iota((1, hold), 1) < counts[0]
    cell = cells[...]
    column = lax.shift_right_logical(cell, jnp.full(cell.shape, shift, I32))
    row = cell & (height - 1)

    def any_of(mask):
        return jnp.max(jnp.where(mask, 1.0, 0.0), axis=0, keepdims=True)

    def turn(line):
        return jnp.sum(jnp.where(eye, line, 0.0), axis=1, keepdims=True)

    left = any_of(column < reach)
    right = any_of(column >= columns - reach)
    side = left + 3.0 * right - 2.0 * left * right
    base = jnp.where(live, owner[...].astype(F32) * 4.0, 4.0 * parts)
    key = jnp.where(live, base + side, base)
    key_col = turn(key)
    before = (key_col < key) | ((key_col == key) & (row_id < col_id))
    rank = jnp.sum(jnp.where(before, 1.0, 0.0), axis=0, keepdims=True)
    begin = jnp.sum(jnp.where(key_col < base, 1.0, 0.0), axis=0, keepdims=True)
    rank_col = turn(rank)
    perm = jnp.where(rank_col == col_f, 1.0, 0.0).astype(BF)

    def sort(values):
        total = None
        for part in split3(values):
            term = mm(part, perm)
            total = term if total is None else total + term
        return total

    weight = jnp.where(live, prec[...], 0.0)
    rest = [weight * depart[...], weight, key, rank - begin, jnp.zeros((4, hold), F32)]
    values = [cell.astype(F32), weights[...]] + rest
    ordered = sort(jnp.concatenate(values, axis=0))
    line = iota((8, hold), 0)
    tail = ordered[2 * stencil : 2 * stencil + 8, :]
    first_half = col_f < float(LANES)
    fourfold = 4.0 * jnp.where(first_half, col_f, col_f - float(LANES))
    for i, (low, high) in enumerate(((0.0, 4.0), (1.0, 3.0), (2.0, 2.0))):
        bound = fourfold + jnp.where(first_half, low, high)
        begins = jnp.sum(jnp.where(key_col < bound, 1.0, 0.0), axis=0, keepdims=True)
        tail = jnp.where(line == 5 + i, begins, tail)
    last = (line == 7) & (iota((8, hold), 1) == hold - 1)

    def mark(part, carry):
        low = part * block - margin
        high = (part + 1) * block + margin
        flag = jnp.where(live, any_of((row >= low) & (row < high)), 0.0)
        place = jnp.sum(jnp.where(row_id < col_id, turn(flag), 0.0), axis=0, keepdims=True)
        marks[pl.ds(part, 1), :] = flag * (place + 1.0)
        return carry

    lax.fori_loop(0, parts, mark, 0, unroll=parts <= GROUP)
    listed = marks[...]
    amounts = jnp.max(listed, axis=1, keepdims=True)
    listed = mm(listed.astype(BF), perm)
    for part in range(parts):
        out[part, 0 : 2 * stencil, :] = ordered[0 : 2 * stencil, :]
        out[part, 2 * stencil : 2 * stencil + 8, :] = jnp.where(
            line == 4,
            listed[part : part + 1, :],
            jnp.where(last, amounts[part : part + 1, :], tail),
        )


class Layout:
    def __init__(self, senders, hold, stencil, parts):
        lines = hold // LANES
        self.table = 3 * hold
        sizes = dict(
            addr=stencil * lines, rows=stencil * lines, listed=lines, slot=lines, start=3 * lines
        )
        self.ints = {}
        at = 0
        for name, size in sizes.items():
            self.ints[name] = (at, size)
            at += senders * size
        self.int_rows = at
        self.floats = {}
        at = 0
        for name, size in dict(wgt=stencil * lines, val=lines).items():
            self.floats[name] = (at, size)
            at += senders * size
        self.float_rows = at


def right(x, by):
    return lax.shift_right_logical(x, jnp.full(x.shape, by, I32))


def nt(a, b):
    return lax.dot_general(a, b, (((1,), (1,)), ((), ())), preferred_element_type=F32)


class Received:
    def __init__(self, recv, sender, me, *, parts, columns, height, capacity, stencil):
        senders, _, hold = recv.shape
        wide = columns + 2 * HALO
        block = height // parts
        high_rows = block + 2 * PAD
        cell = recv[sender, 0:stencil, :].astype(I32)
        self.tail = recv[sender, 2 * stencil : 2 * stencil + 8, :]
        self.whole = self.tail.astype(I32)
        self.pos = self.whole[3:4, :]
        owner = right(self.whole[2:3, :], 2)
        offset = owner - me
        offset = jnp.where(offset > parts // 2, offset - parts, offset)
        offset = jnp.where(offset < -(parts // 2), offset + parts, offset)
        column = right(cell, height.bit_length() - 1)
        row = cell & (height - 1)
        at = offset * columns + column + HALO
        self.addr = jnp.where(
            (at >= 0) & (at < wide),
            (right(row, 7) * wide + at) * LANES + (row & (LANES - 1)),
            (height // LANES) * wide * LANES,
        )
        at_row = row - (block * me - PAD)
        across = owner * columns + column
        self.rows = jnp.where(
            (at_row >= 0) & (at_row < high_rows) & (owner < parts),
            (right(across, 7) * high_rows + at_row) * LANES + (across & (LANES - 1)),
            (columns * parts // LANES) * high_rows * LANES,
        )
        self.owner = jnp.minimum(owner, parts - 1)
        self.back = self.owner * (senders * capacity) + sender * capacity + self.pos


def stack_of(addr, weights, tail, back):
    hold = addr.shape[1]
    rows = [
        (addr & (LANES - 1)).astype(F32),
        weights,
        tail,
        right(addr, 7).astype(F32),
        back.astype(F32),
        jnp.zeros((7, hold), F32),
    ]
    return jnp.concatenate(split3(jnp.concatenate(rows, axis=0)), axis=1)


def gathered(stack, chosen):
    select = jnp.where(chosen, 1.0, 0.0).astype(BF)
    return nt(stack, jnp.concatenate([select] * 3, axis=1))


def merge_lines(block, nowhere, stencil, extra):
    number = iota((stencil, LANES), 0).astype(F32)
    line = block[CODES : CODES + stencil, :]
    leader = jnp.zeros(line.shape, F32)
    for k in reversed(range(stencil)):
        leader = jnp.where(line == line[k : k + 1, :], float(k), leader)
    leads = jnp.where(leader == number, 1.0, 0.0)
    count = jnp.zeros((1, LANES), F32)
    ranks = []
    for k in range(stencil):
        ranks.append(count)
        count = count + leads[k : k + 1, :]
    place = jnp.zeros(line.shape, F32)
    for k in range(stencil):
        place = jnp.where(leader == float(k), ranks[k], place)
    lists = []
    for k in range(stencil):
        found = jnp.where((leads > 0.0) & (place == float(k)), line, 0.0)
        found = jnp.sum(found, axis=0, keepdims=True)
        lists.append(jnp.where(count > float(k), found, nowhere))
    batches = right(count.astype(I32) + (BATCH - 1), BATCH.bit_length() - 1)
    most = jnp.zeros((1, LANES), F32)
    slot = iota((1, LANES), 1)
    for begin in range(0, LANES, BLOCK):
        here = (slot >= begin) & (slot < begin + BLOCK)
        found = jnp.max(jnp.where(here, batches.astype(F32), 0.0), axis=1, keepdims=True)
        most = jnp.where(here, found, most)
    back = block[CODES + stencil : CODES + stencil + 1, :]
    ints = [jnp.concatenate(lists, axis=0).astype(I32), batches]
    ints += [most.astype(I32), back.astype(I32)] + extra
    ints = jnp.concatenate(ints, axis=0)
    ints = jnp.concatenate([ints, jnp.zeros((stencil + 8 - ints.shape[0], LANES), I32)], axis=0)
    rows = [
        block[0:CODES, :],
        place * float(LANES) + block[0:stencil, :],
        jnp.zeros((LANES - CODES - stencil, LANES), F32),
    ]
    return ints, jnp.concatenate(rows, axis=0).T


def unpack_kernel(
    meta, recv, _, ints, floats, own_lines, own, total, *, layout, group, **sizes
):
    senders, _, hold = recv.shape
    lines = hold // LANES
    me = meta[0]
    parts, stencil, capacity = sizes["parts"], sizes["stencil"], sizes["capacity"]
    wide = sizes["columns"] + 2 * HALO
    slots = senders * capacity

    def put(ref, place, sender, value):
        begin, size = place
        count = value.shape[0]
        for i in range(lines):
            part = value[:, i * LANES : (i + 1) * LANES]
            if count % 8 == 0:
                at = pl.multiple_of(begin + sender * size + i * count, 8)
                ref[pl.ds(at, count), :] = part
            else:
                for j in range(count):
                    ref[pl.ds(begin + sender * size + i + j * lines, 1), :] = part[j : j + 1]

    total[...] = jnp.zeros(total.shape, F32)
    place = iota((LANES, hold), 0)
    index = iota((LANES, hold), 1)
    lane = iota((1, LANES), 1)
    halo_block = slots // LANES
    after = lax.rem(me + 1, parts)
    ahead = lax.rem(me + parts - 1, parts)

    def per_sender(sender, carry):
        halo_before, amounts = carry
        got = Received(recv, sender, me, **sizes)
        weights = recv[sender, stencil : 2 * stencil, :]
        within = lax.rem(sender, group) * capacity + got.pos
        put(ints, layout.ints["addr"], sender, got.addr)
        put(ints, layout.ints["rows"], sender, got.rows)
        put(ints, layout.ints["listed"], sender, got.whole[4:5, :])
        put(ints, layout.ints["slot"], sender, got.owner * (group * capacity) + within)
        put(ints, layout.ints["start"], sender, got.whole[5:8, :])
        put(floats, layout.floats["wgt"], sender, weights)
        put(floats, layout.floats["val"], sender, got.tail[0:1, :])

        def bound(line, half, owner):
            part = got.whole[5 + line : 6 + line, half * LANES : (half + 1) * LANES]
            return jnp.sum(jnp.where(lane == owner, part, 0), axis=1, keepdims=True)

        stack = stack_of(got.addr, weights, got.tail, got.back)

        begin, end = bound(0, 0, me), bound(0, 1, me)
        first_slot = sender * capacity
        block_of = first_slot // LANES
        within = place - (first_slot - block_of * LANES)
        chosen = (within >= 0) & (index == begin + within) & (index < end)
        shift = first_slot - block_of * LANES
        here = (lane >= shift) & (lane < shift + (end - begin))
        total[block_of] = jnp.where(here, gathered(stack, chosen), total[block_of])
        amounts = jnp.where(lane == sender, end - begin, amounts)

        first_r, last_r = bound(1, 0, after), bound(1, 1, after)
        first_l, last_l = bound(2, 0, ahead), bound(0, 1, ahead)
        middle = halo_before + (last_r - first_r)
        chosen_r = (index >= first_r) & (index < last_r) & (index - first_r + halo_before == place)
        chosen_l = (index >= first_l) & (index < last_l) & (index - first_l + middle == place)
        halo_after = middle + (last_l - first_l)
        here = (lane >= halo_before) & (lane < halo_after)
        values = gathered(stack, chosen_r | chosen_l)
        total[halo_block] = jnp.where(here, values, total[halo_block])
        return halo_after, amounts

    halo_count, amounts = lax.fori_loop(
        0,
        senders,
        per_sender,
        (jnp.zeros((1, 1), I32), jnp.zeros((1, LANES), I32)),
        unroll=senders <= GROUP,
    )
    extra = [amounts, jnp.broadcast_to(halo_count, (1, LANES))]
    nowhere = float((sizes["height"] // LANES) * wide)
    for i in range(slots // LANES + 1):
        top = i * (stencil + 8)
        own_lines[top : top + stencil + 8, :], own[i * LANES : (i + 1) * LANES, :] = merge_lines(
            total[i], nowhere, stencil, extra
        )


def list_kernel(meta, recv, _, row_lines, row_data, total, **sizes):
    senders, _, hold = recv.shape
    stencil = sizes["stencil"]
    high_rows = sizes["height"] // sizes["parts"] + 2 * PAD
    place = iota((LISTED, hold), 0)
    total[...] = jnp.zeros(total.shape, F32)

    def per_sender(sender, before):
        got = Received(recv, sender, meta[0], **sizes)
        marks = got.whole[4:5, :]
        zeros = jnp.zeros((stencil, hold), F32)
        tail = jnp.concatenate([got.tail[0:1, :], zeros[0:7, :]], axis=0)
        stack = stack_of(got.rows, zeros, tail, got.back)
        values = gathered(stack, (marks > 0) & (marks - 1 + before == place))
        after = before + got.whole[7:8, hold - 1 : hold]
        slot = iota((1, LISTED), 1)
        total[...] = jnp.where((slot >= before) & (slot < after), values, total[...])
        return after

    count = lax.fori_loop(
        0, senders, per_sender, jnp.zeros((1, 1), I32), unroll=senders <= GROUP
    )
    nowhere = float((sizes["columns"] * sizes["parts"] // LANES) * high_rows)
    for i in range(LISTED // LANES):
        top = i * (stencil + 8)
        block = total[:, i * LANES : (i + 1) * LANES]
        (
            row_lines[top : top + stencil + 8, :],
            row_data[i * LANES : (i + 1) * LANES, :],
        ) = merge_lines(block, nowhere, stencil, [jnp.broadcast_to(count, (1, LANES))])


class RowCopies:
    def __init__(self, source, target, room, table, sems, stencil):
        half = 2 * BATCH * room
        self.always = pltpu.make_async_copy(
            source.at[pl.ds(0, half), :], target.at[pl.ds(0, half), :], sems[0]
        )
        size = source.shape[0] - half
        self.seldom = pltpu.make_async_copy(
            source.at[pl.ds(half, size), :], target.at[pl.ds(half, size), :], sems[1]
        )
        self.table, self.room, self.stencil = table, room, stencil

    def rest(self):
        most = word_of(self.table, 0, self.stencil + 1, self.stencil)
        for top in range(BLOCK, self.room, BLOCK):
            most = jnp.maximum(most, word_of(self.table, top, self.stencil + 1, self.stencil))
        return most > 2

    def run_rest(self):
        @pl.when(self.rest())
        def _():
            self.seldom.start()
            self.seldom.wait()


def word_of(table, slot, k, stencil):
    at = lax.shift_right_logical(slot, 7) * ((stencil + 7) * LANES) + slot
    return table[at + k * LANES]


def columns_of(info, begin, stencil):
    return [jnp.broadcast_to(info[:, begin + k : begin + k + 1], info.shape) for k in range(stencil)]


def weight_rows(info, places, stencil):
    lane_f = iota(info.shape, 1).astype(F32)
    codes = columns_of(info, CODES, stencil)
    weights = columns_of(info, stencil, stencil)
    rows = []
    for place in range(stencil):
        row = jnp.zeros(info.shape, F32)
        if place < places:
            at = lane_f + float(LANES * place)
            for k in range(place, stencil):
                term = jnp.where(at == codes[k], weights[k], 0.0)
                row = term if k == place else row + term
        rows.append(row)
    return rows


def block_at(table, top, stencil, action):
    top = pl.multiple_of(top, 8)
    most = word_of(table, top, stencil + 1, stencil)

    @pl.when(most <= 1)
    def _():
        action(top, BATCH)

    @pl.when(most == 2)
    def _():
        action(top, 2 * BATCH)

    @pl.when(most > 2)
    def _():
        action(top, stencil)


def blocks_of(table, top, amount, stencil, action):
    def step(i, carry):
        block_at(table, top + i * BLOCK, stencil, action)
        return carry

    lax.fori_loop(0, lax.div(amount + (BLOCK - 1), BLOCK), step, 0)


def factor_kernel(
    lines_h, data, replies, _, merged_h, mixed, lines_s, table, merged, sems, *, stencil, slots
):
    parts = replies.shape[0]
    lines = slots // LANES
    lines_copy = pltpu.make_async_copy(lines_h, lines_s, sems.at[0])
    lines_copy.start()

    def per_owner(owner, carry):
        for i in range(lines):
            rows = [
                jnp.zeros((stencil, LANES), F32),
                replies[owner, pl.ds(8 + i, stencil, stride=lines), :],
                jnp.zeros((1, LANES), F32),
                replies[owner, i : i + 1, :],
                jnp.zeros((LANES - 2 * stencil - 2, LANES), F32),
            ]
            at = pl.multiple_of(owner * slots + i * LANES, LANES)
            table[pl.ds(at, LANES), :] = jnp.concatenate(rows, axis=0).T
        return carry

    lax.fori_loop(0, parts, per_owner, 0, unroll=parts <= GROUP)
    lines_copy.wait()
    count = jnp.minimum(lines_s[(stencil + 3) * LANES], LISTED)

    def mix(numbers, weights):
        for slot in numbers:
            back = word_of(lines_s, slot, stencil + 2, stencil)
            mixed[pl.ds(slot, 1), :] = data[pl.ds(slot, 1), :] + table[pl.ds(back, 1), :]

    quads(0, count, mix)

    def build(top, places):
        rows = weight_rows(mixed[pl.ds(top, BLOCK), :], places, stencil)
        for place, row in enumerate(rows):
            merged[pl.ds(place * LISTED + top, BLOCK), :] = row

    blocks_of(lines_s, 0, count, stencil, build)
    copies = RowCopies(
        merged, merged_h, LISTED, lines_s, (sems.at[1], sems.at[2]), stencil
    )
    copies.always.start()
    copies.run_rest()
    copies.always.wait()


def most_batches(table, slots, stencil):
    most = word_of(table, slots[0], stencil, stencil)
    for slot in slots[1:]:
        most = jnp.maximum(most, word_of(table, slot, stencil, stencil))
    return most


def scatter_slots(table, merged, room, copies, slots, values, stencil):
    def batch(begin):
        for first in range(0, len(slots), len(copies)):
            todo = []
            some = slice(first, first + len(copies))
            for slot, value, ref in zip(slots[some], values[some], copies):
                for j in range(BATCH):
                    line = word_of(table, slot, begin + j, stencil)
                    row = merged[pl.ds((begin + j) * room + slot, 1), :] * value
                    todo.append((ref, line, ref[pl.ds(line, 1), :] + row))
            for ref, line, row in todo:
                ref[pl.ds(line, 1), :] = row

    def more(i, carry):
        batch(i * BATCH)
        return carry

    batch(0)
    lax.fori_loop(1, most_batches(table, slots, stencil), more, 0)


def band(shape, taps, shift):
    distance = iota(shape, 1) - iota(shape, 0) + shift
    result = jnp.zeros(shape, F32)
    for tap in range(taps.shape[0]):
        result = jnp.where(distance == tap, taps[tap], result)
    return result


def band_rev(shape, taps, shift):
    distance = iota(shape, 0) - iota(shape, 1) + shift
    result = jnp.zeros(shape, F32)
    for tap in range(taps.shape[0]):
        result = jnp.where(distance == tap, taps[tap], result)
    return result


def exact_nt(a, b):
    return lax.dot_general(
        a,
        b,
        (((1,), (1,)), ((), ())),
        precision=lax.Precision.HIGHEST,
        preferred_element_type=F32,
    )


def store_split(ref, index, value):
    high, low = split2(value)
    ref[(0,) + index] = high
    ref[(1,) + index] = low


def bands_kernel(kx, ky, lat2, lon2, lat1, lon1, *, rows_block):
    margin = kx.shape[0] // 2
    window = lat2.shape[2]
    first = band((window, window), ky, margin)
    reach = first[LANES : LANES + WIDE, :]
    place = iota((window, window), 1)
    for variant in range(3):
        kept = first
        if variant == 0:
            kept = jnp.where(place >= LANES, first, 0.0)
        if variant == 2:
            kept = jnp.where(place < LANES + WIDE, first, 0.0)
        store_split(lat2, (variant,), exact_nt(kept, reach))
    size = lon2.shape[1]
    wide = size + 2 * HALO
    depth = (wide + 32 + LANES - 1) // LANES * LANES
    second = band((wide, depth), kx, -(16 - margin))
    store_split(lon2, (), exact_nt(second[HALO : HALO + size, :], second))
    store_split(lat1, (), band_rev((rows_block, rows_block + 2 * PAD), ky, PAD + margin))
    store_split(lon1, (), band((2 * WIDE, WIDE), kx, LANES + margin))


def pairs(low, high, action):
    def step(i, carry):
        one = low + 2 * i
        action(one, jnp.minimum(one + 1, high - 1), one + 1 < high)
        return carry

    lax.fori_loop(0, lax.shift_right_logical(high - low + 1, 1), step, 0)


def quads(low, high, action):
    def step(i, carry):
        one = low + 4 * i
        numbers = [one] + [jnp.minimum(one + j, high - 1) for j in range(1, 4)]
        weights = [None] + [jnp.where(one + j < high, 1.0, 0.0) for j in range(1, 4)]
        action(numbers, weights)
        return carry

    lax.fori_loop(0, lax.shift_right_logical(high - low + 3, 2), step, 0)


def weighted(value, weight):
    return value if weight is None else value * weight


def zero_all(refs):
    rows = refs[0].shape[0]
    step = 256

    def clear(i, carry):
        for ref in refs:
            ref[pl.ds(pl.multiple_of(i * step, 8), step), :] = jnp.zeros((step, LANES), F32)
        return carry

    whole = rows // step
    lax.fori_loop(0, whole, clear, 0)
    if rows % step:
        for ref in refs:
            ref[whole * step : rows, :] = jnp.zeros((rows % step, LANES), F32)


def scatter_entries(copies, entries, lane):
    for start in range(0, len(entries), len(copies)):
        group = []
        for ref, (address, value) in zip(copies, entries[start : start + len(copies)]):
            line = lax.shift_right_logical(address, 7)
            spread = jnp.where(lane == (address & (LANES - 1)), value, 0.0)
            group.append((ref, line, ref[pl.ds(line, 1), :] + spread))
        for ref, line, value in group:
            ref[pl.ds(line, 1), :] = value


def spot(sender, idx, per, stencil):
    return sender * per + idx + lax.shift_right_logical(idx, 7) * ((stencil - 1) * LANES)


def copy_parts(layout, source, target, place, chunk, chunks, group, sem):
    begin, size = place
    words = group * size * LANES
    at = begin * LANES + chunk * words
    return pltpu.make_async_copy(source.at[pl.ds(at, words)], target, sem)


def apply_kernel(
    *refs, first, layout, columns, height, hold, stencil, capacity, senders, parts, levels
):
    refs = list(refs)

    def take(count):
        taken = refs[:count]
        del refs[:count]
        return taken

    meta, ints, floats, own_lines, own = take(5)
    if not first:
        replies_h, replies = take(2)
    std_h, std_l_h, std_r_h, lat2_h, lon2_h = take(5)
    if not first:
        merged_h, _ = take(2)
    field_h, send = take(2)
    if first:
        info_out, merged_h = take(2)
    addr, wgt, start, lines_s, val = take(5)
    if first:
        std_flat, picked, chosen = take(3)
    scale, merged, sums, high_s, low_s, std, std_l, std_r, lat2, lon2, field = take(11)
    copies = take(PAIR)
    sems, in_sems, out_sems, val_sem = take(4)

    me = meta[0]
    wide = columns + 2 * HALO
    blocks = height // LANES
    group = min(GROUP, senders)
    chunks = senders // group
    slots = senders * capacity
    lane = iota((1, LANES), 1)
    per = stencil * hold
    table = layout.table

    def chunk_copies(chunk):
        todo = [
            (ints, addr, layout.ints["addr"]),
            (floats, wgt, layout.floats["wgt"]),
            (ints, start, layout.ints["start"]),
        ]
        if first:
            todo.append((floats, val, layout.floats["val"]))
        return [
            copy_parts(layout, source, target, place, chunk, chunks, group, sems.at[i])
            for i, (source, target, place) in enumerate(todo)
        ]

    def load_chunk(chunk):
        for copy in chunk_copies(chunk):
            copy.start()
        for copy in chunk_copies(chunk):
            copy.wait()

    operands = [
        pltpu.make_async_copy(source, target, in_sems.at[i])
        for i, (source, target) in enumerate(
            (
                (std_h, std),
                (std_l_h, std_l),
                (std_r_h, std_r),
                (lat2_h, lat2),
                (lon2_h, lon2),
            )
        )
    ]
    own_copy = pltpu.make_async_copy(own_lines, lines_s, in_sems.at[5])
    own_copy.start()
    merged_copies = RowCopies(
        *((merged, merged_h) if first else (merged_h, merged)),
        slots + LANES,
        lines_s,
        (in_sems.at[6], in_sems.at[7]),
        stencil,
    )
    if not first:
        merged_copies.always.start()
    for copy in operands:
        copy.start()

    def value_copy(owner):
        at = pl.multiple_of(owner * (replies_h.shape[0] // parts), 1024)
        return pltpu.make_async_copy(
            replies_h.at[pl.ds(at, slots)], val.at[pl.ds(owner * slots, slots)], val_sem.at[owner]
        )

    def each_owner(action):
        def step(owner, carry):
            action(value_copy(owner))
            return carry

        lax.fori_loop(0, parts, step, 0)

    if not first:
        each_owner(lambda copy: copy.start())
    zero_all(copies)
    zero_all([sums])

    lane_of = iota((slots, LANES), 1)
    room = slots + LANES
    column = 2 * stencil if first else 2 * stencil + 2
    scale[...] = jnp.broadcast_to(own[:, column : column + 1], (room, LANES))
    known = own[0:slots, :]
    own_copy.wait()
    if not first:
        merged_copies.always.wait()
        merged_copies.run_rest()

    after = lax.rem(me + 1, parts)
    ahead = lax.rem(me + parts - 1, parts)

    def start_of(sender, owner, row, half):
        return start[sender * table + row * hold + half * LANES + owner]

    def entries_of(sender, idx, value):
        base = spot(sender, idx, per, stencil)
        return [
            (addr[base + k * LANES], wgt[base + k * LANES] * value) for k in range(stencil)
        ]

    def own_line(slot, k):
        return word_of(lines_s, slot, k, stencil)

    def amount_of(sender):
        return lines_s[(stencil + 3) * LANES + sender]

    halo_count = lines_s[(stencil + 4) * LANES]
    halo_fits = halo_count <= LANES

    def own_groups(action, halo):
        if capacity % BLOCK:
            blocks_of(lines_s, 0, slots, stencil, action)
        else:

            def per_sender(sender, carry):
                blocks_of(lines_s, sender * capacity, amount_of(sender), stencil, action)
                return carry

            lax.fori_loop(0, senders, per_sender, 0)
        if halo:
            blocks_of(lines_s, slots, jnp.minimum(halo_count, LANES), stencil, action)

    def build(top, places):
        rows = weight_rows(own[pl.ds(top, BLOCK), :], places, stencil)
        for place, row in enumerate(rows):
            merged[pl.ds(place * room + top, BLOCK), :] = row

    if first:
        own_groups(build, True)
        merged_copies.always.start()
        merged_copies.run_rest()

    def own_quads(action):
        def per_sender(sender, carry):
            base = sender * capacity
            quads(base, base + amount_of(sender), action)
            return carry

        lax.fori_loop(0, senders, per_sender, 0)

    def scatter_known(numbers, weights):
        values = [weighted(scale[pl.ds(i, 1), :], w) for i, w in zip(numbers, weights)]
        scatter_slots(lines_s, merged, room, copies, numbers, values, stencil)

    def scatter_sent(numbers, weights):
        values = [weighted(val[own_line(i, stencil + 2)], w) for i, w in zip(numbers, weights)]
        scatter_slots(lines_s, merged, room, copies, numbers, values, stencil)

    def scatter_halo(chunk):
        def per_sender(sender, carry):
            for owner, low, high in ((after, (1, 0), (1, 1)), (ahead, (2, 0), (0, 1))):
                begin = start_of(sender, owner, 0, 0)

                def value_of(idx, owner=owner, begin=begin):
                    if first:
                        return val[sender * hold + idx]
                    place = (chunk * group + sender) * capacity + idx - begin
                    return val[owner * slots + place]

                def action(one, two, has_two, value_of=value_of):
                    second = jnp.where(has_two, value_of(two), 0.0)
                    scatter_entries(
                        copies,
                        entries_of(sender, one, value_of(one)) + entries_of(sender, two, second),
                        lane,
                    )

                pairs(start_of(sender, owner, *low), start_of(sender, owner, *high), action)
            return carry

        lax.fori_loop(0, group, per_sender, 0)

    own_quads(scatter_known)
    if not first:
        each_owner(lambda copy: copy.wait())

    @pl.when(halo_fits)
    def _():
        quads(slots, slots + halo_count, scatter_known if first else scatter_sent)

    @pl.when(jnp.logical_not(halo_fits))
    def _():
        def step(chunk, carry):
            load_chunk(chunk)
            scatter_halo(chunk)
            return carry

        lax.fori_loop(0, chunks, step, 0)

    for copy in operands:
        copy.wait()

    def prepare(jb):
        lanes = slice(jb * LANES, (jb + 1) * LANES)
        for low, size, source in (
            (0, HALO, std_l),
            (HALO, columns, std),
            (HALO + columns, HALO, std_r),
        ):
            rows = slice(jb * wide + low, jb * wide + low + size)
            total = copies[0][rows, :]
            for ref in copies[1:]:
                total = total + ref[rows, :]
            high, lo = split2(total * source[:, lanes])
            high_s[low : low + size, lanes] = high
            low_s[low : low + size, lanes] = lo
        if first:
            std_flat[jb * wide + HALO : jb * wide + HALO + columns, :] = std[:, lanes]

    smoothed = copies[0]
    size = lon2.shape[1]
    count = height // WIDE
    outgoing = [merged_copies.always] if first else []

    def along_latitude(block):
        variant = 0 if block == 0 else (2 if block == count - 1 else 1)
        low = max(block * WIDE - LANES, 0)
        high = min(block * WIDE + WIDE + LANES, height)
        inner = slice(low - (block * WIDE - LANES), high - (block * WIDE - LANES))
        matrix = (lat2[0, variant, inner, :], lat2[1, variant, inner, :])
        return split2(mm_parts((high_s[:, low:high], low_s[:, low:high]), matrix))

    def along_longitude(block, parts_y):
        lanes = slice(block * WIDE, (block + 1) * WIDE)
        for begin in range(0, columns, size):
            some = min(size, columns - begin)
            rows = slice(begin, begin + some)
            window = slice(begin, begin + some + 2 * HALO)
            matrix = tuple(lon2[i, 0:some, 0 : some + 2 * HALO] for i in range(2))
            result = mm_parts(matrix, (parts_y[0][window, :], parts_y[1][window, :]))
            scaled = result * std[rows, lanes]
            field[rows, lanes] = scaled
            for half in range(WIDE // LANES):
                top = (block * (WIDE // LANES) + half) * wide + HALO + begin
                smoothed[top : top + some, :] = scaled[:, half * LANES : (half + 1) * LANES]
        outgoing.append(
            pltpu.make_async_copy(field.at[:, lanes], field_h.at[:, lanes], out_sems.at[block])
        )
        outgoing[-1].start()

    ready = 0
    waiting = None
    for block in range(count + 1):
        upto = min((block + 1) * (WIDE // LANES) + 1, blocks)
        for jb in range(ready, upto):
            prepare(jb)
        ready = max(ready, upto)
        following = along_latitude(block) if block < count else None
        if block > 0:
            along_longitude(block - 1, waiting)
        waiting = following

    def gather_quad(numbers, weights):
        def batch(begin, totals):
            result = []
            for slot, total in zip(numbers, totals):
                terms = []
                for j in range(BATCH):
                    line = own_line(slot, begin + j)
                    row = merged[pl.ds((begin + j) * room + slot, 1), :]
                    terms.append(row * smoothed[pl.ds(line, 1), :])
                    if first:
                        picked[pl.ds((begin + j) * room + slot, 1), :] = std_flat[
                            pl.ds(line, 1), :
                        ]
                result.append(total + ((terms[0] + terms[1]) + (terms[2] + terms[3])))
            return tuple(result)

        zero = jnp.zeros((1, LANES), F32)
        totals = lax.fori_loop(
            1,
            most_batches(lines_s, numbers, stencil),
            lambda i, totals: batch(i * BATCH, totals),
            batch(0, (zero,) * len(numbers)),
        )
        for slot, total in zip(numbers, totals):
            sums[pl.ds(slot, 1), :] = total

    own_quads(gather_quad)

    def pick(top, places):
        info = own[pl.ds(top, BLOCK), :]
        codes = columns_of(info, CODES, stencil)
        lane_f = iota(info.shape, 1).astype(F32)
        rows = [picked[pl.ds(place * room + top, BLOCK), :] for place in range(places)]
        result = jnp.zeros((BLOCK, LANES), F32)
        for k in range(stencil):
            cell = jnp.zeros((BLOCK, LANES), F32)
            for place in range(min(k + 1, places)):
                at = lane_f + float(LANES * place)
                cell = jnp.where(at == codes[k], rows[place], cell)
            cell = jnp.sum(cell, axis=1, keepdims=True)
            result = jnp.where(lane_f == float(stencil + k), cell, result)
        chosen[pl.ds(top, BLOCK), :] = result * info

    if first:
        own_groups(pick, False)

    def whole(x):
        return jnp.sum(x, axis=0, keepdims=True)

    total = jnp.sum(sums[...], axis=1, keepdims=True)
    lines = slots // LANES
    known = own[0:slots, :]
    source, weight, reply, image0 = (
        known[:, 2 * stencil + i : 2 * stencil + i + 1] for i in range(4)
    )
    if first:
        reply = weight * total
        known = jnp.where(lane_of == 2 * stencil + 2, reply, known)
        known = jnp.where(lane_of == 2 * stencil + 3, total, known)
        info_out[0:slots, :] = known
        info_out[slots:room, :] = own[slots:room, :]
        turned = known.T[2 * stencil + 2 : 2 * stencil + 3, :]
        message = [turned[:, i * LANES : (i + 1) * LANES] for i in range(lines)]
        message.append(
            jnp.where(
                lane == 0, whole(source * total), jnp.where(lane == 1, whole(reply * total), 0.0)
            )
        )
        message.append(jnp.zeros((8 - len(message), LANES), F32))
        factors = chosen[...].T
        for k in range(stencil):
            row = factors[stencil + k : stencil + k + 1, :]
            message += [row[:, i * LANES : (i + 1) * LANES] for i in range(lines)]
        message = jnp.concatenate(message, axis=0)
    else:
        slab = jnp.sum(replies[:, 0:8, :], axis=0)[lines : lines + 1, :]
        length = slab[:, 0:1] / (slab[:, 0:1] + slab[:, 1:2])
        both = source + reply
        s_both = image0 + total
        resid = source - length * both
        s_resid = image0 - length * s_both
        values = [
            resid * s_resid,
            resid * s_both,
            both * s_both,
            resid * image0,
            both * image0,
            weight * s_resid * s_resid,
            weight * s_resid * s_both,
            weight * s_both * s_both,
            weight * s_resid * image0,
            weight * s_both * image0,
            source * image0,
            reply * image0,
        ]
        message = jnp.where(lane == len(values), length, 0.0)
        for i, value in enumerate(values):
            message = jnp.where(lane == i, whole(value), message)
        message = jnp.concatenate([message, jnp.zeros((7, LANES), F32)], axis=0)

    def send_to(i, carry):
        send[i] = message
        return carry

    lax.fori_loop(0, send.shape[0], send_to, 0)
    for copy in outgoing:
        copy.wait()


def final_kernel(
    ints,
    floats,
    replies_h,
    lines_h,
    merged_h,
    mixed,
    totals,
    field0_h,
    field1_h,
    lat1,
    lon1,
    control_h,
    increment_h,
    addr,
    listed,
    slot,
    val,
    factors,
    field0,
    field1,
    control,
    high_s,
    low_s,
    lines_s,
    merged,
    scale,
    *rest,
    layout,
    hold,
    stencil,
    capacity,
    senders,
    parts,
    length,
):
    copies = rest[:PAIR]
    sems, in_sems, out_sems = rest[PAIR:]
    group = min(GROUP, senders)
    chunks = senders // group
    per = stencil * hold
    rows_block = control.shape[0]
    high_rows = rows_block + 2 * PAD
    lane = iota((1, LANES), 1)
    stride = group * capacity
    owner_words = factors.shape[0] // parts
    to_factors = owner_words - stencil * stride

    def chunk_copies(chunk):
        todo = [
            (ints, addr, layout.ints["rows"]),
            (ints, listed, layout.ints["listed"]),
            (ints, slot, layout.ints["slot"]),
            (floats, val, layout.floats["val"]),
        ]
        result = [
            copy_parts(layout, source, target, place, chunk, chunks, group, sems.at[i])
            for i, (source, target, place) in enumerate(todo)
        ]
        words = parts * owner_words
        result.append(
            pltpu.make_async_copy(
                replies_h.at[pl.ds(chunk * words, words)], factors, sems.at[len(todo)]
            )
        )
        return result

    row_copies = RowCopies(
        merged_h, merged, LISTED, lines_s, (in_sems.at[3], in_sems.at[4]), stencil
    )
    listing = [pltpu.make_async_copy(lines_h, lines_s, in_sems.at[2]), row_copies.always]
    for copy in listing:
        copy.start()
    operands = [
        pltpu.make_async_copy(source, target, in_sems.at[i])
        for i, (source, target) in enumerate(
            ((field0_h, field0), (field1_h, field1))
        )
    ]
    for copy in operands:
        copy.start()

    slabs = totals.shape[1]
    every = jnp.sum(totals[...], axis=0)
    norm0 = quad0 = None
    for i in range(slabs):
        line = every[i, 0:1, :]
        a, b = line[:, 10:11], line[:, 11:12]
        norm0 = a if norm0 is None else norm0 + a
        quad0 = b if quad0 is None else quad0 + b
    step0 = norm0 / (norm0 + quad0)
    norm1 = cross = quad1 = quad01 = jnp.zeros((1, 1), F32)
    for i in range(slabs):
        line = every[i, 0:1, :]
        v = [line[:, j : j + 1] for j in range(10)]
        shift = totals[0, i, 0:1, 12:13] - step0
        norm1 = norm1 + (v[0] + shift * (2.0 * v[1] + shift * v[2]))
        cross = cross + (v[3] + shift * v[4])
        quad1 = quad1 + (v[5] + shift * (2.0 * v[6] + shift * v[7]))
        quad01 = quad01 + (v[8] + shift * v[9])
    ratio = norm1 / norm0
    curvature = norm1 + quad1 + ratio * (
        2.0 * (cross + quad01) + ratio * (norm0 + quad0)
    )
    step1 = norm1 / curvature
    first = step0 + step1 * (1.0 - step0 + ratio)
    second = -step0 * step1
    first_line = jnp.broadcast_to(first, (1, LANES))
    second_line = jnp.broadcast_to(second, (1, LANES))

    zero_all(copies)

    data = mixed[...]
    column = 2 * stencil
    scale[...] = first * data[:, column : column + 1] + second * jnp.broadcast_to(
        data[:, column + 1 : column + 2], data.shape
    )
    for copy in listing:
        copy.wait()
    row_copies.run_rest()
    count = lines_s[(stencil + 3) * LANES]

    def add(numbers, weights):
        values = [weighted(scale[pl.ds(i, 1), :], w) for i, w in zip(numbers, weights)]
        scatter_slots(lines_s, merged, LISTED, copies, numbers, values, stencil)

    def scatter_chunk():
        def per_sender(sender, carry):
            def step(idx, inner):
                @pl.when(listed[sender * hold + idx] > 0)
                def _():
                    place = slot[sender * hold + idx]
                    place = place + lax.div(place, stride) * (owner_words - stride)
                    base = spot(sender, idx, per, stencil)
                    z0 = val[sender * hold + idx]
                    value = first_line * z0 + second_line * factors[place]
                    entries = [
                        (addr[base + k * LANES], factors[place + to_factors + k * stride] * value)
                        for k in range(stencil)
                    ]
                    scatter_entries(copies, entries, lane)

                return inner

            lax.fori_loop(0, hold, step, 0)
            return carry

        lax.fori_loop(0, group, per_sender, 0)

    @pl.when(count <= LISTED)
    def _():
        quads(0, count, add)

    @pl.when(count > LISTED)
    def _():
        def step(chunk, carry):
            for copy in chunk_copies(chunk):
                copy.start()
            for copy in chunk_copies(chunk):
                copy.wait()
            scatter_chunk()
            return carry

        lax.fori_loop(0, chunks, step, 0)

    for copy in operands:
        copy.wait()
    increment = field0
    outgoing = []

    pair = WIDE // LANES
    count = length // WIDE

    def along_latitude(block):
        pieces = []
        for half in range(pair):
            rows = slice((block * pair + half) * high_rows, (block * pair + half + 1) * high_rows)
            total = copies[0][rows, :]
            for ref in copies[1:]:
                total = total + ref[rows, :]
            pieces.append(total)
        whole = split2(jnp.concatenate(pieces, axis=1))
        size = lat1.shape[1]
        for top in range(0, rows_block, size):
            window = slice(top, top + size + 2 * PAD)
            along = mm_parts((lat1[0], lat1[1]), (whole[0][window, :], whole[1][window, :]))
            high, low = split2(along)
            high_s[top : top + size, block * WIDE : (block + 1) * WIDE] = high
            low_s[top : top + size, block * WIDE : (block + 1) * WIDE] = low

    def window(ref, block):
        low, high = block * WIDE - LANES, (block + 1) * WIDE + LANES
        if low < 0:
            return jnp.concatenate([ref[:, length + low : length], ref[:, 0:high]], axis=1)
        if high > length:
            return jnp.concatenate([ref[:, low:length], ref[:, 0 : high - length]], axis=1)
        return ref[:, low:high]

    every_lanes = 4

    def send_out(source, target, block, size):
        if block % every_lanes == every_lanes - 1:
            lanes = slice((block + 1 - every_lanes) * size, (block + 1) * size)
            copy = pltpu.make_async_copy(
                source.at[:, lanes], target.at[:, lanes], out_sems.at[len(outgoing)]
            )
            copy.start()
            outgoing.append(copy)

    def combine(block):
        size = increment.shape[1] // count
        lanes = slice(block * size, (block + 1) * size)
        increment[:, lanes] = first * field0[:, lanes] + second * field1[:, lanes]
        send_out(increment, increment_h, block, size)

    def along_longitude(block):
        control[:, block * WIDE : (block + 1) * WIDE] = mm_parts(
            (window(high_s, block), window(low_s, block)), (lon1[0], lon1[1])
        )
        send_out(control, control_h, block, WIDE)

    along_latitude(count - 1)
    along_latitude(0)
    along_latitude(1)
    for block in range(count):
        if 2 <= block + 2 < count - 1:
            along_latitude(block + 2)
        combine(block)
        along_longitude(block)
    for copy in outgoing:
        copy.wait()


def body(
    background_std,
    x_kernel,
    y_kernel,
    obs_owner,
    obs_cells,
    obs_weights,
    innovation,
    obs_precision,
    obs_counts,
):
    parts = lax.axis_size("pencil")
    levels = lax.axis_size("lev")
    me = lax.axis_index("pencil")
    _, columns, height = background_std.shape
    hold, stencil = obs_cells.shape
    margin = x_kernel.shape[1] // 2
    capacity = 2 * hold // parts
    senders = parts
    slots = senders * capacity
    room = slots + LANES
    rows_block = height // parts
    length = columns * parts
    blocks = height // LANES
    wide = columns + 2 * HALO
    group = min(GROUP, senders)
    chunks = senders // group
    layout = Layout(senders, hold, stencil, parts)
    std = background_std[0]

    packed = pl.pallas_call(
        functools.partial(
            pack_kernel, parts=parts, columns=columns, height=height, margin=margin
        ),
        out_shape=jax.ShapeDtypeStruct((parts, PACK, hold), F32),
        in_specs=[smem()] + [vmem()] * 5,
        out_specs=vmem(),
        scratch_shapes=[pltpu.VMEM((parts, hold), F32)],
        compiler_params=params(),
        cost_estimate=cost(12000),
        name="pack",
    )(
        obs_counts,
        obs_owner.T,
        obs_cells.T,
        obs_weights.T,
        innovation[None, :],
        obs_precision[None, :],
    )
    recv = lax.all_to_all(packed, "pencil", split_axis=0, concat_axis=0, tiled=True)

    right_of = [(p, (p + 1) % parts) for p in range(parts)]
    left_of = [(p, (p - 1) % parts) for p in range(parts)]
    std_l = lax.ppermute(std[columns - HALO :, :], "pencil", right_of)
    std_r = lax.ppermute(std[:HALO, :], "pencil", left_of)

    size = min(columns, WIDE - 2 * HALO)
    row_size = min(rows_block, LANES)
    lat2, lon2, lat1, lon1 = pl.pallas_call(
        functools.partial(bands_kernel, rows_block=row_size),
        out_shape=[
            jax.ShapeDtypeStruct((2, 3, 2 * WIDE, WIDE), BF),
            jax.ShapeDtypeStruct((2, size, size + 2 * HALO), BF),
            jax.ShapeDtypeStruct((2, row_size, row_size + 2 * PAD), BF),
            jax.ShapeDtypeStruct((2, 2 * WIDE, WIDE), BF),
        ],
        in_specs=[smem(), smem()],
        out_specs=[vmem()] * 4,
        compiler_params=params(),
        cost_estimate=cost(100),
        name="bands",
    )(x_kernel[0], y_kernel[0])

    meta = jnp.reshape(me, (1,)).astype(I32)
    place = dict(
        parts=parts, columns=columns, height=height, capacity=capacity, stencil=stencil
    )
    ints, floats, own_lines, own = pl.pallas_call(
        functools.partial(unpack_kernel, layout=layout, group=group, **place),
        out_shape=[
            jax.ShapeDtypeStruct((layout.int_rows, LANES), I32),
            jax.ShapeDtypeStruct((layout.float_rows, LANES), F32),
            jax.ShapeDtypeStruct((room // LANES * (stencil + 8), LANES), I32),
            jax.ShapeDtypeStruct((room, LANES), F32),
        ],
        in_specs=[smem(), vmem(), hbm()],
        out_specs=[vmem()] * 4,
        scratch_shapes=[
            pltpu.VMEM((room // LANES, STACK, LANES), F32),
        ],
        compiler_params=params(),
        cost_estimate=cost(100),
        name="unpack",
    )(meta, recv, lat1)
    ints = ints.reshape(-1)
    floats = floats.reshape(-1)
    own_lines = own_lines.reshape(-1)

    acc = pltpu.VMEM((blocks * wide + 8, LANES), F32)
    column_slots = pltpu.VMEM((slots, LANES), F32)
    static = dict(
        layout=layout,
        columns=columns,
        height=height,
        hold=hold,
        stencil=stencil,
        capacity=capacity,
        senders=senders,
        parts=parts,
        levels=levels,
    )
    per = group * stencil * hold
    line = group * hold
    index_scratch = [
        pltpu.SMEM((per,), I32),
        pltpu.SMEM((per,), F32),
        pltpu.SMEM((group * layout.table,), I32),
        pltpu.SMEM((room * (stencil + 8),), I32),
    ]
    work = (
        [
            pltpu.VMEM((room, LANES), F32),
            pltpu.VMEM((stencil * room, LANES), F32),
            column_slots,
        ]
        + [pltpu.VMEM((wide, height), BF)] * 2
        + [
            pltpu.VMEM((columns, height), F32),
            pltpu.VMEM((HALO, height), F32),
            pltpu.VMEM((HALO, height), F32),
            pltpu.VMEM(lat2.shape, BF),
            pltpu.VMEM(lon2.shape, BF),
            pltpu.VMEM((columns, height), F32),
        ]
        + [acc] * PAIR
        + [
            pltpu.SemaphoreType.DMA((4,)),
            pltpu.SemaphoreType.DMA((8,)),
            pltpu.SemaphoreType.DMA((height // WIDE,)),
            pltpu.SemaphoreType.DMA((parts,)),
        ]
    )
    field_shape = jax.ShapeDtypeStruct((columns, height), F32)
    reply_rows = 8 + stencil * slots // LANES
    field0, message, info, merged = pl.pallas_call(
        functools.partial(apply_kernel, first=True, **static),
        out_shape=[
            field_shape,
            jax.ShapeDtypeStruct((parts, reply_rows, LANES), F32),
            jax.ShapeDtypeStruct((room, LANES), F32),
            jax.ShapeDtypeStruct((stencil * room, LANES), F32),
        ],
        in_specs=[smem()] + [hbm()] * 3 + [vmem()] + [hbm()] * 5,
        out_specs=[hbm()] + [vmem()] * 2 + [hbm()],
        scratch_shapes=index_scratch
        + [
            pltpu.SMEM((line,), F32),
            acc,
            pltpu.VMEM((stencil * room, LANES), F32),
            column_slots,
        ]
        + work,
        compiler_params=params(),
        name="apply_first",
    )(meta, ints, floats, own_lines, own, std, std_l, std_r, lat2, lon2)

    replies = lax.all_to_all(message, "pencil", split_axis=0, concat_axis=0, tiled=True)
    back = replies.reshape(-1)
    line_rows = LISTED // LANES * (stencil + 8)
    row_lines, row_data = pl.pallas_call(
        functools.partial(list_kernel, **place),
        out_shape=[
            jax.ShapeDtypeStruct((line_rows, LANES), I32),
            jax.ShapeDtypeStruct((LISTED, LANES), F32),
        ],
        in_specs=[smem(), vmem(), hbm()],
        out_specs=[vmem()] * 2,
        scratch_shapes=[pltpu.VMEM((STACK, LISTED), F32)],
        compiler_params=params(),
        cost_estimate=cost(4000),
        name="list_rows",
    )(meta, recv, info)
    row_lines = row_lines.reshape(-1)

    field1, sums = pl.pallas_call(
        functools.partial(apply_kernel, first=False, **static),
        out_shape=[
            field_shape,
            jax.ShapeDtypeStruct((parts * levels, 8, LANES), F32),
        ],
        in_specs=[smem()] + [hbm()] * 3 + [vmem(), hbm(), vmem()] + [hbm()] * 7,
        out_specs=[hbm(), vmem()],
        scratch_shapes=index_scratch + [pltpu.SMEM((parts * slots,), F32)] + work,
        compiler_params=params(),
        name="apply_second",
    )(
        meta,
        ints,
        floats,
        own_lines,
        info,
        back,
        replies,
        std,
        std_l,
        std_r,
        lat2,
        lon2,
        merged,
        row_data,
    )

    totals = lax.all_to_all(sums, ("pencil", "lev"), split_axis=0, concat_axis=0, tiled=True)
    totals = totals.reshape(parts, levels, 8, LANES)

    listed_rows, mixed = pl.pallas_call(
        functools.partial(factor_kernel, stencil=stencil, slots=slots),
        out_shape=[
            jax.ShapeDtypeStruct((stencil * LISTED, LANES), F32),
            jax.ShapeDtypeStruct((LISTED, LANES), F32),
        ],
        in_specs=[hbm(), vmem(), vmem(), hbm()],
        out_specs=[hbm(), vmem()],
        scratch_shapes=[
            pltpu.SMEM((line_rows * LANES,), I32),
            pltpu.VMEM((parts * slots, LANES), F32),
            pltpu.VMEM((stencil * LISTED, LANES), F32),
            pltpu.SemaphoreType.DMA((3,)),
        ],
        compiler_params=params(),
        cost_estimate=cost(8000),
        name="factor_rows",
    )(row_lines, row_data, replies, sums)

    by_chunk = back
    if chunks > 1:
        by_chunk = jnp.concatenate(
            [replies[:, : slots // LANES, :], replies[:, 8:, :]], axis=1
        ).reshape(parts, stencil + 1, chunks, group * capacity)
        by_chunk = jnp.transpose(by_chunk, (2, 0, 1, 3)).reshape(-1)
    owner_words = by_chunk.shape[0] // (chunks * parts)
    high_rows = rows_block + 2 * PAD
    acc_rows = pltpu.VMEM(((length // LANES) * high_rows + 8, LANES), F32)
    control, increment = pl.pallas_call(
        functools.partial(
            final_kernel,
            layout=layout,
            hold=hold,
            stencil=stencil,
            capacity=capacity,
            senders=senders,
            parts=parts,
            length=length,
        ),
        out_shape=[
            jax.ShapeDtypeStruct((rows_block, length), F32),
            field_shape,
        ],
        in_specs=[hbm()] * 5 + [vmem()] * 2 + [hbm()] * 2 + [vmem()] * 2,
        out_specs=[hbm()] * 2,
        scratch_shapes=[
            pltpu.SMEM((per,), I32),
            pltpu.SMEM((line,), I32),
            pltpu.SMEM((line,), I32),
            pltpu.SMEM((line,), F32),
            pltpu.SMEM((parts * owner_words,), F32),
            pltpu.VMEM((columns, height), F32),
            pltpu.VMEM((columns, height), F32),
            pltpu.VMEM((rows_block, length), F32),
            pltpu.VMEM((rows_block, length), BF),
            pltpu.VMEM((rows_block, length), BF),
            pltpu.SMEM((line_rows * LANES,), I32),
            pltpu.VMEM((stencil * LISTED, LANES), F32),
            pltpu.VMEM((LISTED, LANES), F32),
        ]
        + [acc_rows] * PAIR
        + [
            pltpu.SemaphoreType.DMA((5,)),
            pltpu.SemaphoreType.DMA((5,)),
            pltpu.SemaphoreType.DMA((1 + length // WIDE,)),
        ],
        compiler_params=params(),
        name="outputs",
    )(
        ints,
        floats,
        by_chunk,
        row_lines,
        listed_rows,
        mixed,
        totals,
        field0,
        field1,
        lat1,
        lon1,
    )
    return control[None], increment[None]


def solution(mesh):
    return jax.shard_map(
        body,
        mesh=mesh,
        in_specs=(
            P("lev", "pencil", None),
            P("lev", None),
            P("lev", None),
            P(("pencil", "lev"), None),
            P(("pencil", "lev"), None),
            P(("pencil", "lev"), None),
            P(("pencil", "lev")),
            P(("pencil", "lev")),
            P(("pencil", "lev")),
        ),
        out_specs=(P("lev", "pencil", None), P("lev", "pencil", None)),
        check_vma=False,
    )
```
